32 devices in a mesh: tile: 16 (over z, x, core), pos: 2 (over y).
Axes of the slice: x: 2, y: 2, z: 4, core: 2. Of those that a mesh axis runs over, the one named last changes fastest.
Arguments:
- tile_object: bfloat16 [16, 2, 2, 256, 256], P('tile'), may hold values from -5 to 5
- probe_modes: float32 [2, 256, 2, 256], replicated, may hold values from -6 to 6
- patterns: bfloat16 [16, 2, 2, 256, 256], P('tile', 'pos'), may hold values from 0 to 8
- offsets: int32 [16, 2, 2, 2], P('tile', 'pos'), may hold values from 0 to 255, as said below
- counts: int32 [16, 2], P('tile', 'pos'), may hold values from 0 to 2, as said below
Outputs:
- new_object: bfloat16 [16, 2, 2, 256, 256], P('tile')
- new_probe: float32 [2, 256, 2, 256], replicated
The draws below stay inside these ranges and needn't reach their ends.
Inputs may be any that keep to these rules, and one draw needn't show every extreme that they name: In each tile the 2 counts add up to exactly 2, and one device of every tile holds 2. Tiles in the last tile row have row offsets of at most 0, tiles in the last tile column column offsets of at most 0, so every patch lies inside the object. Slots past a device's count hold offsets too and are not used.
All inputs are finite; a program needn't handle non-finite values.
Results may differ from the reference program's by a relative error of at most 0.011.
Values may be sent and summed in bfloat16 or wider, within the bound.
No kernel may reach another device: no remote copies, remote signals or barrier semaphores. Data moves between devices by JAX's collectives and lax.ppermute only.
A program may use at most 64 MiB of HBM per device.

```python
import math
import jax
import jax.numpy as jnp
import numpy as np
from jax import lax

N = 256
MODES = 2
SLICES = 2
L = 256
GRID_ROWS = 4
BAL = 1
SLOTS = 2
TILES = 16
OWNERS = 2
GRID_COLS = 4
POSITIONS = 32


def draw_offsets(key, part):
    key = jax.random.fold_in(key, 17)
    tile_ids = jnp.arange(TILES, dtype=jnp.int32)
    last_row = tile_ids // GRID_COLS == GRID_ROWS - 1
    last_col = tile_ids % GRID_COLS == GRID_COLS - 1
    row_limit = jnp.where(last_row, L - N + 1, L).astype(jnp.int32)[:, None, None]
    col_limit = jnp.where(last_col, L - N + 1, L).astype(jnp.int32)[:, None, None]
    key_rows, key_cols = jax.random.split(key)
    rows_drawn = jax.random.randint(key_rows, (TILES, OWNERS, SLOTS), 0, row_limit, dtype=jnp.int32)
    cols_drawn = jax.random.randint(key_cols, (TILES, OWNERS, SLOTS), 0, col_limit, dtype=jnp.int32)
    placed = jnp.stack([rows_drawn, cols_drawn], axis=-1)
    placed = placed.at[0, 0, 0].set(L - 1)
    placed = placed.at[TILES - 1, 0, 0].set(0)
    return placed


def draw_counts(key, part):
    key = jax.random.fold_in(key, 29)
    cell_count = (OWNERS - 1) * SLOTS
    spread_rest = BAL * (OWNERS - 2)

    def one_tile(tile_key):
        key_order, key_busy = jax.random.split(tile_key)
        cell_order = jax.random.permutation(key_order, cell_count)
        chosen = (cell_order < spread_rest).astype(jnp.int32)
        others = jnp.sum(chosen.reshape(OWNERS - 1, SLOTS), axis=1).astype(jnp.int32)
        filled = jnp.concatenate([jnp.full((1,), SLOTS, jnp.int32), others])
        busy_owner = jax.random.randint(key_busy, (), 0, OWNERS, dtype=jnp.int32)
        owner_spots = (jnp.arange(OWNERS, dtype=jnp.int32) - busy_owner) % OWNERS
        return jnp.take(filled, owner_spots)
    return jax.vmap(one_tile)(jax.random.split(key, TILES))


def level_of(rng, dims, shards, smallest, largest):
    level = 1.0
    for dim, blocks in shards:
        draws = jax.random.uniform(jax.random.fold_in(jax.random.fold_in(rng, 6), dim), (blocks,), jnp.float32, smallest / len(shards), largest / len(shards))
        level = level * jnp.repeat(jnp.exp(draws), dims[dim] // blocks).reshape((-1,) + (1,) * (len(dims) - 1 - dim))
    return level


def centred(rng, shape, scale, most, cuts=(), kind=jnp.bfloat16):
    values = scale * jax.random.normal(rng, shape, jnp.float32)
    if cuts:
        values = values * level_of(rng, shape, cuts, -0.22, 0.18)
    return jnp.clip(values, -most, most).astype(kind)


def setup_inputs(seed: int = 0) -> dict:
    keys = jax.random.split(jax.random.key(seed), 6)
    tile_object = centred(keys[0], (TILES, SLICES, 2, L, L), 0.7, 5.0, ((0, 16),))
    probe_modes = centred(keys[1], (2, N, MODES, N), 1.0, 6.0, (), jnp.float32)
    patterns = jnp.clip(8.0 * jax.random.uniform(keys[2], (TILES, OWNERS, SLOTS, N, N), jnp.float32) ** level_of(keys[2], (TILES, OWNERS, SLOTS, N, N), ((0, 16), (1, 2)), -0.2, 0.2), 0.0, 8.0).astype(jnp.bfloat16)
    offsets = draw_offsets(jax.random.fold_in(keys[5], 71), 0)
    counts = draw_counts(jax.random.fold_in(keys[5], 71), 0)
    return {"tile_object": tile_object, "probe_modes": probe_modes, "patterns": patterns, "offsets": offsets, "counts": counts}


fresnel_coeff = 0.25
object_rate = 0.05
probe_rate = 0.15

def real_embed(part_re, part_im):
    upper_half = np.concatenate([part_re, -part_im], axis=1)
    lower_half = np.concatenate([part_im, part_re], axis=1)
    stacked = np.concatenate([upper_half, lower_half], axis=0)
    return jnp.asarray(stacked, dtype=jnp.float32).astype(jnp.bfloat16)

def build_tables(pixels):
    indices = np.arange(pixels)
    angles = indices[:, None] * indices[None, :] % pixels * (2.0 * math.pi / pixels)
    norm_scale = 1.0 / math.sqrt(pixels)
    dft_re = np.cos(angles) * norm_scale
    dft_im = -np.sin(angles) * norm_scale
    frequency = np.where(indices < pixels // 2, indices, indices - pixels)
    phases = -2.0 * math.pi * fresnel_coeff / pixels * (frequency * frequency)
    phase_sum = phases[:, None] + angles
    kern_re = np.sum(np.cos(phase_sum), axis=0) / pixels
    kern_im = np.sum(np.sin(phase_sum), axis=0) / pixels
    lag_index = (indices[:, None] - indices[None, :]) % pixels
    prop_re = kern_re[lag_index]
    prop_im = kern_im[lag_index]
    return (real_embed(prop_re, prop_im), real_embed(prop_re, -prop_im), real_embed(dft_re, dft_im), real_embed(dft_re, -dft_im))

def transform(matrix, wave_now):
    pixels = wave_now.shape[1]
    mode_count = wave_now.shape[2]
    flat_wave = wave_now.astype(jnp.bfloat16).reshape(2 * pixels, mode_count * pixels)
    first_pass = jnp.dot(matrix, flat_wave, preferred_element_type=jnp.float32)
    first_pass = first_pass.astype(jnp.bfloat16).reshape(2, pixels, mode_count, pixels).astype(jnp.float32)
    table_re = matrix[:pixels, :pixels].astype(jnp.float32)
    table_im = matrix[pixels:, :pixels].astype(jnp.float32)
    out_re = jnp.einsum('rmc,dc->rmd', first_pass[0], table_re) - jnp.einsum('rmc,dc->rmd', first_pass[1], table_im)
    out_im = jnp.einsum('rmc,dc->rmd', first_pass[0], table_im) + jnp.einsum('rmc,dc->rmd', first_pass[1], table_re)
    return jnp.stack([out_re, out_im])

def complex_mul(first, second):
    return jnp.stack([first[0] * second[0] - first[1] * second[1], first[0] * second[1] + first[1] * second[0]])

def conjugate(complex_value):
    return jnp.stack([complex_value[0], -complex_value[1]])

def position_terms(patch, probe_modes, pattern, matrices):
    depth = patch.shape[0]
    layers = [patch[layer_index][:, :, None, :] for layer_index in range(depth)]
    wave_now = complex_mul(probe_modes, layers[0])
    arrives = []
    for layer_index in range(1, depth):
        moved = transform(matrices[0], wave_now)
        arrives.append(moved)
        wave_now = complex_mul(layers[layer_index], moved)
    far_field = transform(matrices[2], wave_now)
    intensity = lax.optimization_barrier(jnp.sum(far_field[0] * far_field[0] + far_field[1] * far_field[1], axis=1))
    residual = intensity - pattern
    backward = transform(matrices[3], far_field * residual[None, :, None, :])
    slice_grads = [None] * depth
    for layer_index in range(depth - 1, 0, -1):
        slice_grads[layer_index] = lax.optimization_barrier(jnp.sum(complex_mul(conjugate(arrives[layer_index - 1]), backward), axis=2))
        backward = transform(matrices[1], complex_mul(conjugate(layers[layer_index]), backward))
    slice_grads[0] = lax.optimization_barrier(jnp.sum(complex_mul(conjugate(probe_modes), backward), axis=2))
    probe_term = complex_mul(conjugate(layers[0]), backward)
    return (jnp.stack(slice_grads), probe_term)

def reference(tile_object, probe_modes, patterns, offsets, counts):
    matrices = build_tables(N)
    rows_all = GRID_ROWS * L
    cols_all = GRID_COLS * L
    whole_object = tile_object.reshape(GRID_ROWS, GRID_COLS, SLICES, 2, L, L)
    whole_object = jnp.transpose(whole_object, (2, 3, 0, 4, 1, 5)).reshape(SLICES, 2, rows_all, cols_all)
    used_slots = OWNERS * BAL
    count_ends = jnp.cumsum(counts, axis=1).astype(jnp.int32)
    slot_rank = jnp.arange(used_slots, dtype=jnp.int32)
    source = lax.optimization_barrier(jnp.sum((count_ends[:, None, :] <= slot_rank[None, :, None]).astype(jnp.int32), axis=2)).astype(jnp.int32)
    first_used = jnp.take_along_axis(count_ends - counts, source, axis=1).astype(jnp.int32)
    within = (slot_rank[None, :] - first_used).astype(jnp.int32)
    tile_ids = jnp.broadcast_to(jnp.arange(TILES, dtype=jnp.int32)[:, None], (TILES, used_slots))
    flat_tile = tile_ids.reshape(-1)
    flat_source = source.reshape(-1)
    flat_within = within.reshape(-1)
    pos_offsets = offsets[flat_tile, flat_source, flat_within]
    pos_patterns = patterns[flat_tile, flat_source, flat_within]
    top_rows = (flat_tile // GRID_COLS * L + pos_offsets[:, 0]).astype(jnp.int32)
    left_cols = (flat_tile % GRID_COLS * L + pos_offsets[:, 1]).astype(jnp.int32)
    zero_index = jnp.zeros((), jnp.int32)

    def accumulate(totals, position):
        grad_object, grad_probe = totals
        top_row, left_col, pattern = position
        start = (zero_index, zero_index, top_row, left_col)
        patch = lax.dynamic_slice(whole_object, start, (SLICES, 2, N, N)).astype(jnp.float32)
        object_term, probe_term = position_terms(patch, probe_modes, pattern.astype(jnp.float32), matrices)
        current = lax.dynamic_slice(grad_object, start, (SLICES, 2, N, N))
        grad_object = lax.dynamic_update_slice(grad_object, current + object_term, start)
        return ((grad_object, grad_probe + probe_term), None)
    initial = (jnp.zeros((SLICES, 2, rows_all, cols_all), jnp.float32), jnp.zeros(probe_modes.shape, jnp.float32))
    (grad_object, grad_probe), _ = lax.scan(accumulate, initial, (top_rows, left_cols, pos_patterns))
    updated = (whole_object.astype(jnp.float32) - object_rate * grad_object).astype(jnp.bfloat16)
    updated = updated.reshape(SLICES, 2, GRID_ROWS, L, GRID_COLS, L)
    new_object = jnp.transpose(updated, (2, 4, 0, 1, 3, 5)).reshape(TILES, SLICES, 2, L, L)
    new_probe = probe_modes - probe_rate / math.sqrt(POSITIONS) * grad_probe
    return (new_object, new_probe)
```

```python
import functools
import math

import jax
import jax.numpy as jnp
import numpy as np
from jax import lax
from jax.experimental import pallas as pl
from jax.experimental.pallas import tpu as pltpu
from jax.sharding import PartitionSpec as P

GRID_ROWS = 4


fresnel_coeff = 0.25
object_rate = 0.05
probe_rate = 0.15

f32 = jnp.float32
bf16 = jnp.bfloat16


def from_behind(block, axis, distance):
    devices = range(lax.axis_size(axis))
    route = [(i - distance, i) for i in devices if i - distance in devices]
    return lax.ppermute(block, axis, route)


def real_embed(part_re, part_im):
    upper_half = np.concatenate([part_re, -part_im], axis=1)
    lower_half = np.concatenate([part_im, part_re], axis=1)
    stacked = np.concatenate([upper_half, lower_half], axis=0)
    return jnp.asarray(stacked, dtype=f32).astype(bf16)


def build_tables(pixels):
    indices = np.arange(pixels)
    angles = indices[:, None] * indices[None, :] % pixels * (2.0 * math.pi / pixels)
    norm_scale = 1.0 / math.sqrt(pixels)
    dft_re = np.cos(angles) * norm_scale
    dft_im = -np.sin(angles) * norm_scale
    frequency = np.where(indices < pixels // 2, indices, indices - pixels)
    phases = -2.0 * math.pi * fresnel_coeff / pixels * (frequency * frequency)
    phase_sum = phases[:, None] + angles
    kern_re = np.sum(np.cos(phase_sum), axis=0) / pixels
    kern_im = np.sum(np.sin(phase_sum), axis=0) / pixels
    lag_index = (indices[:, None] - indices[None, :]) % pixels
    prop_re = kern_re[lag_index]
    prop_im = kern_im[lag_index]
    return (
        real_embed(prop_re, prop_im),
        real_embed(prop_re, -prop_im),
        real_embed(dft_re, dft_im),
        real_embed(dft_re, -dft_im),
    )


def dot(a, b):
    return jnp.dot(a, b, preferred_element_type=f32)


def position_kernel(
    spot_ref, own_ref, right_ref, below_ref, diag_ref, probe_ref, pattern_ref, prop_ref,
    prop_c_ref, dft_ref, dft_c_ref, home_ref, next_ref, down_ref, term_ref,
):
    depth, _, n, _ = own_ref.shape
    modes = probe_ref.shape[2] // n
    row, col = spot_ref[0], spot_ref[1]
    i_out = lax.broadcasted_iota(jnp.int32, (n, 2 * n), 0)
    i_in = lax.broadcasted_iota(jnp.int32, (n, 2 * n), 1)
    take_rows = (i_in == i_out + row).astype(f32).astype(bf16)
    take_cols_t = (i_in == i_out + col).astype(f32).astype(bf16)
    j_in = lax.broadcasted_iota(jnp.int32, (2 * n, n), 0)
    j_out = lax.broadcasted_iota(jnp.int32, (2 * n, n), 1)
    take_cols = (j_in == j_out + col).astype(f32).astype(bf16)
    take_rows_t = (j_in == j_out + row).astype(f32).astype(bf16)
    wrap_cols = take_cols_t[:, :n] + take_cols_t[:, n:]

    def patch(layer, part):
        window = (layer, part)
        upper = jnp.concatenate([own_ref[window], right_ref[window]], axis=1)
        lower = jnp.concatenate([below_ref[window], diag_ref[window]], axis=1)
        rows = dot(take_rows, jnp.concatenate([upper, lower], axis=0)).astype(bf16)
        return dot(rows, take_cols)

    def spread(layer, part, grad):
        grad = grad.astype(bf16)
        rows = dot(take_rows_t, grad).astype(bf16)
        wide = dot(rows[:n], take_cols_t).astype(bf16)
        home_ref[layer, part] = wide[:, :n]
        next_ref[layer, part] = wide[:, n:]
        down_ref[layer, part] = dot(rows[n:], wrap_cols).astype(bf16)

    def transform(left_ref, right_ref, wave_re, wave_im):
        wave = jnp.concatenate([wave_re.astype(bf16), wave_im.astype(bf16)], axis=0)
        first = dot(left_ref[...], wave).astype(bf16)
        first = jnp.concatenate([first[:n], first[n:]], axis=1)
        out = dot(first, right_ref[...])
        return out[:, :n], out[:, n:]

    layers = [(patch(layer, 0), patch(layer, 1)) for layer in range(depth)]
    near = layers[0]
    far = layers[1]
    arrives = []
    fields = []
    for mode in range(modes):
        lanes = pl.ds(mode * n, n)
        p_re, p_im = probe_ref[0, :, lanes], probe_ref[1, :, lanes]
        a_re, a_im = transform(
            prop_ref, prop_c_ref, p_re * near[0] - p_im * near[1], p_re * near[1] + p_im * near[0]
        )
        arrives.append((a_re, a_im))
        fields.append(
            transform(
                dft_ref, dft_c_ref, far[0] * a_re - far[1] * a_im, far[0] * a_im + far[1] * a_re
            )
        )
    intensity = sum(f_re * f_re + f_im * f_im for f_re, f_im in fields)
    residual = intensity - pattern_ref[...].astype(f32)
    grad_far = [0.0, 0.0]
    grad_near = [0.0, 0.0]
    for mode in range(modes):
        lanes = pl.ds(mode * n, n)
        f_re, f_im = fields[mode]
        a_re, a_im = arrives[mode]
        b_re, b_im = transform(dft_c_ref, dft_ref, f_re * residual, f_im * residual)
        grad_far[0] += a_re * b_re + a_im * b_im
        grad_far[1] += a_re * b_im - a_im * b_re
        b_re, b_im = transform(
            prop_c_ref, prop_ref, far[0] * b_re + far[1] * b_im, far[0] * b_im - far[1] * b_re
        )
        p_re, p_im = probe_ref[0, :, lanes], probe_ref[1, :, lanes]
        grad_near[0] += p_re * b_re + p_im * b_im
        grad_near[1] += p_re * b_im - p_im * b_re
        term_ref[0, :, lanes] = (near[0] * b_re + near[1] * b_im).astype(bf16)
        term_ref[1, :, lanes] = (near[0] * b_im - near[1] * b_re).astype(bf16)
    for layer, grad in enumerate((grad_near, grad_far)):
        for part in range(2):
            spread(layer, part, grad[part])


def position_terms(spot, own, right, below, diag, probe, pattern, tables):
    tile = jax.ShapeDtypeStruct(own.shape, bf16)
    vmem = pl.BlockSpec(memory_space=pltpu.VMEM)
    return pl.pallas_call(
        position_kernel,
        out_shape=(tile, tile, tile, jax.ShapeDtypeStruct(probe.shape, bf16)),
        in_specs=[pl.BlockSpec(memory_space=pltpu.SMEM)] + [vmem] * 10,
        out_specs=(vmem,) * 4,
        compiler_params=pltpu.CompilerParams(vmem_limit_bytes=40 * 2**20),
        cost_estimate=pl.CostEstimate(
            flops=5_000_000_000, bytes_accessed=10_000_000, transcendentals=0
        ),
        name="position",
    )(spot, own, right, below, diag, probe, pattern, *tables)


def pick_position(patterns, offsets, counts):
    owners = lax.axis_size("pos")
    if owners == 2:
        swap = [(0, 1), (1, 0)]
        other_spot = lax.ppermute(offsets[1], "pos", swap)
        other_pattern = lax.ppermute(patterns[1], "pos", swap)
        busy = counts == 2
        return jnp.where(busy, offsets[0], other_spot), jnp.where(busy, patterns[0], other_pattern)
    all_counts = lax.all_gather(counts, "pos")
    ends = jnp.cumsum(all_counts)
    rank = lax.axis_index("pos")
    source = jnp.sum((ends <= rank).astype(jnp.int32))
    slot = rank - (ends[source] - all_counts[source])
    all_offsets = lax.all_gather(offsets, "pos")
    all_patterns = lax.all_gather(patterns, "pos")
    return all_offsets[source, slot], all_patterns[source, slot]


def probe_sum(term):
    devices = lax.axis_size("tile") * lax.axis_size("pos")
    rows = term.shape[0] * term.shape[1] // devices
    blocks = term.reshape(devices, rows, term.shape[2])
    mine = lax.all_to_all(blocks, ("tile", "pos"), 0, 0, tiled=True)
    total = jnp.sum(mine.astype(f32), axis=0).astype(bf16)
    return lax.all_gather(total, ("tile", "pos"), tiled=True).reshape(term.shape)


def shards(tile_object, probe_modes, patterns, offsets, counts):
    pixels = probe_modes.shape[1]
    tables = build_tables(pixels)
    own = tile_object[0]
    grid_cols = lax.axis_size("tile") // GRID_ROWS
    below = from_behind(own, "tile", -grid_cols)
    right = from_behind(own, "tile", -1)
    spot, pattern = pick_position(patterns[0, 0], offsets[0, 0], counts[0, 0])
    spot_above = from_behind(spot, "tile", grid_cols)
    diag = from_behind(below, "tile", -1)
    probe = probe_modes.reshape(2, pixels, -1)
    home, beside, down, term = position_terms(
        spot, own, right, below, diag, probe, pattern, tables
    )
    from_above = from_behind(down, "tile", grid_cols)
    total = probe_sum(term)
    split = jnp.arange(pixels, dtype=jnp.int32) < spot_above[1]
    zero = jnp.zeros((), bf16)
    beside = beside + jnp.where(split, from_above, zero)
    from_left = from_behind(beside, "tile", 1)
    part = (
        home.astype(f32) + jnp.where(split, zero, from_above).astype(f32) + from_left.astype(f32)
    ).astype(bf16)
    part = lax.optimization_barrier(part)
    if lax.axis_size("pos") == 2:
        tile_grad = part.astype(f32) + lax.ppermute(part, "pos", [(0, 1), (1, 0)]).astype(f32)
    else:
        tile_grad = lax.psum(part.astype(f32), "pos")
    new_object = (own.astype(f32) - object_rate * tile_grad).astype(bf16)[None]
    positions_all = lax.axis_size("tile") * lax.axis_size("pos") * (patterns.shape[2] // 2)
    step = probe_rate / math.sqrt(positions_all)
    new_probe = probe_modes - step * total.astype(f32).reshape(probe_modes.shape)
    return (new_object, new_probe)


def solution(mesh):
    placed = (
        P("tile", None, None, None, None),
        P(),
        P("tile", "pos", None, None, None),
        P("tile", "pos", None, None),
        P("tile", "pos"),
    )
    return jax.shard_map(
        shards,
        mesh=mesh,
        in_specs=placed,
        out_specs=(P("tile", None, None, None, None), P()),
        check_vma=False,
    )
```

```python
import math

import jax
import jax.numpy as jnp
import numpy as np
from jax import lax
from jax.experimental import pallas as pl
from jax.experimental.pallas import tpu as pltpu
from jax.sharding import PartitionSpec as P

GRID_ROWS = 4


fresnel_coeff = 0.25
object_rate = 0.05
probe_rate = 0.15

f32 = jnp.float32
bf16 = jnp.bfloat16


def from_behind(block, axis, distance):
    size = lax.axis_size(axis)
    return lax.ppermute(block, axis, [((i - distance) % size, i) for i in range(size)])


def real_embed(part_re, part_im):
    upper_half = np.concatenate([part_re, -part_im], axis=1)
    lower_half = np.concatenate([part_im, part_re], axis=1)
    stacked = np.concatenate([upper_half, lower_half], axis=0)
    return jnp.asarray(stacked, dtype=f32).astype(bf16)


def build_tables(pixels):
    indices = np.arange(pixels)
    angles = indices[:, None] * indices[None, :] % pixels * (2.0 * math.pi / pixels)
    norm_scale = 1.0 / math.sqrt(pixels)
    dft_re = np.cos(angles) * norm_scale
    dft_im = -np.sin(angles) * norm_scale
    frequency = np.where(indices < pixels // 2, indices, indices - pixels)
    phases = -2.0 * math.pi * fresnel_coeff / pixels * (frequency * frequency)
    phase_sum = phases[:, None] + angles
    kern_re = np.sum(np.cos(phase_sum), axis=0) / pixels
    kern_im = np.sum(np.sin(phase_sum), axis=0) / pixels
    lag_index = (indices[:, None] - indices[None, :]) % pixels
    prop_re = kern_re[lag_index]
    prop_im = kern_im[lag_index]
    return (
        real_embed(prop_re, prop_im),
        real_embed(prop_re, -prop_im),
        real_embed(dft_re, dft_im),
        real_embed(dft_re, -dft_im),
    )


def dot(a, b):
    return jnp.dot(a, b, preferred_element_type=f32)


def shift_tables(row, col, n):
    i_out = lax.broadcasted_iota(jnp.int32, (n, 2 * n), 0)
    i_in = lax.broadcasted_iota(jnp.int32, (n, 2 * n), 1)
    j_in = lax.broadcasted_iota(jnp.int32, (2 * n, n), 0)
    j_out = lax.broadcasted_iota(jnp.int32, (2 * n, n), 1)
    rows = (i_in == i_out + row).astype(f32).astype(bf16)
    cols = (j_in == j_out + col).astype(f32).astype(bf16)
    rows_t = (j_in == j_out + row).astype(f32).astype(bf16)
    cols_t = (i_in == i_out + col).astype(f32).astype(bf16)
    return rows, cols, rows_t, cols_t


def patch(shifts, own_ref, right_ref, below_ref, diag_ref, part):
    upper = jnp.concatenate([own_ref[part], right_ref[part]], axis=1)
    lower = jnp.concatenate([below_ref[part], diag_ref[part]], axis=1)
    rows = dot(shifts[0], jnp.concatenate([upper, lower], axis=0)).astype(bf16)
    return dot(rows, shifts[1])


def transform(left_ref, right_ref, wave_re, wave_im):
    n = wave_re.shape[0]
    wave = jnp.concatenate([wave_re.astype(bf16), wave_im.astype(bf16)], axis=0)
    first = dot(left_ref[...], wave).astype(bf16)
    first = jnp.concatenate([first[:n], first[n:]], axis=1)
    out = dot(first, right_ref[...])
    return out[:, :n], out[:, n:]


def arrive_kernel(
    spot_ref, spot_above_ref, own_ref, right_ref, below_ref, diag_ref, probe_ref, prop_ref,
    prop_c_ref, near_ref, arrive_ref, split_ref,
):
    n = own_ref.shape[1]
    lanes = lax.broadcasted_iota(jnp.int32, split_ref.shape, 1)
    split_ref[...] = (lanes < spot_above_ref[1]).astype(f32)
    shifts = shift_tables(spot_ref[0], spot_ref[1], n)
    tiles = (own_ref, right_ref, below_ref, diag_ref)
    near = [patch(shifts, *tiles, part) for part in range(2)]
    for part in range(2):
        near_ref[part] = near[part].astype(bf16)
    for mode in range(probe_ref.shape[2] // n):
        lanes = pl.ds(mode * n, n)
        p_re, p_im = probe_ref[0, :, lanes], probe_ref[1, :, lanes]
        a_re, a_im = transform(
            prop_ref, prop_c_ref, p_re * near[0] - p_im * near[1], p_re * near[1] + p_im * near[0]
        )
        arrive_ref[0, :, lanes] = a_re
        arrive_ref[1, :, lanes] = a_im


def gradient_kernel(
    spot_ref, own_ref, right_ref, below_ref, diag_ref, near_ref, arrive_ref, probe_ref,
    pattern_ref, prop_ref, prop_c_ref, dft_ref, dft_c_ref,
    home0_ref, next0_ref, down0_ref, home1_ref, next1_ref, down1_ref, term_ref,
):
    n = own_ref.shape[1]
    modes = probe_ref.shape[2] // n
    shifts = shift_tables(spot_ref[0], spot_ref[1], n)
    wrap_cols = shifts[3][:, :n] + shifts[3][:, n:]

    def spread(home_ref, next_ref, down_ref, part, grad):
        rows = dot(shifts[2], grad.astype(bf16)).astype(bf16)
        wide = dot(rows[:n], shifts[3]).astype(bf16)
        home_ref[part] = wide[:, :n]
        next_ref[part] = wide[:, n:]
        down_ref[part] = dot(rows[n:], wrap_cols).astype(bf16)

    tiles = (own_ref, right_ref, below_ref, diag_ref)
    far = [patch(shifts, *tiles, part) for part in range(2)]
    fields = []
    for mode in range(modes):
        lanes = pl.ds(mode * n, n)
        a_re, a_im = arrive_ref[0, :, lanes], arrive_ref[1, :, lanes]
        fields.append(
            transform(
                dft_ref, dft_c_ref, far[0] * a_re - far[1] * a_im, far[0] * a_im + far[1] * a_re
            )
        )
    intensity = sum(f_re * f_re + f_im * f_im for f_re, f_im in fields)
    residual = intensity - pattern_ref[...].astype(f32)
    grad_far = [0.0, 0.0]
    waves = []
    for mode in range(modes):
        lanes = pl.ds(mode * n, n)
        f_re, f_im = fields[mode]
        a_re, a_im = arrive_ref[0, :, lanes], arrive_ref[1, :, lanes]
        b_re, b_im = transform(dft_c_ref, dft_ref, f_re * residual, f_im * residual)
        grad_far[0] += a_re * b_re + a_im * b_im
        grad_far[1] += a_re * b_im - a_im * b_re
        waves.append((far[0] * b_re + far[1] * b_im, far[0] * b_im - far[1] * b_re))
    grad_near = [0.0, 0.0]
    near = [near_ref[part].astype(f32) for part in range(2)]
    for mode in range(modes):
        lanes = pl.ds(mode * n, n)
        b_re, b_im = transform(prop_c_ref, prop_ref, *waves[mode])
        p_re, p_im = probe_ref[0, :, lanes], probe_ref[1, :, lanes]
        grad_near[0] += p_re * b_re + p_im * b_im
        grad_near[1] += p_re * b_im - p_im * b_re
        term_ref[0, :, lanes] = (near[0] * b_re + near[1] * b_im).astype(bf16)
        term_ref[1, :, lanes] = (near[0] * b_im - near[1] * b_re).astype(bf16)
    for part in range(2):
        spread(home1_ref, next1_ref, down1_ref, part, grad_far[part])
        spread(home0_ref, next0_ref, down0_ref, part, grad_near[part])


def call_kernel(kernel, outs, flops, spots, *arrays):
    vmem = pl.BlockSpec(memory_space=pltpu.VMEM)
    smem = pl.BlockSpec(memory_space=pltpu.SMEM)
    return pl.pallas_call(
        kernel,
        out_shape=outs,
        in_specs=[smem] * len(spots) + [vmem] * len(arrays),
        out_specs=(vmem,) * len(outs),
        compiler_params=pltpu.CompilerParams(vmem_limit_bytes=16 * 2**20),
        cost_estimate=pl.CostEstimate(flops=flops, bytes_accessed=6_000_000, transcendentals=0),
    )(*spots, *arrays)


def pick_position(patterns, offsets, counts):
    owners = lax.axis_size("pos")
    if owners == 2:
        swap = [(0, 1), (1, 0)]
        other_spot = lax.ppermute(offsets[1], "pos", swap)
        other_pattern = lax.ppermute(patterns[1], "pos", swap)
        busy = counts == 2
        return jnp.where(busy, offsets[0], other_spot), jnp.where(busy, patterns[0], other_pattern)
    all_counts = lax.all_gather(counts, "pos")
    ends = jnp.cumsum(all_counts)
    rank = lax.axis_index("pos")
    source = jnp.sum((ends <= rank).astype(jnp.int32))
    slot = rank - (ends[source] - all_counts[source])
    all_offsets = lax.all_gather(offsets, "pos")
    all_patterns = lax.all_gather(patterns, "pos")
    return all_offsets[source, slot], all_patterns[source, slot]


def block_sum_kernel(blocks_ref, out_ref):
    total = blocks_ref[0].astype(f32)
    for block in range(1, blocks_ref.shape[0]):
        total += blocks_ref[block].astype(f32)
    total = total.astype(bf16)
    for copy in range(out_ref.shape[0]):
        out_ref[copy] = total


def block_sum(blocks, copies):
    vmem = pl.BlockSpec(memory_space=pltpu.VMEM)
    return pl.pallas_call(
        block_sum_kernel,
        out_shape=jax.ShapeDtypeStruct((copies,) + blocks.shape[1:], bf16),
        in_specs=[vmem],
        out_specs=vmem,
        compiler_params=pltpu.CompilerParams(vmem_limit_bytes=4 * 2**20),
        cost_estimate=pl.CostEstimate(
            flops=blocks.size, bytes_accessed=4 * blocks.size, transcendentals=0
        ),
    )(blocks)


def probe_sum(term):
    tiles, owners = lax.axis_size("tile"), lax.axis_size("pos")
    members = tiles // GRID_ROWS * owners
    same_row = [[row * members + i for i in range(members)] for row in range(GRID_ROWS)]
    same_place = [[row * members + i for row in range(GRID_ROWS)] for i in range(members)]
    blocks = term.reshape(members, term.size // term.shape[-1] // members, term.shape[-1])

    def exchange(x, groups):
        return lax.all_to_all(
            x, ("tile", "pos"), 0, 0, axis_index_groups=groups, tiled=True
        )

    blocks = block_sum(exchange(blocks, same_row), GRID_ROWS)
    blocks = block_sum(exchange(blocks, same_place), members)
    return exchange(blocks, same_row).reshape(term.shape)


def shards(tile_object, probe_modes, patterns, offsets, counts):
    pixels = probe_modes.shape[1]
    prop, prop_c, dft, dft_c = build_tables(pixels)
    own = [tile_object[0, 0], tile_object[0, 1]]
    grid_cols = lax.axis_size("tile") // GRID_ROWS
    below = [from_behind(own[s], "tile", -grid_cols) for s in range(2)]
    right = [from_behind(own[s], "tile", -1) for s in range(2)]
    spot, pattern = pick_position(patterns[0, 0], offsets[0, 0], counts[0, 0])
    spot_above = from_behind(spot, "tile", grid_cols)
    diag = [from_behind(below[s], "tile", -1) for s in range(2)]
    probe = probe_modes.reshape(2, pixels, -1)
    tile = jax.ShapeDtypeStruct(own[0].shape, bf16)
    near, arrive, split = call_kernel(
        arrive_kernel,
        (tile, jax.ShapeDtypeStruct(probe.shape, f32), jax.ShapeDtypeStruct((1, pixels), f32)),
        1_500_000_000,
        (spot, spot_above), own[0], right[0], below[0], diag[0], probe, prop, prop_c,
    )
    home0, next0, down0, home1, next1, down1, term = call_kernel(
        gradient_kernel,
        (tile,) * 6 + (jax.ShapeDtypeStruct(probe.shape, bf16),),
        4_000_000_000,
        (spot,), own[1], right[1], below[1], diag[1], near, arrive, probe, pattern,
        prop, prop_c, dft, dft_c,
    )
    total = probe_sum(term)
    split = split[0] > 0
    zero = jnp.zeros((), bf16)
    new_slices = []
    for s, (home, beside, down) in enumerate(((home0, next0, down0), (home1, next1, down1))):
        from_above = from_behind(down, "tile", grid_cols)
        beside = beside + jnp.where(split, from_above, zero)
        from_left = from_behind(beside, "tile", 1)
        kept = home.astype(f32) + jnp.where(split, zero, from_above).astype(f32)
        part = lax.optimization_barrier((kept + from_left.astype(f32)).astype(bf16))
        if lax.axis_size("pos") == 2:
            other = lax.ppermute(part, "pos", [(0, 1), (1, 0)])
            tile_grad = part.astype(f32) + other.astype(f32)
        else:
            tile_grad = lax.psum(part.astype(f32), "pos")
        new_slices.append((own[s].astype(f32) - object_rate * tile_grad).astype(bf16))
    new_object = jnp.stack(new_slices)[None]
    positions_all = lax.axis_size("tile") * lax.axis_size("pos") * (patterns.shape[2] // 2)
    step = probe_rate / math.sqrt(positions_all)
    new_probe = probe_modes - step * total.astype(f32).reshape(probe_modes.shape)
    return (new_object, new_probe)


def solution(mesh):
    placed = (
        P("tile", None, None, None, None),
        P(),
        P("tile", "pos", None, None, None),
        P("tile", "pos", None, None),
        P("tile", "pos"),
    )
    return jax.shard_map(
        shards,
        mesh=mesh,
        in_specs=placed,
        out_specs=(P("tile", None, None, None, None), P()),
        check_vma=False,
    )
```

```python
import math

import jax
import jax.numpy as jnp
import numpy as np
from jax import lax
from jax.experimental import pallas as pl
from jax.experimental.pallas import tpu as pltpu
from jax.sharding import PartitionSpec as P

GRID_ROWS = 4


fresnel_coeff = 0.25
object_rate = 0.05
probe_rate = 0.15

f32 = jnp.float32
bf16 = jnp.bfloat16


def from_behind(block, rows, cols):
    tiles = lax.axis_size("tile")
    across = tiles // GRID_ROWS

    def source(i):
        return (i // across - rows) % GRID_ROWS * across + (i % across - cols) % across

    return lax.ppermute(block, "tile", [(source(i), i) for i in range(tiles)])


def real_embed(part_re, part_im):
    upper_half = np.concatenate([part_re, -part_im], axis=1)
    lower_half = np.concatenate([part_im, part_re], axis=1)
    stacked = np.concatenate([upper_half, lower_half], axis=0)
    return jnp.asarray(stacked, dtype=f32).astype(bf16)


def build_tables(pixels):
    indices = np.arange(pixels)
    angles = indices[:, None] * indices[None, :] % pixels * (2.0 * math.pi / pixels)
    norm_scale = 1.0 / math.sqrt(pixels)
    dft_re = np.cos(angles) * norm_scale
    dft_im = -np.sin(angles) * norm_scale
    frequency = np.where(indices < pixels // 2, indices, indices - pixels)
    phases = -2.0 * math.pi * fresnel_coeff / pixels * (frequency * frequency)
    phase_sum = phases[:, None] + angles
    kern_re = np.sum(np.cos(phase_sum), axis=0) / pixels
    kern_im = np.sum(np.sin(phase_sum), axis=0) / pixels
    lag_index = (indices[:, None] - indices[None, :]) % pixels
    prop_re = kern_re[lag_index]
    prop_im = kern_im[lag_index]
    return real_embed(prop_re, prop_im), real_embed(dft_re, dft_im)


def dot(a, b):
    return jnp.dot(a, b, preferred_element_type=f32)


def shift_tables(offsets_ref, counts_ref, message_ref):
    n = message_ref.shape[1]
    sent = message_ref[n:, :].astype(f32)
    busy = counts_ref[0, 0] == offsets_ref.shape[2]
    row = jnp.where(busy, offsets_ref[0, 0, 0, 0], sent[0:1].astype(jnp.int32))
    col = jnp.where(busy, offsets_ref[0, 0, 0, 1], sent[1:2].astype(jnp.int32))
    i_out = lax.broadcasted_iota(jnp.int32, (n, 2 * n), 0)
    i_in = lax.broadcasted_iota(jnp.int32, (n, 2 * n), 1)
    j_in = lax.broadcasted_iota(jnp.int32, (2 * n, n), 0)
    j_out = lax.broadcasted_iota(jnp.int32, (2 * n, n), 1)
    row2 = jnp.concatenate([row, row], axis=1)
    col2 = jnp.concatenate([col, col], axis=1)
    rows = (i_in == i_out + row2).astype(f32).astype(bf16)
    cols = (j_in == j_out + col).astype(f32).astype(bf16)
    rows_t = (j_in == j_out + row).astype(f32).astype(bf16)
    cols_t = (i_in == i_out + col2).astype(f32).astype(bf16)
    return rows, cols, rows_t, cols_t, col, busy


def patch(shifts, own_ref, right_ref, below_ref, diag_ref, part):
    upper = jnp.concatenate([own_ref[part], right_ref[part]], axis=1)
    lower = jnp.concatenate([below_ref[part], diag_ref[part]], axis=1)
    rows = dot(shifts[0], jnp.concatenate([upper, lower], axis=0)).astype(bf16)
    return dot(rows, shifts[1])


def transform(table_ref, wave_re, wave_im):
    n = wave_re.shape[0]
    table = table_ref[...]
    wave = jnp.concatenate([wave_re.astype(bf16), wave_im.astype(bf16)], axis=0)
    first = dot(table, wave)
    first = jnp.concatenate([first[:n].astype(bf16), (-first[n:]).astype(bf16)], axis=1)
    out = dot(first, table)
    return out[:, :n], out[:, n:]


def probe_plane(probe_ref, part, mode, modes):
    lane_tiles = 2
    n = probe_ref.shape[0] // (2 * lane_tiles * modes)
    step = lane_tiles * modes
    halves = [
        probe_ref[pl.ds(part * n * step + tile * modes + mode, n, stride=step), :]
        for tile in range(lane_tiles)
    ]
    return jnp.concatenate(halves, axis=1)


def cut_kernel(offsets_ref, tile_ref, patterns_ref, *refs):
    slices, message_ref, sems = refs[:-2], refs[-2], refs[-1]
    n = message_ref.shape[1]
    copies = [
        pltpu.make_async_copy(tile_ref.at[0, s], ref, sems.at[s]) for s, ref in enumerate(slices)
    ]
    to_pattern = message_ref.at[pl.ds(0, n), :]
    copies.append(pltpu.make_async_copy(patterns_ref.at[0, 0, 1], to_pattern, sems.at[len(slices)]))
    for copy in copies:
        copy.start()
    at = lax.broadcasted_iota(jnp.int32, (16, n), 0)
    row, col = offsets_ref[0, 0, 1, 0], offsets_ref[0, 0, 1, 1]
    rows = jnp.where(at == 0, row, jnp.where(at == 1, col, 0))
    message_ref[pl.ds(n, 16), :] = rows.astype(f32).astype(bf16)
    for copy in copies:
        copy.wait()


def arrive_kernel(
    offsets_ref, counts_ref, message_ref, own_ref, right_ref, below_ref, diag_ref, probe_ref,
    prop_hbm, near_ref, arrive_ref, prop_ref, sems,
):
    n = own_ref.shape[1]
    modes = arrive_ref.shape[2] // n
    parts = sems.shape[0]
    size = prop_ref.shape[0] // parts
    fetches = []
    for at in range(parts):
        rows = pl.ds(at * size, size)
        copy = pltpu.make_async_copy(prop_hbm.at[rows, :], prop_ref.at[rows, :], sems.at[at])
        copy.start()
        fetches.append(copy)
    shifts = shift_tables(offsets_ref, counts_ref, message_ref)
    tiles = (own_ref, right_ref.at[0], below_ref, diag_ref)
    near = [patch(shifts, *tiles, part) for part in range(2)]
    for part in range(2):
        near_ref[part] = near[part].astype(bf16)
    for copy in fetches:
        copy.wait()
    for mode in range(modes):
        lanes = pl.ds(mode * n, n)
        p_re = probe_plane(probe_ref, 0, mode, modes)
        p_im = probe_plane(probe_ref, 1, mode, modes)
        a_re, a_neg = transform(
            prop_ref, p_re * near[0] - p_im * near[1], p_re * near[1] + p_im * near[0]
        )
        arrive_ref[0, :, lanes] = a_re
        arrive_ref[1, :, lanes] = -a_neg


def gradient_kernel(
    offsets_ref, counts_ref, message_ref, own_ref, right_ref, below_ref, diag_ref,
    near_ref, arrive_ref, probe_ref, patterns_ref, prop_ref, dft_ref,
    home0_ref, next0_ref, down0_ref, home1_ref, next1_ref, down1_ref, keep_ref, give_ref,
    term_ref,
):
    n = own_ref.shape[1]
    modes = arrive_ref.shape[2] // n
    shifts = shift_tables(offsets_ref, counts_ref, message_ref)
    rows_t, cols_t, col, busy = shifts[2:]
    wrap_cols = cols_t[:, :n] + cols_t[:, n:]
    edge = lax.broadcasted_iota(jnp.int32, (16, n), 1) < col
    edge = edge.astype(f32).astype(bf16)

    def spread(home_ref, next_ref, down_ref, grad):
        for part in range(2):
            rows = dot(rows_t, grad[part].astype(bf16)).astype(bf16)
            wide = dot(rows[:n], cols_t).astype(bf16)
            home_ref[part] = wide[:, :n]
            next_ref[part] = wide[:, n:]
            down_ref[pl.ds(part * n, n), :] = dot(rows[n:], wrap_cols).astype(bf16)
        down_ref[pl.ds(2 * n, 16), :] = edge

    tiles = (own_ref, right_ref.at[1], below_ref, diag_ref)
    far = [patch(shifts, *tiles, part) for part in range(2)]
    fields = []
    for mode in range(modes):
        lanes = pl.ds(mode * n, n)
        a_re, a_im = arrive_ref[0, :, lanes], arrive_ref[1, :, lanes]
        fields.append(
            transform(dft_ref, far[0] * a_re - far[1] * a_im, far[0] * a_im + far[1] * a_re)
        )
    intensity = sum(f_re * f_re + f_neg * f_neg for f_re, f_neg in fields)
    pattern = jnp.where(busy, patterns_ref[0, 0, 0].astype(f32), message_ref[:n, :].astype(f32))
    residual = intensity - pattern
    grad_far = [0.0, 0.0]
    waves = []
    for mode in range(modes):
        lanes = pl.ds(mode * n, n)
        f_re, f_neg = fields[mode]
        a_re, a_im = arrive_ref[0, :, lanes], arrive_ref[1, :, lanes]
        b_re, b_im = transform(dft_ref, f_re * residual, f_neg * residual)
        grad_far[0] += a_re * b_re + a_im * b_im
        grad_far[1] += a_re * b_im - a_im * b_re
        waves.append((far[0] * b_re + far[1] * b_im, far[1] * b_re - far[0] * b_im))
    grad_near = [0.0, 0.0]
    near = [near_ref[part].astype(f32) for part in range(2)]
    for mode in range(modes):
        lanes = pl.ds(mode * n, n)
        b_re, b_im = transform(prop_ref, *waves[mode])
        p_re = probe_plane(probe_ref, 0, mode, modes)
        p_im = probe_plane(probe_ref, 1, mode, modes)
        grad_near[0] += p_re * b_re + p_im * b_im
        grad_near[1] += p_re * b_im - p_im * b_re
        term_ref[0, :, lanes] = (near[0] * b_re + near[1] * b_im).astype(bf16)
        term_ref[1, :, lanes] = (near[0] * b_im - near[1] * b_re).astype(bf16)
    core = place_of(core_group())
    keep_ref[...] = term_ref[core]
    give_ref[...] = term_ref[1 - core]
    spread(home1_ref, next1_ref, down1_ref, grad_far)
    spread(home0_ref, next0_ref, down0_ref, grad_near)


def core_group():
    return [lax.axis_size("pos")]


def place_of(group):
    flat = lax.axis_index("tile") * lax.axis_size("pos") + lax.axis_index("pos")
    return sum(flat // mask % 2 * (1 << at) for at, mask in enumerate(group))


def call_kernel(
    kernel, outs, scalars, arrays, flops=1_000_000, scratch=(), limit=16, apart=(), after=()
):
    vmem = pl.BlockSpec(memory_space=pltpu.VMEM)
    smem = pl.BlockSpec(memory_space=pltpu.SMEM)
    hbm = pl.BlockSpec(memory_space=pltpu.HBM)
    anywhere = pl.BlockSpec(memory_space=pl.ANY)
    moved = sum(x.size * x.dtype.itemsize for x in list(arrays) + list(outs))
    used = len(scalars) + len(arrays) + len(apart)

    def body(*refs):
        kernel(*refs[:used], *refs[used + len(after) :])

    return pl.pallas_call(
        body,
        out_shape=outs,
        in_specs=[smem] * len(scalars) + [vmem] * len(arrays) + [hbm] * len(apart)
        + [anywhere] * len(after),
        out_specs=[vmem] * len(outs),
        scratch_shapes=scratch,
        compiler_params=pltpu.CompilerParams(vmem_limit_bytes=limit * 2**20),
        cost_estimate=pl.CostEstimate(flops=flops, bytes_accessed=moved, transcendentals=0),
    )(*scalars, *arrays, *apart, *after)


def shape_of(kind, *dims):
    return jax.ShapeDtypeStruct(dims, kind)


def handed_over(message, patterns, offsets, counts):
    owners = lax.axis_size("pos")
    slots, pixels = patterns.shape[2], patterns.shape[4]
    if owners == slots:
        return lax.ppermute(message, "pos", [(i, 1 - i) for i in range(2)]), counts
    all_counts = lax.all_gather(counts[0, 0], "pos")
    ends = jnp.cumsum(all_counts)
    rank = lax.axis_index("pos")
    source = jnp.sum((ends <= rank).astype(jnp.int32))
    slot = rank - (ends[source] - all_counts[source])
    spot = lax.all_gather(offsets[0, 0], "pos")[source, slot]
    pattern = lax.all_gather(patterns[0, 0], "pos")[source, slot]
    rows = jnp.broadcast_to(spot.astype(bf16)[:, None], (2, pixels))
    blank = jnp.zeros((14, pixels), bf16)
    return jnp.concatenate([pattern, rows, blank], axis=0), jnp.zeros_like(counts)


def fold_kernel(group, keep_ref, *refs):
    blocks = refs[-1]
    got = len(refs) - 1 - blocks.shape[0]
    arrived, keep_out, give_outs = refs[:got], refs[got], refs[got + 1 : -1]
    total = keep_ref[...].astype(f32)
    for ref in arrived:
        total += ref[...].astype(f32)
    size = blocks.shape[1]
    for block in range(blocks.shape[0]):
        blocks[block] = total[block * size : (block + 1) * size]
    here = place_of(group)
    keep_out[...] = blocks[here]
    for distance, ref in enumerate(give_outs, 1):
        ref[...] = blocks[here ^ distance].astype(bf16)


def add_kernel(keep_ref, *refs):
    total = keep_ref[...].astype(f32)
    for ref in refs[:-1]:
        total += ref[...].astype(f32)
    refs[-1][...] = total.astype(bf16)


def place_kernel(group, add, *refs):
    arrived, out_ref, blocks = refs[:-2], refs[-2], refs[-1]
    here = place_of(group)
    for distance, ref in enumerate(arrived):
        blocks[here ^ distance] = ref[...]
    size = blocks.shape[1]
    if add:
        total = blocks[0].astype(f32)
        for block in range(1, blocks.shape[0]):
            total += blocks[block].astype(f32)
        out_ref[...] = total.astype(bf16)
    else:
        for block in range(blocks.shape[0]):
            out_ref[pl.ds(block * size, size), :] = blocks[block]


def probe_kernel(step, modes, mine_ref, other_ref, probe_ref, out_ref):
    core = place_of(core_group())
    lane_tiles = 2
    n = mine_ref.shape[0]
    stride = lane_tiles * modes
    for part in range(2):
        total = jnp.where(core == part, mine_ref[...].astype(f32), other_ref[...].astype(f32))
        for mode in range(modes):
            for tile in range(lane_tiles):
                lane = (mode * lane_tiles + tile) * 128
                where = pl.ds(part * n * stride + tile * modes + mode, n, stride=stride)
                out_ref[where, :] = probe_ref[where, :] - step * total[:, lane : lane + 128]


def exchange_groups():
    tiles, owners = lax.axis_size("tile"), lax.axis_size("pos")
    bits = [1 << bit for bit in range(owners.bit_length() - 1)]
    bits += [owners << bit for bit in range(1, tiles.bit_length() - 1)]
    return [bits[at : at + 2] for at in range(0, len(bits), 2)]


def swap_with(x, group, distance):
    mask = sum(bit for at, bit in enumerate(group) if distance >> at & 1)
    devices = lax.axis_size("tile") * lax.axis_size("pos")
    return lax.ppermute(x, ("tile", "pos"), [(i, i ^ mask) for i in range(devices)])


def joined(group, x, add, after=()):
    blocks = 1 << len(group)
    arrived = [x] + [swap_with(x, group, at) for at in range(1, blocks)]
    rows = x.shape[0] * (1 if add else blocks)
    (out,) = call_kernel(
        lambda *refs: place_kernel(group, add, *refs),
        [shape_of(bf16, rows, x.shape[1])],
        [],
        arrived,
        scratch=[pltpu.VMEM((blocks,) + x.shape, bf16)],
        limit=4,
        after=after,
    )
    return out


def shards(tile_object, probe_modes, patterns, offsets, counts):
    _, pixels, modes, _ = probe_modes.shape
    prop, dft = build_tables(pixels)
    tile = shape_of(bf16, 2, pixels, pixels)
    message = shape_of(bf16, pixels + 16, pixels)
    *own, message = call_kernel(
        cut_kernel,
        [tile, tile, message],
        [offsets],
        [],
        apart=[tile_object, patterns],
        scratch=[pltpu.SemaphoreType.DMA((3,))],
        limit=4,
    )
    below = [from_behind(own[s], -1, 0) for s in range(2)]
    right = from_behind(tile_object[0], 0, -1)
    message, counts = handed_over(message, patterns, offsets, counts)
    diag = [from_behind(below[s], 0, -1) for s in range(2)]
    lane_tiles = pixels // 128
    probe = probe_modes.reshape(2, pixels, modes, lane_tiles, 128)
    probe = probe.transpose(0, 1, 3, 2, 4).reshape(-1, 128)
    width = modes * pixels
    near, arrive = call_kernel(
        arrive_kernel,
        [tile, shape_of(f32, 2, pixels, width)],
        [offsets, counts],
        [message, own[0], right, below[0], diag[0], probe],
        flops=1_500_000_000,
        apart=[prop],
        scratch=[pltpu.VMEM(prop.shape, bf16), pltpu.SemaphoreType.DMA((4,))],
    )
    half = shape_of(bf16, pixels, width)
    down = shape_of(bf16, 2 * pixels + 16, pixels)
    home0, next0, down0, home1, next1, down1, keep, give = call_kernel(
        gradient_kernel,
        [tile, tile, down, tile, tile, down, half, half],
        [offsets, counts],
        [message, own[1], right, below[1], diag[1], near, arrive, probe, patterns, prop, dft],
        flops=4_000_000_000,
        scratch=[pltpu.VMEM((2, pixels, width), bf16)],
    )
    zero = jnp.zeros((), bf16)

    def from_above(down):
        arrived = from_behind(down, 1, 0)
        return arrived[: 2 * pixels].reshape(2, pixels, pixels), arrived[2 * pixels] > 0

    def beside(next_tile, above, split):
        return next_tile + jnp.where(split, above, zero)

    def part(home, above, split, from_left):
        kept = home.astype(f32) + jnp.where(split, zero, above).astype(f32)
        return lax.optimization_barrier((kept + from_left.astype(f32)).astype(bf16))

    def over_owners(part):
        if lax.axis_size("pos") == 2:
            other = lax.ppermute(part, "pos", [(0, 1), (1, 0)])
            return part.astype(f32) + other.astype(f32)
        return lax.psum(part.astype(f32), "pos")

    core, groups = core_group(), exchange_groups()
    arrived = [swap_with(give, core, 1)]
    above1, split1 = from_above(down1)
    above0, split0 = from_above(down0)
    scattered = []
    while len(groups) > 1 and keep.shape[0] >> len(groups[0]) >= 16:
        group, groups = groups[0], groups[1:]
        blocks = 1 << len(group)
        size = keep.shape[0] // blocks
        keep, *gives = call_kernel(
            lambda *refs, group=group: fold_kernel(group, *refs),
            [shape_of(f32, size, width)] + [shape_of(bf16, size, width)] * (blocks - 1),
            [],
            [keep] + arrived,
            scratch=[pltpu.VMEM((blocks, size, width), f32)],
            limit=4,
        )
        arrived = [swap_with(x, group, at) for at, x in enumerate(gives, 1)]
        scattered.append(group)
    beside1 = beside(next1, above1, split1)
    from_left1 = from_behind(beside1, 0, 1)
    (total,) = call_kernel(
        add_kernel,
        [shape_of(bf16, *keep.shape)],
        [],
        [keep] + arrived,
        limit=4,
        after=[beside1],
    )
    beside0 = beside(next0, above0, split0)
    from_left0 = from_behind(beside0, 0, 1)
    part1 = part(home1, above1, split1, from_left1)
    for group in groups:
        total = joined(group, total, True, after=[beside0, part1])
    part0 = part(home0, above0, split0, from_left0)
    for group in reversed(scattered):
        total = joined(group, total, False, after=[part0])
    tile_grads = [over_owners(part0), over_owners(part1)]
    other = swap_with(total, core, 1)
    new_slices = [
        (own[s].astype(f32) - object_rate * tile_grads[s]).astype(bf16) for s in range(2)
    ]
    new_object = jnp.stack(new_slices)[None]
    positions_all = lax.axis_size("tile") * lax.axis_size("pos") * (patterns.shape[2] // 2)
    step = probe_rate / math.sqrt(positions_all)
    (new_probe,) = call_kernel(
        lambda *refs: probe_kernel(step, modes, *refs),
        [shape_of(f32, *probe.shape)],
        [],
        [total, other, probe],
        limit=8,
    )
    new_probe = new_probe.reshape(2, pixels, lane_tiles, modes, 128).transpose(0, 1, 3, 2, 4)
    return (new_object, new_probe.reshape(probe_modes.shape))


def solution(mesh):
    placed = (
        P("tile", None, None, None, None),
        P(),
        P("tile", "pos", None, None, None),
        P("tile", "pos", None, None),
        P("tile", "pos"),
    )
    return jax.shard_map(
        shards,
        mesh=mesh,
        in_specs=placed,
        out_specs=(P("tile", None, None, None, None), P()),
        check_vma=False,
    )
```

```python
import math

import jax
import jax.numpy as jnp
import numpy as np
from jax import lax
from jax.experimental import pallas as pl
from jax.experimental.pallas import tpu as pltpu
from jax.sharding import PartitionSpec as P

GRID_ROWS = 4


fresnel_coeff = 0.25
object_rate = 0.05
probe_rate = 0.15

f32 = jnp.float32
bf16 = jnp.bfloat16


def from_behind(block, rows, cols):
    tiles = lax.axis_size("tile")
    across = tiles // GRID_ROWS

    def source(i):
        return (i // across - rows) % GRID_ROWS * across + (i % across - cols) % across

    return lax.ppermute(block, "tile", [(source(i), i) for i in range(tiles)])


def real_embed(part_re, part_im):
    upper_half = np.concatenate([part_re, -part_im], axis=1)
    lower_half = np.concatenate([part_im, part_re], axis=1)
    stacked = np.concatenate([upper_half, lower_half], axis=0)
    return jnp.asarray(stacked, dtype=f32).astype(bf16)


def build_tables(pixels):
    indices = np.arange(pixels)
    angles = indices[:, None] * indices[None, :] % pixels * (2.0 * math.pi / pixels)
    norm_scale = 1.0 / math.sqrt(pixels)
    dft_re = np.cos(angles) * norm_scale
    dft_im = -np.sin(angles) * norm_scale
    frequency = np.where(indices < pixels // 2, indices, indices - pixels)
    phases = -2.0 * math.pi * fresnel_coeff / pixels * (frequency * frequency)
    phase_sum = phases[:, None] + angles
    kern_re = np.sum(np.cos(phase_sum), axis=0) / pixels
    kern_im = np.sum(np.sin(phase_sum), axis=0) / pixels
    lag_index = (indices[:, None] - indices[None, :]) % pixels
    prop_re = kern_re[lag_index]
    prop_im = kern_im[lag_index]
    return real_embed(prop_re, prop_im), real_embed(dft_re, dft_im)


def dot(a, b):
    return jnp.dot(a, b, preferred_element_type=f32)


def shift_tables(offsets_ref, counts_ref, message_ref):
    n = message_ref.shape[1]
    sent = message_ref[n:, :].astype(f32)
    busy = counts_ref[0, 0] == offsets_ref.shape[2]
    row = jnp.where(busy, offsets_ref[0, 0, 0, 0], sent[0:1].astype(jnp.int32))
    col = jnp.where(busy, offsets_ref[0, 0, 0, 1], sent[1:2].astype(jnp.int32))
    i_out = lax.broadcasted_iota(jnp.int32, (n, 2 * n), 0)
    i_in = lax.broadcasted_iota(jnp.int32, (n, 2 * n), 1)
    j_in = lax.broadcasted_iota(jnp.int32, (2 * n, n), 0)
    j_out = lax.broadcasted_iota(jnp.int32, (2 * n, n), 1)
    row2 = jnp.concatenate([row, row], axis=1)
    col2 = jnp.concatenate([col, col], axis=1)
    rows = (i_in == i_out + row2).astype(f32).astype(bf16)
    cols = (j_in == j_out + col).astype(f32).astype(bf16)
    rows_t = (j_in == j_out + row).astype(f32).astype(bf16)
    cols_t = (i_in == i_out + col2).astype(f32).astype(bf16)
    return rows, cols, rows_t, cols_t, col, busy


def patch(shifts, own_ref, right_ref, below_ref, diag_ref, part):
    upper = jnp.concatenate([own_ref[part], right_ref[part]], axis=1)
    lower = jnp.concatenate([below_ref[part], diag_ref[part]], axis=1)
    rows = dot(shifts[0], jnp.concatenate([upper, lower], axis=0)).astype(bf16)
    return dot(rows, shifts[1])


def transform(table_ref, wave_re, wave_im):
    n = wave_re.shape[0]
    table = table_ref[...]
    wave = jnp.concatenate([wave_re.astype(bf16), wave_im.astype(bf16)], axis=0)
    first = dot(table, wave)
    first = jnp.concatenate([first[:n].astype(bf16), (-first[n:]).astype(bf16)], axis=1)
    out = dot(first, table)
    return out[:, :n], out[:, n:]


def probe_plane(probe_ref, part, mode, modes):
    lane_tiles = 2
    n = probe_ref.shape[0] // (2 * lane_tiles * modes)
    step = lane_tiles * modes
    halves = [
        probe_ref[pl.ds(part * n * step + tile * modes + mode, n, stride=step), :]
        for tile in range(lane_tiles)
    ]
    return jnp.concatenate(halves, axis=1)


def ready_kernel(tile_ref, probe_ref, prop_ref, own_ref, planes_ref, table_ref):
    own_ref[...] = tile_ref[0, 1]
    table_ref[...] = prop_ref[...]
    n = planes_ref.shape[1]
    modes = planes_ref.shape[2] // n
    for part in range(2):
        for mode in range(modes):
            planes_ref[part, :, pl.ds(mode * n, n)] = probe_plane(probe_ref, part, mode, modes)


def arrive_kernel(
    offsets_ref, counts_ref, message_ref, own_ref, right_ref, below_ref, diag_ref, planes_ref,
    prop_ref, near_ref, arrive_ref,
):
    n = own_ref.shape[1]
    shifts = shift_tables(offsets_ref, counts_ref, message_ref)
    tiles = (own_ref, right_ref.at[0], below_ref, diag_ref)
    near = [patch(shifts, *tiles, part) for part in range(2)]
    for part in range(2):
        near_ref[part] = near[part].astype(bf16)
    for mode in range(planes_ref.shape[2] // n):
        lanes = pl.ds(mode * n, n)
        p_re, p_im = planes_ref[0, :, lanes], planes_ref[1, :, lanes]
        a_re, a_neg = transform(
            prop_ref, p_re * near[0] - p_im * near[1], p_re * near[1] + p_im * near[0]
        )
        arrive_ref[0, :, lanes] = a_re
        arrive_ref[1, :, lanes] = -a_neg


def spread(shifts, grad, home_ref, next_ref, down_ref):
    rows_t, cols_t, col = shifts[2:5]
    n = rows_t.shape[1]
    wrap_cols = cols_t[:, :n] + cols_t[:, n:]
    for part in range(2):
        rows = dot(rows_t, grad[part].astype(bf16)).astype(bf16)
        wide = dot(rows[:n], cols_t).astype(bf16)
        home_ref[part] = wide[:, :n]
        next_ref[part] = wide[:, n:]
        down_ref[pl.ds(part * n, n), :] = dot(rows[n:], wrap_cols).astype(bf16)
    edge = lax.broadcasted_iota(jnp.int32, (16, n), 1) < col
    down_ref[pl.ds(2 * n, 16), :] = edge.astype(f32).astype(bf16)


def gradient_kernel(
    offsets_ref, counts_ref, message_ref, own_ref, right_ref, below_ref, diag_ref, near_ref,
    arrive_ref, planes_ref, patterns_ref, prop_ref, dft_ref,
    home_ref, next_ref, down_ref, grad_ref, keep_ref, give_ref, term_ref,
):
    n = own_ref.shape[1]
    modes = planes_ref.shape[2] // n
    shifts = shift_tables(offsets_ref, counts_ref, message_ref)
    busy = shifts[5]
    tiles = (own_ref, right_ref.at[1], below_ref, diag_ref)
    far = [patch(shifts, *tiles, part) for part in range(2)]
    fields = []
    for mode in range(modes):
        lanes = pl.ds(mode * n, n)
        a_re, a_im = arrive_ref[0, :, lanes], arrive_ref[1, :, lanes]
        fields.append(
            transform(dft_ref, far[0] * a_re - far[1] * a_im, far[0] * a_im + far[1] * a_re)
        )
    intensity = sum(f_re * f_re + f_neg * f_neg for f_re, f_neg in fields)
    pattern = jnp.where(busy, patterns_ref[0, 0, 0].astype(f32), message_ref[:n, :].astype(f32))
    residual = intensity - pattern
    grad_far = [0.0, 0.0]
    waves = []
    for mode in range(modes):
        lanes = pl.ds(mode * n, n)
        f_re, f_neg = fields[mode]
        a_re, a_im = arrive_ref[0, :, lanes], arrive_ref[1, :, lanes]
        b_re, b_im = transform(dft_ref, f_re * residual, f_neg * residual)
        grad_far[0] += a_re * b_re + a_im * b_im
        grad_far[1] += a_re * b_im - a_im * b_re
        waves.append((far[0] * b_re + far[1] * b_im, far[1] * b_re - far[0] * b_im))
    grad_near = [0.0, 0.0]
    near = [near_ref[part].astype(f32) for part in range(2)]
    for mode in range(modes):
        lanes = pl.ds(mode * n, n)
        b_re, b_im = transform(prop_ref, *waves[mode])
        p_re, p_im = planes_ref[0, :, lanes], planes_ref[1, :, lanes]
        grad_near[0] += p_re * b_re + p_im * b_im
        grad_near[1] += p_re * b_im - p_im * b_re
        term_ref[0, :, lanes] = (near[0] * b_re + near[1] * b_im).astype(bf16)
        term_ref[1, :, lanes] = (near[0] * b_im - near[1] * b_re).astype(bf16)
    core = place_of(core_group())
    keep_ref[...] = term_ref[core]
    give_ref[...] = term_ref[1 - core]
    for part in range(2):
        grad_ref[part] = grad_near[part].astype(bf16)
    spread(shifts, grad_far, home_ref, next_ref, down_ref)


def spread_kernel(offsets_ref, counts_ref, message_ref, grad_ref, home_ref, next_ref, down_ref):
    shifts = shift_tables(offsets_ref, counts_ref, message_ref)
    spread(shifts, [grad_ref[part] for part in range(2)], home_ref, next_ref, down_ref)


def beside_kernel(next_ref, above_ref, out_ref):
    n = out_ref.shape[1]
    split = above_ref[pl.ds(2 * n, 16), :].astype(f32)[0:1] > 0
    for part in range(2):
        above = above_ref[pl.ds(part * n, n), :].astype(f32)
        total = next_ref[part].astype(f32) + jnp.where(split, above, 0.0)
        out_ref[part] = total.astype(bf16)


def part_kernel(home_ref, above_ref, left_ref, out_ref):
    n = out_ref.shape[1]
    split = above_ref[pl.ds(2 * n, 16), :].astype(f32)[0:1] > 0
    for part in range(2):
        above = above_ref[pl.ds(part * n, n), :].astype(f32)
        total = home_ref[part].astype(f32) + jnp.where(split, 0.0, above)
        out_ref[part] = (total + left_ref[part].astype(f32)).astype(bf16)


def update_kernel(layer, own_ref, part_ref, other_ref, *refs):
    out_hbm, new_ref, sem = refs[-3:]
    grad = part_ref[...].astype(f32) + other_ref[...].astype(f32)
    new_ref[...] = (own_ref[...].astype(f32) - object_rate * grad).astype(bf16)
    copy = pltpu.make_async_copy(new_ref, out_hbm.at[0, layer], sem.at[0])
    copy.start()
    copy.wait()


def core_group():
    return [lax.axis_size("pos")]


def place_of(group):
    flat = lax.axis_index("tile") * lax.axis_size("pos") + lax.axis_index("pos")
    return sum(flat // mask % 2 * (1 << at) for at, mask in enumerate(group))


def job(kernel, outs, arrays, scalars=(), scratch=()):
    return kernel, list(outs), list(scalars), list(arrays), list(scratch)


def run(*jobs, flops=1_000_000, limit=4, after=()):
    vmem = pl.BlockSpec(memory_space=pltpu.VMEM)
    smem = pl.BlockSpec(memory_space=pltpu.SMEM)
    anywhere = pl.BlockSpec(memory_space=pl.ANY)
    kernels, outs, scalars, arrays, scratch = zip(*jobs)
    ins = [x + y for x, y in zip(scalars, arrays)]
    specs = [[smem] * len(x) + [vmem] * len(y) for x, y in zip(scalars, arrays)]

    def taken(refs, lists):
        parts = []
        for items in lists:
            parts.append(refs[: len(items)])
            refs = refs[len(items) :]
        return parts, refs

    def body(*refs):
        in_refs, refs = taken(refs, ins)
        out_refs, refs = taken(refs[len(after) :], outs)
        scratch_refs, _ = taken(refs, scratch)
        for kernel, *parts in zip(kernels, in_refs, out_refs, scratch_refs):
            kernel(*parts[0], *parts[1], *parts[2])

    moved = sum(x.size * x.dtype.itemsize for x in sum(ins, []) + sum(outs, []))
    results = pl.pallas_call(
        body,
        out_shape=sum(outs, []),
        in_specs=sum(specs, []) + [anywhere] * len(after),
        out_specs=[vmem] * len(sum(outs, [])),
        scratch_shapes=sum(scratch, []),
        compiler_params=pltpu.CompilerParams(vmem_limit_bytes=limit * 2**20),
        cost_estimate=pl.CostEstimate(flops=flops, bytes_accessed=moved, transcendentals=0),
    )(*sum(ins, []), *after)
    results, _ = taken(results, outs)
    return results[0] if len(jobs) == 1 else results


def updated(layer, own, part, other, like, so_far, after):
    vmem = pl.BlockSpec(memory_space=pltpu.VMEM)
    anywhere = pl.BlockSpec(memory_space=pl.ANY)
    extra = [x for x in (so_far,) if x is not None] + list(after)
    return pl.pallas_call(
        lambda *refs: update_kernel(layer, *refs),
        out_shape=like,
        in_specs=[vmem] * 3 + [anywhere] * len(extra),
        out_specs=pl.BlockSpec(memory_space=pl.ANY),
        scratch_shapes=[pltpu.VMEM(own.shape, bf16), pltpu.SemaphoreType.DMA((1,))],
        input_output_aliases={} if so_far is None else {3: 0},
        compiler_params=pltpu.CompilerParams(vmem_limit_bytes=4 * 2**20),
        cost_estimate=pl.CostEstimate(
            flops=own.size, bytes_accessed=8 * own.size, transcendentals=0
        ),
    )(own, part, other, *extra)


def shape_of(kind, *dims):
    return jax.ShapeDtypeStruct(dims, kind)


def handed_over(patterns, offsets, counts):
    owners = lax.axis_size("pos")
    slots, pixels = patterns.shape[2], patterns.shape[4]

    def message(pattern, spot):
        at = lax.broadcasted_iota(jnp.int32, (16, pixels), 0)
        rows = jnp.where(at == 0, spot[0], jnp.where(at == 1, spot[1], 0))
        return jnp.concatenate([pattern, rows.astype(bf16)], axis=0)

    if owners == slots:
        sent = message(patterns[0, 0, 1], offsets[0, 0, 1])
        return sent, lax.ppermute(sent, "pos", [(i, 1 - i) for i in range(2)]), counts
    all_counts = lax.all_gather(counts[0, 0], "pos")
    ends = jnp.cumsum(all_counts)
    rank = lax.axis_index("pos")
    source = jnp.sum((ends <= rank).astype(jnp.int32))
    slot = rank - (ends[source] - all_counts[source])
    spot = lax.all_gather(offsets[0, 0], "pos")[source, slot]
    pattern = lax.all_gather(patterns[0, 0], "pos")[source, slot]
    sent = message(pattern, spot)
    return sent, sent, jnp.zeros_like(counts)


def fold_kernel(group, keep_ref, *refs):
    blocks = refs[-1]
    got = len(refs) - 1 - blocks.shape[0]
    arrived, keep_out, give_outs = refs[:got], refs[got], refs[got + 1 : -1]
    total = keep_ref[...].astype(f32)
    for ref in arrived:
        total += ref[...].astype(f32)
    size = blocks.shape[1]
    for block in range(blocks.shape[0]):
        blocks[block] = total[block * size : (block + 1) * size]
    here = place_of(group)
    keep_out[...] = blocks[here]
    for distance, ref in enumerate(give_outs, 1):
        ref[...] = blocks[here ^ distance].astype(bf16)


def add_kernel(keep_ref, *refs):
    total = keep_ref[...].astype(f32)
    for ref in refs[:-1]:
        total += ref[...].astype(f32)
    refs[-1][...] = total.astype(bf16)


def place_kernel(group, add, *refs):
    arrived, out_ref, blocks = refs[:-2], refs[-2], refs[-1]
    here = place_of(group)
    for distance, ref in enumerate(arrived):
        blocks[here ^ distance] = ref[...]
    size = blocks.shape[1]
    if add:
        total = blocks[0].astype(f32)
        for block in range(1, blocks.shape[0]):
            total += blocks[block].astype(f32)
        out_ref[...] = total.astype(bf16)
    else:
        for block in range(blocks.shape[0]):
            out_ref[pl.ds(block * size, size), :] = blocks[block]


def probe_kernel(step, modes, mine_ref, other_ref, probe_ref, out_ref):
    core = place_of(core_group())
    lane_tiles = 2
    n = mine_ref.shape[0]
    stride = lane_tiles * modes
    for part in range(2):
        total = jnp.where(core == part, mine_ref[...].astype(f32), other_ref[...].astype(f32))
        for mode in range(modes):
            for tile in range(lane_tiles):
                lane = (mode * lane_tiles + tile) * 128
                where = pl.ds(part * n * stride + tile * modes + mode, n, stride=stride)
                out_ref[where, :] = probe_ref[where, :] - step * total[:, lane : lane + 128]


def exchange_groups():
    tiles, owners = lax.axis_size("tile"), lax.axis_size("pos")
    bits = [1 << bit for bit in range(owners.bit_length() - 1)]
    bits += [owners << bit for bit in range(1, tiles.bit_length() - 1)]
    return [bits[at : at + 2] for at in range(0, len(bits), 2)]


def swap_with(x, group, distance):
    mask = sum(bit for at, bit in enumerate(group) if distance >> at & 1)
    devices = lax.axis_size("tile") * lax.axis_size("pos")
    return lax.ppermute(x, ("tile", "pos"), [(i, i ^ mask) for i in range(devices)])


def joined(group, x, add):
    blocks = 1 << len(group)
    arrived = [x] + [swap_with(x, group, at) for at in range(1, blocks)]
    return job(
        lambda *refs: place_kernel(group, add, *refs),
        [shape_of(bf16, x.shape[0] * (1 if add else blocks), x.shape[1])],
        arrived,
        scratch=[pltpu.VMEM((blocks,) + x.shape, bf16)],
    )


def folded(group, keep, arrived):
    blocks = 1 << len(group)
    size, width = keep.shape[0] // blocks, keep.shape[1]
    return job(
        lambda *refs: fold_kernel(group, *refs),
        [shape_of(f32, size, width)] + [shape_of(bf16, size, width)] * (blocks - 1),
        [keep] + arrived,
        scratch=[pltpu.VMEM((blocks, size, width), f32)],
    )


def shards(tile_object, probe_modes, patterns, offsets, counts):
    _, pixels, modes, _ = probe_modes.shape
    width = modes * pixels
    lane_tiles = pixels // 128
    prop, dft = build_tables(pixels)
    tile = shape_of(bf16, 2, pixels, pixels)
    planes = shape_of(f32, 2, pixels, width)
    probe = probe_modes.reshape(2, pixels, modes, lane_tiles, 128)
    probe = probe.transpose(0, 1, 3, 2, 4).reshape(-1, 128)

    own0 = tile_object[0, 0]
    below0 = from_behind(own0, -1, 0)
    right = from_behind(tile_object[0], 0, -1)
    sent, message, counts = handed_over(patterns, offsets, counts)
    own1, probe_planes, table = run(
        job(ready_kernel, [tile, planes, shape_of(bf16, *prop.shape)], [tile_object, probe, prop]),
        limit=16,
        after=[own0, sent],
    )
    below1 = from_behind(own1, -1, 0)
    diag0 = from_behind(below0, 0, -1)
    diag1 = from_behind(below1, 0, -1)
    near, arrive = run(
        job(
            arrive_kernel,
            [tile, planes],
            [message, own0, right, below0, diag0, probe_planes, table],
            scalars=[offsets, counts],
        ),
        flops=1_500_000_000,
        limit=16,
    )
    half = shape_of(bf16, pixels, width)
    down = shape_of(bf16, 2 * pixels + 16, pixels)
    home1, next1, down1, grad0, keep, give = run(
        job(
            gradient_kernel,
            [tile, tile, down, tile, half, half],
            [message, own1, right, below1, diag1, near, arrive, probe_planes, patterns, table, dft],
            scalars=[offsets, counts],
            scratch=[pltpu.VMEM((2, pixels, width), bf16)],
        ),
        flops=4_000_000_000,
        limit=16,
    )

    core, groups = core_group(), exchange_groups()
    above1 = from_behind(down1, 1, 0)
    arrived = [swap_with(give, core, 1)]
    side = [
        job(
            spread_kernel,
            [tile, tile, down],
            [message, grad0],
            scalars=[offsets, counts],
        )
    ]
    scattered = []
    while len(groups) > 1 and keep.shape[0] >> len(groups[0]) >= 16:
        group, groups = groups[0], groups[1:]
        done = run(folded(group, keep, arrived), *side, limit=8)
        if side:
            done, (home0, next0, down0) = done
            above0 = from_behind(down0, 1, 0)
            side = []
        keep, *gives = done
        arrived = [swap_with(x, group, at) for at, x in enumerate(gives, 1)]
        scattered.append(group)
    (beside1,), (total,) = run(
        job(beside_kernel, [tile], [next1, above1]),
        job(add_kernel, [shape_of(bf16, *keep.shape)], [keep] + arrived),
    )
    from_left1 = from_behind(beside1, 0, 1)
    (beside0,) = run(job(beside_kernel, [tile], [next0, above0]), after=[total])
    from_left0 = from_behind(beside0, 0, 1)
    (total,), (part1,) = run(
        joined(groups[0], total, True),
        job(part_kernel, [tile], [home1, above1, from_left1]),
        after=[beside0],
    )
    for group in groups[1:]:
        (total,) = run(joined(group, total, True))

    def from_owners(part):
        if lax.axis_size("pos") == 2:
            return lax.ppermute(part, "pos", [(0, 1), (1, 0)])
        return lax.psum(part.astype(f32), "pos") - part.astype(f32)

    other1 = from_owners(part1)
    (total,), (part0,) = run(
        joined(scattered[-1], total, False),
        job(part_kernel, [tile], [home0, above0, from_left0]),
    )
    other0 = from_owners(part0)
    for group in reversed(scattered[:-1]):
        (total,) = run(joined(group, total, False))
    other_half = swap_with(total, core, 1)
    positions_all = lax.axis_size("tile") * lax.axis_size("pos") * (patterns.shape[2] // 2)
    step = probe_rate / math.sqrt(positions_all)
    like = shape_of(bf16, *tile_object.shape)
    new_object = updated(1, own1, part1, other1, like, None, [])
    (new_probe,) = run(
        job(
            lambda *refs: probe_kernel(step, modes, *refs),
            [shape_of(f32, *probe.shape)],
            [total, other_half, probe],
        ),
        limit=8,
    )
    new_object = updated(0, own0, part0, other0, like, new_object, [new_probe])
    new_probe = new_probe.reshape(2, pixels, lane_tiles, modes, 128).transpose(0, 1, 3, 2, 4)
    return (new_object, new_probe.reshape(probe_modes.shape))


def solution(mesh):
    placed = (
        P("tile", None, None, None, None),
        P(),
        P("tile", "pos", None, None, None),
        P("tile", "pos", None, None),
        P("tile", "pos"),
    )
    return jax.shard_map(
        shards,
        mesh=mesh,
        in_specs=placed,
        out_specs=(P("tile", None, None, None, None), P()),
        check_vma=False,
    )
```

```python
import math

import jax
import jax.numpy as jnp
import numpy as np
from jax import lax
from jax.experimental import pallas as pl
from jax.experimental.pallas import tpu as pltpu
from jax.sharding import PartitionSpec as P

GRID_ROWS = 4


fresnel_coeff = 0.25
object_rate = 0.05
probe_rate = 0.15

f32 = jnp.float32
bf16 = jnp.bfloat16


def from_behind(block, rows, cols):
    tiles = lax.axis_size("tile")
    across = tiles // GRID_ROWS

    def source(i):
        return (i // across - rows) % GRID_ROWS * across + (i % across - cols) % across

    return lax.ppermute(block, "tile", [(source(i), i) for i in range(tiles)])


def real_embed(part_re, part_im):
    upper_half = np.concatenate([part_re, -part_im], axis=1)
    lower_half = np.concatenate([part_im, part_re], axis=1)
    stacked = np.concatenate([upper_half, lower_half], axis=0)
    return jnp.asarray(stacked, dtype=f32).astype(bf16)


def build_tables(pixels):
    indices = np.arange(pixels)
    angles = indices[:, None] * indices[None, :] % pixels * (2.0 * math.pi / pixels)
    norm_scale = 1.0 / math.sqrt(pixels)
    dft_re = np.cos(angles) * norm_scale
    dft_im = -np.sin(angles) * norm_scale
    frequency = np.where(indices < pixels // 2, indices, indices - pixels)
    phases = -2.0 * math.pi * fresnel_coeff / pixels * (frequency * frequency)
    phase_sum = phases[:, None] + angles
    kern_re = np.sum(np.cos(phase_sum), axis=0) / pixels
    kern_im = np.sum(np.sin(phase_sum), axis=0) / pixels
    lag_index = (indices[:, None] - indices[None, :]) % pixels
    prop_re = kern_re[lag_index]
    prop_im = kern_im[lag_index]
    return real_embed(prop_re, prop_im), real_embed(dft_re, dft_im)


def dot(a, b):
    return jnp.dot(a, b, preferred_element_type=f32)


def shift_tables(mine_ref, sent_ref):
    n = mine_ref.shape[1]
    mine = mine_ref[n:, :].astype(f32)
    sent = sent_ref[n:, :].astype(f32)
    busy = mine[2:3] > 0
    row = jnp.where(busy, mine[0:1], sent[0:1]).astype(jnp.int32)
    col = jnp.where(busy, mine[1:2], sent[1:2]).astype(jnp.int32)
    i_out = lax.broadcasted_iota(jnp.int32, (n, 2 * n), 0)
    i_in = lax.broadcasted_iota(jnp.int32, (n, 2 * n), 1)
    j_in = lax.broadcasted_iota(jnp.int32, (2 * n, n), 0)
    j_out = lax.broadcasted_iota(jnp.int32, (2 * n, n), 1)
    row2 = jnp.concatenate([row, row], axis=1)
    col2 = jnp.concatenate([col, col], axis=1)
    rows = (i_in == i_out + row2).astype(f32).astype(bf16)
    cols = (j_in == j_out + col).astype(f32).astype(bf16)
    rows_t = (j_in == j_out + row).astype(f32).astype(bf16)
    cols_t = (i_in == i_out + col2).astype(f32).astype(bf16)
    return rows, cols, rows_t, cols_t, col, busy


def patch(shifts, own_ref, right_ref, below_ref, diag_ref, part):
    upper = jnp.concatenate([own_ref[part], right_ref[part]], axis=1)
    lower = jnp.concatenate([below_ref[part], diag_ref[part]], axis=1)
    rows = dot(shifts[0], jnp.concatenate([upper, lower], axis=0)).astype(bf16)
    return dot(rows, shifts[1])


def transform(table_ref, wave_re, wave_im):
    n = wave_re.shape[0]
    table = table_ref[...]
    wave = jnp.concatenate([wave_re.astype(bf16), wave_im.astype(bf16)], axis=0)
    first = dot(table, wave)
    first = jnp.concatenate([first[:n].astype(bf16), (-first[n:]).astype(bf16)], axis=1)
    out = dot(first, table)
    return out[:, :n], out[:, n:]


def probe_plane(probe_ref, part, mode, modes):
    lane_tiles = 2
    n = probe_ref.shape[0] // (2 * lane_tiles * modes)
    step = lane_tiles * modes
    halves = [
        probe_ref[pl.ds(part * n * step + tile * modes + mode, n, stride=step), :]
        for tile in range(lane_tiles)
    ]
    return jnp.concatenate(halves, axis=1)


def ready_kernel(
    offsets_ref, counts_ref, own_ref, patterns_ref, probe_ref, prop_ref,
    own_out, mine_ref, sent_ref, planes_ref, table_ref,
):
    own_out[...] = own_ref[...]
    table_ref[...] = prop_ref[...]
    n = planes_ref.shape[1]
    at = lax.broadcasted_iota(jnp.int32, (16, n), 0)
    busy = (counts_ref[0, 0] == patterns_ref.shape[2]).astype(jnp.int32)
    for slot, ref in enumerate((mine_ref, sent_ref)):
        row, col = offsets_ref[0, 0, slot, 0], offsets_ref[0, 0, slot, 1]
        rows = jnp.where(at == 0, row, jnp.where(at == 1, col, busy))
        ref[pl.ds(0, n), :] = patterns_ref[0, 0, slot]
        ref[pl.ds(n, 16), :] = rows.astype(f32).astype(bf16)
    modes = planes_ref.shape[2] // n
    for part in range(2):
        for mode in range(modes):
            planes_ref[part, :, pl.ds(mode * n, n)] = probe_plane(probe_ref, part, mode, modes)


def arrive_kernel(
    mine_ref, sent_ref, own_ref, right_ref, below_ref, diag_ref, planes_ref, prop_ref,
    near_ref, arrive_ref,
):
    n = own_ref.shape[1]
    shifts = shift_tables(mine_ref, sent_ref)
    tiles = (own_ref, right_ref.at[0], below_ref, diag_ref)
    near = [patch(shifts, *tiles, part) for part in range(2)]
    for part in range(2):
        near_ref[part] = near[part].astype(bf16)
    for mode in range(planes_ref.shape[2] // n):
        lanes = pl.ds(mode * n, n)
        p_re, p_im = planes_ref[0, :, lanes], planes_ref[1, :, lanes]
        a_re, a_neg = transform(
            prop_ref, p_re * near[0] - p_im * near[1], p_re * near[1] + p_im * near[0]
        )
        arrive_ref[0, :, lanes] = a_re
        arrive_ref[1, :, lanes] = -a_neg


def spread(shifts, grad, home_ref, next_ref, down_ref):
    rows_t, cols_t, col = shifts[2:5]
    n = rows_t.shape[1]
    wrap_cols = cols_t[:, :n] + cols_t[:, n:]
    for part in range(2):
        rows = dot(rows_t, grad[part].astype(bf16)).astype(bf16)
        wide = dot(rows[:n], cols_t).astype(bf16)
        home_ref[part] = wide[:, :n]
        next_ref[part] = wide[:, n:]
        down_ref[pl.ds(part * n, n), :] = dot(rows[n:], wrap_cols).astype(bf16)
    edge = lax.broadcasted_iota(jnp.int32, (16, n), 1) < col
    down_ref[pl.ds(2 * n, 16), :] = edge.astype(f32).astype(bf16)


def gradient_kernel(
    mine_ref, sent_ref, own_ref, right_ref, below_ref, diag_ref, near_ref, arrive_ref,
    planes_ref, prop_ref, dft_ref,
    home_ref, next_ref, down_ref, grad_ref, keep_ref, give_ref, term_ref,
):
    n = own_ref.shape[1]
    modes = planes_ref.shape[2] // n
    shifts = shift_tables(mine_ref, sent_ref)
    busy = shifts[5]
    tiles = (own_ref, right_ref.at[1], below_ref, diag_ref)
    far = [patch(shifts, *tiles, part) for part in range(2)]
    fields = []
    for mode in range(modes):
        lanes = pl.ds(mode * n, n)
        a_re, a_im = arrive_ref[0, :, lanes], arrive_ref[1, :, lanes]
        fields.append(
            transform(dft_ref, far[0] * a_re - far[1] * a_im, far[0] * a_im + far[1] * a_re)
        )
    intensity = sum(f_re * f_re + f_neg * f_neg for f_re, f_neg in fields)
    pattern = jnp.where(busy, mine_ref[:n, :].astype(f32), sent_ref[:n, :].astype(f32))
    residual = intensity - pattern
    grad_far = [0.0, 0.0]
    waves = []
    for mode in range(modes):
        lanes = pl.ds(mode * n, n)
        f_re, f_neg = fields[mode]
        a_re, a_im = arrive_ref[0, :, lanes], arrive_ref[1, :, lanes]
        b_re, b_im = transform(dft_ref, f_re * residual, f_neg * residual)
        grad_far[0] += a_re * b_re + a_im * b_im
        grad_far[1] += a_re * b_im - a_im * b_re
        waves.append((far[0] * b_re + far[1] * b_im, far[1] * b_re - far[0] * b_im))
    grad_near = [0.0, 0.0]
    near = [near_ref[part].astype(f32) for part in range(2)]
    for mode in range(modes):
        lanes = pl.ds(mode * n, n)
        b_re, b_im = transform(prop_ref, *waves[mode])
        p_re, p_im = planes_ref[0, :, lanes], planes_ref[1, :, lanes]
        grad_near[0] += p_re * b_re + p_im * b_im
        grad_near[1] += p_re * b_im - p_im * b_re
        term_ref[0, :, lanes] = (near[0] * b_re + near[1] * b_im).astype(bf16)
        term_ref[1, :, lanes] = (near[0] * b_im - near[1] * b_re).astype(bf16)
    core = place_of(core_group())
    keep_ref[...] = term_ref[core]
    give_ref[...] = term_ref[1 - core]
    for part in range(2):
        grad_ref[part] = grad_near[part].astype(bf16)
    spread(shifts, grad_far, home_ref, next_ref, down_ref)


def spread_kernel(mine_ref, sent_ref, grad_ref, home_ref, next_ref, down_ref):
    shifts = shift_tables(mine_ref, sent_ref)
    spread(shifts, [grad_ref[part] for part in range(2)], home_ref, next_ref, down_ref)


def beside_kernel(next_ref, above_ref, out_ref):
    n = out_ref.shape[1]
    split = above_ref[pl.ds(2 * n, 16), :].astype(f32)[0:1] > 0
    for part in range(2):
        above = above_ref[pl.ds(part * n, n), :].astype(f32)
        total = next_ref[part].astype(f32) + jnp.where(split, above, 0.0)
        out_ref[part] = total.astype(bf16)


def part_kernel(home_ref, above_ref, left_ref, out_ref):
    n = out_ref.shape[1]
    split = above_ref[pl.ds(2 * n, 16), :].astype(f32)[0:1] > 0
    for part in range(2):
        above = above_ref[pl.ds(part * n, n), :].astype(f32)
        total = home_ref[part].astype(f32) + jnp.where(split, 0.0, above)
        out_ref[part] = (total + left_ref[part].astype(f32)).astype(bf16)


def update_kernel(layer, own_ref, part_ref, other_ref, *refs):
    out_hbm, new_ref, sem = refs[-3:]
    grad = part_ref[...].astype(f32) + other_ref[...].astype(f32)
    new_ref[...] = (own_ref[...].astype(f32) - object_rate * grad).astype(bf16)
    copy = pltpu.make_async_copy(new_ref, out_hbm.at[0, layer], sem.at[0])
    copy.start()
    copy.wait()


def core_group():
    return [lax.axis_size("pos")]


def place_of(group):
    flat = lax.axis_index("tile") * lax.axis_size("pos") + lax.axis_index("pos")
    return sum(flat // mask % 2 * (1 << at) for at, mask in enumerate(group))


def job(kernel, outs, arrays, scalars=(), scratch=()):
    return kernel, list(outs), list(scalars), list(arrays), list(scratch)


def run(*jobs, flops=1_000_000, limit=4, after=()):
    vmem = pl.BlockSpec(memory_space=pltpu.VMEM)
    smem = pl.BlockSpec(memory_space=pltpu.SMEM)
    anywhere = pl.BlockSpec(memory_space=pl.ANY)
    kernels, outs, scalars, arrays, scratch = zip(*jobs)
    ins = [x + y for x, y in zip(scalars, arrays)]
    specs = [[smem] * len(x) + [vmem] * len(y) for x, y in zip(scalars, arrays)]

    def taken(refs, lists):
        parts = []
        for items in lists:
            parts.append(refs[: len(items)])
            refs = refs[len(items) :]
        return parts, refs

    def body(*refs):
        in_refs, refs = taken(refs, ins)
        out_refs, refs = taken(refs[len(after) :], outs)
        scratch_refs, _ = taken(refs, scratch)
        for kernel, *parts in zip(kernels, in_refs, out_refs, scratch_refs):
            kernel(*parts[0], *parts[1], *parts[2])

    moved = sum(x.size * x.dtype.itemsize for x in sum(ins, []) + sum(outs, []))
    results = pl.pallas_call(
        body,
        out_shape=sum(outs, []),
        in_specs=sum(specs, []) + [anywhere] * len(after),
        out_specs=[vmem] * len(sum(outs, [])),
        scratch_shapes=sum(scratch, []),
        compiler_params=pltpu.CompilerParams(vmem_limit_bytes=limit * 2**20),
        cost_estimate=pl.CostEstimate(flops=flops, bytes_accessed=moved, transcendentals=0),
    )(*sum(ins, []), *after)
    results, _ = taken(results, outs)
    return results[0] if len(jobs) == 1 else results


def updated(layer, own, part, other, like, so_far, after):
    vmem = pl.BlockSpec(memory_space=pltpu.VMEM)
    anywhere = pl.BlockSpec(memory_space=pl.ANY)
    extra = [x for x in (so_far,) if x is not None] + list(after)
    return pl.pallas_call(
        lambda *refs: update_kernel(layer, *refs),
        out_shape=like,
        in_specs=[vmem] * 3 + [anywhere] * len(extra),
        out_specs=pl.BlockSpec(memory_space=pl.ANY),
        scratch_shapes=[pltpu.VMEM(own.shape, bf16), pltpu.SemaphoreType.DMA((1,))],
        input_output_aliases={} if so_far is None else {3: 0},
        compiler_params=pltpu.CompilerParams(vmem_limit_bytes=4 * 2**20),
        cost_estimate=pl.CostEstimate(
            flops=own.size, bytes_accessed=8 * own.size, transcendentals=0
        ),
    )(own, part, other, *extra)


def shape_of(kind, *dims):
    return jax.ShapeDtypeStruct(dims, kind)


def gathered_message(patterns, offsets, counts):
    pixels = patterns.shape[4]
    all_counts = lax.all_gather(counts[0, 0], "pos")
    ends = jnp.cumsum(all_counts)
    rank = lax.axis_index("pos")
    source = jnp.sum((ends <= rank).astype(jnp.int32))
    slot = rank - (ends[source] - all_counts[source])
    spot = lax.all_gather(offsets[0, 0], "pos")[source, slot]
    pattern = lax.all_gather(patterns[0, 0], "pos")[source, slot]
    at = lax.broadcasted_iota(jnp.int32, (16, pixels), 0)
    rows = jnp.where(at == 0, spot[0], jnp.where(at == 1, spot[1], 0))
    return jnp.concatenate([pattern, rows.astype(bf16)], axis=0)


def fold_kernel(group, keep_ref, *refs):
    blocks = refs[-1]
    got = len(refs) - 1 - blocks.shape[0]
    arrived, keep_out, give_outs = refs[:got], refs[got], refs[got + 1 : -1]
    total = keep_ref[...].astype(f32)
    for ref in arrived:
        total += ref[...].astype(f32)
    size = blocks.shape[1]
    for block in range(blocks.shape[0]):
        blocks[block] = total[block * size : (block + 1) * size]
    here = place_of(group)
    keep_out[...] = blocks[here]
    for distance, ref in enumerate(give_outs, 1):
        ref[...] = blocks[here ^ distance].astype(bf16)


def add_kernel(keep_ref, *refs):
    total = keep_ref[...].astype(f32)
    for ref in refs[:-1]:
        total += ref[...].astype(f32)
    refs[-1][...] = total.astype(bf16)


def place_kernel(group, add, *refs):
    arrived, out_ref, blocks = refs[:-2], refs[-2], refs[-1]
    here = place_of(group)
    for distance, ref in enumerate(arrived):
        blocks[here ^ distance] = ref[...]
    size = blocks.shape[1]
    if add:
        total = blocks[0].astype(f32)
        for block in range(1, blocks.shape[0]):
            total += blocks[block].astype(f32)
        out_ref[...] = total.astype(bf16)
    else:
        for block in range(blocks.shape[0]):
            out_ref[pl.ds(block * size, size), :] = blocks[block]


def probe_kernel(step, modes, mine_ref, other_ref, probe_ref, out_ref, token_ref):
    core = place_of(core_group())
    token_ref[...] = jnp.zeros_like(token_ref)
    lane_tiles = 2
    n = mine_ref.shape[0]
    stride = lane_tiles * modes
    for part in range(2):
        total = jnp.where(core == part, mine_ref[...].astype(f32), other_ref[...].astype(f32))
        for mode in range(modes):
            for tile in range(lane_tiles):
                lane = (mode * lane_tiles + tile) * 128
                where = pl.ds(part * n * stride + tile * modes + mode, n, stride=stride)
                out_ref[where, :] = probe_ref[where, :] - step * total[:, lane : lane + 128]


def exchange_groups():
    tiles, owners = lax.axis_size("tile"), lax.axis_size("pos")
    bits = [1 << bit for bit in range(owners.bit_length() - 1)]
    bits += [owners << bit for bit in range(1, tiles.bit_length() - 1)]
    return [bits[at : at + 2] for at in range(0, len(bits), 2)]


def swap_with(x, group, distance):
    mask = sum(bit for at, bit in enumerate(group) if distance >> at & 1)
    devices = lax.axis_size("tile") * lax.axis_size("pos")
    return lax.ppermute(x, ("tile", "pos"), [(i, i ^ mask) for i in range(devices)])


def joined(group, x, arrived, add):
    blocks = 1 << len(group)
    return job(
        lambda *refs: place_kernel(group, add, *refs),
        [shape_of(bf16, x.shape[0] * (1 if add else blocks), x.shape[1])],
        [x] + arrived,
        scratch=[pltpu.VMEM((blocks,) + x.shape, bf16)],
    )


def swapped(x, group):
    return [swap_with(x, group, at) for at in range(1, 1 << len(group))]


def folded(group, keep, arrived):
    blocks = 1 << len(group)
    size, width = keep.shape[0] // blocks, keep.shape[1]
    return job(
        lambda *refs: fold_kernel(group, *refs),
        [shape_of(f32, size, width)] + [shape_of(bf16, size, width)] * (blocks - 1),
        [keep] + arrived,
        scratch=[pltpu.VMEM((blocks, size, width), f32)],
    )


def shards(tile_object, probe_modes, patterns, offsets, counts):
    _, pixels, modes, _ = probe_modes.shape
    width = modes * pixels
    lane_tiles = pixels // 128
    prop, dft = build_tables(pixels)
    tile = shape_of(bf16, 2, pixels, pixels)
    planes = shape_of(f32, 2, pixels, width)
    probe = probe_modes.reshape(2, pixels, modes, lane_tiles, 128)
    probe = probe.transpose(0, 1, 3, 2, 4).reshape(-1, 128)

    own = [tile_object[0, 0], tile_object[0, 1]]
    below0 = from_behind(own[0], -1, 0)
    right = from_behind(tile_object[0], 0, -1)
    exchanged = lax.axis_size("pos") == patterns.shape[2]
    message = shape_of(bf16, pixels + 16, pixels)
    own1, mine, sent, probe_planes, table = run(
        job(
            ready_kernel,
            [tile, message, message, planes, shape_of(bf16, *prop.shape)],
            [own[1], patterns, probe, prop],
            scalars=[offsets, counts if exchanged else jnp.zeros_like(counts)],
        ),
        limit=16,
        after=[own[0]],
    )
    below1 = from_behind(own1, -1, 0)
    if exchanged:
        sent = lax.ppermute(sent, "pos", [(i, 1 - i) for i in range(2)])
    else:
        sent = gathered_message(patterns, offsets, counts)
    diag0 = from_behind(below0, 0, -1)
    diag1 = from_behind(below1, 0, -1)
    near, arrive = run(
        job(
            arrive_kernel,
            [tile, planes],
            [mine, sent, own[0], right, below0, diag0, probe_planes, table],
        ),
        flops=1_500_000_000,
        limit=16,
    )
    half = shape_of(bf16, pixels, width)
    down = shape_of(bf16, 2 * pixels + 16, pixels)
    home1, next1, down1, grad0, keep, give = run(
        job(
            gradient_kernel,
            [tile, tile, down, tile, half, half],
            [mine, sent, own1, right, below1, diag1, near, arrive, probe_planes, table, dft],
            scratch=[pltpu.VMEM((2, pixels, width), bf16)],
        ),
        flops=4_000_000_000,
        limit=16,
    )

    def over_owners(part):
        if lax.axis_size("pos") == 2:
            return lax.ppermute(part, "pos", [(0, 1), (1, 0)])
        return lax.psum(part.astype(f32), "pos") - part.astype(f32)

    core, groups = core_group(), exchange_groups()
    above1 = from_behind(down1, 1, 0)
    arrived = [swap_with(give, core, 1)]
    side = [job(spread_kernel, [tile, tile, down], [mine, sent, grad0])]
    scattered = []
    while len(groups) > 1 and keep.shape[0] >> len(groups[0]) >= 16:
        group, groups = groups[0], groups[1:]
        done = run(folded(group, keep, arrived), *side, limit=8)
        if side:
            done, (home0, next0, down0) = done
            above0 = from_behind(down0, 1, 0)
            side = []
        keep, *gives = done
        arrived = [swap_with(x, group, at) for at, x in enumerate(gives, 1)]
        scattered.append(group)
    (beside1,), (total,) = run(
        job(beside_kernel, [tile], [next1, above1]),
        job(add_kernel, [shape_of(bf16, *keep.shape)], [keep] + arrived),
    )
    from_left1 = from_behind(beside1, 0, 1)
    arrived = swapped(total, groups[0])
    (beside0,) = run(job(beside_kernel, [tile], [next0, above0]), after=arrived[:1])
    from_left0 = from_behind(beside0, 0, 1)
    (part1,) = run(job(part_kernel, [tile], [home1, above1, from_left1]), after=[beside0])
    other1 = over_owners(part1)
    (total,) = run(joined(groups[0], total, arrived, True), after=[part1])
    for group in groups[1:]:
        (total,) = run(joined(group, total, swapped(total, group), True))
    arrived = swapped(total, scattered[-1])
    (part0,) = run(job(part_kernel, [tile], [home0, above0, from_left0]), after=arrived[1:2])
    other0 = over_owners(part0)
    (total,) = run(joined(scattered[-1], total, arrived, False), after=[part0])
    for group in reversed(scattered[:-1]):
        (total,) = run(joined(group, total, swapped(total, group), False))
    other_half = swap_with(total, core, 1)
    positions_all = lax.axis_size("tile") * lax.axis_size("pos") * (patterns.shape[2] // 2)
    step = probe_rate / math.sqrt(positions_all)
    new_probe, token = run(
        job(
            lambda *refs: probe_kernel(step, modes, *refs),
            [shape_of(f32, *probe.shape), shape_of(f32, 8, 128)],
            [total, other_half, probe],
        ),
        limit=8,
    )
    like = shape_of(bf16, *tile_object.shape)
    new_object = updated(1, own1, part1, other1, like, None, [])
    new_object = updated(0, own[0], part0, other0, like, new_object, [token])
    new_probe = new_probe.reshape(2, pixels, lane_tiles, modes, 128).transpose(0, 1, 3, 2, 4)
    return (new_object, new_probe.reshape(probe_modes.shape))


def solution(mesh):
    placed = (
        P("tile", None, None, None, None),
        P(),
        P("tile", "pos", None, None, None),
        P("tile", "pos", None, None),
        P("tile", "pos"),
    )
    return jax.shard_map(
        shards,
        mesh=mesh,
        in_specs=placed,
        out_specs=(P("tile", None, None, None, None), P()),
        check_vma=False,
    )
```

```python
import math

import jax
import jax.numpy as jnp
import numpy as np
from jax import lax
from jax.experimental import pallas as pl
from jax.experimental.pallas import tpu as pltpu
from jax.sharding import PartitionSpec as P

GRID_ROWS = 4


fresnel_coeff = 0.25
object_rate = 0.05
probe_rate = 0.15

f32 = jnp.float32
bf16 = jnp.bfloat16


def from_left(block, cols):
    tiles = lax.axis_size("tile")
    across = tiles // GRID_ROWS
    route = [(i // across * across + (i % across - cols) % across, i) for i in range(tiles)]
    return lax.ppermute(block, "tile", route)


def from_rows(block):
    tiles = lax.axis_size("tile")
    across = tiles // GRID_ROWS
    blocks = []
    for odd in range(2):
        route = []
        for i in range(tiles):
            other = ((i // across + odd) ^ 1) - odd
            route.append((i, i if other in (-1, GRID_ROWS) else other * across + i % across))
        blocks.append(lax.ppermute(block, "tile", route))
    return blocks


def tile_row():
    return lax.axis_index("tile") // (lax.axis_size("tile") // GRID_ROWS)


def real_embed(part_re, part_im):
    upper_half = np.concatenate([part_re, -part_im], axis=1)
    lower_half = np.concatenate([part_im, part_re], axis=1)
    stacked = np.concatenate([upper_half, lower_half], axis=0)
    return jnp.asarray(stacked, dtype=f32).astype(bf16)


def build_tables(pixels):
    indices = np.arange(pixels)
    angles = indices[:, None] * indices[None, :] % pixels * (2.0 * math.pi / pixels)
    norm_scale = 1.0 / math.sqrt(pixels)
    dft_re = np.cos(angles) * norm_scale
    dft_im = -np.sin(angles) * norm_scale
    frequency = np.where(indices < pixels // 2, indices, indices - pixels)
    phases = -2.0 * math.pi * fresnel_coeff / pixels * (frequency * frequency)
    phase_sum = phases[:, None] + angles
    kern_re = np.sum(np.cos(phase_sum), axis=0) / pixels
    kern_im = np.sum(np.sin(phase_sum), axis=0) / pixels
    lag_index = (indices[:, None] - indices[None, :]) % pixels
    prop_re = kern_re[lag_index]
    prop_im = kern_im[lag_index]
    return real_embed(prop_re, prop_im), real_embed(dft_re, dft_im)


def dot(a, b):
    return jnp.dot(a, b, preferred_element_type=f32)


def shift_tables(mine_ref, sent_ref):
    n = mine_ref.shape[1]
    mine = mine_ref[n:, :].astype(f32)
    sent = sent_ref[n:, :].astype(f32)
    busy = mine[2:3] > 0
    row = jnp.where(busy, mine[0:1], sent[0:1]).astype(jnp.int32)
    col = jnp.where(busy, mine[1:2], sent[1:2]).astype(jnp.int32)
    i_out = lax.broadcasted_iota(jnp.int32, (n, 2 * n), 0)
    i_in = lax.broadcasted_iota(jnp.int32, (n, 2 * n), 1)
    j_in = lax.broadcasted_iota(jnp.int32, (2 * n, n), 0)
    j_out = lax.broadcasted_iota(jnp.int32, (2 * n, n), 1)
    row2 = jnp.concatenate([row, row], axis=1)
    col2 = jnp.concatenate([col, col], axis=1)
    rows = (i_in == i_out + row2).astype(f32).astype(bf16)
    cols = (j_in == j_out + col).astype(f32).astype(bf16)
    rows_t = (j_in == j_out + row).astype(f32).astype(bf16)
    cols_t = (i_in == i_out + col2).astype(f32).astype(bf16)
    return rows, cols, rows_t, cols_t, col, busy


def patch(shifts, own_ref, right_ref, below_ref, diag_ref, part):
    upper = jnp.concatenate([own_ref[part], right_ref[part]], axis=1)
    lower = jnp.concatenate([below_ref[part], diag_ref[part]], axis=1)
    rows = dot(shifts[0], jnp.concatenate([upper, lower], axis=0)).astype(bf16)
    return dot(rows, shifts[1])


def transform(table_ref, wave_re, wave_im):
    n = wave_re.shape[0]
    table = table_ref[...]
    wave = jnp.concatenate([wave_re.astype(bf16), wave_im.astype(bf16)], axis=0)
    first = dot(table, wave)
    first = jnp.concatenate([first[:n].astype(bf16), (-first[n:]).astype(bf16)], axis=1)
    out = dot(first, table)
    return out[:, :n], out[:, n:]


def probe_plane(probe_ref, part, mode, modes):
    lane_tiles = 2
    n = probe_ref.shape[0] // (2 * lane_tiles * modes)
    step = lane_tiles * modes
    halves = [
        probe_ref[pl.ds(part * n * step + tile * modes + mode, n, stride=step), :]
        for tile in range(lane_tiles)
    ]
    return jnp.concatenate(halves, axis=1)


def ready_kernel(
    offsets_ref, counts_ref, own_ref, patterns_ref, probe_ref, prop_ref,
    own_out, mine_ref, sent_ref, planes_ref, table_ref,
):
    own_out[...] = own_ref[...]
    table_ref[...] = prop_ref[...]
    n = planes_ref.shape[1]
    at = lax.broadcasted_iota(jnp.int32, (16, n), 0)
    busy = (counts_ref[0, 0] == patterns_ref.shape[2]).astype(jnp.int32)
    for slot, ref in enumerate((mine_ref, sent_ref)):
        row, col = offsets_ref[0, 0, slot, 0], offsets_ref[0, 0, slot, 1]
        rows = jnp.where(at == 0, row, jnp.where(at == 1, col, busy))
        ref[pl.ds(0, n), :] = patterns_ref[0, 0, slot]
        ref[pl.ds(n, 16), :] = rows.astype(f32).astype(bf16)
    modes = planes_ref.shape[2] // n
    for part in range(2):
        for mode in range(modes):
            planes_ref[part, :, pl.ds(mode * n, n)] = probe_plane(probe_ref, part, mode, modes)


def arrive_kernel(
    mine_ref, sent_ref, own_ref, right_ref, below_ref, diag_ref, planes_ref, prop_ref,
    near_ref, arrive_ref,
):
    n = own_ref.shape[1]
    shifts = shift_tables(mine_ref, sent_ref)
    tiles = (own_ref, right_ref.at[0], below_ref, diag_ref)
    near = [patch(shifts, *tiles, part) for part in range(2)]
    for part in range(2):
        near_ref[part] = near[part].astype(bf16)
    for mode in range(planes_ref.shape[2] // n):
        lanes = pl.ds(mode * n, n)
        p_re, p_im = planes_ref[0, :, lanes], planes_ref[1, :, lanes]
        a_re, a_neg = transform(
            prop_ref, p_re * near[0] - p_im * near[1], p_re * near[1] + p_im * near[0]
        )
        arrive_ref[0, :, lanes] = a_re
        arrive_ref[1, :, lanes] = -a_neg


def spread(shifts, grad, home_ref, next_ref, down_ref):
    rows_t, cols_t, col = shifts[2:5]
    n = rows_t.shape[1]
    wrap_cols = cols_t[:, :n] + cols_t[:, n:]
    for part in range(2):
        rows = dot(rows_t, grad[part].astype(bf16)).astype(bf16)
        wide = dot(rows[:n], cols_t).astype(bf16)
        home_ref[part] = wide[:, :n]
        next_ref[part] = wide[:, n:]
        down_ref[pl.ds(part * n, n), :] = dot(rows[n:], wrap_cols).astype(bf16)
    edge = lax.broadcasted_iota(jnp.int32, (16, n), 1) < col
    down_ref[pl.ds(2 * n, 16), :] = edge.astype(f32).astype(bf16)


def gradient_kernel(
    mine_ref, sent_ref, own_ref, right_ref, below_ref, diag_ref, near_ref, arrive_ref,
    planes_ref, prop_ref, dft_ref,
    home_ref, next_ref, down_ref, grad_ref, keep_ref, give_ref, term_ref,
):
    n = own_ref.shape[1]
    modes = planes_ref.shape[2] // n
    shifts = shift_tables(mine_ref, sent_ref)
    busy = shifts[5]
    tiles = (own_ref, right_ref.at[1], below_ref, diag_ref)
    far = [patch(shifts, *tiles, part) for part in range(2)]
    fields = []
    for mode in range(modes):
        lanes = pl.ds(mode * n, n)
        a_re, a_im = arrive_ref[0, :, lanes], arrive_ref[1, :, lanes]
        fields.append(
            transform(dft_ref, far[0] * a_re - far[1] * a_im, far[0] * a_im + far[1] * a_re)
        )
    intensity = sum(f_re * f_re + f_neg * f_neg for f_re, f_neg in fields)
    pattern = jnp.where(busy, mine_ref[:n, :].astype(f32), sent_ref[:n, :].astype(f32))
    residual = intensity - pattern
    grad_far = [0.0, 0.0]
    waves = []
    for mode in range(modes):
        lanes = pl.ds(mode * n, n)
        f_re, f_neg = fields[mode]
        a_re, a_im = arrive_ref[0, :, lanes], arrive_ref[1, :, lanes]
        b_re, b_im = transform(dft_ref, f_re * residual, f_neg * residual)
        grad_far[0] += a_re * b_re + a_im * b_im
        grad_far[1] += a_re * b_im - a_im * b_re
        waves.append((far[0] * b_re + far[1] * b_im, far[1] * b_re - far[0] * b_im))
    grad_near = [0.0, 0.0]
    near = [near_ref[part].astype(f32) for part in range(2)]
    for mode in range(modes):
        lanes = pl.ds(mode * n, n)
        b_re, b_im = transform(prop_ref, *waves[mode])
        p_re, p_im = planes_ref[0, :, lanes], planes_ref[1, :, lanes]
        grad_near[0] += p_re * b_re + p_im * b_im
        grad_near[1] += p_re * b_im - p_im * b_re
        term_ref[0, :, lanes] = (near[0] * b_re + near[1] * b_im).astype(bf16)
        term_ref[1, :, lanes] = (near[0] * b_im - near[1] * b_re).astype(bf16)
    core = place_of(core_group())
    keep_ref[...] = term_ref[core]
    give_ref[...] = term_ref[1 - core]
    for part in range(2):
        grad_ref[part] = grad_near[part].astype(bf16)
    spread(shifts, grad_far, home_ref, next_ref, down_ref)


def spread_kernel(mine_ref, sent_ref, grad_ref, home_ref, next_ref, down_ref):
    shifts = shift_tables(mine_ref, sent_ref)
    spread(shifts, [grad_ref[part] for part in range(2)], home_ref, next_ref, down_ref)


def below_kernel(even_ref, odd_ref, out_ref):
    up = lax.rem(tile_row(), 2) == 0

    @pl.when(up)
    def _():
        out_ref[...] = even_ref[...]

    @pl.when(jnp.logical_not(up))
    def _():
        out_ref[...] = odd_ref[...]


def above_parts(even_ref, odd_ref, n):
    row = tile_row()
    even, odd = even_ref[...].astype(f32), odd_ref[...].astype(f32)
    above = jnp.where(lax.rem(row, 2) == 1, even, jnp.where(row == 0, jnp.zeros_like(odd), odd))
    return [above[:n], above[n : 2 * n]], above[2 * n : 2 * n + 1] > 0


def beside_kernel(next_ref, even_ref, odd_ref, out_ref):
    above, split = above_parts(even_ref, odd_ref, out_ref.shape[1])
    for part in range(2):
        total = next_ref[part].astype(f32) + jnp.where(split, above[part], 0.0)
        out_ref[part] = total.astype(bf16)


def part_kernel(home_ref, even_ref, odd_ref, left_ref, out_ref):
    above, split = above_parts(even_ref, odd_ref, out_ref.shape[1])
    for part in range(2):
        total = home_ref[part].astype(f32) + jnp.where(split, 0.0, above[part])
        out_ref[part] = (total + left_ref[part].astype(f32)).astype(bf16)


def update_kernel(layer, own_ref, part_ref, other_ref, *refs):
    out_hbm, new_ref, sem = refs[-3:]
    grad = part_ref[...].astype(f32) + other_ref[...].astype(f32)
    new_ref[...] = (own_ref[...].astype(f32) - object_rate * grad).astype(bf16)
    copy = pltpu.make_async_copy(new_ref, out_hbm.at[0, layer], sem.at[0])
    copy.start()
    copy.wait()


def core_group():
    return [lax.axis_size("pos")]


def place_of(group):
    flat = lax.axis_index("tile") * lax.axis_size("pos") + lax.axis_index("pos")
    return sum(flat // mask % 2 * (1 << at) for at, mask in enumerate(group))


def job(kernel, outs, arrays, scalars=(), scratch=()):
    return kernel, list(outs), list(scalars), list(arrays), list(scratch)


def run(*jobs, flops=1_000_000, limit=4, after=()):
    vmem = pl.BlockSpec(memory_space=pltpu.VMEM)
    smem = pl.BlockSpec(memory_space=pltpu.SMEM)
    anywhere = pl.BlockSpec(memory_space=pl.ANY)
    kernels, outs, scalars, arrays, scratch = zip(*jobs)
    ins = [x + y for x, y in zip(scalars, arrays)]
    specs = [[smem] * len(x) + [vmem] * len(y) for x, y in zip(scalars, arrays)]

    def taken(refs, lists):
        parts = []
        for items in lists:
            parts.append(refs[: len(items)])
            refs = refs[len(items) :]
        return parts, refs

    def body(*refs):
        in_refs, refs = taken(refs, ins)
        out_refs, refs = taken(refs[len(after) :], outs)
        scratch_refs, _ = taken(refs, scratch)
        for kernel, *parts in zip(kernels, in_refs, out_refs, scratch_refs):
            kernel(*parts[0], *parts[1], *parts[2])

    moved = sum(x.size * x.dtype.itemsize for x in sum(ins, []) + sum(outs, []))
    results = pl.pallas_call(
        body,
        out_shape=sum(outs, []),
        in_specs=sum(specs, []) + [anywhere] * len(after),
        out_specs=[vmem] * len(sum(outs, [])),
        scratch_shapes=sum(scratch, []),
        compiler_params=pltpu.CompilerParams(vmem_limit_bytes=limit * 2**20),
        cost_estimate=pl.CostEstimate(flops=flops, bytes_accessed=moved, transcendentals=0),
    )(*sum(ins, []), *after)
    results, _ = taken(results, outs)
    return results[0] if len(jobs) == 1 else results


def updated(layer, own, part, other, like, so_far, after):
    vmem = pl.BlockSpec(memory_space=pltpu.VMEM)
    anywhere = pl.BlockSpec(memory_space=pl.ANY)
    extra = [x for x in (so_far,) if x is not None] + list(after)
    return pl.pallas_call(
        lambda *refs: update_kernel(layer, *refs),
        out_shape=like,
        in_specs=[vmem] * 3 + [anywhere] * len(extra),
        out_specs=pl.BlockSpec(memory_space=pl.ANY),
        scratch_shapes=[pltpu.VMEM(own.shape, bf16), pltpu.SemaphoreType.DMA((1,))],
        input_output_aliases={} if so_far is None else {3: 0},
        compiler_params=pltpu.CompilerParams(vmem_limit_bytes=4 * 2**20),
        cost_estimate=pl.CostEstimate(
            flops=own.size, bytes_accessed=8 * own.size, transcendentals=0
        ),
    )(own, part, other, *extra)


def shape_of(kind, *dims):
    return jax.ShapeDtypeStruct(dims, kind)


def gathered_message(patterns, offsets, counts):
    pixels = patterns.shape[4]
    all_counts = lax.all_gather(counts[0, 0], "pos")
    ends = jnp.cumsum(all_counts)
    rank = lax.axis_index("pos")
    source = jnp.sum((ends <= rank).astype(jnp.int32))
    slot = rank - (ends[source] - all_counts[source])
    spot = lax.all_gather(offsets[0, 0], "pos")[source, slot]
    pattern = lax.all_gather(patterns[0, 0], "pos")[source, slot]
    at = lax.broadcasted_iota(jnp.int32, (16, pixels), 0)
    rows = jnp.where(at == 0, spot[0], jnp.where(at == 1, spot[1], 0))
    return jnp.concatenate([pattern, rows.astype(bf16)], axis=0)


def fold_kernel(group, keep_ref, *refs):
    blocks = refs[-1]
    got = len(refs) - 1 - blocks.shape[0]
    arrived, keep_out, give_outs = refs[:got], refs[got], refs[got + 1 : -1]
    total = keep_ref[...].astype(f32)
    for ref in arrived:
        total += ref[...].astype(f32)
    size = blocks.shape[1]
    for block in range(blocks.shape[0]):
        blocks[block] = total[block * size : (block + 1) * size]
    here = place_of(group)
    keep_out[...] = blocks[here]
    for distance, ref in enumerate(give_outs, 1):
        ref[...] = blocks[here ^ distance].astype(bf16)


def add_kernel(keep_ref, *refs):
    total = keep_ref[...].astype(f32)
    for ref in refs[:-1]:
        total += ref[...].astype(f32)
    refs[-1][...] = total.astype(bf16)


def place_kernel(group, add, *refs):
    arrived, out_ref, blocks = refs[:-2], refs[-2], refs[-1]
    here = place_of(group)
    for distance, ref in enumerate(arrived):
        blocks[here ^ distance] = ref[...]
    size = blocks.shape[1]
    if add:
        total = blocks[0].astype(f32)
        for block in range(1, blocks.shape[0]):
            total += blocks[block].astype(f32)
        out_ref[...] = total.astype(bf16)
    else:
        for block in range(blocks.shape[0]):
            out_ref[pl.ds(block * size, size), :] = blocks[block]


def probe_kernel(step, modes, mine_ref, other_ref, probe_ref, out_ref, token_ref):
    core = place_of(core_group())
    token_ref[...] = jnp.zeros_like(token_ref)
    lane_tiles = 2
    n = mine_ref.shape[0]
    stride = lane_tiles * modes
    for part in range(2):
        total = jnp.where(core == part, mine_ref[...].astype(f32), other_ref[...].astype(f32))
        for mode in range(modes):
            for tile in range(lane_tiles):
                lane = (mode * lane_tiles + tile) * 128
                where = pl.ds(part * n * stride + tile * modes + mode, n, stride=stride)
                out_ref[where, :] = probe_ref[where, :] - step * total[:, lane : lane + 128]


def exchange_groups():
    tiles, owners = lax.axis_size("tile"), lax.axis_size("pos")
    bits = [1 << bit for bit in range(owners.bit_length() - 1)]
    bits += [owners << bit for bit in range(1, tiles.bit_length() - 1)]
    return [bits[at : at + 2] for at in range(0, len(bits), 2)]


def swap_with(x, group, distance):
    mask = sum(bit for at, bit in enumerate(group) if distance >> at & 1)
    devices = lax.axis_size("tile") * lax.axis_size("pos")
    return lax.ppermute(x, ("tile", "pos"), [(i, i ^ mask) for i in range(devices)])


def joined(group, x, arrived, add):
    blocks = 1 << len(group)
    return job(
        lambda *refs: place_kernel(group, add, *refs),
        [shape_of(bf16, x.shape[0] * (1 if add else blocks), x.shape[1])],
        [x] + arrived,
        scratch=[pltpu.VMEM((blocks,) + x.shape, bf16)],
    )


def swapped(x, group):
    return [swap_with(x, group, at) for at in range(1, 1 << len(group))]


def folded(group, keep, arrived):
    blocks = 1 << len(group)
    size, width = keep.shape[0] // blocks, keep.shape[1]
    return job(
        lambda *refs: fold_kernel(group, *refs),
        [shape_of(f32, size, width)] + [shape_of(bf16, size, width)] * (blocks - 1),
        [keep] + arrived,
        scratch=[pltpu.VMEM((blocks, size, width), f32)],
    )


def shards(tile_object, probe_modes, patterns, offsets, counts):
    _, pixels, modes, _ = probe_modes.shape
    width = modes * pixels
    lane_tiles = pixels // 128
    prop, dft = build_tables(pixels)
    tile = shape_of(bf16, 2, pixels, pixels)
    planes = shape_of(f32, 2, pixels, width)
    probe = probe_modes.reshape(2, pixels, modes, lane_tiles, 128)
    probe = probe.transpose(0, 1, 3, 2, 4).reshape(-1, 128)

    own = [tile_object[0, 0], tile_object[0, 1]]
    rows0 = from_rows(own[0])
    right = from_left(tile_object[0], -1)
    exchanged = lax.axis_size("pos") == patterns.shape[2]
    message = shape_of(bf16, pixels + 16, pixels)
    own1, mine, sent, probe_planes, table = run(
        job(
            ready_kernel,
            [tile, message, message, planes, shape_of(bf16, *prop.shape)],
            [own[1], patterns, probe, prop],
            scalars=[offsets, counts if exchanged else jnp.zeros_like(counts)],
        ),
        limit=16,
        after=[own[0]],
    )
    rows1 = from_rows(own1)
    if exchanged:
        sent = lax.ppermute(sent, "pos", [(i, 1 - i) for i in range(2)])
    else:
        sent = gathered_message(patterns, offsets, counts)
    (below0,) = run(job(below_kernel, [tile], rows0))
    diag0 = from_left(below0, -1)
    (below1,) = run(job(below_kernel, [tile], rows1))
    diag1 = from_left(below1, -1)
    near, arrive = run(
        job(
            arrive_kernel,
            [tile, planes],
            [mine, sent, own[0], right, below0, diag0, probe_planes, table],
        ),
        flops=1_500_000_000,
        limit=16,
    )
    half = shape_of(bf16, pixels, width)
    down = shape_of(bf16, 2 * pixels + 16, pixels)
    home1, next1, down1, grad0, keep, give = run(
        job(
            gradient_kernel,
            [tile, tile, down, tile, half, half],
            [mine, sent, own1, right, below1, diag1, near, arrive, probe_planes, table, dft],
            scratch=[pltpu.VMEM((2, pixels, width), bf16)],
        ),
        flops=4_000_000_000,
        limit=16,
    )

    def over_owners(part):
        if lax.axis_size("pos") == 2:
            return lax.ppermute(part, "pos", [(0, 1), (1, 0)])
        return lax.psum(part.astype(f32), "pos") - part.astype(f32)

    core, groups = core_group(), exchange_groups()
    above1 = from_rows(down1)
    arrived = [swap_with(give, core, 1)]
    side = [job(spread_kernel, [tile, tile, down], [mine, sent, grad0])]
    scattered = []
    while len(groups) > 1 and keep.shape[0] >> len(groups[0]) >= 16:
        group, groups = groups[0], groups[1:]
        done = run(folded(group, keep, arrived), *side, limit=8)
        if side:
            done, (home0, next0, down0) = done
            above0 = from_rows(down0)
            side = []
        keep, *gives = done
        arrived = [swap_with(x, group, at) for at, x in enumerate(gives, 1)]
        scattered.append(group)
    (beside1,), (total,) = run(
        job(beside_kernel, [tile], [next1, *above1]),
        job(add_kernel, [shape_of(bf16, *keep.shape)], [keep] + arrived),
    )
    left1 = from_left(beside1, 1)
    (total,), (part1,), (beside0,) = run(
        joined(groups[0], total, swapped(total, groups[0]), True),
        job(part_kernel, [tile], [home1, *above1, left1]),
        job(beside_kernel, [tile], [next0, *above0]),
    )
    for group in groups[1:]:
        (total,) = run(joined(group, total, swapped(total, group), True))
    other1 = over_owners(part1)
    left0 = from_left(beside0, 1)
    (total,), (part0,) = run(
        joined(scattered[-1], total, swapped(total, scattered[-1]), False),
        job(part_kernel, [tile], [home0, *above0, left0]),
    )
    for group in reversed(scattered[:-1]):
        (total,) = run(joined(group, total, swapped(total, group), False))
    other0 = over_owners(part0)
    other_half = swap_with(total, core, 1)
    positions_all = lax.axis_size("tile") * lax.axis_size("pos") * (patterns.shape[2] // 2)
    step = probe_rate / math.sqrt(positions_all)
    new_probe, token = run(
        job(
            lambda *refs: probe_kernel(step, modes, *refs),
            [shape_of(f32, *probe.shape), shape_of(f32, 8, 128)],
            [total, other_half, probe],
        ),
        limit=8,
    )
    like = shape_of(bf16, *tile_object.shape)
    new_object = updated(1, own1, part1, other1, like, None, [])
    new_object = updated(0, own[0], part0, other0, like, new_object, [token])
    new_probe = new_probe.reshape(2, pixels, lane_tiles, modes, 128).transpose(0, 1, 3, 2, 4)
    return (new_object, new_probe.reshape(probe_modes.shape))


def solution(mesh):
    placed = (
        P("tile", None, None, None, None),
        P(),
        P("tile", "pos", None, None, None),
        P("tile", "pos", None, None),
        P("tile", "pos"),
    )
    return jax.shard_map(
        shards,
        mesh=mesh,
        in_specs=placed,
        out_specs=(P("tile", None, None, None, None), P()),
        check_vma=False,
    )
```

```python
import math

import jax
import jax.numpy as jnp
import numpy as np
from jax import lax
from jax.experimental import pallas as pl
from jax.experimental.pallas import tpu as pltpu
from jax.sharding import PartitionSpec as P

GRID_ROWS = 4


fresnel_coeff = 0.25
object_rate = 0.05
probe_rate = 0.15

f32 = jnp.float32
bf16 = jnp.bfloat16


def from_behind(block, rows, cols):
    tiles = lax.axis_size("tile")
    across = tiles // GRID_ROWS

    def source(i):
        return (i // across - rows) % GRID_ROWS * across + (i % across - cols) % across

    return lax.ppermute(block, "tile", [(source(i), i) for i in range(tiles)])


def real_embed(part_re, part_im):
    upper_half = np.concatenate([part_re, -part_im], axis=1)
    lower_half = np.concatenate([part_im, part_re], axis=1)
    stacked = np.concatenate([upper_half, lower_half], axis=0)
    return jnp.asarray(stacked, dtype=f32).astype(bf16)


def build_tables(pixels):
    indices = np.arange(pixels)
    angles = indices[:, None] * indices[None, :] % pixels * (2.0 * math.pi / pixels)
    norm_scale = 1.0 / math.sqrt(pixels)
    dft_re = np.cos(angles) * norm_scale
    dft_im = -np.sin(angles) * norm_scale
    frequency = np.where(indices < pixels // 2, indices, indices - pixels)
    phases = -2.0 * math.pi * fresnel_coeff / pixels * (frequency * frequency)
    phase_sum = phases[:, None] + angles
    kern_re = np.sum(np.cos(phase_sum), axis=0) / pixels
    kern_im = np.sum(np.sin(phase_sum), axis=0) / pixels
    lag_index = (indices[:, None] - indices[None, :]) % pixels
    prop_re = kern_re[lag_index]
    prop_im = kern_im[lag_index]
    return real_embed(prop_re, prop_im), real_embed(dft_re, dft_im)


def dot(a, b):
    return jnp.dot(a, b, preferred_element_type=f32)


def shift_tables(mine_ref, sent_ref):
    n = mine_ref.shape[1]
    mine = mine_ref[n:, :].astype(f32)
    sent = sent_ref[n:, :].astype(f32)
    busy = mine[2:3] > 0
    row = jnp.where(busy, mine[0:1], sent[0:1]).astype(jnp.int32)
    col = jnp.where(busy, mine[1:2], sent[1:2]).astype(jnp.int32)
    i_out = lax.broadcasted_iota(jnp.int32, (n, 2 * n), 0)
    i_in = lax.broadcasted_iota(jnp.int32, (n, 2 * n), 1)
    j_in = lax.broadcasted_iota(jnp.int32, (2 * n, n), 0)
    j_out = lax.broadcasted_iota(jnp.int32, (2 * n, n), 1)
    row2 = jnp.concatenate([row, row], axis=1)
    col2 = jnp.concatenate([col, col], axis=1)
    rows = (i_in == i_out + row2).astype(f32).astype(bf16)
    cols = (j_in == j_out + col).astype(f32).astype(bf16)
    rows_t = (j_in == j_out + row).astype(f32).astype(bf16)
    cols_t = (i_in == i_out + col2).astype(f32).astype(bf16)
    return rows, cols, rows_t, cols_t, col, busy


def patch(shifts, own_ref, right_ref, below_ref, diag_ref, part):
    upper = jnp.concatenate([own_ref[part], right_ref[part]], axis=1)
    lower = jnp.concatenate([below_ref[part], diag_ref[part]], axis=1)
    rows = dot(shifts[0], jnp.concatenate([upper, lower], axis=0)).astype(bf16)
    return dot(rows, shifts[1])


def transform(table_ref, wave_re, wave_im):
    n = wave_re.shape[0]
    table = table_ref[...]
    wave = jnp.concatenate([wave_re.astype(bf16), wave_im.astype(bf16)], axis=0)
    first = dot(table, wave)
    first = jnp.concatenate([first[:n].astype(bf16), (-first[n:]).astype(bf16)], axis=1)
    out = dot(first, table)
    return out[:, :n], out[:, n:]


def probe_plane(probe_ref, part, mode, modes):
    lane_tiles = 2
    n = probe_ref.shape[0] // (2 * lane_tiles * modes)
    step = lane_tiles * modes
    halves = [
        probe_ref[pl.ds(part * n * step + tile * modes + mode, n, stride=step), :]
        for tile in range(lane_tiles)
    ]
    return jnp.concatenate(halves, axis=1)


def ready_kernel(
    offsets_ref, counts_ref, own_ref, patterns_ref, probe_ref, prop_ref,
    own_out, mine_ref, sent_ref, planes_ref, table_ref,
):
    own_out[...] = own_ref[...]
    table_ref[...] = prop_ref[...]
    n = planes_ref.shape[1]
    at = lax.broadcasted_iota(jnp.int32, (16, n), 0)
    busy = (counts_ref[0, 0] == patterns_ref.shape[2]).astype(jnp.int32)
    for slot, ref in enumerate((mine_ref, sent_ref)):
        row, col = offsets_ref[0, 0, slot, 0], offsets_ref[0, 0, slot, 1]
        rows = jnp.where(at == 0, row, jnp.where(at == 1, col, busy))
        ref[pl.ds(0, n), :] = patterns_ref[0, 0, slot]
        ref[pl.ds(n, 16), :] = rows.astype(f32).astype(bf16)
    modes = planes_ref.shape[2] // n
    for part in range(2):
        for mode in range(modes):
            planes_ref[part, :, pl.ds(mode * n, n)] = probe_plane(probe_ref, part, mode, modes)


def arrive_kernel(
    mine_ref, sent_ref, own_ref, right_ref, below_ref, diag_ref, planes_ref, prop_ref,
    near_ref, arrive_ref,
):
    n = own_ref.shape[1]
    shifts = shift_tables(mine_ref, sent_ref)
    tiles = (own_ref, right_ref.at[0], below_ref, diag_ref)
    near = [patch(shifts, *tiles, part) for part in range(2)]
    for part in range(2):
        near_ref[part] = near[part].astype(bf16)
    for mode in range(planes_ref.shape[2] // n):
        lanes = pl.ds(mode * n, n)
        p_re, p_im = planes_ref[0, :, lanes], planes_ref[1, :, lanes]
        a_re, a_neg = transform(
            prop_ref, p_re * near[0] - p_im * near[1], p_re * near[1] + p_im * near[0]
        )
        arrive_ref[0, :, lanes] = a_re
        arrive_ref[1, :, lanes] = -a_neg


def spread(shifts, grad, home_ref, next_ref, down_ref):
    rows_t, cols_t, col = shifts[2:5]
    n = rows_t.shape[1]
    wrap_cols = cols_t[:, :n] + cols_t[:, n:]
    for part in range(2):
        rows = dot(rows_t, grad[part].astype(bf16)).astype(bf16)
        wide = dot(rows[:n], cols_t).astype(bf16)
        home_ref[part] = wide[:, :n]
        next_ref[part] = wide[:, n:]
        down_ref[pl.ds(part * n, n), :] = dot(rows[n:], wrap_cols).astype(bf16)
    edge = lax.broadcasted_iota(jnp.int32, (16, n), 1) < col
    down_ref[pl.ds(2 * n, 16), :] = edge.astype(f32).astype(bf16)


def gradient_kernel(
    mine_ref, sent_ref, own_ref, right_ref, below_ref, diag_ref, near_ref, arrive_ref,
    planes_ref, prop_ref, dft_ref,
    home_ref, next_ref, down_ref, grad_ref, keep_ref, give_ref, term_ref,
):
    n = own_ref.shape[1]
    modes = planes_ref.shape[2] // n
    shifts = shift_tables(mine_ref, sent_ref)
    busy = shifts[5]
    tiles = (own_ref, right_ref.at[1], below_ref, diag_ref)
    far = [patch(shifts, *tiles, part) for part in range(2)]
    fields = []
    for mode in range(modes):
        lanes = pl.ds(mode * n, n)
        a_re, a_im = arrive_ref[0, :, lanes], arrive_ref[1, :, lanes]
        fields.append(
            transform(dft_ref, far[0] * a_re - far[1] * a_im, far[0] * a_im + far[1] * a_re)
        )
    intensity = sum(f_re * f_re + f_neg * f_neg for f_re, f_neg in fields)
    pattern = jnp.where(busy, mine_ref[:n, :].astype(f32), sent_ref[:n, :].astype(f32))
    residual = intensity - pattern
    grad_far = [0.0, 0.0]
    waves = []
    for mode in range(modes):
        lanes = pl.ds(mode * n, n)
        f_re, f_neg = fields[mode]
        a_re, a_im = arrive_ref[0, :, lanes], arrive_ref[1, :, lanes]
        b_re, b_im = transform(dft_ref, f_re * residual, f_neg * residual)
        grad_far[0] += a_re * b_re + a_im * b_im
        grad_far[1] += a_re * b_im - a_im * b_re
        waves.append((far[0] * b_re + far[1] * b_im, far[1] * b_re - far[0] * b_im))
    grad_near = [0.0, 0.0]
    near = [near_ref[part].astype(f32) for part in range(2)]
    for mode in range(modes):
        lanes = pl.ds(mode * n, n)
        b_re, b_im = transform(prop_ref, *waves[mode])
        p_re, p_im = planes_ref[0, :, lanes], planes_ref[1, :, lanes]
        grad_near[0] += p_re * b_re + p_im * b_im
        grad_near[1] += p_re * b_im - p_im * b_re
        term_ref[0, :, lanes] = (near[0] * b_re + near[1] * b_im).astype(bf16)
        term_ref[1, :, lanes] = (near[0] * b_im - near[1] * b_re).astype(bf16)
    core = place_of(core_group())
    keep_ref[...] = term_ref[core]
    give_ref[...] = term_ref[1 - core]
    for part in range(2):
        grad_ref[part] = grad_near[part].astype(bf16)
    spread(shifts, grad_far, home_ref, next_ref, down_ref)


def spread_kernel(mine_ref, sent_ref, grad_ref, home_ref, next_ref, down_ref):
    shifts = shift_tables(mine_ref, sent_ref)
    spread(shifts, [grad_ref[part] for part in range(2)], home_ref, next_ref, down_ref)


def above_parts(above_ref, n):
    parts = [above_ref[pl.ds(part * n, n), :].astype(f32) for part in range(2)]
    return parts, above_ref[pl.ds(2 * n, 16), :].astype(f32)[0:1] > 0


def beside_kernel(next_ref, above_ref, out_ref):
    above, split = above_parts(above_ref, out_ref.shape[1])
    for part in range(2):
        total = next_ref[part].astype(f32) + jnp.where(split, above[part], 0.0)
        out_ref[part] = total.astype(bf16)


def part_kernel(home_ref, above_ref, left_ref, out_ref):
    above, split = above_parts(above_ref, out_ref.shape[1])
    for part in range(2):
        total = home_ref[part].astype(f32) + jnp.where(split, 0.0, above[part])
        out_ref[part] = (total + left_ref[part].astype(f32)).astype(bf16)


def update_kernel(layer, own_ref, part_ref, other_ref, *refs):
    out_hbm, new_ref, sem = refs[-3:]
    grad = part_ref[...].astype(f32) + other_ref[...].astype(f32)
    new_ref[...] = (own_ref[...].astype(f32) - object_rate * grad).astype(bf16)
    copy = pltpu.make_async_copy(new_ref, out_hbm.at[0, layer], sem.at[0])
    copy.start()
    copy.wait()


def core_group():
    return [lax.axis_size("pos")]


def place_of(group):
    flat = lax.axis_index("tile") * lax.axis_size("pos") + lax.axis_index("pos")
    return sum(flat // mask % 2 * (1 << at) for at, mask in enumerate(group))


def job(kernel, outs, arrays, scalars=(), scratch=()):
    return kernel, list(outs), list(scalars), list(arrays), list(scratch)


def run(*jobs, flops=1_000_000, limit=4, after=()):
    vmem = pl.BlockSpec(memory_space=pltpu.VMEM)
    smem = pl.BlockSpec(memory_space=pltpu.SMEM)
    anywhere = pl.BlockSpec(memory_space=pl.ANY)
    kernels, outs, scalars, arrays, scratch = zip(*jobs)
    ins = [x + y for x, y in zip(scalars, arrays)]
    specs = [[smem] * len(x) + [vmem] * len(y) for x, y in zip(scalars, arrays)]

    def taken(refs, lists):
        parts = []
        for items in lists:
            parts.append(refs[: len(items)])
            refs = refs[len(items) :]
        return parts, refs

    def body(*refs):
        in_refs, refs = taken(refs, ins)
        out_refs, refs = taken(refs[len(after) :], outs)
        scratch_refs, _ = taken(refs, scratch)
        for kernel, *parts in zip(kernels, in_refs, out_refs, scratch_refs):
            kernel(*parts[0], *parts[1], *parts[2])

    moved = sum(x.size * x.dtype.itemsize for x in sum(ins, []) + sum(outs, []))
    results = pl.pallas_call(
        body,
        out_shape=sum(outs, []),
        in_specs=sum(specs, []) + [anywhere] * len(after),
        out_specs=[vmem] * len(sum(outs, [])),
        scratch_shapes=sum(scratch, []),
        compiler_params=pltpu.CompilerParams(vmem_limit_bytes=limit * 2**20),
        cost_estimate=pl.CostEstimate(flops=flops, bytes_accessed=moved, transcendentals=0),
    )(*sum(ins, []), *after)
    results, _ = taken(results, outs)
    return results[0] if len(jobs) == 1 else results


def updated(layer, own, part, other, like, so_far, after):
    vmem = pl.BlockSpec(memory_space=pltpu.VMEM)
    anywhere = pl.BlockSpec(memory_space=pl.ANY)
    extra = [x for x in (so_far,) if x is not None] + list(after)
    return pl.pallas_call(
        lambda *refs: update_kernel(layer, *refs),
        out_shape=like,
        in_specs=[vmem] * 3 + [anywhere] * len(extra),
        out_specs=pl.BlockSpec(memory_space=pl.ANY),
        scratch_shapes=[pltpu.VMEM(own.shape, bf16), pltpu.SemaphoreType.DMA((1,))],
        input_output_aliases={} if so_far is None else {3: 0},
        compiler_params=pltpu.CompilerParams(vmem_limit_bytes=4 * 2**20),
        cost_estimate=pl.CostEstimate(
            flops=own.size, bytes_accessed=8 * own.size, transcendentals=0
        ),
    )(own, part, other, *extra)


def shape_of(kind, *dims):
    return jax.ShapeDtypeStruct(dims, kind)


def gathered_message(patterns, offsets, counts):
    pixels = patterns.shape[4]
    all_counts = lax.all_gather(counts[0, 0], "pos")
    ends = jnp.cumsum(all_counts)
    rank = lax.axis_index("pos")
    source = jnp.sum((ends <= rank).astype(jnp.int32))
    slot = rank - (ends[source] - all_counts[source])
    spot = lax.all_gather(offsets[0, 0], "pos")[source, slot]
    pattern = lax.all_gather(patterns[0, 0], "pos")[source, slot]
    at = lax.broadcasted_iota(jnp.int32, (16, pixels), 0)
    rows = jnp.where(at == 0, spot[0], jnp.where(at == 1, spot[1], 0))
    return jnp.concatenate([pattern, rows.astype(bf16)], axis=0)


def fold_kernel(group, keep_ref, *refs):
    blocks = refs[-1]
    got = len(refs) - 1 - blocks.shape[0]
    arrived, keep_out, give_outs = refs[:got], refs[got], refs[got + 1 : -1]
    total = keep_ref[...].astype(f32)
    for ref in arrived:
        total += ref[...].astype(f32)
    size = blocks.shape[1]
    for block in range(blocks.shape[0]):
        blocks[block] = total[block * size : (block + 1) * size]
    here = place_of(group)
    keep_out[...] = blocks[here]
    for distance, ref in enumerate(give_outs, 1):
        ref[...] = blocks[here ^ distance].astype(bf16)


def add_kernel(keep_ref, *refs):
    total = keep_ref[...].astype(f32)
    for ref in refs[:-1]:
        total += ref[...].astype(f32)
    refs[-1][...] = total.astype(bf16)


def place_kernel(group, *refs):
    arrived, out_ref, blocks = refs[:-2], refs[-2], refs[-1]
    here = place_of(group)
    for distance, ref in enumerate(arrived):
        blocks[here ^ distance] = ref[...]
    size = blocks.shape[1]
    for block in range(blocks.shape[0]):
        out_ref[pl.ds(block * size, size), :] = blocks[block]


def probe_kernel(step, modes, mine_ref, other_ref, probe_ref, out_ref, token_ref):
    core = place_of(core_group())
    token_ref[...] = jnp.zeros_like(token_ref)
    lane_tiles = 2
    n = mine_ref.shape[0]
    stride = lane_tiles * modes
    for part in range(2):
        total = jnp.where(core == part, mine_ref[...].astype(f32), other_ref[...].astype(f32))
        for mode in range(modes):
            for tile in range(lane_tiles):
                lane = (mode * lane_tiles + tile) * 128
                where = pl.ds(part * n * stride + tile * modes + mode, n, stride=stride)
                out_ref[where, :] = probe_ref[where, :] - step * total[:, lane : lane + 128]


def exchange_groups():
    tiles, owners = lax.axis_size("tile"), lax.axis_size("pos")
    bits = [1 << bit for bit in range(owners.bit_length() - 1)]
    bits += [owners << bit for bit in range(1, tiles.bit_length() - 1)]
    return [bits[at : at + 2] for at in range(0, len(bits), 2)]


def swap_with(x, group, distance):
    mask = sum(bit for at, bit in enumerate(group) if distance >> at & 1)
    devices = lax.axis_size("tile") * lax.axis_size("pos")
    return lax.ppermute(x, ("tile", "pos"), [(i, i ^ mask) for i in range(devices)])


def joined(group, x, arrived):
    blocks = 1 << len(group)
    return job(
        lambda *refs: place_kernel(group, *refs),
        [shape_of(bf16, x.shape[0] * blocks, x.shape[1])],
        [x] + arrived,
        scratch=[pltpu.VMEM((blocks,) + x.shape, bf16)],
    )


def added(x, arrived):
    return job(add_kernel, [shape_of(bf16, *x.shape)], [x] + arrived)


def swapped(x, group):
    return [swap_with(x, group, at) for at in range(1, 1 << len(group))]


def folded(group, keep, arrived):
    blocks = 1 << len(group)
    size, width = keep.shape[0] // blocks, keep.shape[1]
    return job(
        lambda *refs: fold_kernel(group, *refs),
        [shape_of(f32, size, width)] + [shape_of(bf16, size, width)] * (blocks - 1),
        [keep] + arrived,
        scratch=[pltpu.VMEM((blocks, size, width), f32)],
    )


def shards(tile_object, probe_modes, patterns, offsets, counts):
    _, pixels, modes, _ = probe_modes.shape
    width = modes * pixels
    lane_tiles = pixels // 128
    prop, dft = build_tables(pixels)
    tile = shape_of(bf16, 2, pixels, pixels)
    planes = shape_of(f32, 2, pixels, width)
    probe = probe_modes.reshape(2, pixels, modes, lane_tiles, 128)
    probe = probe.transpose(0, 1, 3, 2, 4).reshape(-1, 128)

    own = [tile_object[0, 0], tile_object[0, 1]]
    below0 = from_behind(own[0], -1, 0)
    right = from_behind(tile_object[0], 0, -1)
    exchanged = lax.axis_size("pos") == patterns.shape[2]
    message = shape_of(bf16, pixels + 16, pixels)
    own1, mine, sent, probe_planes, table = run(
        job(
            ready_kernel,
            [tile, message, message, planes, shape_of(bf16, *prop.shape)],
            [own[1], patterns, probe, prop],
            scalars=[offsets, counts if exchanged else jnp.zeros_like(counts)],
        ),
        limit=16,
        after=[own[0]],
    )
    below1 = from_behind(own1, -1, 0)
    if exchanged:
        sent = lax.ppermute(sent, "pos", [(i, 1 - i) for i in range(2)])
    else:
        sent = gathered_message(patterns, offsets, counts)
    diag0 = from_behind(below0, 0, -1)
    diag1 = from_behind(below1, 0, -1)
    near, arrive = run(
        job(
            arrive_kernel,
            [tile, planes],
            [mine, sent, own[0], right, below0, diag0, probe_planes, table],
        ),
        flops=1_500_000_000,
        limit=16,
    )
    half = shape_of(bf16, pixels, width)
    down = shape_of(bf16, 2 * pixels + 16, pixels)
    home1, next1, down1, grad0, keep, give = run(
        job(
            gradient_kernel,
            [tile, tile, down, tile, half, half],
            [mine, sent, own1, right, below1, diag1, near, arrive, probe_planes, table, dft],
            scratch=[pltpu.VMEM((2, pixels, width), bf16)],
        ),
        flops=4_000_000_000,
        limit=16,
    )

    def over_owners(part):
        if lax.axis_size("pos") == 2:
            return lax.ppermute(part, "pos", [(0, 1), (1, 0)])
        return lax.psum(part.astype(f32), "pos") - part.astype(f32)

    core, groups = core_group(), exchange_groups()
    above1 = from_behind(down1, 1, 0)
    arrived = [swap_with(give, core, 1)]
    side = [job(spread_kernel, [tile, tile, down], [mine, sent, grad0])]
    scattered = []
    while len(groups) > 1 and keep.shape[0] >> len(groups[0]) >= 16:
        group, groups = groups[0], groups[1:]
        done = run(folded(group, keep, arrived), *side, limit=8)
        if side:
            done, (home0, next0, down0) = done
            above0 = from_behind(down0, 1, 0)
            side = []
        keep, *gives = done
        arrived = [swap_with(x, group, at) for at, x in enumerate(gives, 1)]
        scattered.append(group)
    (total,), (beside1,) = run(
        added(keep, arrived), job(beside_kernel, [tile], [next1, above1])
    )
    left1 = from_behind(beside1, 0, 1)
    first, second, *others = [[bit] for group in groups for bit in group]
    (total,), (beside0,), (part1,) = run(
        added(total, swapped(total, first)),
        job(beside_kernel, [tile], [next0, above0]),
        job(part_kernel, [tile], [home1, above1, left1]),
    )
    left0 = from_behind(beside0, 0, 1)
    other1 = over_owners(part1)
    (total,), (part0,) = run(
        added(total, swapped(total, second)),
        job(part_kernel, [tile], [home0, above0, left0]),
    )
    other0 = over_owners(part0)
    for group in others:
        (total,) = run(added(total, swapped(total, group)))
    for group in reversed(scattered):
        (total,) = run(joined(group, total, swapped(total, group)))
    other_half = swap_with(total, core, 1)
    positions_all = lax.axis_size("tile") * lax.axis_size("pos") * (patterns.shape[2] // 2)
    step = probe_rate / math.sqrt(positions_all)
    new_probe, token = run(
        job(
            lambda *refs: probe_kernel(step, modes, *refs),
            [shape_of(f32, *probe.shape), shape_of(f32, 8, 128)],
            [total, other_half, probe],
        ),
        limit=8,
    )
    like = shape_of(bf16, *tile_object.shape)
    new_object = updated(1, own1, part1, other1, like, None, [])
    new_object = updated(0, own[0], part0, other0, like, new_object, [token])
    new_probe = new_probe.reshape(2, pixels, lane_tiles, modes, 128).transpose(0, 1, 3, 2, 4)
    return (new_object, new_probe.reshape(probe_modes.shape))


def solution(mesh):
    placed = (
        P("tile", None, None, None, None),
        P(),
        P("tile", "pos", None, None, None),
        P("tile", "pos", None, None),
        P("tile", "pos"),
    )
    return jax.shard_map(
        shards,
        mesh=mesh,
        in_specs=placed,
        out_specs=(P("tile", None, None, None, None), P()),
        check_vma=False,
    )
```

```python
import math

import jax
import jax.numpy as jnp
import numpy as np
from jax import lax
from jax.experimental import pallas as pl
from jax.experimental.pallas import tpu as pltpu
from jax.sharding import PartitionSpec as P

GRID_ROWS = 4


fresnel_coeff = 0.25
object_rate = 0.05
probe_rate = 0.15

f32 = jnp.float32
bf16 = jnp.bfloat16


def from_behind(block, rows, cols):
    tiles = lax.axis_size("tile")
    across = tiles // GRID_ROWS

    def source(i):
        return (i // across - rows) % GRID_ROWS * across + (i % across - cols) % across

    return lax.ppermute(block, "tile", [(source(i), i) for i in range(tiles)])


def real_embed(part_re, part_im):
    upper_half = np.concatenate([part_re, -part_im], axis=1)
    lower_half = np.concatenate([part_im, part_re], axis=1)
    stacked = np.concatenate([upper_half, lower_half], axis=0)
    return jnp.asarray(stacked, dtype=f32).astype(bf16)


def build_tables(pixels):
    indices = np.arange(pixels)
    angles = indices[:, None] * indices[None, :] % pixels * (2.0 * math.pi / pixels)
    norm_scale = 1.0 / math.sqrt(pixels)
    dft_re = np.cos(angles) * norm_scale
    dft_im = -np.sin(angles) * norm_scale
    frequency = np.where(indices < pixels // 2, indices, indices - pixels)
    phases = -2.0 * math.pi * fresnel_coeff / pixels * (frequency * frequency)
    phase_sum = phases[:, None] + angles
    kern_re = np.sum(np.cos(phase_sum), axis=0) / pixels
    kern_im = np.sum(np.sin(phase_sum), axis=0) / pixels
    lag_index = (indices[:, None] - indices[None, :]) % pixels
    prop_re = kern_re[lag_index]
    prop_im = kern_im[lag_index]
    return real_embed(prop_re, prop_im), real_embed(dft_re, dft_im)


def dot(a, b):
    return jnp.dot(a, b, preferred_element_type=f32)


def shift_tables(mine_ref, sent_ref):
    n = mine_ref.shape[1]
    mine = mine_ref[n:, :].astype(f32)
    sent = sent_ref[n:, :].astype(f32)
    busy = mine[2:3] > 0
    row = jnp.where(busy, mine[0:1], sent[0:1]).astype(jnp.int32)
    col = jnp.where(busy, mine[1:2], sent[1:2]).astype(jnp.int32)
    i_out = lax.broadcasted_iota(jnp.int32, (n, 2 * n), 0)
    i_in = lax.broadcasted_iota(jnp.int32, (n, 2 * n), 1)
    j_in = lax.broadcasted_iota(jnp.int32, (2 * n, n), 0)
    j_out = lax.broadcasted_iota(jnp.int32, (2 * n, n), 1)
    row2 = jnp.concatenate([row, row], axis=1)
    col2 = jnp.concatenate([col, col], axis=1)
    rows = (i_in == i_out + row2).astype(f32).astype(bf16)
    cols = (j_in == j_out + col).astype(f32).astype(bf16)
    rows_t = (j_in == j_out + row).astype(f32).astype(bf16)
    cols_t = (i_in == i_out + col2).astype(f32).astype(bf16)
    return rows, cols, rows_t, cols_t, col, busy


def patch(shifts, own_ref, right_ref, below_ref, diag_ref, part):
    upper = jnp.concatenate([own_ref[part], right_ref[part]], axis=1)
    lower = jnp.concatenate([below_ref[part], diag_ref[part]], axis=1)
    rows = dot(shifts[0], jnp.concatenate([upper, lower], axis=0)).astype(bf16)
    return dot(rows, shifts[1])


def transform(table_ref, wave_re, wave_im):
    n = wave_re.shape[0]
    table = table_ref[...]
    wave = jnp.concatenate([wave_re.astype(bf16), wave_im.astype(bf16)], axis=0)
    first = dot(table, wave)
    first = jnp.concatenate([first[:n].astype(bf16), (-first[n:]).astype(bf16)], axis=1)
    out = dot(first, table)
    return out[:, :n], out[:, n:]


def probe_plane(probe_ref, part, mode, modes):
    lane_tiles = 2
    n = probe_ref.shape[0] // (2 * lane_tiles * modes)
    step = lane_tiles * modes
    halves = [
        probe_ref[pl.ds(part * n * step + tile * modes + mode, n, stride=step), :]
        for tile in range(lane_tiles)
    ]
    return jnp.concatenate(halves, axis=1)


def message_kernel(offsets_ref, counts_ref, own_ref, patterns_ref, own_out, mine_ref, sent_ref):
    own_out[...] = own_ref[...]
    n = mine_ref.shape[1]
    at = lax.broadcasted_iota(jnp.int32, (16, n), 0)
    busy = (counts_ref[0, 0] == patterns_ref.shape[2]).astype(jnp.int32)
    for slot, ref in enumerate((mine_ref, sent_ref)):
        row, col = offsets_ref[0, 0, slot, 0], offsets_ref[0, 0, slot, 1]
        rows = jnp.where(at == 0, row, jnp.where(at == 1, col, busy))
        ref[pl.ds(0, n), :] = patterns_ref[0, 0, slot]
        ref[pl.ds(n, 16), :] = rows.astype(f32).astype(bf16)


def ready_kernel(probe_ref, prop_ref, planes_ref, table_ref):
    table_ref[...] = prop_ref[...]
    n = planes_ref.shape[1]
    modes = planes_ref.shape[2] // n
    for part in range(2):
        for mode in range(modes):
            planes_ref[part, :, pl.ds(mode * n, n)] = probe_plane(probe_ref, part, mode, modes)


def arrive_kernel(
    mine_ref, sent_ref, own_ref, right_ref, below_ref, diag_ref, planes_ref, prop_ref,
    near_ref, arrive_ref,
):
    n = own_ref.shape[1]
    shifts = shift_tables(mine_ref, sent_ref)
    tiles = (own_ref, right_ref.at[0], below_ref, diag_ref)
    near = [patch(shifts, *tiles, part) for part in range(2)]
    for part in range(2):
        near_ref[part] = near[part].astype(bf16)
    for mode in range(planes_ref.shape[2] // n):
        lanes = pl.ds(mode * n, n)
        p_re, p_im = planes_ref[0, :, lanes], planes_ref[1, :, lanes]
        a_re, a_neg = transform(
            prop_ref, p_re * near[0] - p_im * near[1], p_re * near[1] + p_im * near[0]
        )
        arrive_ref[0, :, lanes] = a_re
        arrive_ref[1, :, lanes] = -a_neg


def spread(shifts, grad, home_ref, next_ref, down_ref):
    rows_t, cols_t, col = shifts[2:5]
    n = rows_t.shape[1]
    wrap_cols = cols_t[:, :n] + cols_t[:, n:]
    for part in range(2):
        rows = dot(rows_t, grad[part].astype(bf16)).astype(bf16)
        wide = dot(rows[:n], cols_t).astype(bf16)
        home_ref[part] = wide[:, :n]
        next_ref[part] = wide[:, n:]
        down_ref[pl.ds(part * n, n), :] = dot(rows[n:], wrap_cols).astype(bf16)
    edge = lax.broadcasted_iota(jnp.int32, (16, n), 1) < col
    down_ref[pl.ds(2 * n, 16), :] = edge.astype(f32).astype(bf16)


def gradient_kernel(
    mine_ref, sent_ref, own_ref, right_ref, below_ref, diag_ref, near_ref, arrive_ref,
    planes_ref, prop_ref, dft_ref,
    home_ref, next_ref, down_ref, grad_ref, keep_ref, give_ref, term_ref,
):
    n = own_ref.shape[1]
    modes = planes_ref.shape[2] // n
    shifts = shift_tables(mine_ref, sent_ref)
    busy = shifts[5]
    tiles = (own_ref, right_ref.at[1], below_ref, diag_ref)
    far = [patch(shifts, *tiles, part) for part in range(2)]
    fields = []
    for mode in range(modes):
        lanes = pl.ds(mode * n, n)
        a_re, a_im = arrive_ref[0, :, lanes], arrive_ref[1, :, lanes]
        fields.append(
            transform(dft_ref, far[0] * a_re - far[1] * a_im, far[0] * a_im + far[1] * a_re)
        )
    intensity = sum(f_re * f_re + f_neg * f_neg for f_re, f_neg in fields)
    pattern = jnp.where(busy, mine_ref[:n, :].astype(f32), sent_ref[:n, :].astype(f32))
    residual = intensity - pattern
    grad_far = [0.0, 0.0]
    waves = []
    for mode in range(modes):
        lanes = pl.ds(mode * n, n)
        f_re, f_neg = fields[mode]
        a_re, a_im = arrive_ref[0, :, lanes], arrive_ref[1, :, lanes]
        b_re, b_im = transform(dft_ref, f_re * residual, f_neg * residual)
        grad_far[0] += a_re * b_re + a_im * b_im
        grad_far[1] += a_re * b_im - a_im * b_re
        waves.append((far[0] * b_re + far[1] * b_im, far[1] * b_re - far[0] * b_im))
    grad_near = [0.0, 0.0]
    near = [near_ref[part].astype(f32) for part in range(2)]
    for mode in range(modes):
        lanes = pl.ds(mode * n, n)
        b_re, b_im = transform(prop_ref, *waves[mode])
        p_re, p_im = planes_ref[0, :, lanes], planes_ref[1, :, lanes]
        grad_near[0] += p_re * b_re + p_im * b_im
        grad_near[1] += p_re * b_im - p_im * b_re
        term_ref[0, :, lanes] = (near[0] * b_re + near[1] * b_im).astype(bf16)
        term_ref[1, :, lanes] = (near[0] * b_im - near[1] * b_re).astype(bf16)
    core = place_of(core_group())
    keep_ref[...] = term_ref[core]
    give_ref[...] = term_ref[1 - core]
    for part in range(2):
        grad_ref[part] = grad_near[part].astype(bf16)
    spread(shifts, grad_far, home_ref, next_ref, down_ref)


def spread_kernel(mine_ref, sent_ref, grad_ref, home_ref, next_ref, down_ref):
    shifts = shift_tables(mine_ref, sent_ref)
    spread(shifts, [grad_ref[part] for part in range(2)], home_ref, next_ref, down_ref)


def above_parts(above_ref, n):
    parts = [above_ref[pl.ds(part * n, n), :].astype(f32) for part in range(2)]
    return parts, above_ref[pl.ds(2 * n, 16), :].astype(f32)[0:1] > 0


def beside_kernel(next_ref, above_ref, out_ref):
    above, split = above_parts(above_ref, out_ref.shape[1])
    for part in range(2):
        total = next_ref[part].astype(f32) + jnp.where(split, above[part], 0.0)
        out_ref[part] = total.astype(bf16)


def part_kernel(home_ref, above_ref, left_ref, out_ref):
    above, split = above_parts(above_ref, out_ref.shape[1])
    for part in range(2):
        total = home_ref[part].astype(f32) + jnp.where(split, 0.0, above[part])
        out_ref[part] = (total + left_ref[part].astype(f32)).astype(bf16)


def update_kernel(layer, own_ref, part_ref, other_ref, *refs):
    out_hbm, token_ref, new_ref, sem = refs[-4:]
    token_ref[...] = jnp.zeros_like(token_ref)
    grad = part_ref[...].astype(f32) + other_ref[...].astype(f32)
    new_ref[...] = (own_ref[...].astype(f32) - object_rate * grad).astype(bf16)
    copy = pltpu.make_async_copy(new_ref, out_hbm.at[0, layer], sem.at[0])
    copy.start()
    copy.wait()


def core_group():
    return [lax.axis_size("pos")]


def place_of(group):
    flat = lax.axis_index("tile") * lax.axis_size("pos") + lax.axis_index("pos")
    return sum(flat // mask % 2 * (1 << at) for at, mask in enumerate(group))


def job(kernel, outs, arrays, scalars=(), scratch=()):
    return kernel, list(outs), list(scalars), list(arrays), list(scratch)


def run(*jobs, flops=1_000_000, limit=4, after=()):
    vmem = pl.BlockSpec(memory_space=pltpu.VMEM)
    smem = pl.BlockSpec(memory_space=pltpu.SMEM)
    anywhere = pl.BlockSpec(memory_space=pl.ANY)
    kernels, outs, scalars, arrays, scratch = zip(*jobs)
    ins = [x + y for x, y in zip(scalars, arrays)]
    specs = [[smem] * len(x) + [vmem] * len(y) for x, y in zip(scalars, arrays)]

    def taken(refs, lists):
        parts = []
        for items in lists:
            parts.append(refs[: len(items)])
            refs = refs[len(items) :]
        return parts, refs

    def body(*refs):
        in_refs, refs = taken(refs, ins)
        out_refs, refs = taken(refs[len(after) :], outs)
        scratch_refs, _ = taken(refs, scratch)
        for kernel, *parts in zip(kernels, in_refs, out_refs, scratch_refs):
            kernel(*parts[0], *parts[1], *parts[2])

    moved = sum(x.size * x.dtype.itemsize for x in sum(ins, []) + sum(outs, []))
    results = pl.pallas_call(
        body,
        out_shape=sum(outs, []),
        in_specs=sum(specs, []) + [anywhere] * len(after),
        out_specs=[vmem] * len(sum(outs, [])),
        scratch_shapes=sum(scratch, []),
        compiler_params=pltpu.CompilerParams(vmem_limit_bytes=limit * 2**20),
        cost_estimate=pl.CostEstimate(flops=flops, bytes_accessed=moved, transcendentals=0),
    )(*sum(ins, []), *after)
    results, _ = taken(results, outs)
    return results[0] if len(jobs) == 1 else results


def updated(layer, own, part, other, like, so_far=None, flops=0):
    vmem = pl.BlockSpec(memory_space=pltpu.VMEM)
    anywhere = pl.BlockSpec(memory_space=pl.ANY)
    extra = [x for x in (so_far,) if x is not None]
    return pl.pallas_call(
        lambda *refs: update_kernel(layer, *refs),
        out_shape=[like, shape_of(f32, 8, 128)],
        in_specs=[vmem] * 3 + [anywhere] * len(extra),
        out_specs=[anywhere, vmem],
        scratch_shapes=[pltpu.VMEM(own.shape, bf16), pltpu.SemaphoreType.DMA((1,))],
        input_output_aliases={} if so_far is None else {3: 0},
        compiler_params=pltpu.CompilerParams(vmem_limit_bytes=4 * 2**20),
        cost_estimate=pl.CostEstimate(
            flops=own.size + flops, bytes_accessed=8 * own.size, transcendentals=0
        ),
    )(own, part, other, *extra)


def shape_of(kind, *dims):
    return jax.ShapeDtypeStruct(dims, kind)


def gathered_message(patterns, offsets, counts):
    pixels = patterns.shape[4]
    all_counts = lax.all_gather(counts[0, 0], "pos")
    ends = jnp.cumsum(all_counts)
    rank = lax.axis_index("pos")
    source = jnp.sum((ends <= rank).astype(jnp.int32))
    slot = rank - (ends[source] - all_counts[source])
    spot = lax.all_gather(offsets[0, 0], "pos")[source, slot]
    pattern = lax.all_gather(patterns[0, 0], "pos")[source, slot]
    at = lax.broadcasted_iota(jnp.int32, (16, pixels), 0)
    rows = jnp.where(at == 0, spot[0], jnp.where(at == 1, spot[1], 0))
    return jnp.concatenate([pattern, rows.astype(bf16)], axis=0)


def fold_kernel(group, keep_ref, *refs):
    blocks = refs[-1]
    got = len(refs) - 1 - blocks.shape[0]
    arrived, keep_out, give_outs = refs[:got], refs[got], refs[got + 1 : -1]
    total = keep_ref[...].astype(f32)
    for ref in arrived:
        total += ref[...].astype(f32)
    size = blocks.shape[1]
    for block in range(blocks.shape[0]):
        blocks[block] = total[block * size : (block + 1) * size]
    here = place_of(group)
    keep_out[...] = blocks[here]
    for distance, ref in enumerate(give_outs, 1):
        ref[...] = blocks[here ^ distance].astype(bf16)


def add_kernel(keep_ref, *refs):
    total = keep_ref[...].astype(f32)
    for ref in refs[:-1]:
        total += ref[...].astype(f32)
    refs[-1][...] = total.astype(bf16)


def place_kernel(group, *refs):
    arrived, out_ref, blocks = refs[:-2], refs[-2], refs[-1]
    here = place_of(group)
    for distance, ref in enumerate(arrived):
        blocks[here ^ distance] = ref[...]
    size = blocks.shape[1]
    for block in range(blocks.shape[0]):
        out_ref[pl.ds(block * size, size), :] = blocks[block]


def probe_kernel(step, modes, mine_ref, other_ref, probe_ref, out_ref):
    core = place_of(core_group())
    lane_tiles = 2
    n = mine_ref.shape[0]
    stride = lane_tiles * modes
    for part in range(2):
        total = jnp.where(core == part, mine_ref[...].astype(f32), other_ref[...].astype(f32))
        for mode in range(modes):
            for tile in range(lane_tiles):
                lane = (mode * lane_tiles + tile) * 128
                where = pl.ds(part * n * stride + tile * modes + mode, n, stride=stride)
                out_ref[where, :] = probe_ref[where, :] - step * total[:, lane : lane + 128]


def exchange_groups():
    tiles, owners = lax.axis_size("tile"), lax.axis_size("pos")
    bits = [1 << bit for bit in range(owners.bit_length() - 1)]
    bits += [owners << bit for bit in range(1, tiles.bit_length() - 1)]
    return [bits[at : at + 2] for at in range(0, len(bits), 2)]


def swap_with(x, group, distance):
    mask = sum(bit for at, bit in enumerate(group) if distance >> at & 1)
    devices = lax.axis_size("tile") * lax.axis_size("pos")
    return lax.ppermute(x, ("tile", "pos"), [(i, i ^ mask) for i in range(devices)])


def joined(group, x, arrived):
    blocks = 1 << len(group)
    return job(
        lambda *refs: place_kernel(group, *refs),
        [shape_of(bf16, x.shape[0] * blocks, x.shape[1])],
        [x] + arrived,
        scratch=[pltpu.VMEM((blocks,) + x.shape, bf16)],
    )


def added(x, arrived):
    return job(add_kernel, [shape_of(bf16, *x.shape)], [x] + arrived)


def swapped(x, group):
    return [swap_with(x, group, at) for at in range(1, 1 << len(group))]


def folded(group, keep, arrived):
    blocks = 1 << len(group)
    size, width = keep.shape[0] // blocks, keep.shape[1]
    return job(
        lambda *refs: fold_kernel(group, *refs),
        [shape_of(f32, size, width)] + [shape_of(bf16, size, width)] * (blocks - 1),
        [keep] + arrived,
        scratch=[pltpu.VMEM((blocks, size, width), f32)],
    )


def shards(tile_object, probe_modes, patterns, offsets, counts):
    _, pixels, modes, _ = probe_modes.shape
    width = modes * pixels
    lane_tiles = pixels // 128
    prop, dft = build_tables(pixels)
    tile = shape_of(bf16, 2, pixels, pixels)
    planes = shape_of(f32, 2, pixels, width)
    probe = probe_modes.reshape(2, pixels, modes, lane_tiles, 128)
    probe = probe.transpose(0, 1, 3, 2, 4).reshape(-1, 128)

    own = [tile_object[0, 0], tile_object[0, 1]]
    below0 = from_behind(own[0], -1, 0)
    right = from_behind(tile_object[0], 0, -1)
    exchanged = lax.axis_size("pos") == patterns.shape[2]
    message = shape_of(bf16, pixels + 16, pixels)
    own1, mine, sent = run(
        job(
            message_kernel,
            [tile, message, message],
            [own[1], patterns],
            scalars=[offsets, counts if exchanged else jnp.zeros_like(counts)],
        ),
        limit=4,
        after=[own[0]],
    )
    probe_planes, table = run(
        job(ready_kernel, [planes, shape_of(bf16, *prop.shape)], [probe, prop]),
        limit=8,
        after=[own1],
    )
    below1 = from_behind(own1, -1, 0)
    if exchanged:
        sent = lax.ppermute(sent, "pos", [(i, 1 - i) for i in range(2)])
    else:
        sent = gathered_message(patterns, offsets, counts)
    diag0 = from_behind(below0, 0, -1)
    diag1 = from_behind(below1, 0, -1)
    near, arrive = run(
        job(
            arrive_kernel,
            [tile, planes],
            [mine, sent, own[0], right, below0, diag0, probe_planes, table],
        ),
        flops=1_500_000_000,
        limit=16,
    )
    half = shape_of(bf16, pixels, width)
    down = shape_of(bf16, 2 * pixels + 16, pixels)
    home1, next1, down1, grad0, keep, give = run(
        job(
            gradient_kernel,
            [tile, tile, down, tile, half, half],
            [mine, sent, own1, right, below1, diag1, near, arrive, probe_planes, table, dft],
            scratch=[pltpu.VMEM((2, pixels, width), bf16)],
        ),
        flops=4_000_000_000,
        limit=16,
    )

    def over_owners(part):
        if lax.axis_size("pos") == 2:
            return lax.ppermute(part, "pos", [(0, 1), (1, 0)])
        return lax.psum(part.astype(f32), "pos") - part.astype(f32)

    core, groups = core_group(), exchange_groups()
    above1 = from_behind(down1, 1, 0)
    arrived = [swap_with(give, core, 1)]
    side = [job(spread_kernel, [tile, tile, down], [mine, sent, grad0])]
    scattered = []
    while len(groups) > 1 and keep.shape[0] >> len(groups[0]) >= 16:
        group, groups = groups[0], groups[1:]
        done = run(folded(group, keep, arrived), *side, limit=8)
        if side:
            done, (home0, next0, down0) = done
            above0 = from_behind(down0, 1, 0)
            side = []
        keep, *gives = done
        arrived = [swap_with(x, group, at) for at, x in enumerate(gives, 1)]
        scattered.append(group)
    (total,), (beside1,) = run(
        added(keep, arrived), job(beside_kernel, [tile], [next1, above1])
    )
    left1 = from_behind(beside1, 0, 1)
    first, second, *others = [[bit] for group in groups for bit in group]
    (total,), (beside0,), (part1,) = run(
        added(total, swapped(total, first)),
        job(beside_kernel, [tile], [next0, above0]),
        job(part_kernel, [tile], [home1, above1, left1]),
    )
    left0 = from_behind(beside0, 0, 1)
    other1 = over_owners(part1)
    (total,), (part0,) = run(
        added(total, swapped(total, second)),
        job(part_kernel, [tile], [home0, above0, left0]),
    )
    other0 = over_owners(part0)
    for group in others:
        (total,) = run(added(total, swapped(total, group)))
    like = shape_of(bf16, *tile_object.shape)
    new_object, token = updated(1, own1, part1, other1, like)
    for group in reversed(scattered):
        (total,) = run(joined(group, total, swapped(total, group)), after=[token])
    other_half = swap_with(total, core, 1)
    new_object, token = updated(
        0, own[0], part0, other0, like, so_far=new_object, flops=3_000_000_000
    )
    positions_all = lax.axis_size("tile") * lax.axis_size("pos") * (patterns.shape[2] // 2)
    step = probe_rate / math.sqrt(positions_all)
    (new_probe,) = run(
        job(
            lambda *refs: probe_kernel(step, modes, *refs),
            [shape_of(f32, *probe.shape)],
            [total, other_half, probe],
        ),
        limit=8,
        after=[token],
    )
    new_probe = new_probe.reshape(2, pixels, lane_tiles, modes, 128).transpose(0, 1, 3, 2, 4)
    return (new_object, new_probe.reshape(probe_modes.shape))


def solution(mesh):
    placed = (
        P("tile", None, None, None, None),
        P(),
        P("tile", "pos", None, None, None),
        P("tile", "pos", None, None),
        P("tile", "pos"),
    )
    return jax.shard_map(
        shards,
        mesh=mesh,
        in_specs=placed,
        out_specs=(P("tile", None, None, None, None), P()),
        check_vma=False,
    )
```

```python
import math

import jax
import jax.numpy as jnp
import numpy as np
from jax import lax
from jax.experimental import pallas as pl
from jax.experimental.pallas import tpu as pltpu
from jax.sharding import PartitionSpec as P

GRID_ROWS = 4


fresnel_coeff = 0.25
object_rate = 0.05
probe_rate = 0.15

LATE = [5_000_000_000] * 8 + [0, 0]

f32 = jnp.float32
bf16 = jnp.bfloat16


def from_behind(block, rows, cols):
    tiles = lax.axis_size("tile")
    across = tiles // GRID_ROWS

    def source(i):
        return (i // across - rows) % GRID_ROWS * across + (i % across - cols) % across

    return lax.ppermute(block, "tile", [(source(i), i) for i in range(tiles)])


def real_embed(part_re, part_im):
    upper_half = np.concatenate([part_re, -part_im], axis=1)
    lower_half = np.concatenate([part_im, part_re], axis=1)
    stacked = np.concatenate([upper_half, lower_half], axis=0)
    return jnp.asarray(stacked, dtype=f32).astype(bf16)


def build_tables(pixels):
    indices = np.arange(pixels)
    angles = indices[:, None] * indices[None, :] % pixels * (2.0 * math.pi / pixels)
    norm_scale = 1.0 / math.sqrt(pixels)
    dft_re = np.cos(angles) * norm_scale
    dft_im = -np.sin(angles) * norm_scale
    frequency = np.where(indices < pixels // 2, indices, indices - pixels)
    phases = -2.0 * math.pi * fresnel_coeff / pixels * (frequency * frequency)
    phase_sum = phases[:, None] + angles
    kern_re = np.sum(np.cos(phase_sum), axis=0) / pixels
    kern_im = np.sum(np.sin(phase_sum), axis=0) / pixels
    lag_index = (indices[:, None] - indices[None, :]) % pixels
    prop_re = kern_re[lag_index]
    prop_im = kern_im[lag_index]
    return real_embed(prop_re, prop_im), real_embed(dft_re, dft_im)


def dot(a, b):
    return jnp.dot(a, b, preferred_element_type=f32)


def shift_tables(mine_ref, sent_ref):
    n = mine_ref.shape[1]
    mine = mine_ref[n:, :].astype(f32)
    sent = sent_ref[n:, :].astype(f32)
    busy = mine[2:3] > 0
    row = jnp.where(busy, mine[0:1], sent[0:1]).astype(jnp.int32)
    col = jnp.where(busy, mine[1:2], sent[1:2]).astype(jnp.int32)
    i_out = lax.broadcasted_iota(jnp.int32, (n, 2 * n), 0)
    i_in = lax.broadcasted_iota(jnp.int32, (n, 2 * n), 1)
    j_in = lax.broadcasted_iota(jnp.int32, (2 * n, n), 0)
    j_out = lax.broadcasted_iota(jnp.int32, (2 * n, n), 1)
    row2 = jnp.concatenate([row, row], axis=1)
    col2 = jnp.concatenate([col, col], axis=1)
    rows = (i_in == i_out + row2).astype(f32).astype(bf16)
    cols = (j_in == j_out + col).astype(f32).astype(bf16)
    rows_t = (j_in == j_out + row).astype(f32).astype(bf16)
    cols_t = (i_in == i_out + col2).astype(f32).astype(bf16)
    return rows, cols, rows_t, cols_t, col, busy


def patch(shifts, own_ref, right_ref, below_ref, diag_ref, part):
    upper = jnp.concatenate([own_ref[part], right_ref[part]], axis=1)
    lower = jnp.concatenate([below_ref[part], diag_ref[part]], axis=1)
    rows = dot(shifts[0], jnp.concatenate([upper, lower], axis=0)).astype(bf16)
    return dot(rows, shifts[1])


def stacked(wave_re, wave_im):
    return jnp.concatenate([wave_re.astype(bf16), wave_im.astype(bf16)], axis=0)


def transform(table_ref, wave):
    n = wave.shape[1]
    table = table_ref[...]
    first = dot(table, wave)
    first = jnp.concatenate([first[:n].astype(bf16), (-first[n:]).astype(bf16)], axis=1)
    out = dot(first, table)
    return out[:, :n], out[:, n:]


def probe_plane(probe_ref, part, mode, modes):
    lane_tiles = 2
    n = probe_ref.shape[0] // (2 * lane_tiles * modes)
    step = lane_tiles * modes
    halves = [
        probe_ref[pl.ds(part * n * step + tile * modes + mode, n, stride=step), :]
        for tile in range(lane_tiles)
    ]
    return jnp.concatenate(halves, axis=1)


def message_kernel(offsets_ref, counts_ref, own_ref, patterns_ref, own_out, mine_ref, sent_ref):
    own_out[...] = own_ref[...]
    n = mine_ref.shape[1]
    at = lax.broadcasted_iota(jnp.int32, (16, n), 0)
    busy = (counts_ref[0, 0] == patterns_ref.shape[2]).astype(jnp.int32)
    for slot, ref in enumerate((mine_ref, sent_ref)):
        row, col = offsets_ref[0, 0, slot, 0], offsets_ref[0, 0, slot, 1]
        rows = jnp.where(at == 0, row, jnp.where(at == 1, col, busy))
        ref[pl.ds(0, n), :] = patterns_ref[0, 0, slot]
        ref[pl.ds(n, 16), :] = rows.astype(f32).astype(bf16)


def ready_kernel(probe_ref, prop_ref, planes_ref, table_ref):
    table_ref[...] = prop_ref[...]
    n = planes_ref.shape[1]
    modes = planes_ref.shape[2] // n
    for part in range(2):
        for mode in range(modes):
            planes_ref[part, :, pl.ds(mode * n, n)] = probe_plane(probe_ref, part, mode, modes)


def arrive_kernel(
    mine_ref, sent_ref, own_ref, right_ref, below_ref, diag_ref, planes_ref, prop_ref,
    near_ref, arrive_ref,
):
    n = own_ref.shape[1]
    shifts = shift_tables(mine_ref, sent_ref)
    tiles = (own_ref, right_ref.at[0], below_ref, diag_ref)
    near = [patch(shifts, *tiles, part) for part in range(2)]
    for part in range(2):
        near_ref[part] = near[part].astype(bf16)
    for mode in range(planes_ref.shape[2] // n):
        lanes = pl.ds(mode * n, n)
        p_re, p_im = planes_ref[0, :, lanes], planes_ref[1, :, lanes]
        wave = stacked(p_re * near[0] - p_im * near[1], p_re * near[1] + p_im * near[0])
        a_re, a_neg = transform(prop_ref, wave)
        arrive_ref[0, :, lanes] = a_re
        arrive_ref[1, :, lanes] = -a_neg


def spread(shifts, grad, home_ref, next_ref, down_ref):
    rows_t, cols_t, col = shifts[2:5]
    n = rows_t.shape[1]
    wrap_cols = cols_t[:, :n] + cols_t[:, n:]
    for part in range(2):
        rows = dot(rows_t, grad[part].astype(bf16)).astype(bf16)
        wide = dot(rows[:n], cols_t).astype(bf16)
        home_ref[part] = wide[:, :n]
        next_ref[part] = wide[:, n:]
        down_ref[pl.ds(part * n, n), :] = dot(rows[n:], wrap_cols).astype(bf16)
    edge = lax.broadcasted_iota(jnp.int32, (16, n), 1) < col
    down_ref[pl.ds(2 * n, 16), :] = edge.astype(f32).astype(bf16)


def far_kernel(
    mine_ref, sent_ref, own_ref, right_ref, below_ref, diag_ref, arrive_ref, dft_ref,
    home_ref, next_ref, down_ref, waves_ref,
):
    n = own_ref.shape[1]
    modes = arrive_ref.shape[2] // n
    shifts = shift_tables(mine_ref, sent_ref)
    busy = shifts[5]
    tiles = (own_ref, right_ref.at[1], below_ref, diag_ref)
    far = [patch(shifts, *tiles, part) for part in range(2)]
    fields = []
    for mode in range(modes):
        lanes = pl.ds(mode * n, n)
        a_re, a_im = arrive_ref[0, :, lanes], arrive_ref[1, :, lanes]
        wave = stacked(far[0] * a_re - far[1] * a_im, far[0] * a_im + far[1] * a_re)
        fields.append(transform(dft_ref, wave))
    intensity = sum(f_re * f_re + f_neg * f_neg for f_re, f_neg in fields)
    pattern = jnp.where(busy, mine_ref[:n, :].astype(f32), sent_ref[:n, :].astype(f32))
    residual = intensity - pattern
    grad = [0.0, 0.0]
    for mode in range(modes):
        lanes = pl.ds(mode * n, n)
        f_re, f_neg = fields[mode]
        a_re, a_im = arrive_ref[0, :, lanes], arrive_ref[1, :, lanes]
        b_re, b_im = transform(dft_ref, stacked(f_re * residual, f_neg * residual))
        grad[0] += a_re * b_re + a_im * b_im
        grad[1] += a_re * b_im - a_im * b_re
        wave = stacked(far[0] * b_re + far[1] * b_im, far[1] * b_re - far[0] * b_im)
        waves_ref[:, lanes] = wave
    spread(shifts, grad, home_ref, next_ref, down_ref)


def near_kernel(near_ref, planes_ref, waves_ref, prop_ref, grad_ref, keep_ref, give_ref, term_ref):
    n = near_ref.shape[1]
    grad = [0.0, 0.0]
    near = [near_ref[part].astype(f32) for part in range(2)]
    for mode in range(planes_ref.shape[2] // n):
        lanes = pl.ds(mode * n, n)
        b_re, b_im = transform(prop_ref, waves_ref[:, lanes])
        p_re, p_im = planes_ref[0, :, lanes], planes_ref[1, :, lanes]
        grad[0] += p_re * b_re + p_im * b_im
        grad[1] += p_re * b_im - p_im * b_re
        term_ref[0, :, lanes] = (near[0] * b_re + near[1] * b_im).astype(bf16)
        term_ref[1, :, lanes] = (near[0] * b_im - near[1] * b_re).astype(bf16)
    core = place_of(core_group())
    keep_ref[...] = term_ref[core]
    give_ref[...] = term_ref[1 - core]
    for part in range(2):
        grad_ref[part] = grad[part].astype(bf16)


def spread_kernel(mine_ref, sent_ref, grad_ref, home_ref, next_ref, down_ref):
    shifts = shift_tables(mine_ref, sent_ref)
    spread(shifts, [grad_ref[part] for part in range(2)], home_ref, next_ref, down_ref)


def above_parts(above_ref, n):
    parts = [above_ref[pl.ds(part * n, n), :].astype(f32) for part in range(2)]
    return parts, above_ref[pl.ds(2 * n, 16), :].astype(f32)[0:1] > 0


def beside_kernel(next_ref, above_ref, out_ref):
    above, split = above_parts(above_ref, out_ref.shape[1])
    for part in range(2):
        total = next_ref[part].astype(f32) + jnp.where(split, above[part], 0.0)
        out_ref[part] = total.astype(bf16)


def part_kernel(home_ref, above_ref, left_ref, out_ref):
    above, split = above_parts(above_ref, out_ref.shape[1])
    for part in range(2):
        total = home_ref[part].astype(f32) + jnp.where(split, 0.0, above[part])
        out_ref[part] = (total + left_ref[part].astype(f32)).astype(bf16)


def update_kernel(layer, own_ref, part_ref, other_ref, *refs):
    out_hbm, token_ref, new_ref, sem = refs[-4:]
    token_ref[...] = jnp.zeros_like(token_ref)
    grad = part_ref[...].astype(f32) + other_ref[...].astype(f32)
    new_ref[...] = (own_ref[...].astype(f32) - object_rate * grad).astype(bf16)
    copy = pltpu.make_async_copy(new_ref, out_hbm.at[0, layer], sem.at[0])
    copy.start()
    copy.wait()


def core_group():
    return [lax.axis_size("pos")]


def place_of(group):
    flat = lax.axis_index("tile") * lax.axis_size("pos") + lax.axis_index("pos")
    return sum(flat // mask % 2 * (1 << at) for at, mask in enumerate(group))


def job(kernel, outs, arrays, scalars=(), scratch=()):
    return kernel, list(outs), list(scalars), list(arrays), list(scratch)


def run(*jobs, flops=1_000_000, limit=4, after=()):
    vmem = pl.BlockSpec(memory_space=pltpu.VMEM)
    smem = pl.BlockSpec(memory_space=pltpu.SMEM)
    anywhere = pl.BlockSpec(memory_space=pl.ANY)
    kernels, outs, scalars, arrays, scratch = zip(*jobs)
    ins = [x + y for x, y in zip(scalars, arrays)]
    specs = [[smem] * len(x) + [vmem] * len(y) for x, y in zip(scalars, arrays)]

    def taken(refs, lists):
        parts = []
        for items in lists:
            parts.append(refs[: len(items)])
            refs = refs[len(items) :]
        return parts, refs

    def body(*refs):
        in_refs, refs = taken(refs, ins)
        out_refs, refs = taken(refs[len(after) :], outs)
        scratch_refs, _ = taken(refs, scratch)
        for kernel, *parts in zip(kernels, in_refs, out_refs, scratch_refs):
            kernel(*parts[0], *parts[1], *parts[2])

    moved = sum(x.size * x.dtype.itemsize for x in sum(ins, []) + sum(outs, []))
    results = pl.pallas_call(
        body,
        out_shape=sum(outs, []),
        in_specs=sum(specs, []) + [anywhere] * len(after),
        out_specs=[vmem] * len(sum(outs, [])),
        scratch_shapes=sum(scratch, []),
        compiler_params=pltpu.CompilerParams(vmem_limit_bytes=limit * 2**20),
        cost_estimate=pl.CostEstimate(flops=flops, bytes_accessed=moved, transcendentals=0),
    )(*sum(ins, []), *after)
    results, _ = taken(results, outs)
    return results[0] if len(jobs) == 1 else results


def updated(layer, own, part, other, like, so_far=None, flops=0, after=()):
    vmem = pl.BlockSpec(memory_space=pltpu.VMEM)
    anywhere = pl.BlockSpec(memory_space=pl.ANY)
    extra = [x for x in (so_far,) if x is not None] + list(after)
    return pl.pallas_call(
        lambda *refs: update_kernel(layer, *refs),
        out_shape=[like, shape_of(f32, 8, 128)],
        in_specs=[vmem] * 3 + [anywhere] * len(extra),
        out_specs=[anywhere, vmem],
        scratch_shapes=[pltpu.VMEM(own.shape, bf16), pltpu.SemaphoreType.DMA((1,))],
        input_output_aliases={} if so_far is None else {3: 0},
        compiler_params=pltpu.CompilerParams(vmem_limit_bytes=4 * 2**20),
        cost_estimate=pl.CostEstimate(
            flops=own.size + flops, bytes_accessed=8 * own.size, transcendentals=0
        ),
    )(own, part, other, *extra)


def shape_of(kind, *dims):
    return jax.ShapeDtypeStruct(dims, kind)


def gathered_message(patterns, offsets, counts):
    pixels = patterns.shape[4]
    all_counts = lax.all_gather(counts[0, 0], "pos")
    ends = jnp.cumsum(all_counts)
    rank = lax.axis_index("pos")
    source = jnp.sum((ends <= rank).astype(jnp.int32))
    slot = rank - (ends[source] - all_counts[source])
    spot = lax.all_gather(offsets[0, 0], "pos")[source, slot]
    pattern = lax.all_gather(patterns[0, 0], "pos")[source, slot]
    at = lax.broadcasted_iota(jnp.int32, (16, pixels), 0)
    rows = jnp.where(at == 0, spot[0], jnp.where(at == 1, spot[1], 0))
    return jnp.concatenate([pattern, rows.astype(bf16)], axis=0)


def fold_kernel(group, keep_ref, *refs):
    blocks = refs[-1]
    got = len(refs) - 1 - blocks.shape[0]
    arrived, keep_out, give_outs = refs[:got], refs[got], refs[got + 1 : -1]
    total = keep_ref[...].astype(f32)
    for ref in arrived:
        total += ref[...].astype(f32)
    size = blocks.shape[1]
    for block in range(blocks.shape[0]):
        blocks[block] = total[block * size : (block + 1) * size]
    here = place_of(group)
    keep_out[...] = blocks[here]
    for distance, ref in enumerate(give_outs, 1):
        ref[...] = blocks[here ^ distance].astype(bf16)


def add_kernel(keep_ref, *refs):
    total = keep_ref[...].astype(f32)
    for ref in refs[:-1]:
        total += ref[...].astype(f32)
    refs[-1][...] = total.astype(bf16)


def place_kernel(group, *refs):
    arrived, out_ref, blocks = refs[:-2], refs[-2], refs[-1]
    here = place_of(group)
    for distance, ref in enumerate(arrived):
        blocks[here ^ distance] = ref[...]
    size = blocks.shape[1]
    for block in range(blocks.shape[0]):
        out_ref[pl.ds(block * size, size), :] = blocks[block]


def probe_kernel(step, modes, mine_ref, other_ref, probe_ref, out_ref, token_ref):
    token_ref[...] = jnp.zeros_like(token_ref)
    core = place_of(core_group())
    lane_tiles = 2
    n = mine_ref.shape[0]
    stride = lane_tiles * modes
    for part in range(2):
        total = jnp.where(core == part, mine_ref[...].astype(f32), other_ref[...].astype(f32))
        for mode in range(modes):
            for tile in range(lane_tiles):
                lane = (mode * lane_tiles + tile) * 128
                where = pl.ds(part * n * stride + tile * modes + mode, n, stride=stride)
                out_ref[where, :] = probe_ref[where, :] - step * total[:, lane : lane + 128]


def exchange_groups():
    tiles, owners = lax.axis_size("tile"), lax.axis_size("pos")
    bits = [1 << bit for bit in range(owners.bit_length() - 1)]
    bits += [owners << bit for bit in range(1, tiles.bit_length() - 1)]
    return [bits[at : at + 2] for at in range(0, len(bits), 2)]


def swap_with(x, group, distance):
    mask = sum(bit for at, bit in enumerate(group) if distance >> at & 1)
    devices = lax.axis_size("tile") * lax.axis_size("pos")
    return lax.ppermute(x, ("tile", "pos"), [(i, i ^ mask) for i in range(devices)])


def joined(group, x, arrived):
    blocks = 1 << len(group)
    return job(
        lambda *refs: place_kernel(group, *refs),
        [shape_of(bf16, x.shape[0] * blocks, x.shape[1])],
        [x] + arrived,
        scratch=[pltpu.VMEM((blocks,) + x.shape, bf16)],
    )


def added(x, arrived):
    return job(add_kernel, [shape_of(bf16, *x.shape)], [x] + arrived)


def swapped(x, group):
    return [swap_with(x, group, at) for at in range(1, 1 << len(group))]


def folded(group, keep, arrived):
    blocks = 1 << len(group)
    size, width = keep.shape[0] // blocks, keep.shape[1]
    return job(
        lambda *refs: fold_kernel(group, *refs),
        [shape_of(f32, size, width)] + [shape_of(bf16, size, width)] * (blocks - 1),
        [keep] + arrived,
        scratch=[pltpu.VMEM((blocks, size, width), f32)],
    )


def shards(tile_object, probe_modes, patterns, offsets, counts):
    _, pixels, modes, _ = probe_modes.shape
    width = modes * pixels
    lane_tiles = pixels // 128
    prop, dft = build_tables(pixels)
    tile = shape_of(bf16, 2, pixels, pixels)
    planes = shape_of(f32, 2, pixels, width)
    probe = probe_modes.reshape(2, pixels, modes, lane_tiles, 128)
    probe = probe.transpose(0, 1, 3, 2, 4).reshape(-1, 128)

    own = [tile_object[0, 0], tile_object[0, 1]]
    below0 = from_behind(own[0], -1, 0)
    right = from_behind(tile_object[0], 0, -1)
    exchanged = lax.axis_size("pos") == patterns.shape[2]
    message = shape_of(bf16, pixels + 16, pixels)
    own1, mine, sent = run(
        job(
            message_kernel,
            [tile, message, message],
            [own[1], patterns],
            scalars=[offsets, counts if exchanged else jnp.zeros_like(counts)],
        ),
        limit=4,
        after=[own[0]],
    )
    probe_planes, table = run(
        job(ready_kernel, [planes, shape_of(bf16, *prop.shape)], [probe, prop]),
        limit=8,
        after=[own1],
    )
    below1 = from_behind(own1, -1, 0)
    if exchanged:
        sent = lax.ppermute(sent, "pos", [(i, 1 - i) for i in range(2)])
    else:
        sent = gathered_message(patterns, offsets, counts)
    diag0 = from_behind(below0, 0, -1)
    diag1 = from_behind(below1, 0, -1)
    near, arrive = run(
        job(
            arrive_kernel,
            [tile, planes],
            [mine, sent, own[0], right, below0, diag0, probe_planes, table],
        ),
        flops=1_500_000_000,
        limit=16,
    )
    half = shape_of(bf16, pixels, width)
    down = shape_of(bf16, 2 * pixels + 16, pixels)
    home1, next1, down1, waves = run(
        job(
            far_kernel,
            [tile, tile, down, shape_of(bf16, 2 * pixels, width)],
            [mine, sent, own1, right, below1, diag1, arrive, dft],
        ),
        flops=3_000_000_000,
        limit=16,
    )
    above1 = from_behind(down1, 1, 0)
    grad0, keep, give = run(
        job(
            near_kernel,
            [tile, half, half],
            [near, probe_planes, waves, table],
            scratch=[pltpu.VMEM((2, pixels, width), bf16)],
        ),
        flops=1_500_000_000,
        limit=16,
    )

    def over_owners(part):
        if lax.axis_size("pos") == 2:
            return lax.ppermute(part, "pos", [(0, 1), (1, 0)])
        return lax.psum(part.astype(f32), "pos") - part.astype(f32)

    core, groups = core_group(), exchange_groups()
    arrived = [swap_with(give, core, 1)]
    side = [job(spread_kernel, [tile, tile, down], [mine, sent, grad0])]
    scattered = []
    while len(groups) > 1 and keep.shape[0] >> len(groups[0]) >= 16:
        group, groups = groups[0], groups[1:]
        done = run(folded(group, keep, arrived), *side, limit=8)
        if side:
            done, (home0, next0, down0) = done
            above0 = from_behind(down0, 1, 0)
            side = []
        keep, *gives = done
        arrived = [swap_with(x, group, at) for at, x in enumerate(gives, 1)]
        scattered.append(group)
    first, second, *others = [[bit] for group in groups for bit in group]
    (total,) = run(added(keep, arrived))
    arrived = swapped(total, first)
    (beside1,) = run(
        job(beside_kernel, [tile], [next1, above1]), after=[total], flops=LATE[0]
    )
    left1 = from_behind(beside1, 0, 1)
    (total,) = run(added(total, arrived), after=[beside1], flops=LATE[1])
    arrived = swapped(total, second)
    (part1,) = run(
        job(part_kernel, [tile], [home1, above1, left1]), after=[total], flops=LATE[2]
    )
    other1 = over_owners(part1)
    (beside0,) = run(
        job(beside_kernel, [tile], [next0, above0]), after=[part1], flops=LATE[3]
    )
    left0 = from_behind(beside0, 0, 1)
    (total,) = run(added(total, arrived), after=[beside0], flops=LATE[4])
    for group in others:
        (total,) = run(added(total, swapped(total, group)))
    arrived = swapped(total, scattered[-1])
    (part0,) = run(
        job(part_kernel, [tile], [home0, above0, left0]), after=[total], flops=LATE[5]
    )
    other0 = over_owners(part0)
    (total,) = run(joined(scattered[-1], total, arrived), after=[part0], flops=LATE[6])
    for group in reversed(scattered[:-1]):
        (total,) = run(joined(group, total, swapped(total, group)))
    other_half = swap_with(total, core, 1)
    like = shape_of(bf16, *tile_object.shape)
    new_object, token = updated(1, own1, part1, other1, like, flops=LATE[7], after=[total])
    positions_all = lax.axis_size("tile") * lax.axis_size("pos") * (patterns.shape[2] // 2)
    step = probe_rate / math.sqrt(positions_all)
    new_probe, token = run(
        job(
            lambda *refs: probe_kernel(step, modes, *refs),
            [shape_of(f32, *probe.shape), shape_of(f32, 8, 128)],
            [total, other_half, probe],
        ),
        limit=8,
        after=[token],
        flops=LATE[8],
    )
    new_object, _ = updated(
        0, own[0], part0, other0, like, so_far=new_object, flops=LATE[9], after=[token]
    )
    new_probe = new_probe.reshape(2, pixels, lane_tiles, modes, 128).transpose(0, 1, 3, 2, 4)
    return (new_object, new_probe.reshape(probe_modes.shape))


def solution(mesh):
    placed = (
        P("tile", None, None, None, None),
        P(),
        P("tile", "pos", None, None, None),
        P("tile", "pos", None, None),
        P("tile", "pos"),
    )
    return jax.shard_map(
        shards,
        mesh=mesh,
        in_specs=placed,
        out_specs=(P("tile", None, None, None, None), P()),
        check_vma=False,
    )
```

```python
import math

import jax
import jax.numpy as jnp
import numpy as np
from jax import lax
from jax.experimental import pallas as pl
from jax.experimental.pallas import tpu as pltpu
from jax.sharding import PartitionSpec as P

GRID_ROWS = 4


fresnel_coeff = 0.25
object_rate = 0.05
probe_rate = 0.15

LATE = [0, 8_000_000_000, 0, 30_000_000_000, 0, 15_000_000_000, 0, 4_000_000_000]

f32 = jnp.float32
bf16 = jnp.bfloat16


def from_behind(block, rows, cols):
    tiles = lax.axis_size("tile")
    across = tiles // GRID_ROWS

    def source(i):
        return (i // across - rows) % GRID_ROWS * across + (i % across - cols) % across

    return lax.ppermute(block, "tile", [(source(i), i) for i in range(tiles)])


def real_embed(part_re, part_im):
    upper_half = np.concatenate([part_re, -part_im], axis=1)
    lower_half = np.concatenate([part_im, part_re], axis=1)
    stacked = np.concatenate([upper_half, lower_half], axis=0)
    return jnp.asarray(stacked, dtype=f32).astype(bf16)


def build_tables(pixels):
    indices = np.arange(pixels)
    angles = indices[:, None] * indices[None, :] % pixels * (2.0 * math.pi / pixels)
    norm_scale = 1.0 / math.sqrt(pixels)
    dft_re = np.cos(angles) * norm_scale
    dft_im = -np.sin(angles) * norm_scale
    frequency = np.where(indices < pixels // 2, indices, indices - pixels)
    phases = -2.0 * math.pi * fresnel_coeff / pixels * (frequency * frequency)
    phase_sum = phases[:, None] + angles
    kern_re = np.sum(np.cos(phase_sum), axis=0) / pixels
    kern_im = np.sum(np.sin(phase_sum), axis=0) / pixels
    lag_index = (indices[:, None] - indices[None, :]) % pixels
    prop_re = kern_re[lag_index]
    prop_im = kern_im[lag_index]
    return real_embed(prop_re, prop_im), real_embed(dft_re, dft_im)


def dot(a, b):
    return jnp.dot(a, b, preferred_element_type=f32)


def shift_tables(mine_ref, sent_ref):
    n = mine_ref.shape[1]
    mine = mine_ref[n:, :].astype(f32)
    sent = sent_ref[n:, :].astype(f32)
    busy = mine[2:3] > 0
    row = jnp.where(busy, mine[0:1], sent[0:1]).astype(jnp.int32)
    col = jnp.where(busy, mine[1:2], sent[1:2]).astype(jnp.int32)
    i_out = lax.broadcasted_iota(jnp.int32, (n, 2 * n), 0)
    i_in = lax.broadcasted_iota(jnp.int32, (n, 2 * n), 1)
    j_in = lax.broadcasted_iota(jnp.int32, (2 * n, n), 0)
    j_out = lax.broadcasted_iota(jnp.int32, (2 * n, n), 1)
    row2 = jnp.concatenate([row, row], axis=1)
    col2 = jnp.concatenate([col, col], axis=1)
    rows = (i_in == i_out + row2).astype(f32).astype(bf16)
    cols = (j_in == j_out + col).astype(f32).astype(bf16)
    rows_t = (j_in == j_out + row).astype(f32).astype(bf16)
    cols_t = (i_in == i_out + col2).astype(f32).astype(bf16)
    return rows, cols, rows_t, cols_t, col, busy


def patch(shifts, own_ref, right_ref, below_ref, diag_ref, part):
    upper = jnp.concatenate([own_ref[part], right_ref[part]], axis=1)
    lower = jnp.concatenate([below_ref[part], diag_ref[part]], axis=1)
    rows = dot(shifts[0], jnp.concatenate([upper, lower], axis=0)).astype(bf16)
    return dot(rows, shifts[1])


def stacked(wave_re, wave_im):
    return jnp.concatenate([wave_re.astype(bf16), wave_im.astype(bf16)], axis=0)


def transform(table_ref, wave):
    n = wave.shape[1]
    table = table_ref[...]
    first = dot(table, wave)
    first = jnp.concatenate([first[:n].astype(bf16), (-first[n:]).astype(bf16)], axis=1)
    out = dot(first, table)
    return out[:, :n], out[:, n:]


def probe_plane(probe_ref, part, mode, modes):
    lane_tiles = 2
    n = probe_ref.shape[0] // (2 * lane_tiles * modes)
    step = lane_tiles * modes
    halves = [
        probe_ref[pl.ds(part * n * step + tile * modes + mode, n, stride=step), :]
        for tile in range(lane_tiles)
    ]
    return jnp.concatenate(halves, axis=1)


def message_kernel(offsets_ref, counts_ref, own_ref, patterns_ref, own_out, mine_ref, sent_ref):
    own_out[...] = own_ref[...]
    n = mine_ref.shape[1]
    at = lax.broadcasted_iota(jnp.int32, (16, n), 0)
    busy = (counts_ref[0, 0] == patterns_ref.shape[2]).astype(jnp.int32)
    for slot, ref in enumerate((mine_ref, sent_ref)):
        row, col = offsets_ref[0, 0, slot, 0], offsets_ref[0, 0, slot, 1]
        rows = jnp.where(at == 0, row, jnp.where(at == 1, col, busy))
        ref[pl.ds(0, n), :] = patterns_ref[0, 0, slot]
        ref[pl.ds(n, 16), :] = rows.astype(f32).astype(bf16)


def ready_kernel(probe_ref, prop_ref, planes_ref, table_ref):
    table_ref[...] = prop_ref[...]
    n = planes_ref.shape[1]
    modes = planes_ref.shape[2] // n
    for part in range(2):
        for mode in range(modes):
            planes_ref[part, :, pl.ds(mode * n, n)] = probe_plane(probe_ref, part, mode, modes)


def arrive_kernel(
    mine_ref, sent_ref, own_ref, right_ref, below_ref, diag_ref, planes_ref, prop_ref,
    near_ref, arrive_ref,
):
    n = own_ref.shape[1]
    shifts = shift_tables(mine_ref, sent_ref)
    tiles = (own_ref, right_ref.at[0], below_ref, diag_ref)
    near = [patch(shifts, *tiles, part) for part in range(2)]
    for part in range(2):
        near_ref[part] = near[part].astype(bf16)
    for mode in range(planes_ref.shape[2] // n):
        lanes = pl.ds(mode * n, n)
        p_re, p_im = planes_ref[0, :, lanes], planes_ref[1, :, lanes]
        wave = stacked(p_re * near[0] - p_im * near[1], p_re * near[1] + p_im * near[0])
        a_re, a_neg = transform(prop_ref, wave)
        arrive_ref[0, :, lanes] = a_re
        arrive_ref[1, :, lanes] = -a_neg


def spread(shifts, grad, home_ref, next_ref, down_ref, layer):
    rows_t, cols_t = shifts[2:4]
    n = rows_t.shape[1]
    wrap_cols = cols_t[:, :n] + cols_t[:, n:]
    for part in range(2):
        rows = dot(rows_t, grad[part].astype(bf16)).astype(bf16)
        wide = dot(rows[:n], cols_t).astype(bf16)
        home_ref[part] = wide[:, :n]
        next_ref[part] = wide[:, n:]
        where = pl.ds((2 * layer + part) * n, n)
        down_ref[where, :] = dot(rows[n:], wrap_cols).astype(bf16)


def gradient_kernel(
    mine_ref, sent_ref, own_ref, right_ref, below_ref, diag_ref, near_ref, arrive_ref, planes_ref,
    prop_ref, dft_ref,
    home0_ref, next0_ref, home1_ref, next1_ref, down_ref, keep_ref, give_ref, term_ref,
):
    n = own_ref.shape[1]
    modes = planes_ref.shape[2] // n
    shifts = shift_tables(mine_ref, sent_ref)
    busy = shifts[5]
    tiles = (own_ref, right_ref.at[1], below_ref, diag_ref)
    far = [patch(shifts, *tiles, part) for part in range(2)]
    fields = []
    for mode in range(modes):
        lanes = pl.ds(mode * n, n)
        a_re, a_im = arrive_ref[0, :, lanes], arrive_ref[1, :, lanes]
        wave = stacked(far[0] * a_re - far[1] * a_im, far[0] * a_im + far[1] * a_re)
        fields.append(transform(dft_ref, wave))
    intensity = sum(f_re * f_re + f_neg * f_neg for f_re, f_neg in fields)
    pattern = jnp.where(busy, mine_ref[:n, :].astype(f32), sent_ref[:n, :].astype(f32))
    residual = intensity - pattern
    waves = []
    grad = [0.0, 0.0]
    for mode in range(modes):
        lanes = pl.ds(mode * n, n)
        f_re, f_neg = fields[mode]
        a_re, a_im = arrive_ref[0, :, lanes], arrive_ref[1, :, lanes]
        b_re, b_im = transform(dft_ref, stacked(f_re * residual, f_neg * residual))
        grad[0] += a_re * b_re + a_im * b_im
        grad[1] += a_re * b_im - a_im * b_re
        waves.append(stacked(far[0] * b_re + far[1] * b_im, far[1] * b_re - far[0] * b_im))
    spread(shifts, grad, home1_ref, next1_ref, down_ref, 1)
    grad = [0.0, 0.0]
    near = [near_ref[part].astype(f32) for part in range(2)]
    for mode in range(modes):
        lanes = pl.ds(mode * n, n)
        b_re, b_im = transform(prop_ref, waves[mode])
        p_re, p_im = planes_ref[0, :, lanes], planes_ref[1, :, lanes]
        grad[0] += p_re * b_re + p_im * b_im
        grad[1] += p_re * b_im - p_im * b_re
        term_ref[0, :, lanes] = (near[0] * b_re + near[1] * b_im).astype(bf16)
        term_ref[1, :, lanes] = (near[0] * b_im - near[1] * b_re).astype(bf16)
    core = place_of(core_group())
    keep_ref[...] = term_ref[core]
    give_ref[...] = term_ref[1 - core]
    spread(shifts, grad, home0_ref, next0_ref, down_ref, 0)
    edge = lax.broadcasted_iota(jnp.int32, (16, n), 1) < shifts[4]
    down_ref[pl.ds(4 * n, 16), :] = edge.astype(f32).astype(bf16)


def above_parts(above_ref, layer, n):
    where = [pl.ds((2 * layer + part) * n, n) for part in range(2)]
    split = above_ref[pl.ds(4 * n, 16), :].astype(f32)[0:1] > 0
    return [above_ref[rows, :].astype(f32) for rows in where], split


def beside_kernel(layer, next_ref, above_ref, out_ref):
    above, split = above_parts(above_ref, layer, out_ref.shape[1])
    for part in range(2):
        total = next_ref[part].astype(f32) + jnp.where(split, above[part], 0.0)
        out_ref[part] = total.astype(bf16)


def part_kernel(layer, home_ref, above_ref, left_ref, out_ref):
    above, split = above_parts(above_ref, layer, out_ref.shape[1])
    for part in range(2):
        total = home_ref[part].astype(f32) + jnp.where(split, 0.0, above[part])
        out_ref[part] = (total + left_ref[part].astype(f32)).astype(bf16)


def update_kernel(layer, own_ref, part_ref, other_ref, *refs):
    out_hbm, token_ref, new_ref, sem = refs[-4:]
    token_ref[...] = jnp.zeros_like(token_ref)
    grad = part_ref[...].astype(f32) + other_ref[...].astype(f32)
    new_ref[...] = (own_ref[...].astype(f32) - object_rate * grad).astype(bf16)
    copy = pltpu.make_async_copy(new_ref, out_hbm.at[0, layer], sem.at[0])
    copy.start()
    copy.wait()


def core_group():
    return [lax.axis_size("pos")]


def place_of(group):
    flat = lax.axis_index("tile") * lax.axis_size("pos") + lax.axis_index("pos")
    return sum(flat // mask % 2 * (1 << at) for at, mask in enumerate(group))


def job(kernel, outs, arrays, scalars=(), scratch=()):
    return kernel, list(outs), list(scalars), list(arrays), list(scratch)


def run(*jobs, flops=1_000_000, limit=4, after=()):
    vmem = pl.BlockSpec(memory_space=pltpu.VMEM)
    smem = pl.BlockSpec(memory_space=pltpu.SMEM)
    anywhere = pl.BlockSpec(memory_space=pl.ANY)
    kernels, outs, scalars, arrays, scratch = zip(*jobs)
    ins = [x + y for x, y in zip(scalars, arrays)]
    specs = [[smem] * len(x) + [vmem] * len(y) for x, y in zip(scalars, arrays)]

    def taken(refs, lists):
        parts = []
        for items in lists:
            parts.append(refs[: len(items)])
            refs = refs[len(items) :]
        return parts, refs

    def body(*refs):
        in_refs, refs = taken(refs, ins)
        out_refs, refs = taken(refs[len(after) :], outs)
        scratch_refs, _ = taken(refs, scratch)
        for kernel, *parts in zip(kernels, in_refs, out_refs, scratch_refs):
            kernel(*parts[0], *parts[1], *parts[2])

    moved = sum(x.size * x.dtype.itemsize for x in sum(ins, []) + sum(outs, []))
    results = pl.pallas_call(
        body,
        out_shape=sum(outs, []),
        in_specs=sum(specs, []) + [anywhere] * len(after),
        out_specs=[vmem] * len(sum(outs, [])),
        scratch_shapes=sum(scratch, []),
        compiler_params=pltpu.CompilerParams(vmem_limit_bytes=limit * 2**20),
        cost_estimate=pl.CostEstimate(flops=flops, bytes_accessed=moved, transcendentals=0),
    )(*sum(ins, []), *after)
    results, _ = taken(results, outs)
    return results[0] if len(jobs) == 1 else results


def updated(layer, own, part, other, like, so_far=None, flops=0, after=()):
    vmem = pl.BlockSpec(memory_space=pltpu.VMEM)
    anywhere = pl.BlockSpec(memory_space=pl.ANY)
    extra = [x for x in (so_far,) if x is not None] + list(after)
    return pl.pallas_call(
        lambda *refs: update_kernel(layer, *refs),
        out_shape=[like, shape_of(f32, 8, 128)],
        in_specs=[vmem] * 3 + [anywhere] * len(extra),
        out_specs=[anywhere, vmem],
        scratch_shapes=[pltpu.VMEM(own.shape, bf16), pltpu.SemaphoreType.DMA((1,))],
        input_output_aliases={} if so_far is None else {3: 0},
        compiler_params=pltpu.CompilerParams(vmem_limit_bytes=4 * 2**20),
        cost_estimate=pl.CostEstimate(
            flops=own.size + flops, bytes_accessed=8 * own.size, transcendentals=0
        ),
    )(own, part, other, *extra)


def shape_of(kind, *dims):
    return jax.ShapeDtypeStruct(dims, kind)


def gathered_message(patterns, offsets, counts):
    pixels = patterns.shape[4]
    all_counts = lax.all_gather(counts[0, 0], "pos")
    ends = jnp.cumsum(all_counts)
    rank = lax.axis_index("pos")
    source = jnp.sum((ends <= rank).astype(jnp.int32))
    slot = rank - (ends[source] - all_counts[source])
    spot = lax.all_gather(offsets[0, 0], "pos")[source, slot]
    pattern = lax.all_gather(patterns[0, 0], "pos")[source, slot]
    at = lax.broadcasted_iota(jnp.int32, (16, pixels), 0)
    rows = jnp.where(at == 0, spot[0], jnp.where(at == 1, spot[1], 0))
    return jnp.concatenate([pattern, rows.astype(bf16)], axis=0)


def fold_kernel(group, keep_ref, *refs):
    blocks = refs[-1]
    got = len(refs) - 1 - blocks.shape[0]
    arrived, keep_out, give_outs = refs[:got], refs[got], refs[got + 1 : -1]
    total = keep_ref[...].astype(f32)
    for ref in arrived:
        total += ref[...].astype(f32)
    size = blocks.shape[1]
    for block in range(blocks.shape[0]):
        blocks[block] = total[block * size : (block + 1) * size]
    here = place_of(group)
    keep_out[...] = blocks[here]
    for distance, ref in enumerate(give_outs, 1):
        ref[...] = blocks[here ^ distance].astype(bf16)


def add_kernel(keep_ref, *refs):
    total = keep_ref[...].astype(f32)
    for ref in refs[:-1]:
        total += ref[...].astype(f32)
    refs[-1][...] = total.astype(bf16)


def place_kernel(group, *refs):
    arrived, out_ref, blocks = refs[:-2], refs[-2], refs[-1]
    here = place_of(group)
    for distance, ref in enumerate(arrived):
        blocks[here ^ distance] = ref[...]
    size = blocks.shape[1]
    for block in range(blocks.shape[0]):
        out_ref[pl.ds(block * size, size), :] = blocks[block]


def probe_kernel(step, modes, mine_ref, other_ref, probe_ref, out_ref):
    core = place_of(core_group())
    lane_tiles = 2
    n = mine_ref.shape[0]
    stride = lane_tiles * modes
    for part in range(2):
        total = jnp.where(core == part, mine_ref[...].astype(f32), other_ref[...].astype(f32))
        for mode in range(modes):
            for tile in range(lane_tiles):
                lane = (mode * lane_tiles + tile) * 128
                where = pl.ds(part * n * stride + tile * modes + mode, n, stride=stride)
                out_ref[where, :] = probe_ref[where, :] - step * total[:, lane : lane + 128]


def exchange_groups():
    tiles, owners = lax.axis_size("tile"), lax.axis_size("pos")
    bits = [1 << bit for bit in range(owners.bit_length() - 1)]
    bits += [owners << bit for bit in range(1, tiles.bit_length() - 1)]
    return [bits[at : at + 2] for at in range(0, len(bits), 2)]


def swap_with(x, group, distance):
    mask = sum(bit for at, bit in enumerate(group) if distance >> at & 1)
    devices = lax.axis_size("tile") * lax.axis_size("pos")
    return lax.ppermute(x, ("tile", "pos"), [(i, i ^ mask) for i in range(devices)])


def joined(group, x, arrived):
    blocks = 1 << len(group)
    return job(
        lambda *refs: place_kernel(group, *refs),
        [shape_of(bf16, x.shape[0] * blocks, x.shape[1])],
        [x] + arrived,
        scratch=[pltpu.VMEM((blocks,) + x.shape, bf16)],
    )


def added(x, arrived):
    return job(add_kernel, [shape_of(bf16, *x.shape)], [x] + arrived)


def swapped(x, group):
    return [swap_with(x, group, at) for at in range(1, 1 << len(group))]


def folded(group, keep, arrived):
    blocks = 1 << len(group)
    size, width = keep.shape[0] // blocks, keep.shape[1]
    return job(
        lambda *refs: fold_kernel(group, *refs),
        [shape_of(f32, size, width)] + [shape_of(bf16, size, width)] * (blocks - 1),
        [keep] + arrived,
        scratch=[pltpu.VMEM((blocks, size, width), f32)],
    )


def shards(tile_object, probe_modes, patterns, offsets, counts):
    _, pixels, modes, _ = probe_modes.shape
    width = modes * pixels
    lane_tiles = pixels // 128
    prop, dft = build_tables(pixels)
    tile = shape_of(bf16, 2, pixels, pixels)
    planes = shape_of(f32, 2, pixels, width)
    probe = probe_modes.reshape(2, pixels, modes, lane_tiles, 128)
    probe = probe.transpose(0, 1, 3, 2, 4).reshape(-1, 128)

    own = [tile_object[0, 0], tile_object[0, 1]]
    below0 = from_behind(own[0], -1, 0)
    right = from_behind(tile_object[0], 0, -1)
    exchanged = lax.axis_size("pos") == patterns.shape[2]
    message = shape_of(bf16, pixels + 16, pixels)
    own1, mine, sent = run(
        job(
            message_kernel,
            [tile, message, message],
            [own[1], patterns],
            scalars=[offsets, counts if exchanged else jnp.zeros_like(counts)],
        ),
        limit=4,
        after=[own[0]],
    )
    probe_planes, table = run(
        job(ready_kernel, [planes, shape_of(bf16, *prop.shape)], [probe, prop]),
        limit=8,
        after=[own1],
    )
    below1 = from_behind(own1, -1, 0)
    if exchanged:
        sent = lax.ppermute(sent, "pos", [(i, 1 - i) for i in range(2)])
    else:
        sent = gathered_message(patterns, offsets, counts)
    diag0 = from_behind(below0, 0, -1)
    diag1 = from_behind(below1, 0, -1)
    near, arrive = run(
        job(
            arrive_kernel,
            [tile, planes],
            [mine, sent, own[0], right, below0, diag0, probe_planes, table],
        ),
        flops=1_500_000_000,
        limit=16,
    )
    half = shape_of(bf16, pixels, width)
    home0, next0, home1, next1, down, keep, give = run(
        job(
            gradient_kernel,
            [tile] * 4 + [shape_of(bf16, 4 * pixels + 16, pixels), half, half],
            [mine, sent, own1, right, below1, diag1, near, arrive, probe_planes, table, dft],
            scratch=[pltpu.VMEM((2, pixels, width), bf16)],
        ),
        flops=4_000_000_000,
        limit=16,
    )

    def over_owners(part):
        if lax.axis_size("pos") == 2:
            return lax.ppermute(part, "pos", [(0, 1), (1, 0)])
        return lax.psum(part.astype(f32), "pos") - part.astype(f32)

    def beside(layer, next_tile):
        kernel = lambda *refs: beside_kernel(layer, *refs)
        return job(kernel, [tile], [next_tile, above])

    def part(layer, home, left):
        kernel = lambda *refs: part_kernel(layer, *refs)
        return job(kernel, [tile], [home, above, left])

    core, groups = core_group(), exchange_groups()
    above = from_behind(down, 1, 0)
    arrived = [swap_with(give, core, 1)]
    scattered = []
    while len(groups) > 1 and keep.shape[0] >> len(groups[0]) >= 16:
        group, groups = groups[0], groups[1:]
        keep, *gives = run(folded(group, keep, arrived))
        arrived = [swap_with(x, group, at) for at, x in enumerate(gives, 1)]
        scattered.append(group)
    first, second, *others = [[bit] for group in groups for bit in group]
    (total,) = run(added(keep, arrived))
    arrived = swapped(total, first)
    (beside1,), (beside0,) = run(
        beside(1, next1), beside(0, next0), after=[total], flops=LATE[0]
    )
    left1 = from_behind(beside1, 0, 1)
    left0 = from_behind(beside0, 0, 1)
    (total,) = run(added(total, arrived), after=[beside1], flops=LATE[1])
    arrived = swapped(total, second)
    (part1,) = run(part(1, home1, left1), after=[total], flops=LATE[2])
    other1 = over_owners(part1)
    (total,) = run(added(total, arrived), after=[part1], flops=LATE[3])
    for group in others:
        (total,) = run(added(total, swapped(total, group)))
    arrived = swapped(total, scattered[-1])
    (part0,) = run(part(0, home0, left0), after=[total], flops=LATE[4])
    other0 = over_owners(part0)
    like = shape_of(bf16, *tile_object.shape)
    new_object, token = updated(1, own1, part1, other1, like, flops=LATE[5], after=[part0])
    (total,) = run(joined(scattered[-1], total, arrived), after=[token], flops=LATE[6])
    for group in reversed(scattered[:-1]):
        (total,) = run(joined(group, total, swapped(total, group)))
    other_half = swap_with(total, core, 1)
    new_object, token = updated(
        0, own[0], part0, other0, like, so_far=new_object, flops=LATE[7], after=[total]
    )
    positions_all = lax.axis_size("tile") * lax.axis_size("pos") * (patterns.shape[2] // 2)
    step = probe_rate / math.sqrt(positions_all)
    (new_probe,) = run(
        job(
            lambda *refs: probe_kernel(step, modes, *refs),
            [shape_of(f32, *probe.shape)],
            [total, other_half, probe],
        ),
        limit=8,
        after=[token],
    )
    new_probe = new_probe.reshape(2, pixels, lane_tiles, modes, 128).transpose(0, 1, 3, 2, 4)
    return (new_object, new_probe.reshape(probe_modes.shape))


def solution(mesh):
    placed = (
        P("tile", None, None, None, None),
        P(),
        P("tile", "pos", None, None, None),
        P("tile", "pos", None, None),
        P("tile", "pos"),
    )
    return jax.shard_map(
        shards,
        mesh=mesh,
        in_specs=placed,
        out_specs=(P("tile", None, None, None, None), P()),
        check_vma=False,
    )
```

```python
import math

import jax
import jax.numpy as jnp
import numpy as np
from jax import lax
from jax.experimental import pallas as pl
from jax.experimental.pallas import tpu as pltpu
from jax.sharding import PartitionSpec as P

GRID_ROWS = 4


fresnel_coeff = 0.25
object_rate = 0.05
probe_rate = 0.15

LATE = [0, 0, 5_000_000_000, 5_000_000_000, 0, 0, 15_000_000_000, 0, 4_000_000_000]

f32 = jnp.float32
bf16 = jnp.bfloat16


def from_behind(block, rows, cols):
    tiles = lax.axis_size("tile")
    across = tiles // GRID_ROWS

    def source(i):
        return (i // across - rows) % GRID_ROWS * across + (i % across - cols) % across

    return lax.ppermute(block, "tile", [(source(i), i) for i in range(tiles)])


def real_embed(part_re, part_im):
    upper_half = np.concatenate([part_re, -part_im], axis=1)
    lower_half = np.concatenate([part_im, part_re], axis=1)
    stacked = np.concatenate([upper_half, lower_half], axis=0)
    return jnp.asarray(stacked, dtype=f32).astype(bf16)


def build_tables(pixels):
    indices = np.arange(pixels)
    angles = indices[:, None] * indices[None, :] % pixels * (2.0 * math.pi / pixels)
    norm_scale = 1.0 / math.sqrt(pixels)
    dft_re = np.cos(angles) * norm_scale
    dft_im = -np.sin(angles) * norm_scale
    frequency = np.where(indices < pixels // 2, indices, indices - pixels)
    phases = -2.0 * math.pi * fresnel_coeff / pixels * (frequency * frequency)
    phase_sum = phases[:, None] + angles
    kern_re = np.sum(np.cos(phase_sum), axis=0) / pixels
    kern_im = np.sum(np.sin(phase_sum), axis=0) / pixels
    lag_index = (indices[:, None] - indices[None, :]) % pixels
    prop_re = kern_re[lag_index]
    prop_im = kern_im[lag_index]
    return real_embed(prop_re, prop_im), real_embed(dft_re, dft_im)


def dot(a, b):
    return jnp.dot(a, b, preferred_element_type=f32)


def shift_tables(mine_ref, sent_ref):
    n = mine_ref.shape[1]
    mine = mine_ref[n:, :].astype(f32)
    sent = sent_ref[n:, :].astype(f32)
    busy = mine[2:3] > 0
    row = jnp.where(busy, mine[0:1], sent[0:1]).astype(jnp.int32)
    col = jnp.where(busy, mine[1:2], sent[1:2]).astype(jnp.int32)
    i_out = lax.broadcasted_iota(jnp.int32, (n, 2 * n), 0)
    i_in = lax.broadcasted_iota(jnp.int32, (n, 2 * n), 1)
    j_in = lax.broadcasted_iota(jnp.int32, (2 * n, n), 0)
    j_out = lax.broadcasted_iota(jnp.int32, (2 * n, n), 1)
    row2 = jnp.concatenate([row, row], axis=1)
    col2 = jnp.concatenate([col, col], axis=1)
    rows = (i_in == i_out + row2).astype(f32).astype(bf16)
    cols = (j_in == j_out + col).astype(f32).astype(bf16)
    rows_t = (j_in == j_out + row).astype(f32).astype(bf16)
    cols_t = (i_in == i_out + col2).astype(f32).astype(bf16)
    return rows, cols, rows_t, cols_t, col, busy


def patch(shifts, own_ref, right_ref, below_ref, diag_ref, part):
    upper = jnp.concatenate([own_ref[part], right_ref[part]], axis=1)
    lower = jnp.concatenate([below_ref[part], diag_ref[part]], axis=1)
    rows = dot(shifts[0], jnp.concatenate([upper, lower], axis=0)).astype(bf16)
    return dot(rows, shifts[1])


def stacked(wave_re, wave_im):
    return jnp.concatenate([wave_re.astype(bf16), wave_im.astype(bf16)], axis=0)


def transform(table_ref, wave):
    n = wave.shape[1]
    table = table_ref[...]
    first = dot(table, wave)
    first = jnp.concatenate([first[:n].astype(bf16), (-first[n:]).astype(bf16)], axis=1)
    out = dot(first, table)
    return out[:, :n], out[:, n:]


def probe_plane(probe_ref, part, mode, modes):
    lane_tiles = 2
    n = probe_ref.shape[0] // (2 * lane_tiles * modes)
    step = lane_tiles * modes
    halves = [
        probe_ref[pl.ds(part * n * step + tile * modes + mode, n, stride=step), :]
        for tile in range(lane_tiles)
    ]
    return jnp.concatenate(halves, axis=1)


def message_kernel(offsets_ref, counts_ref, own_ref, patterns_ref, own_out, mine_ref, sent_ref):
    own_out[...] = own_ref[...]
    n = mine_ref.shape[1]
    at = lax.broadcasted_iota(jnp.int32, (16, n), 0)
    busy = (counts_ref[0, 0] == patterns_ref.shape[2]).astype(jnp.int32)
    for slot, ref in enumerate((mine_ref, sent_ref)):
        row, col = offsets_ref[0, 0, slot, 0], offsets_ref[0, 0, slot, 1]
        rows = jnp.where(at == 0, row, jnp.where(at == 1, col, busy))
        ref[pl.ds(0, n), :] = patterns_ref[0, 0, slot]
        ref[pl.ds(n, 16), :] = rows.astype(f32).astype(bf16)


def ready_kernel(probe_ref, prop_ref, planes_ref, table_ref):
    table_ref[...] = prop_ref[...]
    n = planes_ref.shape[1]
    modes = planes_ref.shape[2] // n
    for part in range(2):
        for mode in range(modes):
            planes_ref[part, :, pl.ds(mode * n, n)] = probe_plane(probe_ref, part, mode, modes)


def arrive_kernel(
    mine_ref, sent_ref, own_ref, right_ref, below_ref, diag_ref, planes_ref, prop_ref,
    near_ref, arrive_ref,
):
    n = own_ref.shape[1]
    shifts = shift_tables(mine_ref, sent_ref)
    tiles = (own_ref, right_ref.at[0], below_ref, diag_ref)
    near = [patch(shifts, *tiles, part) for part in range(2)]
    for part in range(2):
        near_ref[part] = near[part].astype(bf16)
    for mode in range(planes_ref.shape[2] // n):
        lanes = pl.ds(mode * n, n)
        p_re, p_im = planes_ref[0, :, lanes], planes_ref[1, :, lanes]
        wave = stacked(p_re * near[0] - p_im * near[1], p_re * near[1] + p_im * near[0])
        a_re, a_neg = transform(prop_ref, wave)
        arrive_ref[0, :, lanes] = a_re
        arrive_ref[1, :, lanes] = -a_neg


def spread(shifts, grad, home_ref, next_ref, down_ref):
    rows_t, cols_t, col = shifts[2:5]
    n = rows_t.shape[1]
    wrap_cols = cols_t[:, :n] + cols_t[:, n:]
    for part in range(2):
        rows = dot(rows_t, grad[part].astype(bf16)).astype(bf16)
        wide = dot(rows[:n], cols_t).astype(bf16)
        home_ref[part] = wide[:, :n]
        next_ref[part] = wide[:, n:]
        down_ref[pl.ds(part * n, n), :] = dot(rows[n:], wrap_cols).astype(bf16)
    edge = lax.broadcasted_iota(jnp.int32, (16, n), 1) < col
    down_ref[pl.ds(2 * n, 16), :] = edge.astype(f32).astype(bf16)


def spread_kernel(mine_ref, sent_ref, grad_ref, home_ref, next_ref, down_ref):
    shifts = shift_tables(mine_ref, sent_ref)
    spread(shifts, [grad_ref[part] for part in range(2)], home_ref, next_ref, down_ref)


def gradient_kernel(
    mine_ref, sent_ref, own_ref, right_ref, below_ref, diag_ref, near_ref, arrive_ref, planes_ref,
    prop_ref, dft_ref,
    home_ref, next_ref, down_ref, grad_ref, keep_ref, give_ref, term_ref,
):
    n = own_ref.shape[1]
    modes = planes_ref.shape[2] // n
    shifts = shift_tables(mine_ref, sent_ref)
    busy = shifts[5]
    tiles = (own_ref, right_ref.at[1], below_ref, diag_ref)
    far = [patch(shifts, *tiles, part) for part in range(2)]
    fields = []
    for mode in range(modes):
        lanes = pl.ds(mode * n, n)
        a_re, a_im = arrive_ref[0, :, lanes], arrive_ref[1, :, lanes]
        wave = stacked(far[0] * a_re - far[1] * a_im, far[0] * a_im + far[1] * a_re)
        fields.append(transform(dft_ref, wave))
    intensity = sum(f_re * f_re + f_neg * f_neg for f_re, f_neg in fields)
    pattern = jnp.where(busy, mine_ref[:n, :].astype(f32), sent_ref[:n, :].astype(f32))
    residual = intensity - pattern
    waves = []
    grad = [0.0, 0.0]
    for mode in range(modes):
        lanes = pl.ds(mode * n, n)
        f_re, f_neg = fields[mode]
        a_re, a_im = arrive_ref[0, :, lanes], arrive_ref[1, :, lanes]
        b_re, b_im = transform(dft_ref, stacked(f_re * residual, f_neg * residual))
        grad[0] += a_re * b_re + a_im * b_im
        grad[1] += a_re * b_im - a_im * b_re
        waves.append(stacked(far[0] * b_re + far[1] * b_im, far[1] * b_re - far[0] * b_im))
    spread(shifts, grad, home_ref, next_ref, down_ref)
    grad = [0.0, 0.0]
    near = [near_ref[part].astype(f32) for part in range(2)]
    for mode in range(modes):
        lanes = pl.ds(mode * n, n)
        b_re, b_im = transform(prop_ref, waves[mode])
        p_re, p_im = planes_ref[0, :, lanes], planes_ref[1, :, lanes]
        grad[0] += p_re * b_re + p_im * b_im
        grad[1] += p_re * b_im - p_im * b_re
        term_ref[0, :, lanes] = (near[0] * b_re + near[1] * b_im).astype(bf16)
        term_ref[1, :, lanes] = (near[0] * b_im - near[1] * b_re).astype(bf16)
    core = place_of(core_group())
    keep_ref[...] = term_ref[core]
    give_ref[...] = term_ref[1 - core]
    for part in range(2):
        grad_ref[part] = grad[part].astype(bf16)


def above_parts(above_ref, n):
    parts = [above_ref[pl.ds(part * n, n), :].astype(f32) for part in range(2)]
    return parts, above_ref[pl.ds(2 * n, 16), :].astype(f32)[0:1] > 0


def beside_kernel(next_ref, above_ref, out_ref):
    above, split = above_parts(above_ref, out_ref.shape[1])
    for part in range(2):
        total = next_ref[part].astype(f32) + jnp.where(split, above[part], 0.0)
        out_ref[part] = total.astype(bf16)


def part_kernel(home_ref, above_ref, left_ref, out_ref):
    above, split = above_parts(above_ref, out_ref.shape[1])
    for part in range(2):
        total = home_ref[part].astype(f32) + jnp.where(split, 0.0, above[part])
        out_ref[part] = (total + left_ref[part].astype(f32)).astype(bf16)


def update_kernel(layer, own_ref, part_ref, other_ref, *refs):
    out_hbm, token_ref, new_ref, sem = refs[-4:]
    token_ref[...] = jnp.zeros_like(token_ref)
    grad = part_ref[...].astype(f32) + other_ref[...].astype(f32)
    new_ref[...] = (own_ref[...].astype(f32) - object_rate * grad).astype(bf16)
    copy = pltpu.make_async_copy(new_ref, out_hbm.at[0, layer], sem.at[0])
    copy.start()
    copy.wait()


def core_group():
    return [lax.axis_size("pos")]


def place_of(group):
    flat = lax.axis_index("tile") * lax.axis_size("pos") + lax.axis_index("pos")
    return sum(flat // mask % 2 * (1 << at) for at, mask in enumerate(group))


def job(kernel, outs, arrays, scalars=(), scratch=()):
    return kernel, list(outs), list(scalars), list(arrays), list(scratch)


def run(*jobs, flops=1_000_000, limit=4, after=()):
    vmem = pl.BlockSpec(memory_space=pltpu.VMEM)
    smem = pl.BlockSpec(memory_space=pltpu.SMEM)
    anywhere = pl.BlockSpec(memory_space=pl.ANY)
    kernels, outs, scalars, arrays, scratch = zip(*jobs)
    ins = [x + y for x, y in zip(scalars, arrays)]
    specs = [[smem] * len(x) + [vmem] * len(y) for x, y in zip(scalars, arrays)]

    def taken(refs, lists):
        parts = []
        for items in lists:
            parts.append(refs[: len(items)])
            refs = refs[len(items) :]
        return parts, refs

    def body(*refs):
        in_refs, refs = taken(refs, ins)
        out_refs, refs = taken(refs[len(after) :], outs)
        scratch_refs, _ = taken(refs, scratch)
        for kernel, *parts in zip(kernels, in_refs, out_refs, scratch_refs):
            kernel(*parts[0], *parts[1], *parts[2])

    moved = sum(x.size * x.dtype.itemsize for x in sum(ins, []) + sum(outs, []))
    results = pl.pallas_call(
        body,
        out_shape=sum(outs, []),
        in_specs=sum(specs, []) + [anywhere] * len(after),
        out_specs=[vmem] * len(sum(outs, [])),
        scratch_shapes=sum(scratch, []),
        compiler_params=pltpu.CompilerParams(vmem_limit_bytes=limit * 2**20),
        cost_estimate=pl.CostEstimate(flops=flops, bytes_accessed=moved, transcendentals=0),
    )(*sum(ins, []), *after)
    results, _ = taken(results, outs)
    return results[0] if len(jobs) == 1 else results


def updated(layer, own, part, other, like, so_far=None, flops=0, after=()):
    vmem = pl.BlockSpec(memory_space=pltpu.VMEM)
    anywhere = pl.BlockSpec(memory_space=pl.ANY)
    extra = [x for x in (so_far,) if x is not None] + list(after)
    return pl.pallas_call(
        lambda *refs: update_kernel(layer, *refs),
        out_shape=[like, shape_of(f32, 8, 128)],
        in_specs=[vmem] * 3 + [anywhere] * len(extra),
        out_specs=[anywhere, vmem],
        scratch_shapes=[pltpu.VMEM(own.shape, bf16), pltpu.SemaphoreType.DMA((1,))],
        input_output_aliases={} if so_far is None else {3: 0},
        compiler_params=pltpu.CompilerParams(vmem_limit_bytes=4 * 2**20),
        cost_estimate=pl.CostEstimate(
            flops=own.size + flops, bytes_accessed=8 * own.size, transcendentals=0
        ),
    )(own, part, other, *extra)


def shape_of(kind, *dims):
    return jax.ShapeDtypeStruct(dims, kind)


def gathered_message(patterns, offsets, counts):
    pixels = patterns.shape[4]
    all_counts = lax.all_gather(counts[0, 0], "pos")
    ends = jnp.cumsum(all_counts)
    rank = lax.axis_index("pos")
    source = jnp.sum((ends <= rank).astype(jnp.int32))
    slot = rank - (ends[source] - all_counts[source])
    spot = lax.all_gather(offsets[0, 0], "pos")[source, slot]
    pattern = lax.all_gather(patterns[0, 0], "pos")[source, slot]
    at = lax.broadcasted_iota(jnp.int32, (16, pixels), 0)
    rows = jnp.where(at == 0, spot[0], jnp.where(at == 1, spot[1], 0))
    return jnp.concatenate([pattern, rows.astype(bf16)], axis=0)


def fold_kernel(group, keep_ref, *refs):
    blocks = refs[-1]
    got = len(refs) - 1 - blocks.shape[0]
    arrived, keep_out, give_outs = refs[:got], refs[got], refs[got + 1 : -1]
    total = keep_ref[...].astype(f32)
    for ref in arrived:
        total += ref[...].astype(f32)
    size = blocks.shape[1]
    for block in range(blocks.shape[0]):
        blocks[block] = total[block * size : (block + 1) * size]
    here = place_of(group)
    keep_out[...] = blocks[here]
    for distance, ref in enumerate(give_outs, 1):
        ref[...] = blocks[here ^ distance].astype(bf16)


def add_kernel(keep_ref, *refs):
    total = keep_ref[...].astype(f32)
    for ref in refs[:-1]:
        total += ref[...].astype(f32)
    refs[-1][...] = total.astype(bf16)


def place_kernel(group, *refs):
    arrived, out_ref, blocks = refs[:-2], refs[-2], refs[-1]
    here = place_of(group)
    for distance, ref in enumerate(arrived):
        blocks[here ^ distance] = ref[...]
    size = blocks.shape[1]
    for block in range(blocks.shape[0]):
        out_ref[pl.ds(block * size, size), :] = blocks[block]


def probe_kernel(step, modes, mine_ref, other_ref, probe_ref, out_ref):
    core = place_of(core_group())
    lane_tiles = 2
    n = mine_ref.shape[0]
    stride = lane_tiles * modes
    for part in range(2):
        total = jnp.where(core == part, mine_ref[...].astype(f32), other_ref[...].astype(f32))
        for mode in range(modes):
            for tile in range(lane_tiles):
                lane = (mode * lane_tiles + tile) * 128
                where = pl.ds(part * n * stride + tile * modes + mode, n, stride=stride)
                out_ref[where, :] = probe_ref[where, :] - step * total[:, lane : lane + 128]


def exchange_groups():
    tiles, owners = lax.axis_size("tile"), lax.axis_size("pos")
    bits = [1 << bit for bit in range(owners.bit_length() - 1)]
    bits += [owners << bit for bit in range(1, tiles.bit_length() - 1)]
    return [bits[at : at + 2] for at in range(0, len(bits), 2)]


def swap_with(x, group, distance):
    mask = sum(bit for at, bit in enumerate(group) if distance >> at & 1)
    devices = lax.axis_size("tile") * lax.axis_size("pos")
    return lax.ppermute(x, ("tile", "pos"), [(i, i ^ mask) for i in range(devices)])


def joined(group, x, arrived):
    blocks = 1 << len(group)
    return job(
        lambda *refs: place_kernel(group, *refs),
        [shape_of(bf16, x.shape[0] * blocks, x.shape[1])],
        [x] + arrived,
        scratch=[pltpu.VMEM((blocks,) + x.shape, bf16)],
    )


def added(x, arrived):
    return job(add_kernel, [shape_of(bf16, *x.shape)], [x] + arrived)


def swapped(x, group):
    return [swap_with(x, group, at) for at in range(1, 1 << len(group))]


def folded(group, keep, arrived):
    blocks = 1 << len(group)
    size, width = keep.shape[0] // blocks, keep.shape[1]
    return job(
        lambda *refs: fold_kernel(group, *refs),
        [shape_of(f32, size, width)] + [shape_of(bf16, size, width)] * (blocks - 1),
        [keep] + arrived,
        scratch=[pltpu.VMEM((blocks, size, width), f32)],
    )


def shards(tile_object, probe_modes, patterns, offsets, counts):
    _, pixels, modes, _ = probe_modes.shape
    width = modes * pixels
    lane_tiles = pixels // 128
    prop, dft = build_tables(pixels)
    tile = shape_of(bf16, 2, pixels, pixels)
    planes = shape_of(f32, 2, pixels, width)
    probe = probe_modes.reshape(2, pixels, modes, lane_tiles, 128)
    probe = probe.transpose(0, 1, 3, 2, 4).reshape(-1, 128)

    own = [tile_object[0, 0], tile_object[0, 1]]
    below0 = from_behind(own[0], -1, 0)
    right = from_behind(tile_object[0], 0, -1)
    exchanged = lax.axis_size("pos") == patterns.shape[2]
    message = shape_of(bf16, pixels + 16, pixels)
    own1, mine, sent = run(
        job(
            message_kernel,
            [tile, message, message],
            [own[1], patterns],
            scalars=[offsets, counts if exchanged else jnp.zeros_like(counts)],
        ),
        limit=4,
        after=[own[0]],
    )
    probe_planes, table = run(
        job(ready_kernel, [planes, shape_of(bf16, *prop.shape)], [probe, prop]),
        limit=8,
        after=[own1],
    )
    below1 = from_behind(own1, -1, 0)
    if exchanged:
        sent = lax.ppermute(sent, "pos", [(i, 1 - i) for i in range(2)])
    else:
        sent = gathered_message(patterns, offsets, counts)
    diag0 = from_behind(below0, 0, -1)
    diag1 = from_behind(below1, 0, -1)
    near, arrive = run(
        job(
            arrive_kernel,
            [tile, planes],
            [mine, sent, own[0], right, below0, diag0, probe_planes, table],
        ),
        flops=1_500_000_000,
        limit=16,
    )
    half = shape_of(bf16, pixels, width)
    down = shape_of(bf16, 2 * pixels + 16, pixels)
    home1, next1, down1, grad0, keep, give = run(
        job(
            gradient_kernel,
            [tile, tile, down, tile, half, half],
            [mine, sent, own1, right, below1, diag1, near, arrive, probe_planes, table, dft],
            scratch=[pltpu.VMEM((2, pixels, width), bf16)],
        ),
        flops=4_000_000_000,
        limit=16,
    )

    def over_owners(part):
        if lax.axis_size("pos") == 2:
            return lax.ppermute(part, "pos", [(0, 1), (1, 0)])
        return lax.psum(part.astype(f32), "pos") - part.astype(f32)

    def beside(next_tile, above):
        return job(beside_kernel, [tile], [next_tile, above])

    def part(home, above, left):
        return job(part_kernel, [tile], [home, above, left])

    core, groups = core_group(), exchange_groups()
    above1 = from_behind(down1, 1, 0)
    arrived = [swap_with(give, core, 1)]
    side = [job(spread_kernel, [tile, tile, down], [mine, sent, grad0])]
    scattered = []
    while len(groups) > 1 and keep.shape[0] >> len(groups[0]) >= 16:
        group, groups = groups[0], groups[1:]
        done = run(folded(group, keep, arrived), *side, limit=8)
        if side:
            done, (home0, next0, down0) = done
            above0 = from_behind(down0, 1, 0)
            side = []
        keep, *gives = done
        arrived = [swap_with(x, group, at) for at, x in enumerate(gives, 1)]
        scattered.append(group)
    first, second, *others = [[bit] for group in groups for bit in group]
    (total,) = run(added(keep, arrived))
    arrived = swapped(total, first)
    (beside1,) = run(beside(next1, above1), after=[total], flops=LATE[0])
    left1 = from_behind(beside1, 0, 1)
    (part1,) = run(part(home1, above1, left1), flops=LATE[1])
    other1 = over_owners(part1)
    (beside0,) = run(beside(next0, above0), after=[part1], flops=LATE[2])
    left0 = from_behind(beside0, 0, 1)
    (total,) = run(added(total, arrived), after=[beside0], flops=LATE[3])
    arrived = swapped(total, second)
    (total,) = run(added(total, arrived), flops=LATE[4])
    for group in others:
        (total,) = run(added(total, swapped(total, group)))
    arrived = swapped(total, scattered[-1])
    (part0,) = run(part(home0, above0, left0), after=[total], flops=LATE[5])
    other0 = over_owners(part0)
    like = shape_of(bf16, *tile_object.shape)
    new_object, token = updated(1, own1, part1, other1, like, flops=LATE[6], after=[part0])
    (total,) = run(joined(scattered[-1], total, arrived), after=[token], flops=LATE[7])
    for group in reversed(scattered[:-1]):
        (total,) = run(joined(group, total, swapped(total, group)))
    other_half = swap_with(total, core, 1)
    new_object, token = updated(
        0, own[0], part0, other0, like, so_far=new_object, flops=LATE[8], after=[total]
    )
    positions_all = lax.axis_size("tile") * lax.axis_size("pos") * (patterns.shape[2] // 2)
    step = probe_rate / math.sqrt(positions_all)
    (new_probe,) = run(
        job(
            lambda *refs: probe_kernel(step, modes, *refs),
            [shape_of(f32, *probe.shape)],
            [total, other_half, probe],
        ),
        limit=8,
        after=[token],
    )
    new_probe = new_probe.reshape(2, pixels, lane_tiles, modes, 128).transpose(0, 1, 3, 2, 4)
    return (new_object, new_probe.reshape(probe_modes.shape))


def solution(mesh):
    placed = (
        P("tile", None, None, None, None),
        P(),
        P("tile", "pos", None, None, None),
        P("tile", "pos", None, None),
        P("tile", "pos"),
    )
    return jax.shard_map(
        shards,
        mesh=mesh,
        in_specs=placed,
        out_specs=(P("tile", None, None, None, None), P()),
        check_vma=False,
    )
```

```python
import math

import jax
import jax.numpy as jnp
import numpy as np
from jax import lax
from jax.experimental import pallas as pl
from jax.experimental.pallas import tpu as pltpu
from jax.sharding import PartitionSpec as P

GRID_ROWS = 4


fresnel_coeff = 0.25
object_rate = 0.05
probe_rate = 0.15

LATE = [0, 0, 5_000_000_000, 5_000_000_000, 0, 0, 15_000_000_000, 0, 4_000_000_000]

f32 = jnp.float32
bf16 = jnp.bfloat16


def from_below(block):
    tiles = lax.axis_size("tile")
    across = tiles // GRID_ROWS
    return lax.ppermute(block, "tile", [(i + across, i) for i in range(tiles - across)])


def from_behind(block, rows, cols):
    tiles = lax.axis_size("tile")
    across = tiles // GRID_ROWS

    def source(i):
        return (i // across - rows) % GRID_ROWS * across + (i % across - cols) % across

    return lax.ppermute(block, "tile", [(source(i), i) for i in range(tiles)])


def real_embed(part_re, part_im):
    upper_half = np.concatenate([part_re, -part_im], axis=1)
    lower_half = np.concatenate([part_im, part_re], axis=1)
    stacked = np.concatenate([upper_half, lower_half], axis=0)
    return jnp.asarray(stacked, dtype=f32).astype(bf16)


def build_tables(pixels):
    indices = np.arange(pixels)
    angles = indices[:, None] * indices[None, :] % pixels * (2.0 * math.pi / pixels)
    norm_scale = 1.0 / math.sqrt(pixels)
    dft_re = np.cos(angles) * norm_scale
    dft_im = -np.sin(angles) * norm_scale
    frequency = np.where(indices < pixels // 2, indices, indices - pixels)
    phases = -2.0 * math.pi * fresnel_coeff / pixels * (frequency * frequency)
    phase_sum = phases[:, None] + angles
    kern_re = np.sum(np.cos(phase_sum), axis=0) / pixels
    kern_im = np.sum(np.sin(phase_sum), axis=0) / pixels
    lag_index = (indices[:, None] - indices[None, :]) % pixels
    prop_re = kern_re[lag_index]
    prop_im = kern_im[lag_index]
    return real_embed(prop_re, prop_im), real_embed(dft_re, dft_im)


def dot(a, b):
    return jnp.dot(a, b, preferred_element_type=f32)


def shift_tables(mine_ref, sent_ref):
    n = mine_ref.shape[1]
    mine = mine_ref[n:, :].astype(f32)
    sent = sent_ref[n:, :].astype(f32)
    busy = mine[2:3] > 0
    row = jnp.where(busy, mine[0:1], sent[0:1]).astype(jnp.int32)
    col = jnp.where(busy, mine[1:2], sent[1:2]).astype(jnp.int32)
    i_out = lax.broadcasted_iota(jnp.int32, (n, 2 * n), 0)
    i_in = lax.broadcasted_iota(jnp.int32, (n, 2 * n), 1)
    j_in = lax.broadcasted_iota(jnp.int32, (2 * n, n), 0)
    j_out = lax.broadcasted_iota(jnp.int32, (2 * n, n), 1)
    row2 = jnp.concatenate([row, row], axis=1)
    col2 = jnp.concatenate([col, col], axis=1)
    rows = (i_in == i_out + row2).astype(f32).astype(bf16)
    cols = (j_in == j_out + col).astype(f32).astype(bf16)
    rows_t = (j_in == j_out + row).astype(f32).astype(bf16)
    cols_t = (i_in == i_out + col2).astype(f32).astype(bf16)
    return rows, cols, rows_t, cols_t, col, busy


def halve_kernel(block_ref, *half_refs):
    for part, ref in enumerate(half_refs):
        ref[...] = block_ref[part]


def patch(shifts, own_ref, right_ref, below_ref, diag_refs, part):
    upper = jnp.concatenate([own_ref[part], right_ref[part]], axis=1)
    lower = jnp.concatenate([below_ref[part], diag_refs[part][...]], axis=1)
    rows = dot(shifts[0], jnp.concatenate([upper, lower], axis=0)).astype(bf16)
    return dot(rows, shifts[1])


def stacked(wave_re, wave_im):
    return jnp.concatenate([wave_re.astype(bf16), wave_im.astype(bf16)], axis=0)


def transform(table_ref, wave):
    n = wave.shape[1]
    table = table_ref[...]
    first = dot(table, wave)
    first = jnp.concatenate([first[:n].astype(bf16), (-first[n:]).astype(bf16)], axis=1)
    out = dot(first, table)
    return out[:, :n], out[:, n:]


def probe_plane(probe_ref, part, mode, modes):
    lane_tiles = 2
    n = probe_ref.shape[0] // (2 * lane_tiles * modes)
    step = lane_tiles * modes
    halves = [
        probe_ref[pl.ds(part * n * step + tile * modes + mode, n, stride=step), :]
        for tile in range(lane_tiles)
    ]
    return jnp.concatenate(halves, axis=1)


def message_kernel(offsets_ref, counts_ref, own_ref, patterns_ref, own_out, mine_ref, sent_ref):
    own_out[...] = own_ref[...]
    n = mine_ref.shape[1]
    at = lax.broadcasted_iota(jnp.int32, (16, n), 0)
    busy = (counts_ref[0, 0] == patterns_ref.shape[2]).astype(jnp.int32)
    for slot, ref in enumerate((mine_ref, sent_ref)):
        row, col = offsets_ref[0, 0, slot, 0], offsets_ref[0, 0, slot, 1]
        rows = jnp.where(at == 0, row, jnp.where(at == 1, col, busy))
        ref[pl.ds(0, n), :] = patterns_ref[0, 0, slot]
        ref[pl.ds(n, 16), :] = rows.astype(f32).astype(bf16)


def ready_kernel(probe_ref, prop_ref, planes_ref, table_ref):
    table_ref[...] = prop_ref[...]
    n = planes_ref.shape[1]
    modes = planes_ref.shape[2] // n
    for part in range(2):
        for mode in range(modes):
            planes_ref[part, :, pl.ds(mode * n, n)] = probe_plane(probe_ref, part, mode, modes)


def arrive_kernel(
    mine_ref, sent_ref, own_ref, right_ref, below_ref, diag_ref, planes_ref, prop_ref,
    near_ref, arrive_ref,
):
    n = own_ref.shape[1]
    shifts = shift_tables(mine_ref, sent_ref)
    tiles = (own_ref, right_ref.at[0], below_ref, [diag_ref.at[part] for part in range(2)])
    near = [patch(shifts, *tiles, part) for part in range(2)]
    for part in range(2):
        near_ref[part] = near[part].astype(bf16)
    for mode in range(planes_ref.shape[2] // n):
        lanes = pl.ds(mode * n, n)
        p_re, p_im = planes_ref[0, :, lanes], planes_ref[1, :, lanes]
        wave = stacked(p_re * near[0] - p_im * near[1], p_re * near[1] + p_im * near[0])
        a_re, a_neg = transform(prop_ref, wave)
        arrive_ref[0, :, lanes] = a_re
        arrive_ref[1, :, lanes] = -a_neg


def spread(shifts, grad, home_ref, next_ref, down_ref):
    rows_t, cols_t, col = shifts[2:5]
    n = rows_t.shape[1]
    wrap_cols = cols_t[:, :n] + cols_t[:, n:]
    for part in range(2):
        rows = dot(rows_t, grad[part].astype(bf16)).astype(bf16)
        wide = dot(rows[:n], cols_t).astype(bf16)
        home_ref[part] = wide[:, :n]
        next_ref[part] = wide[:, n:]
        down_ref[pl.ds(part * n, n), :] = dot(rows[n:], wrap_cols).astype(bf16)
    edge = lax.broadcasted_iota(jnp.int32, (16, n), 1) < col
    down_ref[pl.ds(2 * n, 16), :] = edge.astype(f32).astype(bf16)


def spread_kernel(mine_ref, sent_ref, grad_ref, home_ref, next_ref, down_ref):
    shifts = shift_tables(mine_ref, sent_ref)
    spread(shifts, [grad_ref[part] for part in range(2)], home_ref, next_ref, down_ref)


def gradient_kernel(
    mine_ref, sent_ref, own_ref, right_ref, below_ref, diag_re_ref, diag_im_ref, near_ref,
    arrive_ref, planes_ref, prop_ref, dft_ref,
    home_ref, next_ref, down_ref, grad_ref, keep_ref, give_ref, term_ref,
):
    n = own_ref.shape[1]
    modes = planes_ref.shape[2] // n
    shifts = shift_tables(mine_ref, sent_ref)
    busy = shifts[5]
    tiles = (own_ref, right_ref.at[1], below_ref, (diag_re_ref, diag_im_ref))
    far = [patch(shifts, *tiles, part) for part in range(2)]
    fields = []
    for mode in range(modes):
        lanes = pl.ds(mode * n, n)
        a_re, a_im = arrive_ref[0, :, lanes], arrive_ref[1, :, lanes]
        wave = stacked(far[0] * a_re - far[1] * a_im, far[0] * a_im + far[1] * a_re)
        fields.append(transform(dft_ref, wave))
    intensity = sum(f_re * f_re + f_neg * f_neg for f_re, f_neg in fields)
    pattern = jnp.where(busy, mine_ref[:n, :].astype(f32), sent_ref[:n, :].astype(f32))
    residual = intensity - pattern
    waves = []
    grad = [0.0, 0.0]
    for mode in range(modes):
        lanes = pl.ds(mode * n, n)
        f_re, f_neg = fields[mode]
        a_re, a_im = arrive_ref[0, :, lanes], arrive_ref[1, :, lanes]
        b_re, b_im = transform(dft_ref, stacked(f_re * residual, f_neg * residual))
        grad[0] += a_re * b_re + a_im * b_im
        grad[1] += a_re * b_im - a_im * b_re
        waves.append(stacked(far[0] * b_re + far[1] * b_im, far[1] * b_re - far[0] * b_im))
    spread(shifts, grad, home_ref, next_ref, down_ref)
    grad = [0.0, 0.0]
    near = [near_ref[part].astype(f32) for part in range(2)]
    for mode in range(modes):
        lanes = pl.ds(mode * n, n)
        b_re, b_im = transform(prop_ref, waves[mode])
        p_re, p_im = planes_ref[0, :, lanes], planes_ref[1, :, lanes]
        grad[0] += p_re * b_re + p_im * b_im
        grad[1] += p_re * b_im - p_im * b_re
        term_ref[0, :, lanes] = (near[0] * b_re + near[1] * b_im).astype(bf16)
        term_ref[1, :, lanes] = (near[0] * b_im - near[1] * b_re).astype(bf16)
    core = place_of(core_group())
    keep_ref[...] = term_ref[core]
    give_ref[...] = term_ref[1 - core]
    for part in range(2):
        grad_ref[part] = grad[part].astype(bf16)


def above_parts(above_ref, n):
    parts = [above_ref[pl.ds(part * n, n), :].astype(f32) for part in range(2)]
    return parts, above_ref[pl.ds(2 * n, 16), :].astype(f32)[0:1] > 0


def beside_kernel(next_ref, above_ref, *out_refs):
    above, split = above_parts(above_ref, next_ref.shape[1])
    for part, ref in enumerate(out_refs):
        total = next_ref[part].astype(f32) + jnp.where(split, above[part], 0.0)
        ref[...] = total.astype(bf16)


def part_kernel(home_ref, above_ref, left_re_ref, left_im_ref, out_ref):
    above, split = above_parts(above_ref, out_ref.shape[1])
    for part, left_ref in enumerate((left_re_ref, left_im_ref)):
        total = home_ref[part].astype(f32) + jnp.where(split, 0.0, above[part])
        out_ref[part] = (total + left_ref[...].astype(f32)).astype(bf16)


def update_kernel(layer, own_ref, part_ref, other_ref, *refs):
    out_hbm, token_ref, new_ref, sem = refs[-4:]
    token_ref[...] = jnp.zeros_like(token_ref)
    grad = part_ref[...].astype(f32) + other_ref[...].astype(f32)
    new_ref[...] = (own_ref[...].astype(f32) - object_rate * grad).astype(bf16)
    copy = pltpu.make_async_copy(new_ref, out_hbm.at[0, layer], sem.at[0])
    copy.start()
    copy.wait()


def core_group():
    return [lax.axis_size("pos")]


def place_of(group):
    flat = lax.axis_index("tile") * lax.axis_size("pos") + lax.axis_index("pos")
    return sum(flat // mask % 2 * (1 << at) for at, mask in enumerate(group))


def job(kernel, outs, arrays, scalars=(), scratch=()):
    return kernel, list(outs), list(scalars), list(arrays), list(scratch)


def run(*jobs, flops=1_000_000, limit=4, after=()):
    vmem = pl.BlockSpec(memory_space=pltpu.VMEM)
    smem = pl.BlockSpec(memory_space=pltpu.SMEM)
    anywhere = pl.BlockSpec(memory_space=pl.ANY)
    kernels, outs, scalars, arrays, scratch = zip(*jobs)
    ins = [x + y for x, y in zip(scalars, arrays)]
    specs = [[smem] * len(x) + [vmem] * len(y) for x, y in zip(scalars, arrays)]

    def taken(refs, lists):
        parts = []
        for items in lists:
            parts.append(refs[: len(items)])
            refs = refs[len(items) :]
        return parts, refs

    def body(*refs):
        in_refs, refs = taken(refs, ins)
        out_refs, refs = taken(refs[len(after) :], outs)
        scratch_refs, _ = taken(refs, scratch)
        for kernel, *parts in zip(kernels, in_refs, out_refs, scratch_refs):
            kernel(*parts[0], *parts[1], *parts[2])

    moved = sum(x.size * x.dtype.itemsize for x in sum(ins, []) + sum(outs, []))
    results = pl.pallas_call(
        body,
        out_shape=sum(outs, []),
        in_specs=sum(specs, []) + [anywhere] * len(after),
        out_specs=[vmem] * len(sum(outs, [])),
        scratch_shapes=sum(scratch, []),
        compiler_params=pltpu.CompilerParams(vmem_limit_bytes=limit * 2**20),
        cost_estimate=pl.CostEstimate(flops=flops, bytes_accessed=moved, transcendentals=0),
    )(*sum(ins, []), *after)
    results, _ = taken(results, outs)
    return results[0] if len(jobs) == 1 else results


def updated(layer, own, part, other, like, so_far=None, flops=0, after=()):
    vmem = pl.BlockSpec(memory_space=pltpu.VMEM)
    anywhere = pl.BlockSpec(memory_space=pl.ANY)
    extra = [x for x in (so_far,) if x is not None] + list(after)
    return pl.pallas_call(
        lambda *refs: update_kernel(layer, *refs),
        out_shape=[like, shape_of(f32, 8, 128)],
        in_specs=[vmem] * 3 + [anywhere] * len(extra),
        out_specs=[anywhere, vmem],
        scratch_shapes=[pltpu.VMEM(own.shape, bf16), pltpu.SemaphoreType.DMA((1,))],
        input_output_aliases={} if so_far is None else {3: 0},
        compiler_params=pltpu.CompilerParams(vmem_limit_bytes=4 * 2**20),
        cost_estimate=pl.CostEstimate(
            flops=own.size + flops, bytes_accessed=8 * own.size, transcendentals=0
        ),
    )(own, part, other, *extra)


def shape_of(kind, *dims):
    return jax.ShapeDtypeStruct(dims, kind)


def gathered_message(patterns, offsets, counts):
    pixels = patterns.shape[4]
    all_counts = lax.all_gather(counts[0, 0], "pos")
    ends = jnp.cumsum(all_counts)
    rank = lax.axis_index("pos")
    source = jnp.sum((ends <= rank).astype(jnp.int32))
    slot = rank - (ends[source] - all_counts[source])
    spot = lax.all_gather(offsets[0, 0], "pos")[source, slot]
    pattern = lax.all_gather(patterns[0, 0], "pos")[source, slot]
    at = lax.broadcasted_iota(jnp.int32, (16, pixels), 0)
    rows = jnp.where(at == 0, spot[0], jnp.where(at == 1, spot[1], 0))
    return jnp.concatenate([pattern, rows.astype(bf16)], axis=0)


def fold_kernel(group, keep_ref, *refs):
    blocks = refs[-1]
    got = len(refs) - 1 - blocks.shape[0]
    arrived, keep_out, give_outs = refs[:got], refs[got], refs[got + 1 : -1]
    total = keep_ref[...].astype(f32)
    for ref in arrived:
        total += ref[...].astype(f32)
    size = blocks.shape[1]
    for block in range(blocks.shape[0]):
        blocks[block] = total[block * size : (block + 1) * size]
    here = place_of(group)
    keep_out[...] = blocks[here]
    for distance, ref in enumerate(give_outs, 1):
        ref[...] = blocks[here ^ distance].astype(bf16)


def add_kernel(keep_ref, *refs):
    total = keep_ref[...].astype(f32)
    for ref in refs[:-1]:
        total += ref[...].astype(f32)
    refs[-1][...] = total.astype(bf16)


def place_kernel(group, *refs):
    arrived, out_ref, blocks = refs[:-2], refs[-2], refs[-1]
    here = place_of(group)
    for distance, ref in enumerate(arrived):
        blocks[here ^ distance] = ref[...]
    size = blocks.shape[1]
    for block in range(blocks.shape[0]):
        out_ref[pl.ds(block * size, size), :] = blocks[block]


def probe_kernel(step, modes, mine_ref, other_ref, probe_ref, out_ref):
    core = place_of(core_group())
    lane_tiles = 2
    n = mine_ref.shape[0]
    stride = lane_tiles * modes
    for part in range(2):
        total = jnp.where(core == part, mine_ref[...].astype(f32), other_ref[...].astype(f32))
        for mode in range(modes):
            for tile in range(lane_tiles):
                lane = (mode * lane_tiles + tile) * 128
                where = pl.ds(part * n * stride + tile * modes + mode, n, stride=stride)
                out_ref[where, :] = probe_ref[where, :] - step * total[:, lane : lane + 128]


def exchange_groups():
    tiles, owners = lax.axis_size("tile"), lax.axis_size("pos")
    bits = [1 << bit for bit in range(owners.bit_length() - 1)]
    bits += [owners << bit for bit in range(1, tiles.bit_length() - 1)]
    return [bits[at : at + 2] for at in range(0, len(bits), 2)]


def swap_with(x, group, distance):
    mask = sum(bit for at, bit in enumerate(group) if distance >> at & 1)
    devices = lax.axis_size("tile") * lax.axis_size("pos")
    return lax.ppermute(x, ("tile", "pos"), [(i, i ^ mask) for i in range(devices)])


def joined(group, x, arrived):
    blocks = 1 << len(group)
    return job(
        lambda *refs: place_kernel(group, *refs),
        [shape_of(bf16, x.shape[0] * blocks, x.shape[1])],
        [x] + arrived,
        scratch=[pltpu.VMEM((blocks,) + x.shape, bf16)],
    )


def added(x, arrived):
    return job(add_kernel, [shape_of(bf16, *x.shape)], [x] + arrived)


def swapped(x, group):
    return [swap_with(x, group, at) for at in range(1, 1 << len(group))]


def folded(group, keep, arrived):
    blocks = 1 << len(group)
    size, width = keep.shape[0] // blocks, keep.shape[1]
    return job(
        lambda *refs: fold_kernel(group, *refs),
        [shape_of(f32, size, width)] + [shape_of(bf16, size, width)] * (blocks - 1),
        [keep] + arrived,
        scratch=[pltpu.VMEM((blocks, size, width), f32)],
    )


def shards(tile_object, probe_modes, patterns, offsets, counts):
    _, pixels, modes, _ = probe_modes.shape
    width = modes * pixels
    lane_tiles = pixels // 128
    prop, dft = build_tables(pixels)
    tile = shape_of(bf16, 2, pixels, pixels)
    plane = shape_of(bf16, pixels, pixels)
    planes = shape_of(f32, 2, pixels, width)
    probe = probe_modes.reshape(2, pixels, modes, lane_tiles, 128)
    probe = probe.transpose(0, 1, 3, 2, 4).reshape(-1, 128)

    own = [tile_object[0, 0], tile_object[0, 1]]
    below0 = from_below(own[0])
    right = from_behind(tile_object[0], 0, -1)
    exchanged = lax.axis_size("pos") == patterns.shape[2]
    message = shape_of(bf16, pixels + 16, pixels)
    own1, mine, sent = run(
        job(
            message_kernel,
            [tile, message, message],
            [own[1], patterns],
            scalars=[offsets, counts if exchanged else jnp.zeros_like(counts)],
        ),
        limit=4,
        after=[own[0]],
    )
    probe_planes, table = run(
        job(ready_kernel, [planes, shape_of(bf16, *prop.shape)], [probe, prop]),
        limit=8,
        after=[own1],
    )
    below1 = from_below(own1)
    if exchanged:
        sent = lax.ppermute(sent, "pos", [(i, 1 - i) for i in range(2)])
    else:
        sent = gathered_message(patterns, offsets, counts)
    diag0 = from_behind(below0, 0, -1)
    halves = run(job(halve_kernel, [plane, plane], [below1]))
    diag1 = [from_behind(half, 0, -1) for half in halves]
    near, arrive = run(
        job(
            arrive_kernel,
            [tile, planes],
            [mine, sent, own[0], right, below0, diag0, probe_planes, table],
        ),
        flops=1_500_000_000,
        limit=16,
    )
    half = shape_of(bf16, pixels, width)
    down = shape_of(bf16, 2 * pixels + 16, pixels)
    home1, next1, down1, grad0, keep, give = run(
        job(
            gradient_kernel,
            [tile, tile, down, tile, half, half],
            [mine, sent, own1, right, below1, *diag1, near, arrive, probe_planes, table, dft],
            scratch=[pltpu.VMEM((2, pixels, width), bf16)],
        ),
        flops=4_000_000_000,
        limit=16,
    )

    def over_owners(part):
        if lax.axis_size("pos") == 2:
            return lax.ppermute(part, "pos", [(0, 1), (1, 0)])
        return lax.psum(part.astype(f32), "pos") - part.astype(f32)

    def beside(next_tile, above):
        return job(beside_kernel, [plane, plane], [next_tile, above])

    def part(home, above, left):
        return job(part_kernel, [tile], [home, above, *left])

    core, groups = core_group(), exchange_groups()
    above1 = from_behind(down1, 1, 0)
    arrived = [swap_with(give, core, 1)]
    side = [job(spread_kernel, [tile, tile, down], [mine, sent, grad0])]
    scattered = []
    while len(groups) > 1 and keep.shape[0] >> len(groups[0]) >= 16:
        group, groups = groups[0], groups[1:]
        done = run(folded(group, keep, arrived), *side, limit=8)
        if side:
            done, (home0, next0, down0) = done
            above0 = from_behind(down0, 1, 0)
            side = []
        keep, *gives = done
        arrived = [swap_with(x, group, at) for at, x in enumerate(gives, 1)]
        scattered.append(group)
    first, second, *others = [[bit] for group in groups for bit in group]
    (total,) = run(added(keep, arrived))
    arrived = swapped(total, first)
    beside1 = run(beside(next1, above1), after=[total], flops=LATE[0])
    left1 = [from_behind(half, 0, 1) for half in beside1]
    (part1,) = run(part(home1, above1, left1), flops=LATE[1])
    other1 = over_owners(part1)
    beside0 = run(beside(next0, above0), after=[part1], flops=LATE[2])
    left0 = [from_behind(half, 0, 1) for half in beside0]
    (total,) = run(added(total, arrived), after=beside0[:1], flops=LATE[3])
    arrived = swapped(total, second)
    (total,) = run(added(total, arrived), flops=LATE[4])
    for group in others:
        (total,) = run(added(total, swapped(total, group)))
    arrived = swapped(total, scattered[-1])
    (part0,) = run(part(home0, above0, left0), after=[total], flops=LATE[5])
    other0 = over_owners(part0)
    like = shape_of(bf16, *tile_object.shape)
    new_object, token = updated(1, own1, part1, other1, like, flops=LATE[6], after=[part0])
    (total,) = run(joined(scattered[-1], total, arrived), after=[token], flops=LATE[7])
    for group in reversed(scattered[:-1]):
        (total,) = run(joined(group, total, swapped(total, group)))
    other_half = swap_with(total, core, 1)
    new_object, token = updated(
        0, own[0], part0, other0, like, so_far=new_object, flops=LATE[8], after=[total]
    )
    positions_all = lax.axis_size("tile") * lax.axis_size("pos") * (patterns.shape[2] // 2)
    step = probe_rate / math.sqrt(positions_all)
    (new_probe,) = run(
        job(
            lambda *refs: probe_kernel(step, modes, *refs),
            [shape_of(f32, *probe.shape)],
            [total, other_half, probe],
        ),
        limit=8,
        after=[token],
    )
    new_probe = new_probe.reshape(2, pixels, lane_tiles, modes, 128).transpose(0, 1, 3, 2, 4)
    return (new_object, new_probe.reshape(probe_modes.shape))


def solution(mesh):
    placed = (
        P("tile", None, None, None, None),
        P(),
        P("tile", "pos", None, None, None),
        P("tile", "pos", None, None),
        P("tile", "pos"),
    )
    return jax.shard_map(
        shards,
        mesh=mesh,
        in_specs=placed,
        out_specs=(P("tile", None, None, None, None), P()),
        check_vma=False,
    )
```

```python
import math

import jax
import jax.numpy as jnp
import numpy as np
from jax import lax
from jax.experimental import pallas as pl
from jax.experimental.pallas import tpu as pltpu
from jax.sharding import PartitionSpec as P

GRID_ROWS = 4


fresnel_coeff = 0.25
object_rate = 0.05
probe_rate = 0.15

LATE = [work * 1_000_000_000 for work in (0, 8, 0, 0, 8, 0, 8, 4)]

f32 = jnp.float32
bf16 = jnp.bfloat16


def from_behind(block, rows, cols):
    tiles = lax.axis_size("tile")
    across = tiles // GRID_ROWS

    def source(i):
        return (i // across - rows) % GRID_ROWS * across + (i % across - cols) % across

    return lax.ppermute(block, "tile", [(source(i), i) for i in range(tiles)])


def real_embed(part_re, part_im):
    upper_half = np.concatenate([part_re, -part_im], axis=1)
    lower_half = np.concatenate([part_im, part_re], axis=1)
    stacked = np.concatenate([upper_half, lower_half], axis=0)
    return jnp.asarray(stacked, dtype=f32).astype(bf16)


def build_tables(pixels):
    indices = np.arange(pixels)
    angles = indices[:, None] * indices[None, :] % pixels * (2.0 * math.pi / pixels)
    norm_scale = 1.0 / math.sqrt(pixels)
    dft_re = np.cos(angles) * norm_scale
    dft_im = -np.sin(angles) * norm_scale
    frequency = np.where(indices < pixels // 2, indices, indices - pixels)
    phases = -2.0 * math.pi * fresnel_coeff / pixels * (frequency * frequency)
    phase_sum = phases[:, None] + angles
    kern_re = np.sum(np.cos(phase_sum), axis=0) / pixels
    kern_im = np.sum(np.sin(phase_sum), axis=0) / pixels
    lag_index = (indices[:, None] - indices[None, :]) % pixels
    prop_re = kern_re[lag_index]
    prop_im = kern_im[lag_index]
    return real_embed(prop_re, prop_im), real_embed(dft_re, dft_im)


def dot(a, b):
    return jnp.dot(a, b, preferred_element_type=f32)


def spots(mine_ref, sent_ref):
    n = mine_ref.shape[1]
    mine = mine_ref[n:, :].astype(f32)
    busy = mine[2:3] > 0
    rows = jnp.where(busy, mine, sent_ref[n:, :].astype(f32)).astype(jnp.int32)
    return (rows[0:1], rows[1:2]), (rows[3:4], rows[4:5]), busy


def shift_in(spot):
    row, col = spot
    n = row.shape[1]
    i_out = lax.broadcasted_iota(jnp.int32, (n, 2 * n), 0)
    i_in = lax.broadcasted_iota(jnp.int32, (n, 2 * n), 1)
    j_in = lax.broadcasted_iota(jnp.int32, (2 * n, n), 0)
    j_out = lax.broadcasted_iota(jnp.int32, (2 * n, n), 1)
    rows = i_in == i_out + jnp.concatenate([row, row], axis=1)
    cols = j_in == j_out + col
    return rows.astype(f32).astype(bf16), cols.astype(f32).astype(bf16)


def shift_out(spot):
    row, col = spot
    n = row.shape[1]
    i_out = lax.broadcasted_iota(jnp.int32, (n, 2 * n), 0)
    i_in = lax.broadcasted_iota(jnp.int32, (n, 2 * n), 1)
    j_in = lax.broadcasted_iota(jnp.int32, (2 * n, n), 0)
    j_out = lax.broadcasted_iota(jnp.int32, (2 * n, n), 1)
    rows = j_in == j_out + row
    cols = i_in == i_out + jnp.concatenate([col, col], axis=1)
    return rows.astype(f32).astype(bf16), cols.astype(f32).astype(bf16)


def patch(shifts, own_ref, right_ref, below_ref, diag_ref, part):
    upper = jnp.concatenate([own_ref[part], right_ref[part]], axis=1)
    lower = jnp.concatenate([below_ref[part], diag_ref[part]], axis=1)
    rows = dot(shifts[0], jnp.concatenate([upper, lower], axis=0)).astype(bf16)
    return dot(rows, shifts[1])


def stacked(wave_re, wave_im):
    return jnp.concatenate([wave_re.astype(bf16), wave_im.astype(bf16)], axis=0)


def transform(table_ref, wave):
    n = wave.shape[1]
    table = table_ref[...]
    first = dot(table, wave)
    first = jnp.concatenate([first[:n].astype(bf16), (-first[n:]).astype(bf16)], axis=1)
    out = dot(first, table)
    return out[:, :n], out[:, n:]


def probe_plane(probe_ref, part, mode, modes):
    lane_tiles = 2
    n = probe_ref.shape[0] // (2 * lane_tiles * modes)
    step = lane_tiles * modes
    halves = [
        probe_ref[pl.ds(part * n * step + tile * modes + mode, n, stride=step), :]
        for tile in range(lane_tiles)
    ]
    return jnp.concatenate(halves, axis=1)


def message_kernel(offsets_ref, counts_ref, own_ref, patterns_ref, own_out, mine_ref, sent_ref):
    own_out[...] = own_ref[...]
    n = mine_ref.shape[1]
    at = lax.broadcasted_iota(jnp.int32, (16, n), 0)
    busy = (counts_ref[0, 0] == patterns_ref.shape[2]).astype(jnp.int32)
    for slot, ref in enumerate((mine_ref, sent_ref)):
        row, col = offsets_ref[0, 0, slot, 0], offsets_ref[0, 0, slot, 1]
        row2, col2 = offsets_ref[0, 0, 1 - slot, 0], offsets_ref[0, 0, 1 - slot, 1]
        rows = jnp.where(at == 0, row, jnp.where(at == 1, col, busy))
        rows = jnp.where(at == 3, row2, jnp.where(at == 4, col2, rows))
        ref[pl.ds(0, n), :] = patterns_ref[0, 0, slot]
        ref[pl.ds(n, 16), :] = rows.astype(f32).astype(bf16)


def ready_kernel(probe_ref, prop_ref, planes_ref, table_ref):
    table_ref[...] = prop_ref[...]
    n = planes_ref.shape[1]
    modes = planes_ref.shape[2] // n
    for part in range(2):
        for mode in range(modes):
            planes_ref[part, :, pl.ds(mode * n, n)] = probe_plane(probe_ref, part, mode, modes)


def arrive_kernel(
    mine_ref, sent_ref, own_ref, right_ref, below_ref, diag_ref, planes_ref, prop_ref,
    near_ref, arrive_ref,
):
    n = own_ref.shape[1]
    shifts = shift_in(spots(mine_ref, sent_ref)[0])
    tiles = (own_ref, right_ref.at[0], below_ref, diag_ref)
    near = [patch(shifts, *tiles, part) for part in range(2)]
    for part in range(2):
        near_ref[part] = near[part].astype(bf16)
    for mode in range(planes_ref.shape[2] // n):
        lanes = pl.ds(mode * n, n)
        p_re, p_im = planes_ref[0, :, lanes], planes_ref[1, :, lanes]
        wave = stacked(p_re * near[0] - p_im * near[1], p_re * near[1] + p_im * near[0])
        a_re, a_neg = transform(prop_ref, wave)
        arrive_ref[0, :, lanes] = a_re
        arrive_ref[1, :, lanes] = -a_neg


def gradient_kernel(
    mine_ref, sent_ref, own_ref, right_ref, below_ref, diag_ref, near_ref, arrive_ref, planes_ref,
    prop_ref, dft_ref,
    kept_ref, given_ref, keep_ref, give_ref, grad_ref, term_ref, *, layer
):
    n = own_ref.shape[1]
    modes = planes_ref.shape[2] // n
    spot, _, busy = spots(mine_ref, sent_ref)
    shifts = shift_in(spot)
    tiles = (own_ref, right_ref.at[1], below_ref, diag_ref)
    far = [patch(shifts, *tiles, part) for part in range(2)]
    fields = []
    for mode in range(modes):
        lanes = pl.ds(mode * n, n)
        a_re, a_im = arrive_ref[0, :, lanes], arrive_ref[1, :, lanes]
        wave = stacked(far[0] * a_re - far[1] * a_im, far[0] * a_im + far[1] * a_re)
        fields.append(transform(dft_ref, wave))
    intensity = sum(f_re * f_re + f_neg * f_neg for f_re, f_neg in fields)
    pattern = jnp.where(busy, mine_ref[:n, :].astype(f32), sent_ref[:n, :].astype(f32))
    residual = intensity - pattern
    waves = []
    grad = [0.0, 0.0]
    for mode in range(modes):
        lanes = pl.ds(mode * n, n)
        f_re, f_neg = fields[mode]
        a_re, a_im = arrive_ref[0, :, lanes], arrive_ref[1, :, lanes]
        b_re, b_im = transform(dft_ref, stacked(f_re * residual, f_neg * residual))
        grad[0] += a_re * b_re + a_im * b_im
        grad[1] += a_re * b_im - a_im * b_re
        waves.append(stacked(far[0] * b_re + far[1] * b_im, far[1] * b_re - far[0] * b_im))
    for part in range(2):
        grad_ref[1, part] = grad[part].astype(bf16)
    grad = [0.0, 0.0]
    near = [near_ref[part].astype(f32) for part in range(2)]
    for mode in range(modes):
        lanes = pl.ds(mode * n, n)
        b_re, b_im = transform(prop_ref, waves[mode])
        p_re, p_im = planes_ref[0, :, lanes], planes_ref[1, :, lanes]
        grad[0] += p_re * b_re + p_im * b_im
        grad[1] += p_re * b_im - p_im * b_re
        term_ref[0, :, lanes] = (near[0] * b_re + near[1] * b_im).astype(bf16)
        term_ref[1, :, lanes] = (near[0] * b_im - near[1] * b_re).astype(bf16)
    core = place_of(core_group())
    keep_ref[...] = term_ref[core]
    give_ref[...] = term_ref[1 - core]
    for part in range(2):
        grad_ref[0, part] = grad[part].astype(bf16)
    layer = layer()
    kept_ref[...] = grad_ref[layer]
    given_ref[...] = grad_ref[1 - layer]


def spread_kernel(
    mine_ref, sent_ref, kept_ref, got_ref, home_ref, below_ref, right_ref, diag_ref
):
    n = mine_ref.shape[1]
    first, second, _ = spots(mine_ref, sent_ref)
    rows1, cols1 = shift_out(first)
    rows2, cols2 = shift_out(second)
    cols = jnp.concatenate([cols1, cols2], axis=0)
    for part in range(2):
        tall1 = dot(rows1, kept_ref[part]).astype(bf16)
        tall2 = dot(rows2, got_ref[part]).astype(bf16)
        wide = dot(jnp.concatenate([tall1, tall2], axis=1), cols)
        home_ref[part] = wide[:n, :n]
        right_ref[part] = wide[:n, n:].astype(bf16)
        below_ref[part] = wide[n:, :n]
        diag_ref[part] = wide[n:, n:].astype(bf16)


def beside_kernel(home_ref, below_ref, right_ref, diag_ref, home_out, down_ref):
    home_out[...] = home_ref[...] + right_ref[...].astype(f32)
    down_ref[...] = (below_ref[...] + diag_ref[...].astype(f32)).astype(bf16)


def slice_kernel(layer, own0_ref, own1_ref, home_ref, above_ref, out_ref):
    grad = home_ref[...] + above_ref[...].astype(f32)
    own = jnp.where(layer() == 0, own0_ref[...].astype(f32), own1_ref[...].astype(f32))
    out_ref[...] = (own - object_rate * grad).astype(bf16)


def token_kernel(token_ref):
    token_ref[...] = jnp.zeros_like(token_ref)


def core_group():
    return [lax.axis_size("pos")]


def place_of(group):
    flat = lax.axis_index("tile") * lax.axis_size("pos") + lax.axis_index("pos")
    return sum(flat // mask % 2 * (1 << at) for at, mask in enumerate(group))


def job(kernel, outs, arrays, scalars=(), scratch=()):
    return kernel, list(outs), list(scalars), list(arrays), list(scratch)


def run(*jobs, flops=1_000_000, limit=4, after=()):
    vmem = pl.BlockSpec(memory_space=pltpu.VMEM)
    smem = pl.BlockSpec(memory_space=pltpu.SMEM)
    anywhere = pl.BlockSpec(memory_space=pl.ANY)
    kernels, outs, scalars, arrays, scratch = zip(*jobs)
    ins = [x + y for x, y in zip(scalars, arrays)]
    specs = [[smem] * len(x) + [vmem] * len(y) for x, y in zip(scalars, arrays)]

    def taken(refs, lists):
        parts = []
        for items in lists:
            parts.append(refs[: len(items)])
            refs = refs[len(items) :]
        return parts, refs

    def body(*refs):
        in_refs, refs = taken(refs, ins)
        out_refs, refs = taken(refs[len(after) :], outs)
        scratch_refs, _ = taken(refs, scratch)
        for kernel, *parts in zip(kernels, in_refs, out_refs, scratch_refs):
            kernel(*parts[0], *parts[1], *parts[2])

    moved = sum(x.size * x.dtype.itemsize for x in sum(ins, []) + sum(outs, []))
    results = pl.pallas_call(
        body,
        out_shape=sum(outs, []),
        in_specs=sum(specs, []) + [anywhere] * len(after),
        out_specs=[vmem] * len(sum(outs, [])),
        scratch_shapes=sum(scratch, []),
        compiler_params=pltpu.CompilerParams(vmem_limit_bytes=limit * 2**20),
        cost_estimate=pl.CostEstimate(flops=flops, bytes_accessed=moved, transcendentals=0),
    )(*sum(ins, []), *after)
    results, _ = taken(results, outs)
    return results[0] if len(jobs) == 1 else results


def finished(layer, step, modes, halves, probe, slices, like, after):
    vmem = pl.BlockSpec(memory_space=pltpu.VMEM)
    anywhere = pl.BlockSpec(memory_space=pl.ANY)
    inputs = [*halves, probe, *slices]

    def body(*refs):
        blocks, (out_probe, out_tile, sems) = refs[3 : len(inputs)], refs[-3:]
        places = [layer(), 1 - layer()][: len(blocks)]
        copies = [
            pltpu.make_async_copy(block, out_tile.at[0, place], sems.at[at])
            for at, (block, place) in enumerate(zip(blocks, places))
        ]
        for copy in copies:
            copy.start()
        probe_kernel(step, modes, *refs[:3], out_probe)
        for copy in copies:
            copy.wait()

    return pl.pallas_call(
        body,
        out_shape=[shape_of(f32, *probe.shape), like],
        in_specs=[vmem] * len(inputs) + [anywhere] * len(after),
        out_specs=[vmem, anywhere],
        scratch_shapes=[pltpu.SemaphoreType.DMA((2,))],
        compiler_params=pltpu.CompilerParams(vmem_limit_bytes=8 * 2**20),
        cost_estimate=pl.CostEstimate(
            flops=4 * probe.size, bytes_accessed=12 * probe.size, transcendentals=0
        ),
    )(*inputs, *after)


def shape_of(kind, *dims):
    return jax.ShapeDtypeStruct(dims, kind)


def gathered_message(patterns, offsets, counts):
    pixels = patterns.shape[4]
    all_counts = lax.all_gather(counts[0, 0], "pos")
    ends = jnp.cumsum(all_counts)
    rank = lax.axis_index("pos")
    source = jnp.sum((ends <= rank).astype(jnp.int32))
    slot = rank - (ends[source] - all_counts[source])
    spot = lax.all_gather(offsets[0, 0], "pos")[source, slot]
    pattern = lax.all_gather(patterns[0, 0], "pos")[source, slot]
    at = lax.broadcasted_iota(jnp.int32, (16, pixels), 0)
    rows = jnp.where(at == 0, spot[0], jnp.where(at == 1, spot[1], 0))
    return jnp.concatenate([pattern, rows.astype(bf16)], axis=0)


def fold_kernel(group, keep_ref, *refs):
    blocks = refs[-1]
    got = len(refs) - 1 - blocks.shape[0]
    arrived, keep_out, give_outs = refs[:got], refs[got], refs[got + 1 : -1]
    total = keep_ref[...].astype(f32)
    for ref in arrived:
        total += ref[...].astype(f32)
    size = blocks.shape[1]
    for block in range(blocks.shape[0]):
        blocks[block] = total[block * size : (block + 1) * size]
    here = place_of(group)
    keep_out[...] = blocks[here]
    for distance, ref in enumerate(give_outs, 1):
        ref[...] = blocks[here ^ distance].astype(bf16)


def add_kernel(keep_ref, *refs):
    total = keep_ref[...].astype(f32)
    for ref in refs[:-1]:
        total += ref[...].astype(f32)
    refs[-1][...] = total.astype(bf16)


def place_kernel(group, *refs):
    arrived, out_ref, blocks = refs[:-2], refs[-2], refs[-1]
    here = place_of(group)
    for distance, ref in enumerate(arrived):
        blocks[here ^ distance] = ref[...]
    size = blocks.shape[1]
    for block in range(blocks.shape[0]):
        out_ref[pl.ds(block * size, size), :] = blocks[block]


def probe_kernel(step, modes, mine_ref, other_ref, probe_ref, out_ref):
    core = place_of(core_group())
    lane_tiles = 2
    n = mine_ref.shape[0]
    stride = lane_tiles * modes
    for part in range(2):
        total = jnp.where(core == part, mine_ref[...].astype(f32), other_ref[...].astype(f32))
        for mode in range(modes):
            for tile in range(lane_tiles):
                lane = (mode * lane_tiles + tile) * 128
                where = pl.ds(part * n * stride + tile * modes + mode, n, stride=stride)
                out_ref[where, :] = probe_ref[where, :] - step * total[:, lane : lane + 128]


def exchange_groups():
    tiles, owners = lax.axis_size("tile"), lax.axis_size("pos")
    bits = [1 << bit for bit in range(owners.bit_length() - 1)]
    bits += [owners << bit for bit in range(1, tiles.bit_length() - 1)]
    return [bits[at : at + 2] for at in range(0, len(bits), 2)]


def swap_with(x, group, distance):
    mask = sum(bit for at, bit in enumerate(group) if distance >> at & 1)
    devices = lax.axis_size("tile") * lax.axis_size("pos")
    return lax.ppermute(x, ("tile", "pos"), [(i, i ^ mask) for i in range(devices)])


def joined(group, x, arrived):
    blocks = 1 << len(group)
    return job(
        lambda *refs: place_kernel(group, *refs),
        [shape_of(bf16, x.shape[0] * blocks, x.shape[1])],
        [x] + arrived,
        scratch=[pltpu.VMEM((blocks,) + x.shape, bf16)],
    )


def added(x, arrived):
    return job(add_kernel, [shape_of(bf16, *x.shape)], [x] + arrived)


def swapped(x, group):
    return [swap_with(x, group, at) for at in range(1, 1 << len(group))]


def folded(group, keep, arrived):
    blocks = 1 << len(group)
    size, width = keep.shape[0] // blocks, keep.shape[1]
    return job(
        lambda *refs: fold_kernel(group, *refs),
        [shape_of(f32, size, width)] + [shape_of(bf16, size, width)] * (blocks - 1),
        [keep] + arrived,
        scratch=[pltpu.VMEM((blocks, size, width), f32)],
    )


def shards(tile_object, probe_modes, patterns, offsets, counts):
    _, pixels, modes, _ = probe_modes.shape
    width = modes * pixels
    lane_tiles = pixels // 128
    prop, dft = build_tables(pixels)
    tile = shape_of(bf16, 2, pixels, pixels)
    planes = shape_of(f32, 2, pixels, width)
    probe = probe_modes.reshape(2, pixels, modes, lane_tiles, 128)
    probe = probe.transpose(0, 1, 3, 2, 4).reshape(-1, 128)

    own = [tile_object[0, 0], tile_object[0, 1]]
    below0 = from_behind(own[0], -1, 0)
    right = from_behind(tile_object[0], 0, -1)
    exchanged = lax.axis_size("pos") == patterns.shape[2]
    message = shape_of(bf16, pixels + 16, pixels)
    own1, mine, sent = run(
        job(
            message_kernel,
            [tile, message, message],
            [own[1], patterns],
            scalars=[offsets, counts if exchanged else jnp.zeros_like(counts)],
        ),
        limit=4,
        after=[own[0]],
    )
    probe_planes, table = run(
        job(ready_kernel, [planes, shape_of(bf16, *prop.shape)], [probe, prop]),
        limit=8,
        after=[own1],
    )
    below1 = from_behind(own1, -1, 0)
    if exchanged:
        sent = lax.ppermute(sent, "pos", [(i, 1 - i) for i in range(2)])
    else:
        sent = gathered_message(patterns, offsets, counts)
    diag0 = from_behind(below0, 0, -1)
    diag1 = from_behind(below1, 0, -1)
    near, arrive = run(
        job(
            arrive_kernel,
            [tile, planes],
            [mine, sent, own[0], right, below0, diag0, probe_planes, table],
        ),
        flops=1_500_000_000,
        limit=16,
    )
    half = shape_of(bf16, pixels, width)
    grads = pltpu.VMEM((2, 2, pixels, pixels), bf16)
    this_layer = (lambda: lax.axis_index("pos")) if exchanged else (lambda: 0)
    kept, given, keep, give = run(
        job(
            lambda *refs: gradient_kernel(*refs, layer=this_layer),
            [tile, tile, half, half],
            [mine, sent, own1, right, below1, diag1, near, arrive, probe_planes, table, dft],
            scratch=[grads, pltpu.VMEM((2, pixels, width), bf16)],
        ),
        flops=4_000_000_000,
        limit=16,
    )

    swap = [(i, 1 - i) for i in range(2)]
    real = shape_of(f32, 2, pixels, pixels)
    like = shape_of(bf16, *tile_object.shape)

    def laid_out(patch, got, after, flops):
        return run(
            job(spread_kernel, [real, real, tile, tile], [mine, sent, patch, got]),
            limit=16,
            after=after,
            flops=flops,
        )

    core, groups = core_group(), exchange_groups()
    if exchanged:
        got = lax.ppermute(given, "pos", swap)
    arrived = [swap_with(give, core, 1)]
    scattered = []
    while len(groups) > 1 and keep.shape[0] >> len(groups[0]) >= 16:
        group, groups = groups[0], groups[1:]
        keep, *gives = run(folded(group, keep, arrived))
        arrived = [swap_with(x, group, at) for at, x in enumerate(gives, 1)]
        scattered.append(group)
    first, second, *others = [[bit] for group in groups for bit in group]
    if exchanged:
        home, below, to_right, to_diag = laid_out(kept, got, [keep], LATE[0])
        from_left = [from_behind(x, 0, 1) for x in (to_right, to_diag)]
    (total,) = run(added(keep, arrived), after=[to_right] if exchanged else [], flops=LATE[1])
    (total,) = run(added(total, swapped(total, first)), flops=LATE[2])
    arrived = swapped(total, second)
    if exchanged:
        home, down = run(
            job(beside_kernel, [real, tile], [home, below, *from_left]),
            after=[total],
            flops=LATE[3],
        )
        above = from_behind(down, 1, 0)
    (total,) = run(added(total, arrived), after=[down] if exchanged else [], flops=LATE[4])
    for group in others:
        (total,) = run(added(total, swapped(total, group)))
    arrived = swapped(total, scattered[-1])
    if exchanged:
        (this_slice,) = run(
            job(
                lambda *refs: slice_kernel(this_layer, *refs),
                [tile],
                [own[0], own1, home, above],
            ),
            after=[total],
            flops=LATE[5],
        )
        other_slice = lax.ppermute(this_slice, "pos", swap)
    (total,) = run(
        joined(scattered[-1], total, arrived),
        after=[this_slice] if exchanged else [],
        flops=LATE[6],
    )
    for group in reversed(scattered[:-1]):
        (total,) = run(joined(group, total, swapped(total, group)))
    other_half = swap_with(total, core, 1)
    positions_all = lax.axis_size("tile") * lax.axis_size("pos") * (patterns.shape[2] // 2)
    step = probe_rate / math.sqrt(positions_all)
    halves = (total, other_half)
    if exchanged:
        token = run(
            job(token_kernel, [shape_of(f32, 8, 128)], []),
            after=[total, other_slice],
            flops=LATE[7],
        )
        slices = (this_slice, other_slice)
        new_probe, new_object = finished(this_layer, step, modes, halves, probe, slices, like, token)
    else:
        new_probe, _ = finished(this_layer, step, modes, halves, probe, (), like, ())
        slices = []
        for patch_grad, old in ((kept, own[0]), (given, own1)):
            home, below, to_right, to_diag = laid_out(patch_grad, jnp.zeros_like(kept), [], 0)
            from_left = [from_behind(x, 0, 1) for x in (to_right, to_diag)]
            home, down = run(job(beside_kernel, [real, tile], [home, below, *from_left]))
            grad = lax.psum(home + from_behind(down, 1, 0).astype(f32), "pos")
            slices.append((old.astype(f32) - object_rate * grad).astype(bf16))
        new_object = jnp.stack(slices)[None]
    new_probe = new_probe.reshape(2, pixels, lane_tiles, modes, 128).transpose(0, 1, 3, 2, 4)
    return (new_object, new_probe.reshape(probe_modes.shape))


def solution(mesh):
    placed = (
        P("tile", None, None, None, None),
        P(),
        P("tile", "pos", None, None, None),
        P("tile", "pos", None, None),
        P("tile", "pos"),
    )
    return jax.shard_map(
        shards,
        mesh=mesh,
        in_specs=placed,
        out_specs=(P("tile", None, None, None, None), P()),
        check_vma=False,
    )
```

```python
import math

import jax
import jax.numpy as jnp
import numpy as np
from jax import lax
from jax.experimental import pallas as pl
from jax.experimental.pallas import tpu as pltpu
from jax.sharding import PartitionSpec as P

GRID_ROWS = 4


fresnel_coeff = 0.25
object_rate = 0.05
probe_rate = 0.15

LATE = [work * 1_000_000_000 for work in (5, 0, 0, 5, 8, 0, 8, 4)]

f32 = jnp.float32
bf16 = jnp.bfloat16


def from_behind(block, rows, cols):
    tiles = lax.axis_size("tile")
    across = tiles // GRID_ROWS

    def source(i):
        return (i // across - rows) % GRID_ROWS * across + (i % across - cols) % across

    return lax.ppermute(block, "tile", [(source(i), i) for i in range(tiles)])


def real_embed(part_re, part_im):
    upper_half = np.concatenate([part_re, -part_im], axis=1)
    lower_half = np.concatenate([part_im, part_re], axis=1)
    stacked = np.concatenate([upper_half, lower_half], axis=0)
    return jnp.asarray(stacked, dtype=f32).astype(bf16)


def build_tables(pixels):
    indices = np.arange(pixels)
    angles = indices[:, None] * indices[None, :] % pixels * (2.0 * math.pi / pixels)
    norm_scale = 1.0 / math.sqrt(pixels)
    dft_re = np.cos(angles) * norm_scale
    dft_im = -np.sin(angles) * norm_scale
    frequency = np.where(indices < pixels // 2, indices, indices - pixels)
    phases = -2.0 * math.pi * fresnel_coeff / pixels * (frequency * frequency)
    phase_sum = phases[:, None] + angles
    kern_re = np.sum(np.cos(phase_sum), axis=0) / pixels
    kern_im = np.sum(np.sin(phase_sum), axis=0) / pixels
    lag_index = (indices[:, None] - indices[None, :]) % pixels
    prop_re = kern_re[lag_index]
    prop_im = kern_im[lag_index]
    return real_embed(prop_re, prop_im), real_embed(dft_re, dft_im)


def dot(a, b):
    return jnp.dot(a, b, preferred_element_type=f32)


def spots(mine_ref, sent_ref):
    n = mine_ref.shape[1]
    mine = mine_ref[n:, :].astype(f32)
    busy = mine[2:3] > 0
    rows = jnp.where(busy, mine, sent_ref[n:, :].astype(f32)).astype(jnp.int32)
    return (rows[0:1], rows[1:2]), (rows[3:4], rows[4:5]), busy


def shift_in(spot):
    row, col = spot
    n = row.shape[1]
    i_out = lax.broadcasted_iota(jnp.int32, (n, 2 * n), 0)
    i_in = lax.broadcasted_iota(jnp.int32, (n, 2 * n), 1)
    j_in = lax.broadcasted_iota(jnp.int32, (2 * n, n), 0)
    j_out = lax.broadcasted_iota(jnp.int32, (2 * n, n), 1)
    rows = i_in == i_out + jnp.concatenate([row, row], axis=1)
    cols = j_in == j_out + col
    return rows.astype(f32).astype(bf16), cols.astype(f32).astype(bf16)


def shift_out(spot):
    row, col = spot
    n = row.shape[1]
    i_out = lax.broadcasted_iota(jnp.int32, (n, 2 * n), 0)
    i_in = lax.broadcasted_iota(jnp.int32, (n, 2 * n), 1)
    j_in = lax.broadcasted_iota(jnp.int32, (2 * n, n), 0)
    j_out = lax.broadcasted_iota(jnp.int32, (2 * n, n), 1)
    rows = j_in == j_out + row
    cols = i_in == i_out + jnp.concatenate([col, col], axis=1)
    return rows.astype(f32).astype(bf16), cols.astype(f32).astype(bf16)


def patch(shifts, own_ref, right_ref, below_ref, diag_ref, part):
    upper = jnp.concatenate([own_ref[part], right_ref[part]], axis=1)
    lower = jnp.concatenate([below_ref[part], diag_ref[part]], axis=1)
    rows = dot(shifts[0], jnp.concatenate([upper, lower], axis=0)).astype(bf16)
    return dot(rows, shifts[1])


def stacked(wave_re, wave_im):
    return jnp.concatenate([wave_re.astype(bf16), wave_im.astype(bf16)], axis=0)


def transform(table_ref, wave):
    n = wave.shape[1]
    table = table_ref[...]
    first = dot(table, wave)
    first = jnp.concatenate([first[:n].astype(bf16), (-first[n:]).astype(bf16)], axis=1)
    out = dot(first, table)
    return out[:, :n], out[:, n:]


def probe_plane(probe_ref, part, mode, modes):
    lane_tiles = 2
    n = probe_ref.shape[0] // (2 * lane_tiles * modes)
    step = lane_tiles * modes
    halves = [
        probe_ref[pl.ds(part * n * step + tile * modes + mode, n, stride=step), :]
        for tile in range(lane_tiles)
    ]
    return jnp.concatenate(halves, axis=1)


def message_kernel(offsets_ref, counts_ref, own_ref, patterns_ref, own_out, mine_ref, sent_ref):
    own_out[...] = own_ref[...]
    n = mine_ref.shape[1]
    at = lax.broadcasted_iota(jnp.int32, (16, n), 0)
    busy = (counts_ref[0, 0] == patterns_ref.shape[2]).astype(jnp.int32)
    for slot, ref in enumerate((mine_ref, sent_ref)):
        row, col = offsets_ref[0, 0, slot, 0], offsets_ref[0, 0, slot, 1]
        row2, col2 = offsets_ref[0, 0, 1 - slot, 0], offsets_ref[0, 0, 1 - slot, 1]
        rows = jnp.where(at == 0, row, jnp.where(at == 1, col, busy))
        rows = jnp.where(at == 3, row2, jnp.where(at == 4, col2, rows))
        ref[pl.ds(0, n), :] = patterns_ref[0, 0, slot]
        ref[pl.ds(n, 16), :] = rows.astype(f32).astype(bf16)


def ready_kernel(probe_ref, prop_ref, planes_ref, table_ref):
    table_ref[...] = prop_ref[...]
    n = planes_ref.shape[1]
    modes = planes_ref.shape[2] // n
    for part in range(2):
        for mode in range(modes):
            planes_ref[part, :, pl.ds(mode * n, n)] = probe_plane(probe_ref, part, mode, modes)


def arrive_kernel(
    mine_ref, sent_ref, own_ref, right_ref, below_ref, diag_ref, planes_ref, prop_ref,
    near_ref, arrive_ref,
):
    n = own_ref.shape[1]
    shifts = shift_in(spots(mine_ref, sent_ref)[0])
    tiles = (own_ref, right_ref.at[0], below_ref, diag_ref)
    near = [patch(shifts, *tiles, part) for part in range(2)]
    for part in range(2):
        near_ref[part] = near[part].astype(bf16)
    for mode in range(planes_ref.shape[2] // n):
        lanes = pl.ds(mode * n, n)
        p_re, p_im = planes_ref[0, :, lanes], planes_ref[1, :, lanes]
        wave = stacked(p_re * near[0] - p_im * near[1], p_re * near[1] + p_im * near[0])
        a_re, a_neg = transform(prop_ref, wave)
        arrive_ref[0, :, lanes] = a_re
        arrive_ref[1, :, lanes] = -a_neg


def gradient_kernel(
    mine_ref, sent_ref, own_ref, right_ref, below_ref, diag_ref, near_ref, arrive_ref, planes_ref,
    prop_ref, dft_ref,
    kept_ref, given_ref, keep_ref, give_ref, grad_ref, term_ref, *, layer
):
    n = own_ref.shape[1]
    modes = planes_ref.shape[2] // n
    spot, _, busy = spots(mine_ref, sent_ref)
    shifts = shift_in(spot)
    tiles = (own_ref, right_ref.at[1], below_ref, diag_ref)
    far = [patch(shifts, *tiles, part) for part in range(2)]
    fields = []
    for mode in range(modes):
        lanes = pl.ds(mode * n, n)
        a_re, a_im = arrive_ref[0, :, lanes], arrive_ref[1, :, lanes]
        wave = stacked(far[0] * a_re - far[1] * a_im, far[0] * a_im + far[1] * a_re)
        fields.append(transform(dft_ref, wave))
    intensity = sum(f_re * f_re + f_neg * f_neg for f_re, f_neg in fields)
    pattern = jnp.where(busy, mine_ref[:n, :].astype(f32), sent_ref[:n, :].astype(f32))
    residual = intensity - pattern
    waves = []
    grad = [0.0, 0.0]
    for mode in range(modes):
        lanes = pl.ds(mode * n, n)
        f_re, f_neg = fields[mode]
        a_re, a_im = arrive_ref[0, :, lanes], arrive_ref[1, :, lanes]
        b_re, b_im = transform(dft_ref, stacked(f_re * residual, f_neg * residual))
        grad[0] += a_re * b_re + a_im * b_im
        grad[1] += a_re * b_im - a_im * b_re
        waves.append(stacked(far[0] * b_re + far[1] * b_im, far[1] * b_re - far[0] * b_im))
    for part in range(2):
        grad_ref[1, part] = grad[part].astype(bf16)
    grad = [0.0, 0.0]
    near = [near_ref[part].astype(f32) for part in range(2)]
    for mode in range(modes):
        lanes = pl.ds(mode * n, n)
        b_re, b_im = transform(prop_ref, waves[mode])
        p_re, p_im = planes_ref[0, :, lanes], planes_ref[1, :, lanes]
        grad[0] += p_re * b_re + p_im * b_im
        grad[1] += p_re * b_im - p_im * b_re
        term_ref[0, :, lanes] = (near[0] * b_re + near[1] * b_im).astype(bf16)
        term_ref[1, :, lanes] = (near[0] * b_im - near[1] * b_re).astype(bf16)
    core = place_of(core_group())
    keep_ref[...] = term_ref[core]
    give_ref[...] = term_ref[1 - core]
    for part in range(2):
        grad_ref[0, part] = grad[part].astype(bf16)
    layer = layer()
    kept_ref[...] = grad_ref[layer]
    given_ref[...] = grad_ref[1 - layer]


def spread_kernel(
    mine_ref, sent_ref, kept_ref, got_ref, home_ref, below_ref, right_ref, diag_ref
):
    n = mine_ref.shape[1]
    first, second, _ = spots(mine_ref, sent_ref)
    rows1, cols1 = shift_out(first)
    rows2, cols2 = shift_out(second)
    cols = jnp.concatenate([cols1, cols2], axis=0)
    for part in range(2):
        tall1 = dot(rows1, kept_ref[part]).astype(bf16)
        tall2 = dot(rows2, got_ref[part]).astype(bf16)
        wide = dot(jnp.concatenate([tall1, tall2], axis=1), cols)
        home_ref[part] = wide[:n, :n]
        right_ref[part] = wide[:n, n:].astype(bf16)
        below_ref[part] = wide[n:, :n]
        diag_ref[part] = wide[n:, n:].astype(bf16)


def down_kernel(below_ref, diag_ref, down_ref):
    down_ref[...] = (below_ref[...] + diag_ref[...].astype(f32)).astype(bf16)


def slice_kernel(layer, own0_ref, own1_ref, home_ref, left_ref, above_ref, out_ref):
    grad = home_ref[...] + left_ref[...].astype(f32) + above_ref[...].astype(f32)
    own = jnp.where(layer() == 0, own0_ref[...].astype(f32), own1_ref[...].astype(f32))
    out_ref[...] = (own - object_rate * grad).astype(bf16)


def pass_kernel(block_ref, out_ref):
    out_ref[...] = block_ref[...]


def token_kernel(token_ref):
    token_ref[...] = jnp.zeros_like(token_ref)


def core_group():
    return [lax.axis_size("pos")]


def place_of(group):
    flat = lax.axis_index("tile") * lax.axis_size("pos") + lax.axis_index("pos")
    return sum(flat // mask % 2 * (1 << at) for at, mask in enumerate(group))


def job(kernel, outs, arrays, scalars=(), scratch=()):
    return kernel, list(outs), list(scalars), list(arrays), list(scratch)


def run(*jobs, flops=1_000_000, limit=4, after=()):
    vmem = pl.BlockSpec(memory_space=pltpu.VMEM)
    smem = pl.BlockSpec(memory_space=pltpu.SMEM)
    anywhere = pl.BlockSpec(memory_space=pl.ANY)
    kernels, outs, scalars, arrays, scratch = zip(*jobs)
    ins = [x + y for x, y in zip(scalars, arrays)]
    specs = [[smem] * len(x) + [vmem] * len(y) for x, y in zip(scalars, arrays)]

    def taken(refs, lists):
        parts = []
        for items in lists:
            parts.append(refs[: len(items)])
            refs = refs[len(items) :]
        return parts, refs

    def body(*refs):
        in_refs, refs = taken(refs, ins)
        out_refs, refs = taken(refs[len(after) :], outs)
        scratch_refs, _ = taken(refs, scratch)
        for kernel, *parts in zip(kernels, in_refs, out_refs, scratch_refs):
            kernel(*parts[0], *parts[1], *parts[2])

    moved = sum(x.size * x.dtype.itemsize for x in sum(ins, []) + sum(outs, []))
    results = pl.pallas_call(
        body,
        out_shape=sum(outs, []),
        in_specs=sum(specs, []) + [anywhere] * len(after),
        out_specs=[vmem] * len(sum(outs, [])),
        scratch_shapes=sum(scratch, []),
        compiler_params=pltpu.CompilerParams(vmem_limit_bytes=limit * 2**20),
        cost_estimate=pl.CostEstimate(flops=flops, bytes_accessed=moved, transcendentals=0),
    )(*sum(ins, []), *after)
    results, _ = taken(results, outs)
    return results[0] if len(jobs) == 1 else results


def finished(layer, step, modes, halves, probe, slices, like, after):
    vmem = pl.BlockSpec(memory_space=pltpu.VMEM)
    anywhere = pl.BlockSpec(memory_space=pl.ANY)
    inputs = [*halves, probe, *slices]

    def body(*refs):
        blocks, (out_probe, out_tile, sems) = refs[3 : len(inputs)], refs[-3:]
        places = [layer(), 1 - layer()][: len(blocks)]
        copies = [
            pltpu.make_async_copy(block, out_tile.at[0, place], sems.at[at])
            for at, (block, place) in enumerate(zip(blocks, places))
        ]
        for copy in copies:
            copy.start()
        probe_kernel(step, modes, *refs[:3], out_probe)
        for copy in copies:
            copy.wait()

    return pl.pallas_call(
        body,
        out_shape=[shape_of(f32, *probe.shape), like],
        in_specs=[vmem] * len(inputs) + [anywhere] * len(after),
        out_specs=[vmem, anywhere],
        scratch_shapes=[pltpu.SemaphoreType.DMA((2,))],
        compiler_params=pltpu.CompilerParams(vmem_limit_bytes=8 * 2**20),
        cost_estimate=pl.CostEstimate(
            flops=4 * probe.size, bytes_accessed=12 * probe.size, transcendentals=0
        ),
    )(*inputs, *after)


def shape_of(kind, *dims):
    return jax.ShapeDtypeStruct(dims, kind)


def gathered_message(patterns, offsets, counts):
    pixels = patterns.shape[4]
    all_counts = lax.all_gather(counts[0, 0], "pos")
    ends = jnp.cumsum(all_counts)
    rank = lax.axis_index("pos")
    source = jnp.sum((ends <= rank).astype(jnp.int32))
    slot = rank - (ends[source] - all_counts[source])
    spot = lax.all_gather(offsets[0, 0], "pos")[source, slot]
    pattern = lax.all_gather(patterns[0, 0], "pos")[source, slot]
    at = lax.broadcasted_iota(jnp.int32, (16, pixels), 0)
    rows = jnp.where(at == 0, spot[0], jnp.where(at == 1, spot[1], 0))
    return jnp.concatenate([pattern, rows.astype(bf16)], axis=0)


def fold_kernel(group, keep_ref, *refs):
    blocks = refs[-1]
    got = len(refs) - 1 - blocks.shape[0]
    arrived, keep_out, give_outs = refs[:got], refs[got], refs[got + 1 : -1]
    total = keep_ref[...].astype(f32)
    for ref in arrived:
        total += ref[...].astype(f32)
    size = blocks.shape[1]
    for block in range(blocks.shape[0]):
        blocks[block] = total[block * size : (block + 1) * size]
    here = place_of(group)
    keep_out[...] = blocks[here]
    for distance, ref in enumerate(give_outs, 1):
        ref[...] = blocks[here ^ distance].astype(bf16)


def add_kernel(keep_ref, *refs):
    total = keep_ref[...].astype(f32)
    for ref in refs[:-1]:
        total += ref[...].astype(f32)
    refs[-1][...] = total.astype(bf16)


def place_kernel(group, *refs):
    arrived, out_ref, blocks = refs[:-2], refs[-2], refs[-1]
    here = place_of(group)
    for distance, ref in enumerate(arrived):
        blocks[here ^ distance] = ref[...]
    size = blocks.shape[1]
    for block in range(blocks.shape[0]):
        out_ref[pl.ds(block * size, size), :] = blocks[block]


def probe_kernel(step, modes, mine_ref, other_ref, probe_ref, out_ref):
    core = place_of(core_group())
    lane_tiles = 2
    n = mine_ref.shape[0]
    stride = lane_tiles * modes
    for part in range(2):
        total = jnp.where(core == part, mine_ref[...].astype(f32), other_ref[...].astype(f32))
        for mode in range(modes):
            for tile in range(lane_tiles):
                lane = (mode * lane_tiles + tile) * 128
                where = pl.ds(part * n * stride + tile * modes + mode, n, stride=stride)
                out_ref[where, :] = probe_ref[where, :] - step * total[:, lane : lane + 128]


def exchange_groups():
    tiles, owners = lax.axis_size("tile"), lax.axis_size("pos")
    bits = [1 << bit for bit in range(owners.bit_length() - 1)]
    bits += [owners << bit for bit in range(1, tiles.bit_length() - 1)]
    return [bits[at : at + 2] for at in range(0, len(bits), 2)]


def swap_with(x, group, distance):
    mask = sum(bit for at, bit in enumerate(group) if distance >> at & 1)
    devices = lax.axis_size("tile") * lax.axis_size("pos")
    return lax.ppermute(x, ("tile", "pos"), [(i, i ^ mask) for i in range(devices)])


def joined(group, x, arrived):
    blocks = 1 << len(group)
    return job(
        lambda *refs: place_kernel(group, *refs),
        [shape_of(bf16, x.shape[0] * blocks, x.shape[1])],
        [x] + arrived,
        scratch=[pltpu.VMEM((blocks,) + x.shape, bf16)],
    )


def added(x, arrived):
    return job(add_kernel, [shape_of(bf16, *x.shape)], [x] + arrived)


def swapped(x, group):
    return [swap_with(x, group, at) for at in range(1, 1 << len(group))]


def folded(group, keep, arrived):
    blocks = 1 << len(group)
    size, width = keep.shape[0] // blocks, keep.shape[1]
    return job(
        lambda *refs: fold_kernel(group, *refs),
        [shape_of(f32, size, width)] + [shape_of(bf16, size, width)] * (blocks - 1),
        [keep] + arrived,
        scratch=[pltpu.VMEM((blocks, size, width), f32)],
    )


def shards(tile_object, probe_modes, patterns, offsets, counts):
    _, pixels, modes, _ = probe_modes.shape
    width = modes * pixels
    lane_tiles = pixels // 128
    prop, dft = build_tables(pixels)
    tile = shape_of(bf16, 2, pixels, pixels)
    planes = shape_of(f32, 2, pixels, width)
    probe = probe_modes.reshape(2, pixels, modes, lane_tiles, 128)
    probe = probe.transpose(0, 1, 3, 2, 4).reshape(-1, 128)

    own = [tile_object[0, 0], tile_object[0, 1]]
    below0 = from_behind(own[0], -1, 0)
    right = from_behind(tile_object[0], 0, -1)
    exchanged = lax.axis_size("pos") == patterns.shape[2]
    message = shape_of(bf16, pixels + 16, pixels)
    own1, mine, sent = run(
        job(
            message_kernel,
            [tile, message, message],
            [own[1], patterns],
            scalars=[offsets, counts if exchanged else jnp.zeros_like(counts)],
        ),
        limit=4,
        after=[own[0]],
    )
    probe_planes, table = run(
        job(ready_kernel, [planes, shape_of(bf16, *prop.shape)], [probe, prop]),
        limit=8,
        after=[own1],
    )
    below1 = from_behind(own1, -1, 0)
    if exchanged:
        sent = lax.ppermute(sent, "pos", [(i, 1 - i) for i in range(2)])
    else:
        sent = gathered_message(patterns, offsets, counts)
    diag0 = from_behind(below0, 0, -1)
    diag1 = from_behind(below1, 0, -1)
    near, arrive = run(
        job(
            arrive_kernel,
            [tile, planes],
            [mine, sent, own[0], right, below0, diag0, probe_planes, table],
        ),
        flops=1_500_000_000,
        limit=16,
    )
    half = shape_of(bf16, pixels, width)
    grads = pltpu.VMEM((2, 2, pixels, pixels), bf16)
    this_layer = (lambda: lax.axis_index("pos")) if exchanged else (lambda: 0)
    kept, given, keep, give = run(
        job(
            lambda *refs: gradient_kernel(*refs, layer=this_layer),
            [tile, tile, half, half],
            [mine, sent, own1, right, below1, diag1, near, arrive, probe_planes, table, dft],
            scratch=[grads, pltpu.VMEM((2, pixels, width), bf16)],
        ),
        flops=4_000_000_000,
        limit=16,
    )

    swap = [(i, 1 - i) for i in range(2)]
    real = shape_of(f32, 2, pixels, pixels)
    like = shape_of(bf16, *tile_object.shape)

    def laid_out(patch, got, after, flops):
        return run(
            job(spread_kernel, [real, real, tile, tile], [mine, sent, patch, got]),
            limit=16,
            after=after,
            flops=flops,
        )

    core, groups = core_group(), exchange_groups()
    if exchanged:
        got = lax.ppermute(given, "pos", swap)
    arrived = [swap_with(give, core, 1)]
    scattered = []
    while len(groups) > 1 and keep.shape[0] >> len(groups[0]) >= 16:
        group, groups = groups[0], groups[1:]
        for bit in reversed(group):
            if exchanged and scattered == [] and bit == group[0]:
                home, below, to_right, to_diag = laid_out(kept, got, [keep], LATE[0])
                diag_in = from_behind(to_diag, 0, 1)
                keep, give = run(folded([bit], keep, arrived), after=[to_right])
            else:
                keep, give = run(folded([bit], keep, arrived))
            arrived = [swap_with(give, [bit], 1)]
        scattered.append(group)
    first, second, *others = [[bit] for group in groups for bit in group]
    (total,) = run(added(keep, arrived), flops=LATE[1])
    (total,) = run(added(total, swapped(total, first)), flops=LATE[2])
    arrived = swapped(total, second)
    if exchanged:
        (down,) = run(
            job(down_kernel, [tile], [below, diag_in]), after=[total], flops=LATE[3]
        )
        above = from_behind(down, 1, 0)
        (total,), (to_right,) = run(
            added(total, arrived), job(pass_kernel, [tile], [to_right]), after=[down], flops=LATE[4]
        )
        left_in = from_behind(to_right, 0, 1)
    else:
        (total,) = run(added(total, arrived))
    for group in others:
        (total,) = run(added(total, swapped(total, group)))
    arrived = swapped(total, scattered[-1])
    if exchanged:
        (this_slice,) = run(
            job(
                lambda *refs: slice_kernel(this_layer, *refs),
                [tile],
                [own[0], own1, home, left_in, above],
            ),
            after=[total],
            flops=LATE[5],
        )
        other_slice = lax.ppermute(this_slice, "pos", swap)
    (total,) = run(
        joined(scattered[-1], total, arrived),
        after=[this_slice] if exchanged else [],
        flops=LATE[6],
    )
    for group in reversed(scattered[:-1]):
        (total,) = run(joined(group, total, swapped(total, group)))
    other_half = swap_with(total, core, 1)
    positions_all = lax.axis_size("tile") * lax.axis_size("pos") * (patterns.shape[2] // 2)
    step = probe_rate / math.sqrt(positions_all)
    halves = (total, other_half)
    if exchanged:
        token = run(
            job(token_kernel, [shape_of(f32, 8, 128)], []),
            after=[total, other_slice],
            flops=LATE[7],
        )
        slices = (this_slice, other_slice)
        new_probe, new_object = finished(this_layer, step, modes, halves, probe, slices, like, token)
    else:
        new_probe, _ = finished(this_layer, step, modes, halves, probe, (), like, ())
        slices = []
        for patch_grad, old in ((kept, own[0]), (given, own1)):
            home, below, to_right, to_diag = laid_out(patch_grad, jnp.zeros_like(kept), [], 0)
            (down,) = run(job(down_kernel, [tile], [below, from_behind(to_diag, 0, 1)]))
            above = from_behind(down, 1, 0).astype(f32)
            grad = lax.psum(home + from_behind(to_right, 0, 1).astype(f32) + above, "pos")
            slices.append((old.astype(f32) - object_rate * grad).astype(bf16))
        new_object = jnp.stack(slices)[None]
    new_probe = new_probe.reshape(2, pixels, lane_tiles, modes, 128).transpose(0, 1, 3, 2, 4)
    return (new_object, new_probe.reshape(probe_modes.shape))


def solution(mesh):
    placed = (
        P("tile", None, None, None, None),
        P(),
        P("tile", "pos", None, None, None),
        P("tile", "pos", None, None),
        P("tile", "pos"),
    )
    return jax.shard_map(
        shards,
        mesh=mesh,
        in_specs=placed,
        out_specs=(P("tile", None, None, None, None), P()),
        check_vma=False,
    )
```

```python
import math

import jax
import jax.numpy as jnp
import numpy as np
from jax import lax
from jax.experimental import pallas as pl
from jax.experimental.pallas import tpu as pltpu
from jax.sharding import PartitionSpec as P

GRID_ROWS = 4


fresnel_coeff = 0.25
object_rate = 0.05
probe_rate = 0.15

LATE = [work * 1_000_000_000 for work in (5, 0, 0, 5, 0, 0, 8, 4)]

f32 = jnp.float32
bf16 = jnp.bfloat16


def from_behind(block, rows, cols):
    tiles = lax.axis_size("tile")
    across = tiles // GRID_ROWS

    def source(i):
        return (i // across - rows) % GRID_ROWS * across + (i % across - cols) % across

    return lax.ppermute(block, "tile", [(source(i), i) for i in range(tiles)])


def real_embed(part_re, part_im):
    upper_half = np.concatenate([part_re, -part_im], axis=1)
    lower_half = np.concatenate([part_im, part_re], axis=1)
    stacked = np.concatenate([upper_half, lower_half], axis=0)
    return jnp.asarray(stacked, dtype=f32).astype(bf16)


def build_tables(pixels):
    indices = np.arange(pixels)
    angles = indices[:, None] * indices[None, :] % pixels * (2.0 * math.pi / pixels)
    norm_scale = 1.0 / math.sqrt(pixels)
    dft_re = np.cos(angles) * norm_scale
    dft_im = -np.sin(angles) * norm_scale
    frequency = np.where(indices < pixels // 2, indices, indices - pixels)
    phases = -2.0 * math.pi * fresnel_coeff / pixels * (frequency * frequency)
    phase_sum = phases[:, None] + angles
    kern_re = np.sum(np.cos(phase_sum), axis=0) / pixels
    kern_im = np.sum(np.sin(phase_sum), axis=0) / pixels
    lag_index = (indices[:, None] - indices[None, :]) % pixels
    prop_re = kern_re[lag_index]
    prop_im = kern_im[lag_index]
    return real_embed(prop_re, prop_im), real_embed(dft_re, dft_im)


def dot(a, b):
    return jnp.dot(a, b, preferred_element_type=f32)


def spots(mine_ref, sent_ref):
    n = mine_ref.shape[1]
    mine = mine_ref[n:, :].astype(f32)
    busy = mine[2:3] > 0
    rows = jnp.where(busy, mine, sent_ref[n:, :].astype(f32)).astype(jnp.int32)
    return (rows[0:1], rows[1:2]), (rows[3:4], rows[4:5]), busy


def shift_in(spot):
    row, col = spot
    n = row.shape[1]
    i_out = lax.broadcasted_iota(jnp.int32, (n, 2 * n), 0)
    i_in = lax.broadcasted_iota(jnp.int32, (n, 2 * n), 1)
    j_in = lax.broadcasted_iota(jnp.int32, (2 * n, n), 0)
    j_out = lax.broadcasted_iota(jnp.int32, (2 * n, n), 1)
    rows = i_in == i_out + jnp.concatenate([row, row], axis=1)
    cols = j_in == j_out + col
    return rows.astype(f32).astype(bf16), cols.astype(f32).astype(bf16)


def shift_out(spot):
    row, col = spot
    n = row.shape[1]
    i_out = lax.broadcasted_iota(jnp.int32, (n, 2 * n), 0)
    i_in = lax.broadcasted_iota(jnp.int32, (n, 2 * n), 1)
    j_in = lax.broadcasted_iota(jnp.int32, (2 * n, n), 0)
    j_out = lax.broadcasted_iota(jnp.int32, (2 * n, n), 1)
    rows = j_in == j_out + row
    cols = i_in == i_out + jnp.concatenate([col, col], axis=1)
    return rows.astype(f32).astype(bf16), cols.astype(f32).astype(bf16)


def patch(shifts, own_ref, right_ref, below_ref, diag_ref, part):
    upper = jnp.concatenate([own_ref[part], right_ref[part]], axis=1)
    lower = jnp.concatenate([below_ref[part], diag_ref[part]], axis=1)
    rows = dot(shifts[0], jnp.concatenate([upper, lower], axis=0)).astype(bf16)
    return dot(rows, shifts[1])


def stacked(wave_re, wave_im):
    return jnp.concatenate([wave_re.astype(bf16), wave_im.astype(bf16)], axis=0)


def transform(table_ref, wave):
    n = wave.shape[1]
    table = table_ref[...]
    first = dot(table, wave)
    first = jnp.concatenate([first[:n].astype(bf16), (-first[n:]).astype(bf16)], axis=1)
    out = dot(first, table)
    return out[:, :n], out[:, n:]


def probe_plane(probe_ref, part, mode, modes):
    lane_tiles = 2
    n = probe_ref.shape[0] // (2 * lane_tiles * modes)
    step = lane_tiles * modes
    halves = [
        probe_ref[pl.ds(part * n * step + tile * modes + mode, n, stride=step), :]
        for tile in range(lane_tiles)
    ]
    return jnp.concatenate(halves, axis=1)


def message_kernel(offsets_ref, counts_ref, own_ref, patterns_ref, own_out, mine_ref, sent_ref):
    own_out[...] = own_ref[...]
    n = mine_ref.shape[1]
    at = lax.broadcasted_iota(jnp.int32, (16, n), 0)
    busy = (counts_ref[0, 0] == patterns_ref.shape[2]).astype(jnp.int32)
    for slot, ref in enumerate((mine_ref, sent_ref)):
        row, col = offsets_ref[0, 0, slot, 0], offsets_ref[0, 0, slot, 1]
        row2, col2 = offsets_ref[0, 0, 1 - slot, 0], offsets_ref[0, 0, 1 - slot, 1]
        rows = jnp.where(at == 0, row, jnp.where(at == 1, col, busy))
        rows = jnp.where(at == 3, row2, jnp.where(at == 4, col2, rows))
        ref[pl.ds(0, n), :] = patterns_ref[0, 0, slot]
        ref[pl.ds(n, 16), :] = rows.astype(f32).astype(bf16)


def ready_kernel(probe_ref, prop_ref, planes_ref, table_ref):
    table_ref[...] = prop_ref[...]
    n = planes_ref.shape[1]
    modes = planes_ref.shape[2] // n
    for part in range(2):
        for mode in range(modes):
            planes_ref[part, :, pl.ds(mode * n, n)] = probe_plane(probe_ref, part, mode, modes)


def arrive_kernel(
    mine_ref, sent_ref, own_ref, right_ref, below_ref, diag_ref, planes_ref, prop_ref,
    near_ref, arrive_ref,
):
    n = own_ref.shape[1]
    shifts = shift_in(spots(mine_ref, sent_ref)[0])
    tiles = (own_ref, right_ref.at[0], below_ref, diag_ref)
    near = [patch(shifts, *tiles, part) for part in range(2)]
    for part in range(2):
        near_ref[part] = near[part].astype(bf16)
    for mode in range(planes_ref.shape[2] // n):
        lanes = pl.ds(mode * n, n)
        p_re, p_im = planes_ref[0, :, lanes], planes_ref[1, :, lanes]
        wave = stacked(p_re * near[0] - p_im * near[1], p_re * near[1] + p_im * near[0])
        a_re, a_neg = transform(prop_ref, wave)
        arrive_ref[0, :, lanes] = a_re
        arrive_ref[1, :, lanes] = -a_neg


def gradient_kernel(
    mine_ref, sent_ref, own_ref, right_ref, below_ref, diag_ref, near_ref, arrive_ref, planes_ref,
    prop_ref, dft_ref,
    kept_ref, given_ref, keep_ref, give_ref, grad_ref, term_ref, *, layer
):
    n = own_ref.shape[1]
    modes = planes_ref.shape[2] // n
    spot, _, busy = spots(mine_ref, sent_ref)
    shifts = shift_in(spot)
    tiles = (own_ref, right_ref.at[1], below_ref, diag_ref)
    far = [patch(shifts, *tiles, part) for part in range(2)]
    fields = []
    for mode in range(modes):
        lanes = pl.ds(mode * n, n)
        a_re, a_im = arrive_ref[0, :, lanes], arrive_ref[1, :, lanes]
        wave = stacked(far[0] * a_re - far[1] * a_im, far[0] * a_im + far[1] * a_re)
        fields.append(transform(dft_ref, wave))
    intensity = sum(f_re * f_re + f_neg * f_neg for f_re, f_neg in fields)
    pattern = jnp.where(busy, mine_ref[:n, :].astype(f32), sent_ref[:n, :].astype(f32))
    residual = intensity - pattern
    waves = []
    grad = [0.0, 0.0]
    for mode in range(modes):
        lanes = pl.ds(mode * n, n)
        f_re, f_neg = fields[mode]
        a_re, a_im = arrive_ref[0, :, lanes], arrive_ref[1, :, lanes]
        b_re, b_im = transform(dft_ref, stacked(f_re * residual, f_neg * residual))
        grad[0] += a_re * b_re + a_im * b_im
        grad[1] += a_re * b_im - a_im * b_re
        waves.append(stacked(far[0] * b_re + far[1] * b_im, far[1] * b_re - far[0] * b_im))
    for part in range(2):
        grad_ref[1, part] = grad[part].astype(bf16)
    grad = [0.0, 0.0]
    near = [near_ref[part].astype(f32) for part in range(2)]
    for mode in range(modes):
        lanes = pl.ds(mode * n, n)
        b_re, b_im = transform(prop_ref, waves[mode])
        p_re, p_im = planes_ref[0, :, lanes], planes_ref[1, :, lanes]
        grad[0] += p_re * b_re + p_im * b_im
        grad[1] += p_re * b_im - p_im * b_re
        term_ref[0, :, lanes] = (near[0] * b_re + near[1] * b_im).astype(bf16)
        term_ref[1, :, lanes] = (near[0] * b_im - near[1] * b_re).astype(bf16)
    core = place_of(core_group())
    keep_ref[...] = term_ref[core]
    give_ref[...] = term_ref[1 - core]
    for part in range(2):
        grad_ref[0, part] = grad[part].astype(bf16)
    layer = layer()
    kept_ref[...] = grad_ref[layer]
    given_ref[...] = grad_ref[1 - layer]


def spread_kernel(
    mine_ref, sent_ref, kept_ref, got_ref, home_ref, below_ref, right_ref, diag_ref
):
    n = mine_ref.shape[1]
    first, second, _ = spots(mine_ref, sent_ref)
    rows1, cols1 = shift_out(first)
    rows2, cols2 = shift_out(second)
    cols = jnp.concatenate([cols1, cols2], axis=0)
    for part in range(2):
        tall1 = dot(rows1, kept_ref[part]).astype(bf16)
        tall2 = dot(rows2, got_ref[part]).astype(bf16)
        wide = dot(jnp.concatenate([tall1, tall2], axis=1), cols)
        home_ref[part] = wide[:n, :n]
        right_ref[part] = wide[:n, n:].astype(bf16)
        below_ref[part] = wide[n:, :n]
        diag_ref[part] = wide[n:, n:].astype(bf16)


def down_kernel(below_ref, diag_ref, down_ref):
    down_ref[...] = (below_ref[...] + diag_ref[...].astype(f32)).astype(bf16)


def slice_kernel(layer, own0_ref, own1_ref, home_ref, above_ref, left_ref, out_ref):
    grad = home_ref[...] + left_ref[...].astype(f32) + above_ref[...].astype(f32)
    own = jnp.where(layer() == 0, own0_ref[...].astype(f32), own1_ref[...].astype(f32))
    out_ref[...] = (own - object_rate * grad).astype(bf16)


def pass_kernel(block_ref, out_ref):
    out_ref[...] = block_ref[...]


def token_kernel(token_ref):
    token_ref[...] = jnp.zeros_like(token_ref)


def core_group():
    return [lax.axis_size("pos")]


def place_of(group):
    flat = lax.axis_index("tile") * lax.axis_size("pos") + lax.axis_index("pos")
    return sum(flat // mask % 2 * (1 << at) for at, mask in enumerate(group))


def job(kernel, outs, arrays, scalars=(), scratch=()):
    return kernel, list(outs), list(scalars), list(arrays), list(scratch)


def run(*jobs, flops=1_000_000, limit=4, after=()):
    vmem = pl.BlockSpec(memory_space=pltpu.VMEM)
    smem = pl.BlockSpec(memory_space=pltpu.SMEM)
    anywhere = pl.BlockSpec(memory_space=pl.ANY)
    kernels, outs, scalars, arrays, scratch = zip(*jobs)
    ins = [x + y for x, y in zip(scalars, arrays)]
    specs = [[smem] * len(x) + [vmem] * len(y) for x, y in zip(scalars, arrays)]

    def taken(refs, lists):
        parts = []
        for items in lists:
            parts.append(refs[: len(items)])
            refs = refs[len(items) :]
        return parts, refs

    def body(*refs):
        in_refs, refs = taken(refs, ins)
        out_refs, refs = taken(refs[len(after) :], outs)
        scratch_refs, _ = taken(refs, scratch)
        for kernel, *parts in zip(kernels, in_refs, out_refs, scratch_refs):
            kernel(*parts[0], *parts[1], *parts[2])

    moved = sum(x.size * x.dtype.itemsize for x in sum(ins, []) + sum(outs, []))
    results = pl.pallas_call(
        body,
        out_shape=sum(outs, []),
        in_specs=sum(specs, []) + [anywhere] * len(after),
        out_specs=[vmem] * len(sum(outs, [])),
        scratch_shapes=sum(scratch, []),
        compiler_params=pltpu.CompilerParams(vmem_limit_bytes=limit * 2**20),
        cost_estimate=pl.CostEstimate(flops=flops, bytes_accessed=moved, transcendentals=0),
    )(*sum(ins, []), *after)
    results, _ = taken(results, outs)
    return results[0] if len(jobs) == 1 else results


def finished(layer, step, modes, halves, probe, slices, like, after):
    vmem = pl.BlockSpec(memory_space=pltpu.VMEM)
    anywhere = pl.BlockSpec(memory_space=pl.ANY)
    inputs = [*halves, probe, *slices]

    def body(*refs):
        blocks, (out_probe, out_tile, sems) = refs[3 : len(inputs)], refs[-3:]
        places = [layer(), 1 - layer()][: len(blocks)]
        copies = [
            pltpu.make_async_copy(block, out_tile.at[0, place], sems.at[at])
            for at, (block, place) in enumerate(zip(blocks, places))
        ]
        for copy in copies:
            copy.start()
        probe_kernel(step, modes, *refs[:3], out_probe)
        for copy in copies:
            copy.wait()

    return pl.pallas_call(
        body,
        out_shape=[shape_of(f32, *probe.shape), like],
        in_specs=[vmem] * len(inputs) + [anywhere] * len(after),
        out_specs=[vmem, anywhere],
        scratch_shapes=[pltpu.SemaphoreType.DMA((2,))],
        compiler_params=pltpu.CompilerParams(vmem_limit_bytes=8 * 2**20),
        cost_estimate=pl.CostEstimate(
            flops=4 * probe.size, bytes_accessed=12 * probe.size, transcendentals=0
        ),
    )(*inputs, *after)


def shape_of(kind, *dims):
    return jax.ShapeDtypeStruct(dims, kind)


def gathered_message(patterns, offsets, counts):
    pixels = patterns.shape[4]
    all_counts = lax.all_gather(counts[0, 0], "pos")
    ends = jnp.cumsum(all_counts)
    rank = lax.axis_index("pos")
    source = jnp.sum((ends <= rank).astype(jnp.int32))
    slot = rank - (ends[source] - all_counts[source])
    spot = lax.all_gather(offsets[0, 0], "pos")[source, slot]
    pattern = lax.all_gather(patterns[0, 0], "pos")[source, slot]
    at = lax.broadcasted_iota(jnp.int32, (16, pixels), 0)
    rows = jnp.where(at == 0, spot[0], jnp.where(at == 1, spot[1], 0))
    return jnp.concatenate([pattern, rows.astype(bf16)], axis=0)


def fold_kernel(group, keep_ref, *refs):
    blocks = refs[-1]
    got = len(refs) - 1 - blocks.shape[0]
    arrived, keep_out, give_outs = refs[:got], refs[got], refs[got + 1 : -1]
    total = keep_ref[...].astype(f32)
    for ref in arrived:
        total += ref[...].astype(f32)
    size = blocks.shape[1]
    for block in range(blocks.shape[0]):
        blocks[block] = total[block * size : (block + 1) * size]
    here = place_of(group)
    keep_out[...] = blocks[here]
    for distance, ref in enumerate(give_outs, 1):
        ref[...] = blocks[here ^ distance].astype(bf16)


def add_kernel(keep_ref, *refs):
    total = keep_ref[...].astype(f32)
    for ref in refs[:-1]:
        total += ref[...].astype(f32)
    refs[-1][...] = total.astype(bf16)


def place_kernel(group, *refs):
    arrived, out_ref, blocks = refs[:-2], refs[-2], refs[-1]
    here = place_of(group)
    for distance, ref in enumerate(arrived):
        blocks[here ^ distance] = ref[...]
    size = blocks.shape[1]
    for block in range(blocks.shape[0]):
        out_ref[pl.ds(block * size, size), :] = blocks[block]


def probe_kernel(step, modes, mine_ref, other_ref, probe_ref, out_ref):
    core = place_of(core_group())
    lane_tiles = 2
    n = mine_ref.shape[0]
    stride = lane_tiles * modes
    for part in range(2):
        total = jnp.where(core == part, mine_ref[...].astype(f32), other_ref[...].astype(f32))
        for mode in range(modes):
            for tile in range(lane_tiles):
                lane = (mode * lane_tiles + tile) * 128
                where = pl.ds(part * n * stride + tile * modes + mode, n, stride=stride)
                out_ref[where, :] = probe_ref[where, :] - step * total[:, lane : lane + 128]


def exchange_groups():
    tiles, owners = lax.axis_size("tile"), lax.axis_size("pos")
    bits = [1 << bit for bit in range(owners.bit_length() - 1)]
    bits += [owners << bit for bit in range(1, tiles.bit_length() - 1)]
    return [bits[at : at + 2] for at in range(0, len(bits), 2)]


def swap_with(x, group, distance):
    mask = sum(bit for at, bit in enumerate(group) if distance >> at & 1)
    devices = lax.axis_size("tile") * lax.axis_size("pos")
    return lax.ppermute(x, ("tile", "pos"), [(i, i ^ mask) for i in range(devices)])


def joined(group, x, arrived):
    blocks = 1 << len(group)
    return job(
        lambda *refs: place_kernel(group, *refs),
        [shape_of(bf16, x.shape[0] * blocks, x.shape[1])],
        [x] + arrived,
        scratch=[pltpu.VMEM((blocks,) + x.shape, bf16)],
    )


def added(x, arrived):
    return job(add_kernel, [shape_of(bf16, *x.shape)], [x] + arrived)


def swapped(x, group):
    return [swap_with(x, group, at) for at in range(1, 1 << len(group))]


def folded(group, keep, arrived):
    blocks = 1 << len(group)
    size, width = keep.shape[0] // blocks, keep.shape[1]
    return job(
        lambda *refs: fold_kernel(group, *refs),
        [shape_of(f32, size, width)] + [shape_of(bf16, size, width)] * (blocks - 1),
        [keep] + arrived,
        scratch=[pltpu.VMEM((blocks, size, width), f32)],
    )


def shards(tile_object, probe_modes, patterns, offsets, counts):
    _, pixels, modes, _ = probe_modes.shape
    width = modes * pixels
    lane_tiles = pixels // 128
    prop, dft = build_tables(pixels)
    tile = shape_of(bf16, 2, pixels, pixels)
    planes = shape_of(f32, 2, pixels, width)
    probe = probe_modes.reshape(2, pixels, modes, lane_tiles, 128)
    probe = probe.transpose(0, 1, 3, 2, 4).reshape(-1, 128)

    own = [tile_object[0, 0], tile_object[0, 1]]
    below0 = from_behind(own[0], -1, 0)
    right = from_behind(tile_object[0], 0, -1)
    exchanged = lax.axis_size("pos") == patterns.shape[2]
    message = shape_of(bf16, pixels + 16, pixels)
    own1, mine, sent = run(
        job(
            message_kernel,
            [tile, message, message],
            [own[1], patterns],
            scalars=[offsets, counts if exchanged else jnp.zeros_like(counts)],
        ),
        limit=4,
        after=[own[0]],
    )
    probe_planes, table = run(
        job(ready_kernel, [planes, shape_of(bf16, *prop.shape)], [probe, prop]),
        limit=8,
        after=[own1],
    )
    below1 = from_behind(own1, -1, 0)
    if exchanged:
        sent = lax.ppermute(sent, "pos", [(i, 1 - i) for i in range(2)])
    else:
        sent = gathered_message(patterns, offsets, counts)
    diag0 = from_behind(below0, 0, -1)
    diag1 = from_behind(below1, 0, -1)
    near, arrive = run(
        job(
            arrive_kernel,
            [tile, planes],
            [mine, sent, own[0], right, below0, diag0, probe_planes, table],
        ),
        flops=1_500_000_000,
        limit=16,
    )
    half = shape_of(bf16, pixels, width)
    grads = pltpu.VMEM((2, 2, pixels, pixels), bf16)
    this_layer = (lambda: lax.axis_index("pos")) if exchanged else (lambda: 0)
    kept, given, keep, give = run(
        job(
            lambda *refs: gradient_kernel(*refs, layer=this_layer),
            [tile, tile, half, half],
            [mine, sent, own1, right, below1, diag1, near, arrive, probe_planes, table, dft],
            scratch=[grads, pltpu.VMEM((2, pixels, width), bf16)],
        ),
        flops=4_000_000_000,
        limit=16,
    )

    swap = [(i, 1 - i) for i in range(2)]
    real = shape_of(f32, 2, pixels, pixels)
    like = shape_of(bf16, *tile_object.shape)

    def laid_out(patch, got, after, flops):
        return run(
            job(spread_kernel, [real, real, tile, tile], [mine, sent, patch, got]),
            limit=16,
            after=after,
            flops=flops,
        )

    core, groups = core_group(), exchange_groups()
    if exchanged:
        got = lax.ppermute(given, "pos", swap)
    arrived = [swap_with(give, core, 1)]
    scattered = []
    while len(groups) > 1 and keep.shape[0] >> len(groups[0]) >= 16:
        group, groups = groups[0], groups[1:]
        for bit in reversed(group):
            if exchanged and scattered == [] and bit == group[0]:
                home, below, to_right, to_diag = laid_out(kept, got, [keep], LATE[0])
                diag_in = from_behind(to_diag, 0, 1)
                keep, give = run(folded([bit], keep, arrived), after=[to_right])
            else:
                keep, give = run(folded([bit], keep, arrived))
            arrived = [swap_with(give, [bit], 1)]
        scattered.append(group)
    first, second, *others = [[bit] for group in groups for bit in group]
    (total,) = run(added(keep, arrived), flops=LATE[1])
    arrived = swapped(total, first)
    if exchanged:
        (down,), (to_right,) = run(
            job(down_kernel, [tile], [below, diag_in]),
            job(pass_kernel, [tile], [to_right]),
            after=[total],
            flops=LATE[2],
        )
        above = from_behind(down, 1, 0)
        left_in = from_behind(to_right, 0, 1)
    (total,) = run(added(total, arrived), after=[down] if exchanged else [], flops=LATE[3])
    (total,) = run(added(total, swapped(total, second)), flops=LATE[4])
    for group in others:
        (total,) = run(added(total, swapped(total, group)))
    arrived = swapped(total, scattered[-1])
    if exchanged:
        (this_slice,) = run(
            job(
                lambda *refs: slice_kernel(this_layer, *refs),
                [tile],
                [own[0], own1, home, above, left_in],
            ),
            after=[total],
            flops=LATE[5],
        )
        other_slice = lax.ppermute(this_slice, "pos", swap)
    (total,) = run(
        joined(scattered[-1], total, arrived),
        after=[this_slice] if exchanged else [],
        flops=LATE[6],
    )
    for group in reversed(scattered[:-1]):
        (total,) = run(joined(group, total, swapped(total, group)))
    other_half = swap_with(total, core, 1)
    positions_all = lax.axis_size("tile") * lax.axis_size("pos") * (patterns.shape[2] // 2)
    step = probe_rate / math.sqrt(positions_all)
    halves = (total, other_half)
    if exchanged:
        token = run(
            job(token_kernel, [shape_of(f32, 8, 128)], []),
            after=[total, other_slice],
            flops=LATE[7],
        )
        slices = (this_slice, other_slice)
        new_probe, new_object = finished(this_layer, step, modes, halves, probe, slices, like, token)
    else:
        new_probe, _ = finished(this_layer, step, modes, halves, probe, (), like, ())
        slices = []
        for patch_grad, old in ((kept, own[0]), (given, own1)):
            home, below, to_right, to_diag = laid_out(patch_grad, jnp.zeros_like(kept), [], 0)
            (down,) = run(job(down_kernel, [tile], [below, from_behind(to_diag, 0, 1)]))
            above = from_behind(down, 1, 0).astype(f32)
            grad = lax.psum(home + from_behind(to_right, 0, 1).astype(f32) + above, "pos")
            slices.append((old.astype(f32) - object_rate * grad).astype(bf16))
        new_object = jnp.stack(slices)[None]
    new_probe = new_probe.reshape(2, pixels, lane_tiles, modes, 128).transpose(0, 1, 3, 2, 4)
    return (new_object, new_probe.reshape(probe_modes.shape))


def solution(mesh):
    placed = (
        P("tile", None, None, None, None),
        P(),
        P("tile", "pos", None, None, None),
        P("tile", "pos", None, None),
        P("tile", "pos"),
    )
    return jax.shard_map(
        shards,
        mesh=mesh,
        in_specs=placed,
        out_specs=(P("tile", None, None, None, None), P()),
        check_vma=False,
    )
```

```python
import math

import jax
import jax.numpy as jnp
import numpy as np
from jax import lax
from jax.experimental import pallas as pl
from jax.experimental.pallas import tpu as pltpu
from jax.sharding import PartitionSpec as P

GRID_ROWS = 4


fresnel_coeff = 0.25
object_rate = 0.05
probe_rate = 0.15

LATE = [work * 1_000_000_000 for work in (0, 8, 0, 0, 8, 0, 8, 4)]

f32 = jnp.float32
bf16 = jnp.bfloat16


def from_behind(block, rows, cols):
    tiles = lax.axis_size("tile")
    across = tiles // GRID_ROWS

    def source(i):
        return (i // across - rows) % GRID_ROWS * across + (i % across - cols) % across

    return lax.ppermute(block, "tile", [(source(i), i) for i in range(tiles)])


def real_embed(part_re, part_im):
    upper_half = np.concatenate([part_re, -part_im], axis=1)
    lower_half = np.concatenate([part_im, part_re], axis=1)
    stacked = np.concatenate([upper_half, lower_half], axis=0)
    return jnp.asarray(stacked, dtype=f32).astype(bf16)


def build_tables(pixels):
    indices = np.arange(pixels)
    angles = indices[:, None] * indices[None, :] % pixels * (2.0 * math.pi / pixels)
    norm_scale = 1.0 / math.sqrt(pixels)
    dft_re = np.cos(angles) * norm_scale
    dft_im = -np.sin(angles) * norm_scale
    frequency = np.where(indices < pixels // 2, indices, indices - pixels)
    phases = -2.0 * math.pi * fresnel_coeff / pixels * (frequency * frequency)
    phase_sum = phases[:, None] + angles
    kern_re = np.sum(np.cos(phase_sum), axis=0) / pixels
    kern_im = np.sum(np.sin(phase_sum), axis=0) / pixels
    lag_index = (indices[:, None] - indices[None, :]) % pixels
    prop_re = kern_re[lag_index]
    prop_im = kern_im[lag_index]
    return real_embed(prop_re, prop_im), real_embed(dft_re, dft_im)


def dot(a, b):
    return jnp.dot(a, b, preferred_element_type=f32)


def spots(mine_ref, sent_ref):
    n = mine_ref.shape[1]
    mine = mine_ref[n:, :].astype(f32)
    busy = mine[2:3] > 0
    rows = jnp.where(busy, mine, sent_ref[n:, :].astype(f32)).astype(jnp.int32)
    return (rows[0:1], rows[1:2]), (rows[3:4], rows[4:5]), busy


def shift_in(spot):
    row, col = spot
    n = row.shape[1]
    i_out = lax.broadcasted_iota(jnp.int32, (n, 2 * n), 0)
    i_in = lax.broadcasted_iota(jnp.int32, (n, 2 * n), 1)
    j_in = lax.broadcasted_iota(jnp.int32, (2 * n, n), 0)
    j_out = lax.broadcasted_iota(jnp.int32, (2 * n, n), 1)
    rows = i_in == i_out + jnp.concatenate([row, row], axis=1)
    cols = j_in == j_out + col
    return rows.astype(f32).astype(bf16), cols.astype(f32).astype(bf16)


def patch(shifts, own_ref, right_ref, below_ref, diag_ref, part):
    upper = jnp.concatenate([own_ref[part], right_ref[part]], axis=1)
    lower = jnp.concatenate([below_ref[part], diag_ref[part]], axis=1)
    rows = dot(shifts[0], jnp.concatenate([upper, lower], axis=0)).astype(bf16)
    return dot(rows, shifts[1])


def stacked(wave_re, wave_im):
    return jnp.concatenate([wave_re.astype(bf16), wave_im.astype(bf16)], axis=0)


def transform(table_ref, wave):
    n = wave.shape[1]
    table = table_ref[...]
    first = dot(table, wave)
    first = jnp.concatenate([first[:n].astype(bf16), (-first[n:]).astype(bf16)], axis=1)
    out = dot(first, table)
    return out[:, :n], out[:, n:]


def probe_plane(probe_ref, part, mode, modes):
    lane_tiles = 2
    n = probe_ref.shape[0] // (2 * lane_tiles * modes)
    step = lane_tiles * modes
    halves = [
        probe_ref[pl.ds(part * n * step + tile * modes + mode, n, stride=step), :]
        for tile in range(lane_tiles)
    ]
    return jnp.concatenate(halves, axis=1)


def message_kernel(offsets_ref, counts_ref, own_ref, patterns_ref, own_out, mine_ref, sent_ref):
    own_out[...] = own_ref[...]
    n = mine_ref.shape[1]
    at = lax.broadcasted_iota(jnp.int32, (16, n), 0)
    busy = (counts_ref[0, 0] == patterns_ref.shape[2]).astype(jnp.int32)
    for slot, ref in enumerate((mine_ref, sent_ref)):
        row, col = offsets_ref[0, 0, slot, 0], offsets_ref[0, 0, slot, 1]
        row2, col2 = offsets_ref[0, 0, 1 - slot, 0], offsets_ref[0, 0, 1 - slot, 1]
        rows = jnp.where(at == 0, row, jnp.where(at == 1, col, busy))
        rows = jnp.where(at == 3, row2, jnp.where(at == 4, col2, rows))
        ref[pl.ds(0, n), :] = patterns_ref[0, 0, slot]
        ref[pl.ds(n, 16), :] = rows.astype(f32).astype(bf16)


def ready_kernel(probe_ref, prop_ref, planes_ref, table_ref):
    table_ref[...] = prop_ref[...]
    n = planes_ref.shape[1]
    modes = planes_ref.shape[2] // n
    for part in range(2):
        for mode in range(modes):
            planes_ref[part, :, pl.ds(mode * n, n)] = probe_plane(probe_ref, part, mode, modes)


def arrive_kernel(
    mine_ref, sent_ref, own_ref, right_ref, below_ref, diag_ref, planes_ref, prop_ref,
    near_ref, arrive_ref,
):
    n = own_ref.shape[1]
    shifts = shift_in(spots(mine_ref, sent_ref)[0])
    tiles = (own_ref, right_ref.at[0], below_ref, diag_ref)
    near = [patch(shifts, *tiles, part) for part in range(2)]
    for part in range(2):
        near_ref[part] = near[part].astype(bf16)
    for mode in range(planes_ref.shape[2] // n):
        lanes = pl.ds(mode * n, n)
        p_re, p_im = planes_ref[0, :, lanes], planes_ref[1, :, lanes]
        wave = stacked(p_re * near[0] - p_im * near[1], p_re * near[1] + p_im * near[0])
        a_re, a_neg = transform(prop_ref, wave)
        arrive_ref[0, :, lanes] = a_re
        arrive_ref[1, :, lanes] = -a_neg


def gradient_kernel(
    mine_ref, sent_ref, own_ref, right_ref, below_ref, diag_ref, near_ref, arrive_ref, planes_ref,
    prop_ref, dft_ref,
    kept_ref, given_ref, keep_ref, give_ref, grad_ref, term_ref, *, layer
):
    n = own_ref.shape[1]
    modes = planes_ref.shape[2] // n
    spot, _, busy = spots(mine_ref, sent_ref)
    shifts = shift_in(spot)
    tiles = (own_ref, right_ref.at[1], below_ref, diag_ref)
    far = [patch(shifts, *tiles, part) for part in range(2)]
    fields = []
    for mode in range(modes):
        lanes = pl.ds(mode * n, n)
        a_re, a_im = arrive_ref[0, :, lanes], arrive_ref[1, :, lanes]
        wave = stacked(far[0] * a_re - far[1] * a_im, far[0] * a_im + far[1] * a_re)
        fields.append(transform(dft_ref, wave))
    intensity = sum(f_re * f_re + f_neg * f_neg for f_re, f_neg in fields)
    pattern = jnp.where(busy, mine_ref[:n, :].astype(f32), sent_ref[:n, :].astype(f32))
    residual = intensity - pattern
    waves = []
    grad = [0.0, 0.0]
    for mode in range(modes):
        lanes = pl.ds(mode * n, n)
        f_re, f_neg = fields[mode]
        a_re, a_im = arrive_ref[0, :, lanes], arrive_ref[1, :, lanes]
        b_re, b_im = transform(dft_ref, stacked(f_re * residual, f_neg * residual))
        grad[0] += a_re * b_re + a_im * b_im
        grad[1] += a_re * b_im - a_im * b_re
        waves.append(stacked(far[0] * b_re + far[1] * b_im, far[1] * b_re - far[0] * b_im))
    for part in range(2):
        grad_ref[1, part] = grad[part].astype(bf16)
    grad = [0.0, 0.0]
    near = [near_ref[part].astype(f32) for part in range(2)]
    for mode in range(modes):
        lanes = pl.ds(mode * n, n)
        b_re, b_im = transform(prop_ref, waves[mode])
        p_re, p_im = planes_ref[0, :, lanes], planes_ref[1, :, lanes]
        grad[0] += p_re * b_re + p_im * b_im
        grad[1] += p_re * b_im - p_im * b_re
        term_ref[0, :, lanes] = (near[0] * b_re + near[1] * b_im).astype(bf16)
        term_ref[1, :, lanes] = (near[0] * b_im - near[1] * b_re).astype(bf16)
    core = place_of(core_group())
    keep_ref[...] = term_ref[core]
    give_ref[...] = term_ref[1 - core]
    for part in range(2):
        grad_ref[0, part] = grad[part].astype(bf16)
    layer = layer()
    kept_ref[...] = grad_ref[layer]
    given_ref[...] = grad_ref[1 - layer]


def laid_rows(mine_ref, sent_ref, kept_ref, got_ref, part, below):
    n = mine_ref.shape[1]
    first, second, _ = spots(mine_ref, sent_ref)
    from_row = n if below else 0
    i_out = lax.broadcasted_iota(jnp.int32, (n, n), 0) + from_row
    i_in = lax.broadcasted_iota(jnp.int32, (n, n), 1)
    tall = []
    for (row, _), ref in ((first, kept_ref), (second, got_ref)):
        rows = (i_out == i_in + row).astype(f32).astype(bf16)
        tall.append(dot(rows, ref[part]).astype(bf16))
    return jnp.concatenate(tall, axis=1)


def laid_cols(mine_ref, sent_ref, beyond):
    n = mine_ref.shape[1]
    first, second, _ = spots(mine_ref, sent_ref)
    from_col = n if beyond else 0
    i_in = lax.broadcasted_iota(jnp.int32, (n, n), 0)
    i_out = lax.broadcasted_iota(jnp.int32, (n, n), 1) + from_col
    cols = [(i_out == i_in + col).astype(f32).astype(bf16) for _, col in (first, second)]
    return jnp.concatenate(cols, axis=0)


def diag_kernel(mine_ref, sent_ref, kept_ref, got_ref, diag_ref):
    cols = laid_cols(mine_ref, sent_ref, True)
    for part in range(2):
        tall = laid_rows(mine_ref, sent_ref, kept_ref, got_ref, part, True)
        diag_ref[part] = dot(tall, cols).astype(bf16)


def spread_kernel(mine_ref, sent_ref, kept_ref, got_ref, home_ref, below_ref, right_ref):
    here = laid_cols(mine_ref, sent_ref, False)
    beyond = laid_cols(mine_ref, sent_ref, True)
    for part in range(2):
        tall = laid_rows(mine_ref, sent_ref, kept_ref, got_ref, part, False)
        home_ref[part] = dot(tall, here)
        right_ref[part] = dot(tall, beyond).astype(bf16)
        tall = laid_rows(mine_ref, sent_ref, kept_ref, got_ref, part, True)
        below_ref[part] = dot(tall, here)


def down_kernel(below_ref, diag_ref, down_ref):
    down_ref[...] = (below_ref[...] + diag_ref[...].astype(f32)).astype(bf16)


def pass_kernel(block_ref, out_ref):
    out_ref[...] = block_ref[...]


def slice_kernel(layer, own0_ref, own1_ref, home_ref, above_ref, left_ref, out_ref):
    grad = home_ref[...] + left_ref[...].astype(f32) + above_ref[...].astype(f32)
    own = jnp.where(layer() == 0, own0_ref[...].astype(f32), own1_ref[...].astype(f32))
    out_ref[...] = (own - object_rate * grad).astype(bf16)


def token_kernel(token_ref):
    token_ref[...] = jnp.zeros_like(token_ref)


def core_group():
    return [lax.axis_size("pos")]


def place_of(group):
    flat = lax.axis_index("tile") * lax.axis_size("pos") + lax.axis_index("pos")
    return sum(flat // mask % 2 * (1 << at) for at, mask in enumerate(group))


def job(kernel, outs, arrays, scalars=(), scratch=()):
    return kernel, list(outs), list(scalars), list(arrays), list(scratch)


def run(*jobs, flops=1_000_000, limit=4, after=()):
    vmem = pl.BlockSpec(memory_space=pltpu.VMEM)
    smem = pl.BlockSpec(memory_space=pltpu.SMEM)
    anywhere = pl.BlockSpec(memory_space=pl.ANY)
    kernels, outs, scalars, arrays, scratch = zip(*jobs)
    ins = [x + y for x, y in zip(scalars, arrays)]
    specs = [[smem] * len(x) + [vmem] * len(y) for x, y in zip(scalars, arrays)]

    def taken(refs, lists):
        parts = []
        for items in lists:
            parts.append(refs[: len(items)])
            refs = refs[len(items) :]
        return parts, refs

    def body(*refs):
        in_refs, refs = taken(refs, ins)
        out_refs, refs = taken(refs[len(after) :], outs)
        scratch_refs, _ = taken(refs, scratch)
        for kernel, *parts in zip(kernels, in_refs, out_refs, scratch_refs):
            kernel(*parts[0], *parts[1], *parts[2])

    moved = sum(x.size * x.dtype.itemsize for x in sum(ins, []) + sum(outs, []))
    results = pl.pallas_call(
        body,
        out_shape=sum(outs, []),
        in_specs=sum(specs, []) + [anywhere] * len(after),
        out_specs=[vmem] * len(sum(outs, [])),
        scratch_shapes=sum(scratch, []),
        compiler_params=pltpu.CompilerParams(vmem_limit_bytes=limit * 2**20),
        cost_estimate=pl.CostEstimate(flops=flops, bytes_accessed=moved, transcendentals=0),
    )(*sum(ins, []), *after)
    results, _ = taken(results, outs)
    return results[0] if len(jobs) == 1 else results


def finished(layer, step, modes, halves, probe, slices, like, after):
    vmem = pl.BlockSpec(memory_space=pltpu.VMEM)
    anywhere = pl.BlockSpec(memory_space=pl.ANY)
    inputs = [*halves, probe, *slices]

    def body(*refs):
        blocks, (out_probe, out_tile, new_ref, sems, probe_sems) = refs[3 : len(inputs)], refs[-5:]
        places = [layer(), 1 - layer()][: len(blocks)]
        copies = [
            pltpu.make_async_copy(block, out_tile.at[0, place], sems.at[at])
            for at, (block, place) in enumerate(zip(blocks, places))
        ]
        for copy in copies:
            copy.start()
        copies += probe_kernel(step, modes, *refs[:3], new_ref, out_probe, probe_sems)
        for copy in copies:
            copy.wait()

    return pl.pallas_call(
        body,
        out_shape=[shape_of(f32, *probe.shape), like],
        in_specs=[vmem] * len(inputs) + [anywhere] * len(after),
        out_specs=[anywhere, anywhere],
        scratch_shapes=[
            pltpu.VMEM(probe.shape, f32),
            pltpu.SemaphoreType.DMA((2,)),
            pltpu.SemaphoreType.DMA((8,)),
        ],
        compiler_params=pltpu.CompilerParams(vmem_limit_bytes=8 * 2**20),
        cost_estimate=pl.CostEstimate(
            flops=4 * probe.size, bytes_accessed=12 * probe.size, transcendentals=0
        ),
    )(*inputs, *after)


def shape_of(kind, *dims):
    return jax.ShapeDtypeStruct(dims, kind)


def gathered_message(patterns, offsets, counts):
    pixels = patterns.shape[4]
    all_counts = lax.all_gather(counts[0, 0], "pos")
    ends = jnp.cumsum(all_counts)
    rank = lax.axis_index("pos")
    source = jnp.sum((ends <= rank).astype(jnp.int32))
    slot = rank - (ends[source] - all_counts[source])
    spot = lax.all_gather(offsets[0, 0], "pos")[source, slot]
    pattern = lax.all_gather(patterns[0, 0], "pos")[source, slot]
    at = lax.broadcasted_iota(jnp.int32, (16, pixels), 0)
    rows = jnp.where(at == 0, spot[0], jnp.where(at == 1, spot[1], 0))
    return jnp.concatenate([pattern, rows.astype(bf16)], axis=0)


def fold_kernel(group, keep_ref, *refs):
    blocks = refs[-1]
    got = len(refs) - 1 - blocks.shape[0]
    arrived, keep_out, give_outs = refs[:got], refs[got], refs[got + 1 : -1]
    total = keep_ref[...].astype(f32)
    for ref in arrived:
        total += ref[...].astype(f32)
    size = blocks.shape[1]
    for block in range(blocks.shape[0]):
        blocks[block] = total[block * size : (block + 1) * size]
    here = place_of(group)
    keep_out[...] = blocks[here]
    for distance, ref in enumerate(give_outs, 1):
        ref[...] = blocks[here ^ distance].astype(bf16)


def add_kernel(keep_ref, *refs):
    total = keep_ref[...].astype(f32)
    for ref in refs[:-1]:
        total += ref[...].astype(f32)
    refs[-1][...] = total.astype(bf16)


def place_kernel(group, *refs):
    arrived, out_ref, blocks = refs[:-2], refs[-2], refs[-1]
    here = place_of(group)
    for distance, ref in enumerate(arrived):
        blocks[here ^ distance] = ref[...]
    size = blocks.shape[1]
    for block in range(blocks.shape[0]):
        out_ref[pl.ds(block * size, size), :] = blocks[block]


def probe_kernel(step, modes, mine_ref, other_ref, probe_ref, new_ref, out_hbm, sems):
    core = place_of(core_group())
    lane_tiles = 2
    n = mine_ref.shape[0]
    stride = lane_tiles * modes
    pieces = sems.shape[0] // 2
    size = n // pieces
    copies = []
    for part in range(2):
        for piece in range(pieces):
            at = pl.ds(piece * size, size)
            mine, other = mine_ref[at, :].astype(f32), other_ref[at, :].astype(f32)
            total = jnp.where(core == part, mine, other)
            start = (part * n + piece * size) * stride
            for mode in range(modes):
                for tile in range(lane_tiles):
                    lane = (mode * lane_tiles + tile) * 128
                    where = pl.ds(start + tile * modes + mode, size, stride=stride)
                    new_ref[where, :] = probe_ref[where, :] - step * total[:, lane : lane + 128]
            rows = pl.ds(start, size * stride)
            copy = pltpu.make_async_copy(
                new_ref.at[rows, :], out_hbm.at[rows, :], sems.at[len(copies)]
            )
            copy.start()
            copies.append(copy)
    return copies


def exchange_groups():
    tiles, owners = lax.axis_size("tile"), lax.axis_size("pos")
    bits = [1 << bit for bit in range(owners.bit_length() - 1)]
    bits += [owners << bit for bit in range(1, tiles.bit_length() - 1)]
    return [bits[at : at + 2] for at in range(0, len(bits), 2)]


def swap_with(x, group, distance):
    mask = sum(bit for at, bit in enumerate(group) if distance >> at & 1)
    devices = lax.axis_size("tile") * lax.axis_size("pos")
    return lax.ppermute(x, ("tile", "pos"), [(i, i ^ mask) for i in range(devices)])


def joined(group, x, arrived):
    blocks = 1 << len(group)
    return job(
        lambda *refs: place_kernel(group, *refs),
        [shape_of(bf16, x.shape[0] * blocks, x.shape[1])],
        [x] + arrived,
        scratch=[pltpu.VMEM((blocks,) + x.shape, bf16)],
    )


def added(x, arrived):
    return job(add_kernel, [shape_of(bf16, *x.shape)], [x] + arrived)


def swapped(x, group):
    return [swap_with(x, group, at) for at in range(1, 1 << len(group))]


def folded(group, keep, arrived):
    blocks = 1 << len(group)
    size, width = keep.shape[0] // blocks, keep.shape[1]
    return job(
        lambda *refs: fold_kernel(group, *refs),
        [shape_of(f32, size, width)] + [shape_of(bf16, size, width)] * (blocks - 1),
        [keep] + arrived,
        scratch=[pltpu.VMEM((blocks, size, width), f32)],
    )


def shards(tile_object, probe_modes, patterns, offsets, counts):
    _, pixels, modes, _ = probe_modes.shape
    width = modes * pixels
    lane_tiles = pixels // 128
    prop, dft = build_tables(pixels)
    tile = shape_of(bf16, 2, pixels, pixels)
    planes = shape_of(f32, 2, pixels, width)
    probe = probe_modes.reshape(2, pixels, modes, lane_tiles, 128)
    probe = probe.transpose(0, 1, 3, 2, 4).reshape(-1, 128)

    own = [tile_object[0, 0], tile_object[0, 1]]
    below0 = from_behind(own[0], -1, 0)
    right = from_behind(tile_object[0], 0, -1)
    exchanged = lax.axis_size("pos") == patterns.shape[2]
    message = shape_of(bf16, pixels + 16, pixels)
    own1, mine, sent = run(
        job(
            message_kernel,
            [tile, message, message],
            [own[1], patterns],
            scalars=[offsets, counts if exchanged else jnp.zeros_like(counts)],
        ),
        limit=4,
        after=[own[0]],
    )
    probe_planes, table = run(
        job(ready_kernel, [planes, shape_of(bf16, *prop.shape)], [probe, prop]),
        limit=8,
        after=[own1],
    )
    below1 = from_behind(own1, -1, 0)
    if exchanged:
        sent = lax.ppermute(sent, "pos", [(i, 1 - i) for i in range(2)])
    else:
        sent = gathered_message(patterns, offsets, counts)
    diag0 = from_behind(below0, 0, -1)
    diag1 = from_behind(below1, 0, -1)
    near, arrive = run(
        job(
            arrive_kernel,
            [tile, planes],
            [mine, sent, own[0], right, below0, diag0, probe_planes, table],
        ),
        flops=1_500_000_000,
        limit=16,
    )
    half = shape_of(bf16, pixels, width)
    grads = pltpu.VMEM((2, 2, pixels, pixels), bf16)
    this_layer = (lambda: lax.axis_index("pos")) if exchanged else (lambda: 0)
    kept, given, keep, give = run(
        job(
            lambda *refs: gradient_kernel(*refs, layer=this_layer),
            [tile, tile, half, half],
            [mine, sent, own1, right, below1, diag1, near, arrive, probe_planes, table, dft],
            scratch=[grads, pltpu.VMEM((2, pixels, width), bf16)],
        ),
        flops=4_000_000_000,
        limit=16,
    )

    swap = [(i, 1 - i) for i in range(2)]
    real = shape_of(f32, 2, pixels, pixels)
    like = shape_of(bf16, *tile_object.shape)

    core, groups = core_group(), exchange_groups()
    if exchanged:
        got = lax.ppermute(given, "pos", swap)
    arrived = [swap_with(give, core, 1)]
    scattered = []
    while len(groups) > 1 and keep.shape[0] >> len(groups[0]) >= 16:
        group, groups = groups[0], groups[1:]
        keep, *gives = run(folded(group, keep, arrived))
        arrived = [swap_with(x, group, at) for at, x in enumerate(gives, 1)]
        scattered.append(group)
    first, second, *others = [[bit] for group in groups for bit in group]
    if exchanged:
        patches = [mine, sent, kept, got]
        (to_diag,) = run(
            job(diag_kernel, [tile], patches), limit=16, after=[keep], flops=LATE[0]
        )
        diag_in = from_behind(to_diag, 0, 1)
        home, below, to_right = run(
            job(spread_kernel, [real, real, tile], patches), limit=16, after=[to_diag]
        )
    (total,) = run(added(keep, arrived), after=[below] if exchanged else [], flops=LATE[1])
    (total,) = run(added(total, swapped(total, first)), flops=LATE[2])
    arrived = swapped(total, second)
    if exchanged:
        (down,), (to_right,) = run(
            job(down_kernel, [tile], [below, diag_in]),
            job(pass_kernel, [tile], [to_right]),
            after=[total],
            flops=LATE[3],
        )
        above = from_behind(down, 1, 0)
        left_in = from_behind(to_right, 0, 1)
    (total,) = run(added(total, arrived), after=[down] if exchanged else [], flops=LATE[4])
    for group in others:
        (total,) = run(added(total, swapped(total, group)))
    arrived = swapped(total, scattered[-1])
    if exchanged:
        (this_slice,) = run(
            job(
                lambda *refs: slice_kernel(this_layer, *refs),
                [tile],
                [own[0], own1, home, above, left_in],
            ),
            after=[total],
            flops=LATE[5],
        )
        other_slice = lax.ppermute(this_slice, "pos", swap)
    (total,) = run(
        joined(scattered[-1], total, arrived),
        after=[this_slice] if exchanged else [],
        flops=LATE[6],
    )
    for group in reversed(scattered[:-1]):
        (total,) = run(joined(group, total, swapped(total, group)))
    other_half = swap_with(total, core, 1)
    positions_all = lax.axis_size("tile") * lax.axis_size("pos") * (patterns.shape[2] // 2)
    step = probe_rate / math.sqrt(positions_all)
    halves = (total, other_half)
    if exchanged:
        token = run(
            job(token_kernel, [shape_of(f32, 8, 128)], []),
            after=[total, other_slice],
            flops=LATE[7],
        )
        slices = (this_slice, other_slice)
        new_probe, new_object = finished(this_layer, step, modes, halves, probe, slices, like, token)
    else:
        new_probe, _ = finished(this_layer, step, modes, halves, probe, (), like, ())
        slices = []
        for patch_grad, old in ((kept, own[0]), (given, own1)):
            patches = [mine, sent, patch_grad, jnp.zeros_like(kept)]
            (to_diag,) = run(job(diag_kernel, [tile], patches), limit=16)
            home, below, to_right = run(
                job(spread_kernel, [real, real, tile], patches), limit=16
            )
            (down,) = run(job(down_kernel, [tile], [below, from_behind(to_diag, 0, 1)]))
            above = from_behind(down, 1, 0).astype(f32)
            grad = lax.psum(home + from_behind(to_right, 0, 1).astype(f32) + above, "pos")
            slices.append((old.astype(f32) - object_rate * grad).astype(bf16))
        new_object = jnp.stack(slices)[None]
    new_probe = new_probe.reshape(2, pixels, lane_tiles, modes, 128).transpose(0, 1, 3, 2, 4)
    return (new_object, new_probe.reshape(probe_modes.shape))


def solution(mesh):
    placed = (
        P("tile", None, None, None, None),
        P(),
        P("tile", "pos", None, None, None),
        P("tile", "pos", None, None),
        P("tile", "pos"),
    )
    return jax.shard_map(
        shards,
        mesh=mesh,
        in_specs=placed,
        out_specs=(P("tile", None, None, None, None), P()),
        check_vma=False,
    )
```

```python
import math

import jax
import jax.numpy as jnp
import numpy as np
from jax import lax
from jax.experimental import pallas as pl
from jax.experimental.pallas import tpu as pltpu
from jax.sharding import PartitionSpec as P

GRID_ROWS = 4


fresnel_coeff = 0.25
object_rate = 0.05
probe_rate = 0.15

LATE = [work * 1_000_000_000 for work in (0, 8, 0, 0, 8, 0, 8, 4)]

f32 = jnp.float32
bf16 = jnp.bfloat16


def from_behind(block, rows, cols):
    tiles = lax.axis_size("tile")
    across = tiles // GRID_ROWS

    def source(i):
        return (i // across - rows) % GRID_ROWS * across + (i % across - cols) % across

    return lax.ppermute(block, "tile", [(source(i), i) for i in range(tiles)])


def real_embed(part_re, part_im):
    upper_half = np.concatenate([part_re, -part_im], axis=1)
    lower_half = np.concatenate([part_im, part_re], axis=1)
    stacked = np.concatenate([upper_half, lower_half], axis=0)
    return jnp.asarray(stacked, dtype=f32).astype(bf16)


def build_tables(pixels):
    indices = np.arange(pixels)
    angles = indices[:, None] * indices[None, :] % pixels * (2.0 * math.pi / pixels)
    norm_scale = 1.0 / math.sqrt(pixels)
    dft_re = np.cos(angles) * norm_scale
    dft_im = -np.sin(angles) * norm_scale
    frequency = np.where(indices < pixels // 2, indices, indices - pixels)
    phases = -2.0 * math.pi * fresnel_coeff / pixels * (frequency * frequency)
    phase_sum = phases[:, None] + angles
    kern_re = np.sum(np.cos(phase_sum), axis=0) / pixels
    kern_im = np.sum(np.sin(phase_sum), axis=0) / pixels
    lag_index = (indices[:, None] - indices[None, :]) % pixels
    prop_re = kern_re[lag_index]
    prop_im = kern_im[lag_index]
    return real_embed(prop_re, prop_im), real_embed(dft_re, dft_im)


def dot(a, b):
    return jnp.dot(a, b, preferred_element_type=f32)


def spots(mine_ref, sent_ref):
    n = mine_ref.shape[1]
    mine = mine_ref[n:, :].astype(f32)
    busy = mine[2:3] > 0
    rows = jnp.where(busy, mine, sent_ref[n:, :].astype(f32)).astype(jnp.int32)
    return (rows[0:1], rows[1:2]), (rows[3:4], rows[4:5]), busy


def shift_in(spot):
    row, col = spot
    n = row.shape[1]
    i_out = lax.broadcasted_iota(jnp.int32, (n, 2 * n), 0)
    i_in = lax.broadcasted_iota(jnp.int32, (n, 2 * n), 1)
    j_in = lax.broadcasted_iota(jnp.int32, (2 * n, n), 0)
    j_out = lax.broadcasted_iota(jnp.int32, (2 * n, n), 1)
    rows = i_in == i_out + jnp.concatenate([row, row], axis=1)
    cols = j_in == j_out + col
    return rows.astype(f32).astype(bf16), cols.astype(f32).astype(bf16)


def shift_out(spot):
    row, col = spot
    n = row.shape[1]
    i_out = lax.broadcasted_iota(jnp.int32, (n, 2 * n), 0)
    i_in = lax.broadcasted_iota(jnp.int32, (n, 2 * n), 1)
    j_in = lax.broadcasted_iota(jnp.int32, (2 * n, n), 0)
    j_out = lax.broadcasted_iota(jnp.int32, (2 * n, n), 1)
    rows = j_in == j_out + row
    cols = i_in == i_out + jnp.concatenate([col, col], axis=1)
    return rows.astype(f32).astype(bf16), cols.astype(f32).astype(bf16)


def patch(shifts, own_ref, right_ref, below_ref, diag_ref, part):
    upper = jnp.concatenate([own_ref[part], right_ref[part]], axis=1)
    lower = jnp.concatenate([below_ref[part], diag_ref[part]], axis=1)
    rows = dot(shifts[0], jnp.concatenate([upper, lower], axis=0)).astype(bf16)
    return dot(rows, shifts[1])


def stacked(wave_re, wave_im):
    return jnp.concatenate([wave_re.astype(bf16), wave_im.astype(bf16)], axis=0)


def transform(table_ref, wave):
    n = wave.shape[1]
    table = table_ref[...]
    first = dot(table, wave)
    first = jnp.concatenate([first[:n].astype(bf16), (-first[n:]).astype(bf16)], axis=1)
    out = dot(first, table)
    return out[:, :n], out[:, n:]


def probe_plane(probe_ref, part, mode, modes):
    lane_tiles = 2
    n = probe_ref.shape[0] // (2 * lane_tiles * modes)
    step = lane_tiles * modes
    halves = [
        probe_ref[pl.ds(part * n * step + tile * modes + mode, n, stride=step), :]
        for tile in range(lane_tiles)
    ]
    return jnp.concatenate(halves, axis=1)


def message_kernel(offsets_ref, counts_ref, own_ref, patterns_ref, own_out, mine_ref, sent_ref):
    own_out[...] = own_ref[...]
    n = mine_ref.shape[1]
    at = lax.broadcasted_iota(jnp.int32, (16, n), 0)
    busy = (counts_ref[0, 0] == patterns_ref.shape[2]).astype(jnp.int32)
    for slot, ref in enumerate((mine_ref, sent_ref)):
        row, col = offsets_ref[0, 0, slot, 0], offsets_ref[0, 0, slot, 1]
        row2, col2 = offsets_ref[0, 0, 1 - slot, 0], offsets_ref[0, 0, 1 - slot, 1]
        rows = jnp.where(at == 0, row, jnp.where(at == 1, col, busy))
        rows = jnp.where(at == 3, row2, jnp.where(at == 4, col2, rows))
        ref[pl.ds(0, n), :] = patterns_ref[0, 0, slot]
        ref[pl.ds(n, 16), :] = rows.astype(f32).astype(bf16)


def ready_kernel(probe_ref, prop_ref, planes_ref, table_ref):
    table_ref[...] = prop_ref[...]
    n = planes_ref.shape[1]
    modes = planes_ref.shape[2] // n
    for part in range(2):
        for mode in range(modes):
            planes_ref[part, :, pl.ds(mode * n, n)] = probe_plane(probe_ref, part, mode, modes)


def arrive_kernel(
    mine_ref, sent_ref, own_ref, right_ref, below_ref, diag_ref, planes_ref, prop_ref,
    near_ref, arrive_ref,
):
    n = own_ref.shape[1]
    shifts = shift_in(spots(mine_ref, sent_ref)[0])
    tiles = (own_ref, right_ref.at[0], below_ref, diag_ref)
    near = [patch(shifts, *tiles, part) for part in range(2)]
    for part in range(2):
        near_ref[part] = near[part].astype(bf16)
    for mode in range(planes_ref.shape[2] // n):
        lanes = pl.ds(mode * n, n)
        p_re, p_im = planes_ref[0, :, lanes], planes_ref[1, :, lanes]
        wave = stacked(p_re * near[0] - p_im * near[1], p_re * near[1] + p_im * near[0])
        a_re, a_neg = transform(prop_ref, wave)
        arrive_ref[0, :, lanes] = a_re
        arrive_ref[1, :, lanes] = -a_neg


def gradient_kernel(
    mine_ref, sent_ref, own_ref, right_ref, below_ref, diag_ref, near_ref, arrive_ref, planes_ref,
    prop_ref, dft_ref,
    kept_ref, given_ref, keep_ref, give1_ref, give2_ref, grad_ref, term_ref, *, layer
):
    n = own_ref.shape[1]
    modes = planes_ref.shape[2] // n
    spot, _, busy = spots(mine_ref, sent_ref)
    shifts = shift_in(spot)
    tiles = (own_ref, right_ref.at[1], below_ref, diag_ref)
    far = [patch(shifts, *tiles, part) for part in range(2)]
    fields = []
    for mode in range(modes):
        lanes = pl.ds(mode * n, n)
        a_re, a_im = arrive_ref[0, :, lanes], arrive_ref[1, :, lanes]
        wave = stacked(far[0] * a_re - far[1] * a_im, far[0] * a_im + far[1] * a_re)
        fields.append(transform(dft_ref, wave))
    intensity = sum(f_re * f_re + f_neg * f_neg for f_re, f_neg in fields)
    pattern = jnp.where(busy, mine_ref[:n, :].astype(f32), sent_ref[:n, :].astype(f32))
    residual = intensity - pattern
    waves = []
    grad = [0.0, 0.0]
    for mode in range(modes):
        lanes = pl.ds(mode * n, n)
        f_re, f_neg = fields[mode]
        a_re, a_im = arrive_ref[0, :, lanes], arrive_ref[1, :, lanes]
        b_re, b_im = transform(dft_ref, stacked(f_re * residual, f_neg * residual))
        grad[0] += a_re * b_re + a_im * b_im
        grad[1] += a_re * b_im - a_im * b_re
        waves.append(stacked(far[0] * b_re + far[1] * b_im, far[1] * b_re - far[0] * b_im))
    for part in range(2):
        grad_ref[1, part] = grad[part].astype(bf16)
    grad = [0.0, 0.0]
    near = [near_ref[part].astype(f32) for part in range(2)]
    for mode in range(modes):
        lanes = pl.ds(mode * n, n)
        b_re, b_im = transform(prop_ref, waves[mode])
        p_re, p_im = planes_ref[0, :, lanes], planes_ref[1, :, lanes]
        grad[0] += p_re * b_re + p_im * b_im
        grad[1] += p_re * b_im - p_im * b_re
        term_ref[0, :, lanes] = (near[0] * b_re + near[1] * b_im).astype(bf16)
        term_ref[1, :, lanes] = (near[0] * b_im - near[1] * b_re).astype(bf16)
    core = place_of(core_group())
    keep_ref[...] = term_ref[core]
    give1_ref[...] = term_ref[1 - core, : n // 2]
    give2_ref[...] = term_ref[1 - core, n // 2 :]
    for part in range(2):
        grad_ref[0, part] = grad[part].astype(bf16)
    layer = layer()
    kept_ref[...] = grad_ref[layer]
    given_ref[...] = grad_ref[1 - layer]


def spread_kernel(
    mine_ref, sent_ref, kept_ref, got_ref, home_ref, below_ref, right_ref, diag_ref
):
    n = mine_ref.shape[1]
    first, second, _ = spots(mine_ref, sent_ref)
    rows1, cols1 = shift_out(first)
    rows2, cols2 = shift_out(second)
    cols = jnp.concatenate([cols1, cols2], axis=0)
    for part in range(2):
        tall1 = dot(rows1, kept_ref[part]).astype(bf16)
        tall2 = dot(rows2, got_ref[part]).astype(bf16)
        wide = dot(jnp.concatenate([tall1, tall2], axis=1), cols)
        home_ref[part] = wide[:n, :n]
        right_ref[part] = wide[:n, n:].astype(bf16)
        below_ref[part] = wide[n:, :n]
        diag_ref[part] = wide[n:, n:].astype(bf16)


def beside_kernel(home_ref, below_ref, right_ref, diag_ref, home_out, down_ref):
    home_out[...] = home_ref[...] + right_ref[...].astype(f32)
    down_ref[...] = (below_ref[...] + diag_ref[...].astype(f32)).astype(bf16)


def slice_kernel(layer, own0_ref, own1_ref, home_ref, above_ref, out_ref):
    grad = home_ref[...] + above_ref[...].astype(f32)
    own = jnp.where(layer() == 0, own0_ref[...].astype(f32), own1_ref[...].astype(f32))
    out_ref[...] = (own - object_rate * grad).astype(bf16)


def token_kernel(token_ref):
    token_ref[...] = jnp.zeros_like(token_ref)


def core_group():
    return [lax.axis_size("pos")]


def place_of(group):
    flat = lax.axis_index("tile") * lax.axis_size("pos") + lax.axis_index("pos")
    return sum(flat // mask % 2 * (1 << at) for at, mask in enumerate(group))


def job(kernel, outs, arrays, scalars=(), scratch=()):
    return kernel, list(outs), list(scalars), list(arrays), list(scratch)


def run(*jobs, flops=1_000_000, limit=4, after=()):
    vmem = pl.BlockSpec(memory_space=pltpu.VMEM)
    smem = pl.BlockSpec(memory_space=pltpu.SMEM)
    anywhere = pl.BlockSpec(memory_space=pl.ANY)
    kernels, outs, scalars, arrays, scratch = zip(*jobs)
    ins = [x + y for x, y in zip(scalars, arrays)]
    specs = [[smem] * len(x) + [vmem] * len(y) for x, y in zip(scalars, arrays)]

    def taken(refs, lists):
        parts = []
        for items in lists:
            parts.append(refs[: len(items)])
            refs = refs[len(items) :]
        return parts, refs

    def body(*refs):
        in_refs, refs = taken(refs, ins)
        out_refs, refs = taken(refs[len(after) :], outs)
        scratch_refs, _ = taken(refs, scratch)
        for kernel, *parts in zip(kernels, in_refs, out_refs, scratch_refs):
            kernel(*parts[0], *parts[1], *parts[2])

    moved = sum(x.size * x.dtype.itemsize for x in sum(ins, []) + sum(outs, []))
    results = pl.pallas_call(
        body,
        out_shape=sum(outs, []),
        in_specs=sum(specs, []) + [anywhere] * len(after),
        out_specs=[vmem] * len(sum(outs, [])),
        scratch_shapes=sum(scratch, []),
        compiler_params=pltpu.CompilerParams(vmem_limit_bytes=limit * 2**20),
        cost_estimate=pl.CostEstimate(flops=flops, bytes_accessed=moved, transcendentals=0),
    )(*sum(ins, []), *after)
    results, _ = taken(results, outs)
    return results[0] if len(jobs) == 1 else results


def finished(layer, step, modes, halves, probe, slices, like, after):
    vmem = pl.BlockSpec(memory_space=pltpu.VMEM)
    anywhere = pl.BlockSpec(memory_space=pl.ANY)
    inputs = [*halves, probe, *slices]

    def body(*refs):
        blocks, (out_probe, out_tile, new_ref, sems, probe_sems) = refs[3 : len(inputs)], refs[-5:]
        places = [layer(), 1 - layer()][: len(blocks)]
        copies = [
            pltpu.make_async_copy(block, out_tile.at[0, place], sems.at[at])
            for at, (block, place) in enumerate(zip(blocks, places))
        ]
        for copy in copies:
            copy.start()
        copies += probe_kernel(step, modes, *refs[:3], new_ref, out_probe, probe_sems)
        for copy in copies:
            copy.wait()

    return pl.pallas_call(
        body,
        out_shape=[shape_of(f32, *probe.shape), like],
        in_specs=[vmem] * len(inputs) + [anywhere] * len(after),
        out_specs=[anywhere, anywhere],
        scratch_shapes=[
            pltpu.VMEM(probe.shape, f32),
            pltpu.SemaphoreType.DMA((2,)),
            pltpu.SemaphoreType.DMA((8,)),
        ],
        compiler_params=pltpu.CompilerParams(vmem_limit_bytes=8 * 2**20),
        cost_estimate=pl.CostEstimate(
            flops=4 * probe.size, bytes_accessed=12 * probe.size, transcendentals=0
        ),
    )(*inputs, *after)


def shape_of(kind, *dims):
    return jax.ShapeDtypeStruct(dims, kind)


def gathered_message(patterns, offsets, counts):
    pixels = patterns.shape[4]
    all_counts = lax.all_gather(counts[0, 0], "pos")
    ends = jnp.cumsum(all_counts)
    rank = lax.axis_index("pos")
    source = jnp.sum((ends <= rank).astype(jnp.int32))
    slot = rank - (ends[source] - all_counts[source])
    spot = lax.all_gather(offsets[0, 0], "pos")[source, slot]
    pattern = lax.all_gather(patterns[0, 0], "pos")[source, slot]
    at = lax.broadcasted_iota(jnp.int32, (16, pixels), 0)
    rows = jnp.where(at == 0, spot[0], jnp.where(at == 1, spot[1], 0))
    return jnp.concatenate([pattern, rows.astype(bf16)], axis=0)


def fold_kernel(group, keep_ref, *refs):
    blocks = refs[-1]
    got = len(refs) - 1 - blocks.shape[0]
    arrived, keep_out, give_outs = refs[:got], refs[got], refs[got + 1 : -1]
    total = keep_ref[...].astype(f32)
    if arrived[0].shape != keep_ref.shape:
        total += jnp.concatenate([ref[...].astype(f32) for ref in arrived], axis=0)
    else:
        for ref in arrived:
            total += ref[...].astype(f32)
    size = blocks.shape[1]
    for block in range(blocks.shape[0]):
        blocks[block] = total[block * size : (block + 1) * size]
    here = place_of(group)
    keep_out[...] = blocks[here]
    for distance, ref in enumerate(give_outs, 1):
        ref[...] = blocks[here ^ distance].astype(bf16)


def add_kernel(keep_ref, *refs):
    total = keep_ref[...].astype(f32)
    for ref in refs[:-1]:
        total += ref[...].astype(f32)
    refs[-1][...] = total.astype(bf16)


def place_kernel(group, *refs):
    arrived, out_ref, blocks = refs[:-2], refs[-2], refs[-1]
    here = place_of(group)
    for distance, ref in enumerate(arrived):
        blocks[here ^ distance] = ref[...]
    size = blocks.shape[1]
    for block in range(blocks.shape[0]):
        out_ref[pl.ds(block * size, size), :] = blocks[block]


def probe_kernel(step, modes, mine_ref, other_ref, probe_ref, new_ref, out_hbm, sems):
    core = place_of(core_group())
    lane_tiles = 2
    n = mine_ref.shape[0]
    stride = lane_tiles * modes
    pieces = sems.shape[0] // 2
    size = n // pieces
    copies = []
    for part in range(2):
        for piece in range(pieces):
            at = pl.ds(piece * size, size)
            mine, other = mine_ref[at, :].astype(f32), other_ref[at, :].astype(f32)
            total = jnp.where(core == part, mine, other)
            start = (part * n + piece * size) * stride
            for mode in range(modes):
                for tile in range(lane_tiles):
                    lane = (mode * lane_tiles + tile) * 128
                    where = pl.ds(start + tile * modes + mode, size, stride=stride)
                    new_ref[where, :] = probe_ref[where, :] - step * total[:, lane : lane + 128]
            rows = pl.ds(start, size * stride)
            copy = pltpu.make_async_copy(
                new_ref.at[rows, :], out_hbm.at[rows, :], sems.at[len(copies)]
            )
            copy.start()
            copies.append(copy)
    return copies


def exchange_groups():
    tiles, owners = lax.axis_size("tile"), lax.axis_size("pos")
    bits = [1 << bit for bit in range(owners.bit_length() - 1)]
    bits += [owners << bit for bit in range(1, tiles.bit_length() - 1)]
    return [bits[at : at + 2] for at in range(0, len(bits), 2)]


def swap_with(x, group, distance):
    mask = sum(bit for at, bit in enumerate(group) if distance >> at & 1)
    devices = lax.axis_size("tile") * lax.axis_size("pos")
    return lax.ppermute(x, ("tile", "pos"), [(i, i ^ mask) for i in range(devices)])


def joined(group, x, arrived):
    blocks = 1 << len(group)
    return job(
        lambda *refs: place_kernel(group, *refs),
        [shape_of(bf16, x.shape[0] * blocks, x.shape[1])],
        [x] + arrived,
        scratch=[pltpu.VMEM((blocks,) + x.shape, bf16)],
    )


def added(x, arrived):
    return job(add_kernel, [shape_of(bf16, *x.shape)], [x] + arrived)


def swapped(x, group):
    return [swap_with(x, group, at) for at in range(1, 1 << len(group))]


def folded(group, keep, arrived):
    blocks = 1 << len(group)
    size, width = keep.shape[0] // blocks, keep.shape[1]
    return job(
        lambda *refs: fold_kernel(group, *refs),
        [shape_of(f32, size, width)] + [shape_of(bf16, size, width)] * (blocks - 1),
        [keep] + arrived,
        scratch=[pltpu.VMEM((blocks, size, width), f32)],
    )


def shards(tile_object, probe_modes, patterns, offsets, counts):
    _, pixels, modes, _ = probe_modes.shape
    width = modes * pixels
    lane_tiles = pixels // 128
    prop, dft = build_tables(pixels)
    tile = shape_of(bf16, 2, pixels, pixels)
    planes = shape_of(f32, 2, pixels, width)
    probe = probe_modes.reshape(2, pixels, modes, lane_tiles, 128)
    probe = probe.transpose(0, 1, 3, 2, 4).reshape(-1, 128)

    own = [tile_object[0, 0], tile_object[0, 1]]
    below0 = from_behind(own[0], -1, 0)
    right = from_behind(tile_object[0], 0, -1)
    exchanged = lax.axis_size("pos") == patterns.shape[2]
    message = shape_of(bf16, pixels + 16, pixels)
    own1, mine, sent = run(
        job(
            message_kernel,
            [tile, message, message],
            [own[1], patterns],
            scalars=[offsets, counts if exchanged else jnp.zeros_like(counts)],
        ),
        limit=4,
        after=[own[0]],
    )
    probe_planes, table = run(
        job(ready_kernel, [planes, shape_of(bf16, *prop.shape)], [probe, prop]),
        limit=8,
        after=[own1],
    )
    below1 = from_behind(own1, -1, 0)
    if exchanged:
        sent = lax.ppermute(sent, "pos", [(i, 1 - i) for i in range(2)])
    else:
        sent = gathered_message(patterns, offsets, counts)
    diag0 = from_behind(below0, 0, -1)
    diag1 = from_behind(below1, 0, -1)
    near, arrive = run(
        job(
            arrive_kernel,
            [tile, planes],
            [mine, sent, own[0], right, below0, diag0, probe_planes, table],
        ),
        flops=1_500_000_000,
        limit=16,
    )
    half = shape_of(bf16, pixels, width)
    quarter = shape_of(bf16, pixels // 2, width)
    grads = pltpu.VMEM((2, 2, pixels, pixels), bf16)
    this_layer = (lambda: lax.axis_index("pos")) if exchanged else (lambda: 0)
    kept, given, keep, *gives = run(
        job(
            lambda *refs: gradient_kernel(*refs, layer=this_layer),
            [tile, tile, half, quarter, quarter],
            [mine, sent, own1, right, below1, diag1, near, arrive, probe_planes, table, dft],
            scratch=[grads, pltpu.VMEM((2, pixels, width), bf16)],
        ),
        flops=4_000_000_000,
        limit=16,
    )

    swap = [(i, 1 - i) for i in range(2)]
    real = shape_of(f32, 2, pixels, pixels)
    like = shape_of(bf16, *tile_object.shape)

    def laid_out(patch, got, after, flops):
        return run(
            job(spread_kernel, [real, real, tile, tile], [mine, sent, patch, got]),
            limit=16,
            after=after,
            flops=flops,
        )

    core, groups = core_group(), exchange_groups()
    if exchanged:
        got = lax.ppermute(given, "pos", swap)
    arrived = [swap_with(x, core, 1) for x in gives]
    scattered = []
    while len(groups) > 1 and keep.shape[0] >> len(groups[0]) >= 16:
        group, groups = groups[0], groups[1:]
        keep, *gives = run(folded(group, keep, arrived))
        arrived = [swap_with(x, group, at) for at, x in enumerate(gives, 1)]
        scattered.append(group)
    first, second, *others = [[bit] for group in groups for bit in group]
    if exchanged:
        home, below, to_right, to_diag = laid_out(kept, got, [keep], LATE[0])
        from_left = [from_behind(x, 0, 1) for x in (to_right, to_diag)]
    (total,) = run(added(keep, arrived), after=[to_right] if exchanged else [], flops=LATE[1])
    (total,) = run(added(total, swapped(total, first)), flops=LATE[2])
    arrived = swapped(total, second)
    if exchanged:
        home, down = run(
            job(beside_kernel, [real, tile], [home, below, *from_left]),
            after=[total],
            flops=LATE[3],
        )
        above = from_behind(down, 1, 0)
    (total,) = run(added(total, arrived), after=[down] if exchanged else [], flops=LATE[4])
    for group in others:
        (total,) = run(added(total, swapped(total, group)))
    arrived = swapped(total, scattered[-1])
    if exchanged:
        (this_slice,) = run(
            job(
                lambda *refs: slice_kernel(this_layer, *refs),
                [tile],
                [own[0], own1, home, above],
            ),
            after=[total],
            flops=LATE[5],
        )
        other_slice = lax.ppermute(this_slice, "pos", swap)
    (total,) = run(
        joined(scattered[-1], total, arrived),
        after=[this_slice] if exchanged else [],
        flops=LATE[6],
    )
    for group in reversed(scattered[:-1]):
        (total,) = run(joined(group, total, swapped(total, group)))
    other_half = swap_with(total, core, 1)
    positions_all = lax.axis_size("tile") * lax.axis_size("pos") * (patterns.shape[2] // 2)
    step = probe_rate / math.sqrt(positions_all)
    halves = (total, other_half)
    if exchanged:
        token = run(
            job(token_kernel, [shape_of(f32, 8, 128)], []),
            after=[total, other_slice],
            flops=LATE[7],
        )
        slices = (this_slice, other_slice)
        new_probe, new_object = finished(this_layer, step, modes, halves, probe, slices, like, token)
    else:
        new_probe, _ = finished(this_layer, step, modes, halves, probe, (), like, ())
        slices = []
        for patch_grad, old in ((kept, own[0]), (given, own1)):
            home, below, to_right, to_diag = laid_out(patch_grad, jnp.zeros_like(kept), [], 0)
            from_left = [from_behind(x, 0, 1) for x in (to_right, to_diag)]
            home, down = run(job(beside_kernel, [real, tile], [home, below, *from_left]))
            grad = lax.psum(home + from_behind(down, 1, 0).astype(f32), "pos")
            slices.append((old.astype(f32) - object_rate * grad).astype(bf16))
        new_object = jnp.stack(slices)[None]
    new_probe = new_probe.reshape(2, pixels, lane_tiles, modes, 128).transpose(0, 1, 3, 2, 4)
    return (new_object, new_probe.reshape(probe_modes.shape))


def solution(mesh):
    placed = (
        P("tile", None, None, None, None),
        P(),
        P("tile", "pos", None, None, None),
        P("tile", "pos", None, None),
        P("tile", "pos"),
    )
    return jax.shard_map(
        shards,
        mesh=mesh,
        in_specs=placed,
        out_specs=(P("tile", None, None, None, None), P()),
        check_vma=False,
    )
```

```python
import math

import jax
import jax.numpy as jnp
import numpy as np
from jax import lax
from jax.experimental import pallas as pl
from jax.experimental.pallas import tpu as pltpu
from jax.sharding import PartitionSpec as P

GRID_ROWS = 4


fresnel_coeff = 0.25
object_rate = 0.05
probe_rate = 0.15

LATE = [work * 1_000_000_000 for work in (0, 8, 0, 0, 0, 0, 8, 4)]

f32 = jnp.float32
bf16 = jnp.bfloat16


def from_behind(block, rows, cols):
    tiles = lax.axis_size("tile")
    across = tiles // GRID_ROWS

    def source(i):
        return (i // across - rows) % GRID_ROWS * across + (i % across - cols) % across

    return lax.ppermute(block, "tile", [(source(i), i) for i in range(tiles)])


def real_embed(part_re, part_im):
    upper_half = np.concatenate([part_re, -part_im], axis=1)
    lower_half = np.concatenate([part_im, part_re], axis=1)
    stacked = np.concatenate([upper_half, lower_half], axis=0)
    return jnp.asarray(stacked, dtype=f32).astype(bf16)


def build_tables(pixels):
    indices = np.arange(pixels)
    angles = indices[:, None] * indices[None, :] % pixels * (2.0 * math.pi / pixels)
    norm_scale = 1.0 / math.sqrt(pixels)
    dft_re = np.cos(angles) * norm_scale
    dft_im = -np.sin(angles) * norm_scale
    frequency = np.where(indices < pixels // 2, indices, indices - pixels)
    phases = -2.0 * math.pi * fresnel_coeff / pixels * (frequency * frequency)
    phase_sum = phases[:, None] + angles
    kern_re = np.sum(np.cos(phase_sum), axis=0) / pixels
    kern_im = np.sum(np.sin(phase_sum), axis=0) / pixels
    lag_index = (indices[:, None] - indices[None, :]) % pixels
    prop_re = kern_re[lag_index]
    prop_im = kern_im[lag_index]
    return real_embed(prop_re, prop_im), real_embed(dft_re, dft_im)


def dot(a, b):
    return jnp.dot(a, b, preferred_element_type=f32)


def spots(mine_ref, sent_ref):
    n = mine_ref.shape[1]
    mine = mine_ref[n:, :].astype(f32)
    busy = mine[2:3] > 0
    rows = jnp.where(busy, mine, sent_ref[n:, :].astype(f32)).astype(jnp.int32)
    return (rows[0:1], rows[1:2]), (rows[3:4], rows[4:5]), busy


def shift_in(spot):
    row, col = spot
    n = row.shape[1]
    i_out = lax.broadcasted_iota(jnp.int32, (n, 2 * n), 0)
    i_in = lax.broadcasted_iota(jnp.int32, (n, 2 * n), 1)
    j_in = lax.broadcasted_iota(jnp.int32, (2 * n, n), 0)
    j_out = lax.broadcasted_iota(jnp.int32, (2 * n, n), 1)
    rows = i_in == i_out + jnp.concatenate([row, row], axis=1)
    cols = j_in == j_out + col
    return rows.astype(f32).astype(bf16), cols.astype(f32).astype(bf16)


def shift_out(spot):
    row, col = spot
    n = row.shape[1]
    i_out = lax.broadcasted_iota(jnp.int32, (n, 2 * n), 0)
    i_in = lax.broadcasted_iota(jnp.int32, (n, 2 * n), 1)
    j_in = lax.broadcasted_iota(jnp.int32, (2 * n, n), 0)
    j_out = lax.broadcasted_iota(jnp.int32, (2 * n, n), 1)
    rows = j_in == j_out + row
    cols = i_in == i_out + jnp.concatenate([col, col], axis=1)
    return rows.astype(f32).astype(bf16), cols.astype(f32).astype(bf16)


def patch(shifts, own_ref, right_ref, below_ref, diag_ref, part):
    upper = jnp.concatenate([own_ref[part], right_ref[part]], axis=1)
    lower = jnp.concatenate([below_ref[part], diag_ref[part]], axis=1)
    rows = dot(shifts[0], jnp.concatenate([upper, lower], axis=0)).astype(bf16)
    return dot(rows, shifts[1])


def stacked(wave_re, wave_im):
    return jnp.concatenate([wave_re.astype(bf16), wave_im.astype(bf16)], axis=0)


def transform(table_ref, wave):
    n = wave.shape[1]
    table = table_ref[...]
    first = dot(table, wave)
    first = jnp.concatenate([first[:n].astype(bf16), (-first[n:]).astype(bf16)], axis=1)
    out = dot(first, table)
    return out[:, :n], out[:, n:]


def probe_plane(probe_ref, part, mode, modes):
    lane_tiles = 2
    n = probe_ref.shape[0] // (2 * lane_tiles * modes)
    step = lane_tiles * modes
    halves = [
        probe_ref[pl.ds(part * n * step + tile * modes + mode, n, stride=step), :]
        for tile in range(lane_tiles)
    ]
    return jnp.concatenate(halves, axis=1)


def message_kernel(offsets_ref, counts_ref, own_ref, patterns_ref, own_out, mine_ref, sent_ref):
    own_out[...] = own_ref[...]
    n = mine_ref.shape[1]
    at = lax.broadcasted_iota(jnp.int32, (16, n), 0)
    busy = (counts_ref[0, 0] == patterns_ref.shape[2]).astype(jnp.int32)
    for slot, ref in enumerate((mine_ref, sent_ref)):
        row, col = offsets_ref[0, 0, slot, 0], offsets_ref[0, 0, slot, 1]
        row2, col2 = offsets_ref[0, 0, 1 - slot, 0], offsets_ref[0, 0, 1 - slot, 1]
        rows = jnp.where(at == 0, row, jnp.where(at == 1, col, busy))
        rows = jnp.where(at == 3, row2, jnp.where(at == 4, col2, rows))
        ref[pl.ds(0, n), :] = patterns_ref[0, 0, slot]
        ref[pl.ds(n, 16), :] = rows.astype(f32).astype(bf16)


def ready_kernel(probe_ref, prop_ref, planes_ref, table_ref):
    table_ref[...] = prop_ref[...]
    n = planes_ref.shape[1]
    modes = planes_ref.shape[2] // n
    for part in range(2):
        for mode in range(modes):
            planes_ref[part, :, pl.ds(mode * n, n)] = probe_plane(probe_ref, part, mode, modes)


def arrive_kernel(
    mine_ref, sent_ref, own_ref, right_ref, below_ref, diag_ref, planes_ref, prop_ref,
    near_ref, arrive_ref,
):
    n = own_ref.shape[1]
    shifts = shift_in(spots(mine_ref, sent_ref)[0])
    tiles = (own_ref, right_ref.at[0], below_ref, diag_ref)
    near = [patch(shifts, *tiles, part) for part in range(2)]
    for part in range(2):
        near_ref[part] = near[part].astype(bf16)
    for mode in range(planes_ref.shape[2] // n):
        lanes = pl.ds(mode * n, n)
        p_re, p_im = planes_ref[0, :, lanes], planes_ref[1, :, lanes]
        wave = stacked(p_re * near[0] - p_im * near[1], p_re * near[1] + p_im * near[0])
        a_re, a_neg = transform(prop_ref, wave)
        arrive_ref[0, :, lanes] = a_re
        arrive_ref[1, :, lanes] = -a_neg


def gradient_kernel(
    mine_ref, sent_ref, own_ref, right_ref, below_ref, diag_ref, near_ref, arrive_ref, planes_ref,
    prop_ref, dft_ref,
    kept_ref, given_ref, keep_ref, give1_ref, give2_ref, grad_ref, term_ref, *, layer
):
    n = own_ref.shape[1]
    modes = planes_ref.shape[2] // n
    spot, _, busy = spots(mine_ref, sent_ref)
    shifts = shift_in(spot)
    tiles = (own_ref, right_ref.at[1], below_ref, diag_ref)
    far = [patch(shifts, *tiles, part) for part in range(2)]
    fields = []
    for mode in range(modes):
        lanes = pl.ds(mode * n, n)
        a_re, a_im = arrive_ref[0, :, lanes], arrive_ref[1, :, lanes]
        wave = stacked(far[0] * a_re - far[1] * a_im, far[0] * a_im + far[1] * a_re)
        fields.append(transform(dft_ref, wave))
    intensity = sum(f_re * f_re + f_neg * f_neg for f_re, f_neg in fields)
    pattern = jnp.where(busy, mine_ref[:n, :].astype(f32), sent_ref[:n, :].astype(f32))
    residual = intensity - pattern
    waves = []
    grad = [0.0, 0.0]
    for mode in range(modes):
        lanes = pl.ds(mode * n, n)
        f_re, f_neg = fields[mode]
        a_re, a_im = arrive_ref[0, :, lanes], arrive_ref[1, :, lanes]
        b_re, b_im = transform(dft_ref, stacked(f_re * residual, f_neg * residual))
        grad[0] += a_re * b_re + a_im * b_im
        grad[1] += a_re * b_im - a_im * b_re
        waves.append(stacked(far[0] * b_re + far[1] * b_im, far[1] * b_re - far[0] * b_im))
    for part in range(2):
        grad_ref[1, part] = grad[part].astype(bf16)
    grad = [0.0, 0.0]
    near = [near_ref[part].astype(f32) for part in range(2)]
    for mode in range(modes):
        lanes = pl.ds(mode * n, n)
        b_re, b_im = transform(prop_ref, waves[mode])
        p_re, p_im = planes_ref[0, :, lanes], planes_ref[1, :, lanes]
        grad[0] += p_re * b_re + p_im * b_im
        grad[1] += p_re * b_im - p_im * b_re
        term_ref[0, :, lanes] = (near[0] * b_re + near[1] * b_im).astype(bf16)
        term_ref[1, :, lanes] = (near[0] * b_im - near[1] * b_re).astype(bf16)
    core = place_of(core_group())
    keep_ref[...] = term_ref[core]
    give1_ref[...] = term_ref[1 - core, : n // 2]
    give2_ref[...] = term_ref[1 - core, n // 2 :]
    for part in range(2):
        grad_ref[0, part] = grad[part].astype(bf16)
    layer = layer()
    kept_ref[...] = grad_ref[layer]
    given_ref[...] = grad_ref[1 - layer]


def spread_kernel(
    mine_ref, sent_ref, kept_ref, got_ref, home_ref, below_ref, right_ref, diag_ref
):
    n = mine_ref.shape[1]
    first, second, _ = spots(mine_ref, sent_ref)
    rows1, cols1 = shift_out(first)
    rows2, cols2 = shift_out(second)
    cols = jnp.concatenate([cols1, cols2], axis=0)
    for part in range(2):
        tall1 = dot(rows1, kept_ref[part]).astype(bf16)
        tall2 = dot(rows2, got_ref[part]).astype(bf16)
        wide = dot(jnp.concatenate([tall1, tall2], axis=1), cols)
        home_ref[part] = wide[:n, :n]
        right_ref[part] = wide[:n, n:].astype(bf16)
        below_ref[part] = wide[n:, :n]
        diag_ref[part] = wide[n:, n:].astype(bf16)


def beside_kernel(home_ref, below_ref, right_ref, diag_ref, home_out, down_ref):
    home_out[...] = home_ref[...] + right_ref[...].astype(f32)
    down_ref[...] = (below_ref[...] + diag_ref[...].astype(f32)).astype(bf16)


def slice_kernel(layer, own0_ref, own1_ref, home_ref, above_ref, out_ref):
    grad = home_ref[...] + above_ref[...].astype(f32)
    own = jnp.where(layer() == 0, own0_ref[...].astype(f32), own1_ref[...].astype(f32))
    out_ref[...] = (own - object_rate * grad).astype(bf16)


def token_kernel(token_ref):
    token_ref[...] = jnp.zeros_like(token_ref)


def core_group():
    return [lax.axis_size("pos")]


def place_of(group):
    flat = lax.axis_index("tile") * lax.axis_size("pos") + lax.axis_index("pos")
    return sum(flat // mask % 2 * (1 << at) for at, mask in enumerate(group))


def job(kernel, outs, arrays, scalars=(), scratch=()):
    return kernel, list(outs), list(scalars), list(arrays), list(scratch)


def run(*jobs, flops=1_000_000, limit=4, after=()):
    vmem = pl.BlockSpec(memory_space=pltpu.VMEM)
    smem = pl.BlockSpec(memory_space=pltpu.SMEM)
    anywhere = pl.BlockSpec(memory_space=pl.ANY)
    kernels, outs, scalars, arrays, scratch = zip(*jobs)
    ins = [x + y for x, y in zip(scalars, arrays)]
    specs = [[smem] * len(x) + [vmem] * len(y) for x, y in zip(scalars, arrays)]

    def taken(refs, lists):
        parts = []
        for items in lists:
            parts.append(refs[: len(items)])
            refs = refs[len(items) :]
        return parts, refs

    def body(*refs):
        in_refs, refs = taken(refs, ins)
        out_refs, refs = taken(refs[len(after) :], outs)
        scratch_refs, _ = taken(refs, scratch)
        for kernel, *parts in zip(kernels, in_refs, out_refs, scratch_refs):
            kernel(*parts[0], *parts[1], *parts[2])

    moved = sum(x.size * x.dtype.itemsize for x in sum(ins, []) + sum(outs, []))
    results = pl.pallas_call(
        body,
        out_shape=sum(outs, []),
        in_specs=sum(specs, []) + [anywhere] * len(after),
        out_specs=[vmem] * len(sum(outs, [])),
        scratch_shapes=sum(scratch, []),
        compiler_params=pltpu.CompilerParams(vmem_limit_bytes=limit * 2**20),
        cost_estimate=pl.CostEstimate(flops=flops, bytes_accessed=moved, transcendentals=0),
    )(*sum(ins, []), *after)
    results, _ = taken(results, outs)
    return results[0] if len(jobs) == 1 else results


def finished(layer, step, modes, halves, probe, slices, like, after):
    vmem = pl.BlockSpec(memory_space=pltpu.VMEM)
    anywhere = pl.BlockSpec(memory_space=pl.ANY)
    inputs = [*halves, probe, *slices]

    def body(*refs):
        blocks, (out_probe, out_tile, new_ref, sems, probe_sems) = refs[3 : len(inputs)], refs[-5:]
        places = [layer(), 1 - layer()][: len(blocks)]
        copies = [
            pltpu.make_async_copy(block, out_tile.at[0, place], sems.at[at])
            for at, (block, place) in enumerate(zip(blocks, places))
        ]
        for copy in copies:
            copy.start()
        copies += probe_kernel(step, modes, *refs[:3], new_ref, out_probe, probe_sems)
        for copy in copies:
            copy.wait()

    return pl.pallas_call(
        body,
        out_shape=[shape_of(f32, *probe.shape), like],
        in_specs=[vmem] * len(inputs) + [anywhere] * len(after),
        out_specs=[anywhere, anywhere],
        scratch_shapes=[
            pltpu.VMEM(probe.shape, f32),
            pltpu.SemaphoreType.DMA((2,)),
            pltpu.SemaphoreType.DMA((8,)),
        ],
        compiler_params=pltpu.CompilerParams(vmem_limit_bytes=8 * 2**20),
        cost_estimate=pl.CostEstimate(
            flops=4 * probe.size, bytes_accessed=12 * probe.size, transcendentals=0
        ),
    )(*inputs, *after)


def shape_of(kind, *dims):
    return jax.ShapeDtypeStruct(dims, kind)


def gathered_message(patterns, offsets, counts):
    pixels = patterns.shape[4]
    all_counts = lax.all_gather(counts[0, 0], "pos")
    ends = jnp.cumsum(all_counts)
    rank = lax.axis_index("pos")
    source = jnp.sum((ends <= rank).astype(jnp.int32))
    slot = rank - (ends[source] - all_counts[source])
    spot = lax.all_gather(offsets[0, 0], "pos")[source, slot]
    pattern = lax.all_gather(patterns[0, 0], "pos")[source, slot]
    at = lax.broadcasted_iota(jnp.int32, (16, pixels), 0)
    rows = jnp.where(at == 0, spot[0], jnp.where(at == 1, spot[1], 0))
    return jnp.concatenate([pattern, rows.astype(bf16)], axis=0)


def fold_kernel(group, keep_ref, *refs):
    blocks = refs[-1]
    got = len(refs) - 1 - blocks.shape[0]
    arrived, keep_out, give_outs = refs[:got], refs[got], refs[got + 1 : -1]
    total = keep_ref[...].astype(f32)
    if arrived[0].shape != keep_ref.shape:
        total += jnp.concatenate([ref[...].astype(f32) for ref in arrived], axis=0)
    else:
        for ref in arrived:
            total += ref[...].astype(f32)
    size = blocks.shape[1]
    for block in range(blocks.shape[0]):
        blocks[block] = total[block * size : (block + 1) * size]
    here = place_of(group)
    keep_out[...] = blocks[here]
    for distance, ref in enumerate(give_outs, 1):
        ref[...] = blocks[here ^ distance].astype(bf16)


def add_kernel(keep_ref, *refs):
    total = keep_ref[...].astype(f32)
    for ref in refs[:-1]:
        total += ref[...].astype(f32)
    refs[-1][...] = total.astype(bf16)


def place_kernel(group, *refs):
    arrived, out_ref, blocks = refs[:-2], refs[-2], refs[-1]
    here = place_of(group)
    for distance, ref in enumerate(arrived):
        blocks[here ^ distance] = ref[...]
    size = blocks.shape[1]
    for block in range(blocks.shape[0]):
        out_ref[pl.ds(block * size, size), :] = blocks[block]


def probe_kernel(step, modes, mine_ref, other_ref, probe_ref, new_ref, out_hbm, sems):
    core = place_of(core_group())
    lane_tiles = 2
    n = mine_ref.shape[0]
    stride = lane_tiles * modes
    pieces = sems.shape[0] // 2
    size = n // pieces
    copies = []
    for part in range(2):
        for piece in range(pieces):
            at = pl.ds(piece * size, size)
            mine, other = mine_ref[at, :].astype(f32), other_ref[at, :].astype(f32)
            total = jnp.where(core == part, mine, other)
            start = (part * n + piece * size) * stride
            for mode in range(modes):
                for tile in range(lane_tiles):
                    lane = (mode * lane_tiles + tile) * 128
                    where = pl.ds(start + tile * modes + mode, size, stride=stride)
                    new_ref[where, :] = probe_ref[where, :] - step * total[:, lane : lane + 128]
            rows = pl.ds(start, size * stride)
            copy = pltpu.make_async_copy(
                new_ref.at[rows, :], out_hbm.at[rows, :], sems.at[len(copies)]
            )
            copy.start()
            copies.append(copy)
    return copies


def exchange_groups():
    tiles, owners = lax.axis_size("tile"), lax.axis_size("pos")
    bits = [1 << bit for bit in range(owners.bit_length() - 1)]
    bits += [owners << bit for bit in range(1, tiles.bit_length() - 1)]
    return [bits[at : at + 2] for at in range(0, len(bits), 2)]


def swap_with(x, group, distance):
    mask = sum(bit for at, bit in enumerate(group) if distance >> at & 1)
    devices = lax.axis_size("tile") * lax.axis_size("pos")
    return lax.ppermute(x, ("tile", "pos"), [(i, i ^ mask) for i in range(devices)])


def joined(group, x, arrived):
    blocks = 1 << len(group)
    return job(
        lambda *refs: place_kernel(group, *refs),
        [shape_of(bf16, x.shape[0] * blocks, x.shape[1])],
        [x] + arrived,
        scratch=[pltpu.VMEM((blocks,) + x.shape, bf16)],
    )


def added(x, arrived):
    return job(add_kernel, [shape_of(bf16, *x.shape)], [x] + arrived)


def swapped(x, group):
    return [swap_with(x, group, at) for at in range(1, 1 << len(group))]


def folded(group, keep, arrived):
    blocks = 1 << len(group)
    size, width = keep.shape[0] // blocks, keep.shape[1]
    return job(
        lambda *refs: fold_kernel(group, *refs),
        [shape_of(f32, size, width)] + [shape_of(bf16, size, width)] * (blocks - 1),
        [keep] + arrived,
        scratch=[pltpu.VMEM((blocks, size, width), f32)],
    )


def shards(tile_object, probe_modes, patterns, offsets, counts):
    _, pixels, modes, _ = probe_modes.shape
    width = modes * pixels
    lane_tiles = pixels // 128
    prop, dft = build_tables(pixels)
    tile = shape_of(bf16, 2, pixels, pixels)
    planes = shape_of(f32, 2, pixels, width)
    probe = probe_modes.reshape(2, pixels, modes, lane_tiles, 128)
    probe = probe.transpose(0, 1, 3, 2, 4).reshape(-1, 128)

    own = [tile_object[0, 0], tile_object[0, 1]]
    below0 = from_behind(own[0], -1, 0)
    right = from_behind(tile_object[0], 0, -1)
    exchanged = lax.axis_size("pos") == patterns.shape[2]
    message = shape_of(bf16, pixels + 16, pixels)
    own1, mine, sent = run(
        job(
            message_kernel,
            [tile, message, message],
            [own[1], patterns],
            scalars=[offsets, counts if exchanged else jnp.zeros_like(counts)],
        ),
        limit=4,
        after=[own[0]],
    )
    probe_planes, table = run(
        job(ready_kernel, [planes, shape_of(bf16, *prop.shape)], [probe, prop]),
        limit=8,
        after=[own1],
    )
    below1 = from_behind(own1, -1, 0)
    if exchanged:
        sent = lax.ppermute(sent, "pos", [(i, 1 - i) for i in range(2)])
    else:
        sent = gathered_message(patterns, offsets, counts)
    diag0 = from_behind(below0, 0, -1)
    diag1 = from_behind(below1, 0, -1)
    near, arrive = run(
        job(
            arrive_kernel,
            [tile, planes],
            [mine, sent, own[0], right, below0, diag0, probe_planes, table],
        ),
        flops=1_500_000_000,
        limit=16,
    )
    half = shape_of(bf16, pixels, width)
    quarter = shape_of(bf16, pixels // 2, width)
    grads = pltpu.VMEM((2, 2, pixels, pixels), bf16)
    this_layer = (lambda: lax.axis_index("pos")) if exchanged else (lambda: 0)
    kept, given, keep, *gives = run(
        job(
            lambda *refs: gradient_kernel(*refs, layer=this_layer),
            [tile, tile, half, quarter, quarter],
            [mine, sent, own1, right, below1, diag1, near, arrive, probe_planes, table, dft],
            scratch=[grads, pltpu.VMEM((2, pixels, width), bf16)],
        ),
        flops=4_000_000_000,
        limit=16,
    )

    swap = [(i, 1 - i) for i in range(2)]
    real = shape_of(f32, 2, pixels, pixels)
    like = shape_of(bf16, *tile_object.shape)

    def laid_out(patch, got, after, flops):
        return run(
            job(spread_kernel, [real, real, tile, tile], [mine, sent, patch, got]),
            limit=16,
            after=after,
            flops=flops,
        )

    core, groups = core_group(), exchange_groups()
    if exchanged:
        got = lax.ppermute(given, "pos", swap)
    arrived = [swap_with(x, core, 1) for x in gives]
    scattered = []
    while len(groups) > 1 and keep.shape[0] >> len(groups[0]) >= 16:
        group, groups = groups[0], groups[1:]
        keep, *gives = run(folded(group, keep, arrived))
        arrived = [swap_with(x, group, at) for at, x in enumerate(gives, 1)]
        scattered.append(group)
    first, second, *others = [[bit] for group in groups for bit in group]
    if exchanged:
        home, below, to_right, to_diag = laid_out(kept, got, [keep], LATE[0])
        from_left = [from_behind(x, 0, 1) for x in (to_right, to_diag)]
    (total,) = run(added(keep, arrived), after=[to_right] if exchanged else [], flops=LATE[1])
    (total,) = run(added(total, swapped(total, first)), flops=LATE[2])
    arrived = swapped(total, second)
    if exchanged:
        home, down = run(
            job(beside_kernel, [real, tile], [home, below, *from_left]),
            after=[total],
            flops=LATE[3],
        )
        above = from_behind(down, 1, 0)
    (total,) = run(added(total, arrived), after=[down] if exchanged else [], flops=LATE[4])
    for group in others:
        (total,) = run(added(total, swapped(total, group)))
    arrived = swapped(total, scattered[-1])
    if exchanged:
        (this_slice,) = run(
            job(
                lambda *refs: slice_kernel(this_layer, *refs),
                [tile],
                [own[0], own1, home, above],
            ),
            after=[total],
            flops=LATE[5],
        )
        other_slice = lax.ppermute(this_slice, "pos", swap)
    (total,) = run(
        joined(scattered[-1], total, arrived),
        after=[this_slice] if exchanged else [],
        flops=LATE[6],
    )
    for group in reversed(scattered[:-1]):
        (total,) = run(joined(group, total, swapped(total, group)))
    other_half = swap_with(total, core, 1)
    positions_all = lax.axis_size("tile") * lax.axis_size("pos") * (patterns.shape[2] // 2)
    step = probe_rate / math.sqrt(positions_all)
    halves = (total, other_half)
    if exchanged:
        token = run(
            job(token_kernel, [shape_of(f32, 8, 128)], []),
            after=[total, other_slice],
            flops=LATE[7],
        )
        slices = (this_slice, other_slice)
        new_probe, new_object = finished(this_layer, step, modes, halves, probe, slices, like, token)
    else:
        new_probe, _ = finished(this_layer, step, modes, halves, probe, (), like, ())
        slices = []
        for patch_grad, old in ((kept, own[0]), (given, own1)):
            home, below, to_right, to_diag = laid_out(patch_grad, jnp.zeros_like(kept), [], 0)
            from_left = [from_behind(x, 0, 1) for x in (to_right, to_diag)]
            home, down = run(job(beside_kernel, [real, tile], [home, below, *from_left]))
            grad = lax.psum(home + from_behind(down, 1, 0).astype(f32), "pos")
            slices.append((old.astype(f32) - object_rate * grad).astype(bf16))
        new_object = jnp.stack(slices)[None]
    new_probe = new_probe.reshape(2, pixels, lane_tiles, modes, 128).transpose(0, 1, 3, 2, 4)
    return (new_object, new_probe.reshape(probe_modes.shape))


def solution(mesh):
    placed = (
        P("tile", None, None, None, None),
        P(),
        P("tile", "pos", None, None, None),
        P("tile", "pos", None, None),
        P("tile", "pos"),
    )
    return jax.shard_map(
        shards,
        mesh=mesh,
        in_specs=placed,
        out_specs=(P("tile", None, None, None, None), P()),
        check_vma=False,
    )
```

```python
import math

import jax
import jax.numpy as jnp
import numpy as np
from jax import lax
from jax.experimental import pallas as pl
from jax.experimental.pallas import tpu as pltpu
from jax.sharding import PartitionSpec as P

GRID_ROWS = 4


fresnel_coeff = 0.25
object_rate = 0.05
probe_rate = 0.15

LATE = [work * 1_000_000_000 for work in (0, 8, 0, 0, 8, 0, 8, 4)]

f32 = jnp.float32
bf16 = jnp.bfloat16


def from_below(block):
    tiles = lax.axis_size("tile")
    across = tiles // GRID_ROWS
    return lax.ppermute(block, "tile", [(i + across, i) for i in range(tiles - across)])


def from_behind(block, rows, cols):
    tiles = lax.axis_size("tile")
    across = tiles // GRID_ROWS

    def source(i):
        return (i // across - rows) % GRID_ROWS * across + (i % across - cols) % across

    return lax.ppermute(block, "tile", [(source(i), i) for i in range(tiles)])


def real_embed(part_re, part_im):
    upper_half = np.concatenate([part_re, -part_im], axis=1)
    lower_half = np.concatenate([part_im, part_re], axis=1)
    stacked = np.concatenate([upper_half, lower_half], axis=0)
    return jnp.asarray(stacked, dtype=f32).astype(bf16)


def build_tables(pixels):
    indices = np.arange(pixels)
    angles = indices[:, None] * indices[None, :] % pixels * (2.0 * math.pi / pixels)
    norm_scale = 1.0 / math.sqrt(pixels)
    dft_re = np.cos(angles) * norm_scale
    dft_im = -np.sin(angles) * norm_scale
    frequency = np.where(indices < pixels // 2, indices, indices - pixels)
    phases = -2.0 * math.pi * fresnel_coeff / pixels * (frequency * frequency)
    phase_sum = phases[:, None] + angles
    kern_re = np.sum(np.cos(phase_sum), axis=0) / pixels
    kern_im = np.sum(np.sin(phase_sum), axis=0) / pixels
    lag_index = (indices[:, None] - indices[None, :]) % pixels
    prop_re = kern_re[lag_index]
    prop_im = kern_im[lag_index]
    return real_embed(prop_re, prop_im), real_embed(dft_re, dft_im)


def dot(a, b):
    return jnp.dot(a, b, preferred_element_type=f32)


def spots(mine_ref, sent_ref):
    n = mine_ref.shape[1]
    mine = mine_ref[n:, :].astype(f32)
    busy = mine[2:3] > 0
    rows = jnp.where(busy, mine, sent_ref[n:, :].astype(f32)).astype(jnp.int32)
    return (rows[0:1], rows[1:2]), (rows[3:4], rows[4:5]), busy


def shift_in(spot):
    row, col = spot
    n = row.shape[1]
    i_out = lax.broadcasted_iota(jnp.int32, (n, 2 * n), 0)
    i_in = lax.broadcasted_iota(jnp.int32, (n, 2 * n), 1)
    j_in = lax.broadcasted_iota(jnp.int32, (2 * n, n), 0)
    j_out = lax.broadcasted_iota(jnp.int32, (2 * n, n), 1)
    rows = i_in == i_out + jnp.concatenate([row, row], axis=1)
    cols = j_in == j_out + col
    return rows.astype(f32).astype(bf16), cols.astype(f32).astype(bf16)


def shift_out(spot):
    row, col = spot
    n = row.shape[1]
    i_out = lax.broadcasted_iota(jnp.int32, (n, 2 * n), 0)
    i_in = lax.broadcasted_iota(jnp.int32, (n, 2 * n), 1)
    j_in = lax.broadcasted_iota(jnp.int32, (2 * n, n), 0)
    j_out = lax.broadcasted_iota(jnp.int32, (2 * n, n), 1)
    rows = j_in == j_out + row
    cols = i_in == i_out + jnp.concatenate([col, col], axis=1)
    return rows.astype(f32).astype(bf16), cols.astype(f32).astype(bf16)


def patch(shifts, own_ref, right_ref, below_ref, diag_ref, part):
    upper = jnp.concatenate([own_ref[part], right_ref[part]], axis=1)
    lower = jnp.concatenate([below_ref[part], diag_ref[part]], axis=1)
    rows = dot(shifts[0], jnp.concatenate([upper, lower], axis=0)).astype(bf16)
    return dot(rows, shifts[1])


def stacked(wave_re, wave_im):
    return jnp.concatenate([wave_re.astype(bf16), wave_im.astype(bf16)], axis=0)


def transform(table_ref, wave):
    n = wave.shape[1]
    table = table_ref[...]
    first = dot(table, wave)
    first = jnp.concatenate([first[:n].astype(bf16), (-first[n:]).astype(bf16)], axis=1)
    out = dot(first, table)
    return out[:, :n], out[:, n:]


def probe_plane(probe_ref, part, mode, modes):
    lane_tiles = 2
    n = probe_ref.shape[0] // (2 * lane_tiles * modes)
    step = lane_tiles * modes
    halves = [
        probe_ref[pl.ds(part * n * step + tile * modes + mode, n, stride=step), :]
        for tile in range(lane_tiles)
    ]
    return jnp.concatenate(halves, axis=1)


def message_kernel(offsets_ref, counts_ref, own_ref, patterns_ref, own_out, mine_ref, sent_ref):
    own_out[...] = own_ref[...]
    n = mine_ref.shape[1]
    at = lax.broadcasted_iota(jnp.int32, (16, n), 0)
    busy = (counts_ref[0, 0] == patterns_ref.shape[2]).astype(jnp.int32)
    for slot, ref in enumerate((mine_ref, sent_ref)):
        row, col = offsets_ref[0, 0, slot, 0], offsets_ref[0, 0, slot, 1]
        row2, col2 = offsets_ref[0, 0, 1 - slot, 0], offsets_ref[0, 0, 1 - slot, 1]
        rows = jnp.where(at == 0, row, jnp.where(at == 1, col, busy))
        rows = jnp.where(at == 3, row2, jnp.where(at == 4, col2, rows))
        ref[pl.ds(0, n), :] = patterns_ref[0, 0, slot]
        ref[pl.ds(n, 16), :] = rows.astype(f32).astype(bf16)


def ready_kernel(probe_ref, prop_ref, planes_ref, table_ref):
    table_ref[...] = prop_ref[...]
    n = planes_ref.shape[1]
    modes = planes_ref.shape[2] // n
    for part in range(2):
        for mode in range(modes):
            planes_ref[part, :, pl.ds(mode * n, n)] = probe_plane(probe_ref, part, mode, modes)


def arrive_kernel(
    mine_ref, sent_ref, own_ref, right_ref, below_ref, diag_ref, planes_ref, prop_ref,
    near_ref, arrive_ref,
):
    n = own_ref.shape[1]
    shifts = shift_in(spots(mine_ref, sent_ref)[0])
    tiles = (own_ref, right_ref.at[0], below_ref, diag_ref)
    near = [patch(shifts, *tiles, part) for part in range(2)]
    for part in range(2):
        near_ref[part] = near[part].astype(bf16)
    for mode in range(planes_ref.shape[2] // n):
        lanes = pl.ds(mode * n, n)
        p_re, p_im = planes_ref[0, :, lanes], planes_ref[1, :, lanes]
        wave = stacked(p_re * near[0] - p_im * near[1], p_re * near[1] + p_im * near[0])
        a_re, a_neg = transform(prop_ref, wave)
        arrive_ref[0, :, lanes] = a_re
        arrive_ref[1, :, lanes] = -a_neg


def gradient_kernel(
    mine_ref, sent_ref, own_ref, right_ref, below_ref, diag_ref, near_ref, arrive_ref, planes_ref,
    prop_ref, dft_ref,
    kept_ref, given_ref, keep_ref, give1_ref, give2_ref, grad_ref, term_ref, *, layer
):
    n = own_ref.shape[1]
    modes = planes_ref.shape[2] // n
    spot, _, busy = spots(mine_ref, sent_ref)
    shifts = shift_in(spot)
    tiles = (own_ref, right_ref.at[1], below_ref, diag_ref)
    far = [patch(shifts, *tiles, part) for part in range(2)]
    fields = []
    for mode in range(modes):
        lanes = pl.ds(mode * n, n)
        a_re, a_im = arrive_ref[0, :, lanes], arrive_ref[1, :, lanes]
        wave = stacked(far[0] * a_re - far[1] * a_im, far[0] * a_im + far[1] * a_re)
        fields.append(transform(dft_ref, wave))
    intensity = sum(f_re * f_re + f_neg * f_neg for f_re, f_neg in fields)
    pattern = jnp.where(busy, mine_ref[:n, :].astype(f32), sent_ref[:n, :].astype(f32))
    residual = intensity - pattern
    waves = []
    grad = [0.0, 0.0]
    for mode in range(modes):
        lanes = pl.ds(mode * n, n)
        f_re, f_neg = fields[mode]
        a_re, a_im = arrive_ref[0, :, lanes], arrive_ref[1, :, lanes]
        b_re, b_im = transform(dft_ref, stacked(f_re * residual, f_neg * residual))
        grad[0] += a_re * b_re + a_im * b_im
        grad[1] += a_re * b_im - a_im * b_re
        waves.append(stacked(far[0] * b_re + far[1] * b_im, far[1] * b_re - far[0] * b_im))
    for part in range(2):
        grad_ref[1, part] = grad[part].astype(bf16)
    grad = [0.0, 0.0]
    near = [near_ref[part].astype(f32) for part in range(2)]
    for mode in range(modes):
        lanes = pl.ds(mode * n, n)
        b_re, b_im = transform(prop_ref, waves[mode])
        p_re, p_im = planes_ref[0, :, lanes], planes_ref[1, :, lanes]
        grad[0] += p_re * b_re + p_im * b_im
        grad[1] += p_re * b_im - p_im * b_re
        term_ref[0, :, lanes] = (near[0] * b_re + near[1] * b_im).astype(bf16)
        term_ref[1, :, lanes] = (near[0] * b_im - near[1] * b_re).astype(bf16)
    core = place_of(core_group())
    keep_ref[...] = term_ref[core]
    give1_ref[...] = term_ref[1 - core, : n // 2]
    give2_ref[...] = term_ref[1 - core, n // 2 :]
    for part in range(2):
        grad_ref[0, part] = grad[part].astype(bf16)
    layer = layer()
    kept_ref[...] = grad_ref[layer]
    given_ref[...] = grad_ref[1 - layer]


def spread_kernel(
    mine_ref, sent_ref, kept_ref, got_ref, home_ref, below_ref, right_ref, diag_ref
):
    n = mine_ref.shape[1]
    first, second, _ = spots(mine_ref, sent_ref)
    rows1, cols1 = shift_out(first)
    rows2, cols2 = shift_out(second)
    cols = jnp.concatenate([cols1, cols2], axis=0)
    for part in range(2):
        tall1 = dot(rows1, kept_ref[part]).astype(bf16)
        tall2 = dot(rows2, got_ref[part]).astype(bf16)
        wide = dot(jnp.concatenate([tall1, tall2], axis=1), cols)
        home_ref[part] = wide[:n, :n]
        right_ref[part] = wide[:n, n:].astype(bf16)
        below_ref[part] = wide[n:, :n]
        diag_ref[part] = wide[n:, n:].astype(bf16)


def beside_kernel(home_ref, below_ref, right_ref, diag_ref, home_out, down_ref):
    home_out[...] = home_ref[...] + right_ref[...].astype(f32)
    down_ref[...] = (below_ref[...] + diag_ref[...].astype(f32)).astype(bf16)


def slice_kernel(layer, own0_ref, own1_ref, home_ref, above_ref, out_ref):
    grad = home_ref[...] + above_ref[...].astype(f32)
    own = jnp.where(layer() == 0, own0_ref[...].astype(f32), own1_ref[...].astype(f32))
    out_ref[...] = (own - object_rate * grad).astype(bf16)


def token_kernel(token_ref):
    token_ref[...] = jnp.zeros_like(token_ref)


def core_group():
    return [lax.axis_size("pos")]


def place_of(group):
    flat = lax.axis_index("tile") * lax.axis_size("pos") + lax.axis_index("pos")
    return sum(flat // mask % 2 * (1 << at) for at, mask in enumerate(group))


def job(kernel, outs, arrays, scalars=(), scratch=()):
    return kernel, list(outs), list(scalars), list(arrays), list(scratch)


def run(*jobs, flops=1_000_000, limit=4, after=()):
    vmem = pl.BlockSpec(memory_space=pltpu.VMEM)
    smem = pl.BlockSpec(memory_space=pltpu.SMEM)
    anywhere = pl.BlockSpec(memory_space=pl.ANY)
    kernels, outs, scalars, arrays, scratch = zip(*jobs)
    ins = [x + y for x, y in zip(scalars, arrays)]
    specs = [[smem] * len(x) + [vmem] * len(y) for x, y in zip(scalars, arrays)]

    def taken(refs, lists):
        parts = []
        for items in lists:
            parts.append(refs[: len(items)])
            refs = refs[len(items) :]
        return parts, refs

    def body(*refs):
        in_refs, refs = taken(refs, ins)
        out_refs, refs = taken(refs[len(after) :], outs)
        scratch_refs, _ = taken(refs, scratch)
        for kernel, *parts in zip(kernels, in_refs, out_refs, scratch_refs):
            kernel(*parts[0], *parts[1], *parts[2])

    moved = sum(x.size * x.dtype.itemsize for x in sum(ins, []) + sum(outs, []))
    results = pl.pallas_call(
        body,
        out_shape=sum(outs, []),
        in_specs=sum(specs, []) + [anywhere] * len(after),
        out_specs=[vmem] * len(sum(outs, [])),
        scratch_shapes=sum(scratch, []),
        compiler_params=pltpu.CompilerParams(vmem_limit_bytes=limit * 2**20),
        cost_estimate=pl.CostEstimate(flops=flops, bytes_accessed=moved, transcendentals=0),
    )(*sum(ins, []), *after)
    results, _ = taken(results, outs)
    return results[0] if len(jobs) == 1 else results


def finished(layer, step, modes, halves, probe, slices, like, after):
    vmem = pl.BlockSpec(memory_space=pltpu.VMEM)
    anywhere = pl.BlockSpec(memory_space=pl.ANY)
    inputs = [*halves, probe, *slices]

    def body(*refs):
        blocks, (out_probe, out_tile, new_ref, sems, probe_sems) = refs[3 : len(inputs)], refs[-5:]
        places = [layer(), 1 - layer()][: len(blocks)]
        copies = [
            pltpu.make_async_copy(block, out_tile.at[0, place], sems.at[at])
            for at, (block, place) in enumerate(zip(blocks, places))
        ]
        for copy in copies:
            copy.start()
        copies += probe_kernel(step, modes, *refs[:3], new_ref, out_probe, probe_sems)
        for copy in copies:
            copy.wait()

    return pl.pallas_call(
        body,
        out_shape=[shape_of(f32, *probe.shape), like],
        in_specs=[vmem] * len(inputs) + [anywhere] * len(after),
        out_specs=[anywhere, anywhere],
        scratch_shapes=[
            pltpu.VMEM(probe.shape, f32),
            pltpu.SemaphoreType.DMA((2,)),
            pltpu.SemaphoreType.DMA((8,)),
        ],
        compiler_params=pltpu.CompilerParams(vmem_limit_bytes=8 * 2**20),
        cost_estimate=pl.CostEstimate(
            flops=4 * probe.size, bytes_accessed=12 * probe.size, transcendentals=0
        ),
    )(*inputs, *after)


def shape_of(kind, *dims):
    return jax.ShapeDtypeStruct(dims, kind)


def gathered_message(patterns, offsets, counts):
    pixels = patterns.shape[4]
    all_counts = lax.all_gather(counts[0, 0], "pos")
    ends = jnp.cumsum(all_counts)
    rank = lax.axis_index("pos")
    source = jnp.sum((ends <= rank).astype(jnp.int32))
    slot = rank - (ends[source] - all_counts[source])
    spot = lax.all_gather(offsets[0, 0], "pos")[source, slot]
    pattern = lax.all_gather(patterns[0, 0], "pos")[source, slot]
    at = lax.broadcasted_iota(jnp.int32, (16, pixels), 0)
    rows = jnp.where(at == 0, spot[0], jnp.where(at == 1, spot[1], 0))
    return jnp.concatenate([pattern, rows.astype(bf16)], axis=0)


def fold_kernel(group, keep_ref, *refs):
    blocks = refs[-1]
    got = len(refs) - 1 - blocks.shape[0]
    arrived, keep_out, give_outs = refs[:got], refs[got], refs[got + 1 : -1]
    total = keep_ref[...].astype(f32)
    if arrived[0].shape != keep_ref.shape:
        total += jnp.concatenate([ref[...].astype(f32) for ref in arrived], axis=0)
    else:
        for ref in arrived:
            total += ref[...].astype(f32)
    size = blocks.shape[1]
    for block in range(blocks.shape[0]):
        blocks[block] = total[block * size : (block + 1) * size]
    here = place_of(group)
    keep_out[...] = blocks[here]
    for distance, ref in enumerate(give_outs, 1):
        ref[...] = blocks[here ^ distance].astype(bf16)


def add_kernel(keep_ref, *refs):
    total = keep_ref[...].astype(f32)
    for ref in refs[:-1]:
        total += ref[...].astype(f32)
    refs[-1][...] = total.astype(bf16)


def place_kernel(group, *refs):
    arrived, out_ref, blocks = refs[:-2], refs[-2], refs[-1]
    here = place_of(group)
    for distance, ref in enumerate(arrived):
        blocks[here ^ distance] = ref[...]
    size = blocks.shape[1]
    for block in range(blocks.shape[0]):
        out_ref[pl.ds(block * size, size), :] = blocks[block]


def probe_kernel(step, modes, mine_ref, other_ref, probe_ref, new_ref, out_hbm, sems):
    core = place_of(core_group())
    lane_tiles = 2
    n = mine_ref.shape[0]
    stride = lane_tiles * modes
    pieces = sems.shape[0] // 2
    size = n // pieces
    copies = []
    for part in range(2):
        for piece in range(pieces):
            at = pl.ds(piece * size, size)
            mine, other = mine_ref[at, :].astype(f32), other_ref[at, :].astype(f32)
            total = jnp.where(core == part, mine, other)
            start = (part * n + piece * size) * stride
            for mode in range(modes):
                for tile in range(lane_tiles):
                    lane = (mode * lane_tiles + tile) * 128
                    where = pl.ds(start + tile * modes + mode, size, stride=stride)
                    new_ref[where, :] = probe_ref[where, :] - step * total[:, lane : lane + 128]
            rows = pl.ds(start, size * stride)
            copy = pltpu.make_async_copy(
                new_ref.at[rows, :], out_hbm.at[rows, :], sems.at[len(copies)]
            )
            copy.start()
            copies.append(copy)
    return copies


def exchange_groups():
    tiles, owners = lax.axis_size("tile"), lax.axis_size("pos")
    bits = [1 << bit for bit in range(owners.bit_length() - 1)]
    bits += [owners << bit for bit in range(1, tiles.bit_length() - 1)]
    return [bits[at : at + 2] for at in range(0, len(bits), 2)]


def swap_with(x, group, distance):
    mask = sum(bit for at, bit in enumerate(group) if distance >> at & 1)
    devices = lax.axis_size("tile") * lax.axis_size("pos")
    return lax.ppermute(x, ("tile", "pos"), [(i, i ^ mask) for i in range(devices)])


def joined(group, x, arrived):
    blocks = 1 << len(group)
    return job(
        lambda *refs: place_kernel(group, *refs),
        [shape_of(bf16, x.shape[0] * blocks, x.shape[1])],
        [x] + arrived,
        scratch=[pltpu.VMEM((blocks,) + x.shape, bf16)],
    )


def added(x, arrived):
    return job(add_kernel, [shape_of(bf16, *x.shape)], [x] + arrived)


def swapped(x, group):
    return [swap_with(x, group, at) for at in range(1, 1 << len(group))]


def folded(group, keep, arrived):
    blocks = 1 << len(group)
    size, width = keep.shape[0] // blocks, keep.shape[1]
    return job(
        lambda *refs: fold_kernel(group, *refs),
        [shape_of(f32, size, width)] + [shape_of(bf16, size, width)] * (blocks - 1),
        [keep] + arrived,
        scratch=[pltpu.VMEM((blocks, size, width), f32)],
    )


def shards(tile_object, probe_modes, patterns, offsets, counts):
    _, pixels, modes, _ = probe_modes.shape
    width = modes * pixels
    lane_tiles = pixels // 128
    prop, dft = build_tables(pixels)
    tile = shape_of(bf16, 2, pixels, pixels)
    planes = shape_of(f32, 2, pixels, width)
    probe = probe_modes.reshape(2, pixels, modes, lane_tiles, 128)
    probe = probe.transpose(0, 1, 3, 2, 4).reshape(-1, 128)

    own = [tile_object[0, 0], tile_object[0, 1]]
    below0 = from_behind(own[0], -1, 0)
    right = from_behind(tile_object[0], 0, -1)
    exchanged = lax.axis_size("pos") == patterns.shape[2]
    message = shape_of(bf16, pixels + 16, pixels)
    own1, mine, sent = run(
        job(
            message_kernel,
            [tile, message, message],
            [own[1], patterns],
            scalars=[offsets, counts if exchanged else jnp.zeros_like(counts)],
        ),
        limit=4,
        after=[own[0]],
    )
    probe_planes, table = run(
        job(ready_kernel, [planes, shape_of(bf16, *prop.shape)], [probe, prop]),
        limit=8,
        after=[own1],
    )
    below1 = from_below(own1)
    if exchanged:
        sent = lax.ppermute(sent, "pos", [(i, 1 - i) for i in range(2)])
    else:
        sent = gathered_message(patterns, offsets, counts)
    diag0 = from_behind(below0, 0, -1)
    diag1 = from_behind(below1, 0, -1)
    near, arrive = run(
        job(
            arrive_kernel,
            [tile, planes],
            [mine, sent, own[0], right, below0, diag0, probe_planes, table],
        ),
        flops=1_500_000_000,
        limit=16,
    )
    half = shape_of(bf16, pixels, width)
    quarter = shape_of(bf16, pixels // 2, width)
    grads = pltpu.VMEM((2, 2, pixels, pixels), bf16)
    this_layer = (lambda: lax.axis_index("pos")) if exchanged else (lambda: 0)
    kept, given, keep, *gives = run(
        job(
            lambda *refs: gradient_kernel(*refs, layer=this_layer),
            [tile, tile, half, quarter, quarter],
            [mine, sent, own1, right, below1, diag1, near, arrive, probe_planes, table, dft],
            scratch=[grads, pltpu.VMEM((2, pixels, width), bf16)],
        ),
        flops=4_000_000_000,
        limit=16,
    )

    swap = [(i, 1 - i) for i in range(2)]
    real = shape_of(f32, 2, pixels, pixels)
    like = shape_of(bf16, *tile_object.shape)

    def laid_out(patch, got, after, flops):
        return run(
            job(spread_kernel, [real, real, tile, tile], [mine, sent, patch, got]),
            limit=16,
            after=after,
            flops=flops,
        )

    core, groups = core_group(), exchange_groups()
    if exchanged:
        got = lax.ppermute(given, "pos", swap)
    arrived = [swap_with(x, core, 1) for x in gives]
    scattered = []
    while len(groups) > 1 and keep.shape[0] >> len(groups[0]) >= 16:
        group, groups = groups[0], groups[1:]
        keep, *gives = run(folded(group, keep, arrived))
        arrived = [swap_with(x, group, at) for at, x in enumerate(gives, 1)]
        scattered.append(group)
    first, second, *others = [[bit] for group in groups for bit in group]
    if exchanged:
        home, below, to_right, to_diag = laid_out(kept, got, [keep], LATE[0])
        from_left = [from_behind(x, 0, 1) for x in (to_right, to_diag)]
    (total,) = run(added(keep, arrived), after=[to_right] if exchanged else [], flops=LATE[1])
    (total,) = run(added(total, swapped(total, first)), flops=LATE[2])
    arrived = swapped(total, second)
    if exchanged:
        home, down = run(
            job(beside_kernel, [real, tile], [home, below, *from_left]),
            after=[total],
            flops=LATE[3],
        )
        above = from_behind(down, 1, 0)
    (total,) = run(added(total, arrived), after=[down] if exchanged else [], flops=LATE[4])
    for group in others:
        (total,) = run(added(total, swapped(total, group)))
    arrived = swapped(total, scattered[-1])
    if exchanged:
        (this_slice,) = run(
            job(
                lambda *refs: slice_kernel(this_layer, *refs),
                [tile],
                [own[0], own1, home, above],
            ),
            after=[total],
            flops=LATE[5],
        )
        other_slice = lax.ppermute(this_slice, "pos", swap)
    (total,) = run(
        joined(scattered[-1], total, arrived),
        after=[this_slice] if exchanged else [],
        flops=LATE[6],
    )
    for group in reversed(scattered[:-1]):
        (total,) = run(joined(group, total, swapped(total, group)))
    other_half = swap_with(total, core, 1)
    positions_all = lax.axis_size("tile") * lax.axis_size("pos") * (patterns.shape[2] // 2)
    step = probe_rate / math.sqrt(positions_all)
    halves = (total, other_half)
    if exchanged:
        token = run(
            job(token_kernel, [shape_of(f32, 8, 128)], []),
            after=[total, other_slice],
            flops=LATE[7],
        )
        slices = (this_slice, other_slice)
        new_probe, new_object = finished(this_layer, step, modes, halves, probe, slices, like, token)
    else:
        new_probe, _ = finished(this_layer, step, modes, halves, probe, (), like, ())
        slices = []
        for patch_grad, old in ((kept, own[0]), (given, own1)):
            home, below, to_right, to_diag = laid_out(patch_grad, jnp.zeros_like(kept), [], 0)
            from_left = [from_behind(x, 0, 1) for x in (to_right, to_diag)]
            home, down = run(job(beside_kernel, [real, tile], [home, below, *from_left]))
            grad = lax.psum(home + from_behind(down, 1, 0).astype(f32), "pos")
            slices.append((old.astype(f32) - object_rate * grad).astype(bf16))
        new_object = jnp.stack(slices)[None]
    new_probe = new_probe.reshape(2, pixels, lane_tiles, modes, 128).transpose(0, 1, 3, 2, 4)
    return (new_object, new_probe.reshape(probe_modes.shape))


def solution(mesh):
    placed = (
        P("tile", None, None, None, None),
        P(),
        P("tile", "pos", None, None, None),
        P("tile", "pos", None, None),
        P("tile", "pos"),
    )
    return jax.shard_map(
        shards,
        mesh=mesh,
        in_specs=placed,
        out_specs=(P("tile", None, None, None, None), P()),
        check_vma=False,
    )
```

```python
import math

import jax
import jax.numpy as jnp
import numpy as np
from jax import lax
from jax.experimental import pallas as pl
from jax.experimental.pallas import tpu as pltpu
from jax.sharding import PartitionSpec as P

GRID_ROWS = 4


fresnel_coeff = 0.25
object_rate = 0.05
probe_rate = 0.15

LATE = [work * 1_000_000_000 for work in (0, 8, 0, 0, 8, 0, 8, 4)]

f32 = jnp.float32
bf16 = jnp.bfloat16


def from_behind(block, rows, cols):
    tiles = lax.axis_size("tile")
    across = tiles // GRID_ROWS

    def source(i):
        return (i // across - rows) % GRID_ROWS * across + (i % across - cols) % across

    return lax.ppermute(block, "tile", [(source(i), i) for i in range(tiles)])


def real_embed(part_re, part_im):
    upper_half = np.concatenate([part_re, -part_im], axis=1)
    lower_half = np.concatenate([part_im, part_re], axis=1)
    stacked = np.concatenate([upper_half, lower_half], axis=0)
    return jnp.asarray(stacked, dtype=f32).astype(bf16)


def build_tables(pixels):
    indices = np.arange(pixels)
    angles = indices[:, None] * indices[None, :] % pixels * (2.0 * math.pi / pixels)
    norm_scale = 1.0 / math.sqrt(pixels)
    dft_re = np.cos(angles) * norm_scale
    dft_im = -np.sin(angles) * norm_scale
    frequency = np.where(indices < pixels // 2, indices, indices - pixels)
    phases = -2.0 * math.pi * fresnel_coeff / pixels * (frequency * frequency)
    phase_sum = phases[:, None] + angles
    kern_re = np.sum(np.cos(phase_sum), axis=0) / pixels
    kern_im = np.sum(np.sin(phase_sum), axis=0) / pixels
    lag_index = (indices[:, None] - indices[None, :]) % pixels
    prop_re = kern_re[lag_index]
    prop_im = kern_im[lag_index]
    return real_embed(prop_re, prop_im), real_embed(dft_re, dft_im)


def dot(a, b):
    return jnp.dot(a, b, preferred_element_type=f32)


def spots(mine_ref, sent_ref):
    n = mine_ref.shape[1]
    mine = mine_ref[n:, :].astype(f32)
    busy = mine[2:3] > 0
    rows = jnp.where(busy, mine, sent_ref[n:, :].astype(f32)).astype(jnp.int32)
    return (rows[0:1], rows[1:2]), (rows[3:4], rows[4:5]), busy


def shift_in(spot):
    row, col = spot
    n = row.shape[1]
    i_out = lax.broadcasted_iota(jnp.int32, (n, 2 * n), 0)
    i_in = lax.broadcasted_iota(jnp.int32, (n, 2 * n), 1)
    j_in = lax.broadcasted_iota(jnp.int32, (2 * n, n), 0)
    j_out = lax.broadcasted_iota(jnp.int32, (2 * n, n), 1)
    rows = i_in == i_out + jnp.concatenate([row, row], axis=1)
    cols = j_in == j_out + col
    return rows.astype(f32).astype(bf16), cols.astype(f32).astype(bf16)


def shift_out(spot):
    row, col = spot
    n = row.shape[1]
    i_out = lax.broadcasted_iota(jnp.int32, (n, 2 * n), 0)
    i_in = lax.broadcasted_iota(jnp.int32, (n, 2 * n), 1)
    j_in = lax.broadcasted_iota(jnp.int32, (2 * n, n), 0)
    j_out = lax.broadcasted_iota(jnp.int32, (2 * n, n), 1)
    rows = j_in == j_out + row
    cols = i_in == i_out + jnp.concatenate([col, col], axis=1)
    return rows.astype(f32).astype(bf16), cols.astype(f32).astype(bf16)


def patch(shifts, own_ref, right_ref, below_ref, diag_ref, part):
    upper = jnp.concatenate([own_ref[part], right_ref[part]], axis=1)
    lower = jnp.concatenate([below_ref[part], diag_ref[part]], axis=1)
    rows = dot(shifts[0], jnp.concatenate([upper, lower], axis=0)).astype(bf16)
    return dot(rows, shifts[1])


def stacked(wave_re, wave_im):
    return jnp.concatenate([wave_re.astype(bf16), wave_im.astype(bf16)], axis=0)


def transform(table_ref, wave):
    n = wave.shape[1]
    table = table_ref[...]
    first = dot(table, wave)
    first = jnp.concatenate([first[:n].astype(bf16), (-first[n:]).astype(bf16)], axis=1)
    out = dot(first, table)
    return out[:, :n], out[:, n:]


def probe_plane(probe_ref, part, mode, modes):
    lane_tiles = 2
    n = probe_ref.shape[0] // (2 * lane_tiles * modes)
    step = lane_tiles * modes
    halves = [
        probe_ref[pl.ds(part * n * step + tile * modes + mode, n, stride=step), :]
        for tile in range(lane_tiles)
    ]
    return jnp.concatenate(halves, axis=1)


def message_kernel(offsets_ref, counts_ref, own_ref, patterns_ref, own_out, mine_ref, sent_ref):
    own_out[...] = own_ref[...]
    n = mine_ref.shape[1]
    at = lax.broadcasted_iota(jnp.int32, (16, n), 0)
    busy = (counts_ref[0, 0] == patterns_ref.shape[2]).astype(jnp.int32)
    for slot, ref in enumerate((mine_ref, sent_ref)):
        row, col = offsets_ref[0, 0, slot, 0], offsets_ref[0, 0, slot, 1]
        row2, col2 = offsets_ref[0, 0, 1 - slot, 0], offsets_ref[0, 0, 1 - slot, 1]
        rows = jnp.where(at == 0, row, jnp.where(at == 1, col, busy))
        rows = jnp.where(at == 3, row2, jnp.where(at == 4, col2, rows))
        ref[pl.ds(0, n), :] = patterns_ref[0, 0, slot]
        ref[pl.ds(n, 16), :] = rows.astype(f32).astype(bf16)


def ready_kernel(probe_ref, prop_ref, planes_ref, table_ref):
    table_ref[...] = prop_ref[...]
    n = planes_ref.shape[1]
    modes = planes_ref.shape[2] // n
    for part in range(2):
        for mode in range(modes):
            planes_ref[part, :, pl.ds(mode * n, n)] = probe_plane(probe_ref, part, mode, modes)


def arrive_kernel(
    mine_ref, sent_ref, own_ref, right_ref, below_ref, diag_ref, planes_ref, prop_ref,
    near_ref, arrive_ref,
):
    n = own_ref.shape[1]
    shifts = shift_in(spots(mine_ref, sent_ref)[0])
    tiles = (own_ref, right_ref.at[0], below_ref, diag_ref)
    near = [patch(shifts, *tiles, part) for part in range(2)]
    for part in range(2):
        near_ref[part] = near[part].astype(bf16)
    for mode in range(planes_ref.shape[2] // n):
        lanes = pl.ds(mode * n, n)
        p_re, p_im = planes_ref[0, :, lanes], planes_ref[1, :, lanes]
        wave = stacked(p_re * near[0] - p_im * near[1], p_re * near[1] + p_im * near[0])
        a_re, a_neg = transform(prop_ref, wave)
        arrive_ref[0, :, lanes] = a_re
        arrive_ref[1, :, lanes] = -a_neg


def gradient_kernel(
    mine_ref, sent_ref, own_ref, right_ref, below_ref, diag_ref, near_ref, arrive_ref, planes_ref,
    prop_ref, dft_ref,
    kept_ref, given_ref, keep_ref, give1_ref, give2_ref, grad_ref, term_ref, *, layer
):
    n = own_ref.shape[1]
    modes = planes_ref.shape[2] // n
    spot, _, busy = spots(mine_ref, sent_ref)
    shifts = shift_in(spot)
    tiles = (own_ref, right_ref.at[1], below_ref, diag_ref)
    far = [patch(shifts, *tiles, part) for part in range(2)]
    fields = []
    for mode in range(modes):
        lanes = pl.ds(mode * n, n)
        a_re, a_im = arrive_ref[0, :, lanes], arrive_ref[1, :, lanes]
        wave = stacked(far[0] * a_re - far[1] * a_im, far[0] * a_im + far[1] * a_re)
        fields.append(transform(dft_ref, wave))
    intensity = sum(f_re * f_re + f_neg * f_neg for f_re, f_neg in fields)
    pattern = jnp.where(busy, mine_ref[:n, :].astype(f32), sent_ref[:n, :].astype(f32))
    residual = intensity - pattern
    waves = []
    grad = [0.0, 0.0]
    for mode in range(modes):
        lanes = pl.ds(mode * n, n)
        f_re, f_neg = fields[mode]
        a_re, a_im = arrive_ref[0, :, lanes], arrive_ref[1, :, lanes]
        b_re, b_im = transform(dft_ref, stacked(f_re * residual, f_neg * residual))
        grad[0] += a_re * b_re + a_im * b_im
        grad[1] += a_re * b_im - a_im * b_re
        waves.append(stacked(far[0] * b_re + far[1] * b_im, far[1] * b_re - far[0] * b_im))
    for part in range(2):
        grad_ref[1, part] = grad[part].astype(bf16)
    grad = [0.0, 0.0]
    near = [near_ref[part].astype(f32) for part in range(2)]
    for mode in range(modes):
        lanes = pl.ds(mode * n, n)
        b_re, b_im = transform(prop_ref, waves[mode])
        p_re, p_im = planes_ref[0, :, lanes], planes_ref[1, :, lanes]
        grad[0] += p_re * b_re + p_im * b_im
        grad[1] += p_re * b_im - p_im * b_re
        term_ref[0, :, lanes] = (near[0] * b_re + near[1] * b_im).astype(bf16)
        term_ref[1, :, lanes] = (near[0] * b_im - near[1] * b_re).astype(bf16)
    core = place_of(core_group())
    keep_ref[...] = term_ref[core]
    give1_ref[...] = term_ref[1 - core, : n // 2]
    give2_ref[...] = term_ref[1 - core, n // 2 :]
    for part in range(2):
        grad_ref[0, part] = grad[part].astype(bf16)
    layer = layer()
    kept_ref[...] = grad_ref[layer]
    given_ref[...] = grad_ref[1 - layer]


def spread_kernel(
    mine_ref, sent_ref, kept_ref, got_ref, home_ref, below_ref, right_ref, diag_ref
):
    n = mine_ref.shape[1]
    first, second, _ = spots(mine_ref, sent_ref)
    rows1, cols1 = shift_out(first)
    rows2, cols2 = shift_out(second)
    cols = jnp.concatenate([cols1, cols2], axis=0)
    for part in range(2):
        tall1 = dot(rows1, kept_ref[part]).astype(bf16)
        tall2 = dot(rows2, got_ref[part]).astype(bf16)
        wide = dot(jnp.concatenate([tall1, tall2], axis=1), cols)
        home_ref[part] = wide[:n, :n]
        right_ref[part] = wide[:n, n:].astype(bf16)
        below_ref[part] = wide[n:, :n]
        diag_ref[part] = wide[n:, n:].astype(bf16)


def beside_kernel(home_ref, below_ref, right_ref, diag_ref, home_out, down_ref):
    home_out[...] = home_ref[...] + right_ref[...].astype(f32)
    down_ref[...] = (below_ref[...] + diag_ref[...].astype(f32)).astype(bf16)


def slice_kernel(layer, own0_ref, own1_ref, home_ref, above_ref, out_ref):
    grad = home_ref[...] + above_ref[...].astype(f32)
    own = jnp.where(layer() == 0, own0_ref[...].astype(f32), own1_ref[...].astype(f32))
    out_ref[...] = (own - object_rate * grad).astype(bf16)


def token_kernel(token_ref):
    token_ref[...] = jnp.zeros_like(token_ref)


def core_group():
    return [lax.axis_size("pos")]


def place_of(group):
    flat = lax.axis_index("tile") * lax.axis_size("pos") + lax.axis_index("pos")
    return sum(flat // mask % 2 * (1 << at) for at, mask in enumerate(group))


def job(kernel, outs, arrays, scalars=(), scratch=()):
    return kernel, list(outs), list(scalars), list(arrays), list(scratch)


def run(*jobs, flops=1_000_000, limit=4, after=()):
    vmem = pl.BlockSpec(memory_space=pltpu.VMEM)
    smem = pl.BlockSpec(memory_space=pltpu.SMEM)
    anywhere = pl.BlockSpec(memory_space=pl.ANY)
    kernels, outs, scalars, arrays, scratch = zip(*jobs)
    ins = [x + y for x, y in zip(scalars, arrays)]
    specs = [[smem] * len(x) + [vmem] * len(y) for x, y in zip(scalars, arrays)]

    def taken(refs, lists):
        parts = []
        for items in lists:
            parts.append(refs[: len(items)])
            refs = refs[len(items) :]
        return parts, refs

    def body(*refs):
        in_refs, refs = taken(refs, ins)
        out_refs, refs = taken(refs[len(after) :], outs)
        scratch_refs, _ = taken(refs, scratch)
        for kernel, *parts in zip(kernels, in_refs, out_refs, scratch_refs):
            kernel(*parts[0], *parts[1], *parts[2])

    moved = sum(x.size * x.dtype.itemsize for x in sum(ins, []) + sum(outs, []))
    results = pl.pallas_call(
        body,
        out_shape=sum(outs, []),
        in_specs=sum(specs, []) + [anywhere] * len(after),
        out_specs=[vmem] * len(sum(outs, [])),
        scratch_shapes=sum(scratch, []),
        compiler_params=pltpu.CompilerParams(vmem_limit_bytes=limit * 2**20),
        cost_estimate=pl.CostEstimate(flops=flops, bytes_accessed=moved, transcendentals=0),
    )(*sum(ins, []), *after)
    results, _ = taken(results, outs)
    return results[0] if len(jobs) == 1 else results


def finished(layer, step, modes, halves, probe, slices, like, after):
    vmem = pl.BlockSpec(memory_space=pltpu.VMEM)
    anywhere = pl.BlockSpec(memory_space=pl.ANY)
    inputs = [*halves, probe, *slices]

    def body(*refs):
        blocks, (out_probe, out_tile, new_ref, sems, probe_sems) = refs[3 : len(inputs)], refs[-5:]
        places = [layer(), 1 - layer()][: len(blocks)]
        copies = [
            pltpu.make_async_copy(block, out_tile.at[0, place], sems.at[at])
            for at, (block, place) in enumerate(zip(blocks, places))
        ]
        for copy in copies:
            copy.start()
        copies += probe_kernel(step, modes, *refs[:3], new_ref, out_probe, probe_sems)
        for copy in copies:
            copy.wait()

    return pl.pallas_call(
        body,
        out_shape=[shape_of(f32, *probe.shape), like],
        in_specs=[vmem] * len(inputs) + [anywhere] * len(after),
        out_specs=[anywhere, anywhere],
        scratch_shapes=[
            pltpu.VMEM(probe.shape, f32),
            pltpu.SemaphoreType.DMA((2,)),
            pltpu.SemaphoreType.DMA((16,)),
        ],
        compiler_params=pltpu.CompilerParams(vmem_limit_bytes=8 * 2**20),
        cost_estimate=pl.CostEstimate(
            flops=4 * probe.size, bytes_accessed=12 * probe.size, transcendentals=0
        ),
    )(*inputs, *after)


def shape_of(kind, *dims):
    return jax.ShapeDtypeStruct(dims, kind)


def gathered_message(patterns, offsets, counts):
    pixels = patterns.shape[4]
    all_counts = lax.all_gather(counts[0, 0], "pos")
    ends = jnp.cumsum(all_counts)
    rank = lax.axis_index("pos")
    source = jnp.sum((ends <= rank).astype(jnp.int32))
    slot = rank - (ends[source] - all_counts[source])
    spot = lax.all_gather(offsets[0, 0], "pos")[source, slot]
    pattern = lax.all_gather(patterns[0, 0], "pos")[source, slot]
    at = lax.broadcasted_iota(jnp.int32, (16, pixels), 0)
    rows = jnp.where(at == 0, spot[0], jnp.where(at == 1, spot[1], 0))
    return jnp.concatenate([pattern, rows.astype(bf16)], axis=0)


def fold_kernel(group, keep_ref, *refs):
    blocks = refs[-1]
    got = len(refs) - 1 - blocks.shape[0]
    arrived, keep_out, give_outs = refs[:got], refs[got], refs[got + 1 : -1]
    total = keep_ref[...].astype(f32)
    if arrived[0].shape != keep_ref.shape:
        total += jnp.concatenate([ref[...].astype(f32) for ref in arrived], axis=0)
    else:
        for ref in arrived:
            total += ref[...].astype(f32)
    size = blocks.shape[1]
    for block in range(blocks.shape[0]):
        blocks[block] = total[block * size : (block + 1) * size]
    here = place_of(group)
    keep_out[...] = blocks[here]
    for distance, ref in enumerate(give_outs, 1):
        ref[...] = blocks[here ^ distance].astype(bf16)


def add_kernel(keep_ref, *refs):
    total = keep_ref[...].astype(f32)
    for ref in refs[:-1]:
        total += ref[...].astype(f32)
    refs[-1][...] = total.astype(bf16)


def place_kernel(group, *refs):
    arrived, out_ref, blocks = refs[:-2], refs[-2], refs[-1]
    here = place_of(group)
    for distance, ref in enumerate(arrived):
        blocks[here ^ distance] = ref[...]
    size = blocks.shape[1]
    for block in range(blocks.shape[0]):
        out_ref[pl.ds(block * size, size), :] = blocks[block]


def probe_kernel(step, modes, mine_ref, other_ref, probe_ref, new_ref, out_hbm, sems):
    core = place_of(core_group())
    lane_tiles = 2
    n = mine_ref.shape[0]
    stride = lane_tiles * modes
    pieces = sems.shape[0] // 2
    size = n // pieces
    copies = []
    for part in range(2):
        for piece in range(pieces):
            at = pl.ds(piece * size, size)
            mine, other = mine_ref[at, :].astype(f32), other_ref[at, :].astype(f32)
            total = jnp.where(core == part, mine, other)
            start = (part * n + piece * size) * stride
            for mode in range(modes):
                for tile in range(lane_tiles):
                    lane = (mode * lane_tiles + tile) * 128
                    where = pl.ds(start + tile * modes + mode, size, stride=stride)
                    new_ref[where, :] = probe_ref[where, :] - step * total[:, lane : lane + 128]
            rows = pl.ds(start, size * stride)
            copy = pltpu.make_async_copy(
                new_ref.at[rows, :], out_hbm.at[rows, :], sems.at[len(copies)]
            )
            copy.start()
            copies.append(copy)
    return copies


def exchange_groups():
    tiles, owners = lax.axis_size("tile"), lax.axis_size("pos")
    bits = [1 << bit for bit in range(owners.bit_length() - 1)]
    bits += [owners << bit for bit in range(1, tiles.bit_length() - 1)]
    return [bits[at : at + 2] for at in range(0, len(bits), 2)]


def swap_with(x, group, distance):
    mask = sum(bit for at, bit in enumerate(group) if distance >> at & 1)
    devices = lax.axis_size("tile") * lax.axis_size("pos")
    return lax.ppermute(x, ("tile", "pos"), [(i, i ^ mask) for i in range(devices)])


def joined(group, x, arrived):
    blocks = 1 << len(group)
    return job(
        lambda *refs: place_kernel(group, *refs),
        [shape_of(bf16, x.shape[0] * blocks, x.shape[1])],
        [x] + arrived,
        scratch=[pltpu.VMEM((blocks,) + x.shape, bf16)],
    )


def added(x, arrived):
    return job(add_kernel, [shape_of(bf16, *x.shape)], [x] + arrived)


def swapped(x, group):
    return [swap_with(x, group, at) for at in range(1, 1 << len(group))]


def folded(group, keep, arrived):
    blocks = 1 << len(group)
    size, width = keep.shape[0] // blocks, keep.shape[1]
    return job(
        lambda *refs: fold_kernel(group, *refs),
        [shape_of(f32, size, width)] + [shape_of(bf16, size, width)] * (blocks - 1),
        [keep] + arrived,
        scratch=[pltpu.VMEM((blocks, size, width), f32)],
    )


def shards(tile_object, probe_modes, patterns, offsets, counts):
    _, pixels, modes, _ = probe_modes.shape
    width = modes * pixels
    lane_tiles = pixels // 128
    prop, dft = build_tables(pixels)
    tile = shape_of(bf16, 2, pixels, pixels)
    planes = shape_of(f32, 2, pixels, width)
    probe = probe_modes.reshape(2, pixels, modes, lane_tiles, 128)
    probe = probe.transpose(0, 1, 3, 2, 4).reshape(-1, 128)

    own = [tile_object[0, 0], tile_object[0, 1]]
    below0 = from_behind(own[0], -1, 0)
    right = from_behind(tile_object[0], 0, -1)
    exchanged = lax.axis_size("pos") == patterns.shape[2]
    message = shape_of(bf16, pixels + 16, pixels)
    own1, mine, sent = run(
        job(
            message_kernel,
            [tile, message, message],
            [own[1], patterns],
            scalars=[offsets, counts if exchanged else jnp.zeros_like(counts)],
        ),
        limit=4,
        after=[own[0]],
    )
    probe_planes, table = run(
        job(ready_kernel, [planes, shape_of(bf16, *prop.shape)], [probe, prop]),
        limit=8,
        after=[own1],
    )
    below1 = from_behind(own1, -1, 0)
    if exchanged:
        sent = lax.ppermute(sent, "pos", [(i, 1 - i) for i in range(2)])
    else:
        sent = gathered_message(patterns, offsets, counts)
    diag0 = from_behind(below0, 0, -1)
    diag1 = from_behind(below1, 0, -1)
    near, arrive = run(
        job(
            arrive_kernel,
            [tile, planes],
            [mine, sent, own[0], right, below0, diag0, probe_planes, table],
        ),
        flops=1_500_000_000,
        limit=16,
    )
    half = shape_of(bf16, pixels, width)
    quarter = shape_of(bf16, pixels // 2, width)
    grads = pltpu.VMEM((2, 2, pixels, pixels), bf16)
    this_layer = (lambda: lax.axis_index("pos")) if exchanged else (lambda: 0)
    kept, given, keep, *gives = run(
        job(
            lambda *refs: gradient_kernel(*refs, layer=this_layer),
            [tile, tile, half, quarter, quarter],
            [mine, sent, own1, right, below1, diag1, near, arrive, probe_planes, table, dft],
            scratch=[grads, pltpu.VMEM((2, pixels, width), bf16)],
        ),
        flops=4_000_000_000,
        limit=16,
    )

    swap = [(i, 1 - i) for i in range(2)]
    real = shape_of(f32, 2, pixels, pixels)
    like = shape_of(bf16, *tile_object.shape)

    def laid_out(patch, got, after, flops):
        return run(
            job(spread_kernel, [real, real, tile, tile], [mine, sent, patch, got]),
            limit=16,
            after=after,
            flops=flops,
        )

    core, groups = core_group(), exchange_groups()
    if exchanged:
        got = lax.ppermute(given, "pos", swap)
    arrived = [swap_with(x, core, 1) for x in gives]
    scattered = []
    while len(groups) > 1 and keep.shape[0] >> len(groups[0]) >= 16:
        group, groups = groups[0], groups[1:]
        keep, *gives = run(folded(group, keep, arrived))
        arrived = [swap_with(x, group, at) for at, x in enumerate(gives, 1)]
        scattered.append(group)
    first, second, *others = [[bit] for group in groups for bit in group]
    if exchanged:
        home, below, to_right, to_diag = laid_out(kept, got, [keep], LATE[0])
        from_left = [from_behind(x, 0, 1) for x in (to_right, to_diag)]
    (total,) = run(added(keep, arrived), after=[to_right] if exchanged else [], flops=LATE[1])
    (total,) = run(added(total, swapped(total, first)), flops=LATE[2])
    arrived = swapped(total, second)
    if exchanged:
        home, down = run(
            job(beside_kernel, [real, tile], [home, below, *from_left]),
            after=[total],
            flops=LATE[3],
        )
        above = from_behind(down, 1, 0)
    (total,) = run(added(total, arrived), after=[down] if exchanged else [], flops=LATE[4])
    for group in others:
        (total,) = run(added(total, swapped(total, group)))
    arrived = swapped(total, scattered[-1])
    if exchanged:
        (this_slice,) = run(
            job(
                lambda *refs: slice_kernel(this_layer, *refs),
                [tile],
                [own[0], own1, home, above],
            ),
            after=[total],
            flops=LATE[5],
        )
        other_slice = lax.ppermute(this_slice, "pos", swap)
    (total,) = run(
        joined(scattered[-1], total, arrived),
        after=[this_slice] if exchanged else [],
        flops=LATE[6],
    )
    for group in reversed(scattered[:-1]):
        (total,) = run(joined(group, total, swapped(total, group)))
    other_half = swap_with(total, core, 1)
    positions_all = lax.axis_size("tile") * lax.axis_size("pos") * (patterns.shape[2] // 2)
    step = probe_rate / math.sqrt(positions_all)
    halves = (total, other_half)
    if exchanged:
        token = run(
            job(token_kernel, [shape_of(f32, 8, 128)], []),
            after=[total, other_slice],
            flops=LATE[7],
        )
        slices = (this_slice, other_slice)
        new_probe, new_object = finished(this_layer, step, modes, halves, probe, slices, like, token)
    else:
        new_probe, _ = finished(this_layer, step, modes, halves, probe, (), like, ())
        slices = []
        for patch_grad, old in ((kept, own[0]), (given, own1)):
            home, below, to_right, to_diag = laid_out(patch_grad, jnp.zeros_like(kept), [], 0)
            from_left = [from_behind(x, 0, 1) for x in (to_right, to_diag)]
            home, down = run(job(beside_kernel, [real, tile], [home, below, *from_left]))
            grad = lax.psum(home + from_behind(down, 1, 0).astype(f32), "pos")
            slices.append((old.astype(f32) - object_rate * grad).astype(bf16))
        new_object = jnp.stack(slices)[None]
    new_probe = new_probe.reshape(2, pixels, lane_tiles, modes, 128).transpose(0, 1, 3, 2, 4)
    return (new_object, new_probe.reshape(probe_modes.shape))


def solution(mesh):
    placed = (
        P("tile", None, None, None, None),
        P(),
        P("tile", "pos", None, None, None),
        P("tile", "pos", None, None),
        P("tile", "pos"),
    )
    return jax.shard_map(
        shards,
        mesh=mesh,
        in_specs=placed,
        out_specs=(P("tile", None, None, None, None), P()),
        check_vma=False,
    )
```
